32 devices in a mesh: fsdp: 8 (over z, y), dp: 4 (over x, core).
Axes of the slice: x: 2, y: 2, z: 4, core: 2. Of those that a mesh axis runs over, the one named last changes fastest.
Arguments:
- tokens: bfloat16 [32768, 768], P(('fsdp', 'dp')), may hold values from -6 to 6
- cotangent: bfloat16 [32768, 768], P(('fsdp', 'dp')), may hold values from -6 to 6
- lengths: int32 [128], P(('fsdp', 'dp')), may hold values from 65 to 256, as said below
- buckets: int32 [128], P(('fsdp', 'dp')), may hold values from 0 to 1, as said below
- qkv_weight: bfloat16 [768, 2304], P('fsdp', 'dp'), may hold values from -0.21875 to 0.21875
- query_value_bias: bfloat16 [1536], P('fsdp'), may hold values from -1.5 to 1.5
- out_weight: bfloat16 [768, 768], P('fsdp', 'dp'), may hold values from -0.21875 to 0.21875
- out_bias: bfloat16 [768], P('fsdp'), may hold values from -1.5 to 1.5
- up_weight: bfloat16 [768, 3072], P('fsdp', 'dp'), may hold values from -0.21875 to 0.21875
- up_bias: bfloat16 [3072], P('fsdp'), may hold values from -1.5 to 1.5
- down_weight: bfloat16 [3072, 768], P('fsdp', 'dp'), may hold values from -0.109375 to 0.109375
- down_bias: bfloat16 [768], P('fsdp'), may hold values from -1.5 to 1.5
- first_gain: bfloat16 [768], P('fsdp'), may hold values from 0.5 to 1.5
- first_shift: bfloat16 [768], P('fsdp'), may hold values from -1.5 to 1.5
- mix_gain: bfloat16 [768], P('fsdp'), may hold values from 0.5 to 1.5
- mix_shift: bfloat16 [768], P('fsdp'), may hold values from -1.5 to 1.5
- second_gain: bfloat16 [768], P('fsdp'), may hold values from 0.5 to 1.5
- second_shift: bfloat16 [768], P('fsdp'), may hold values from -1.5 to 1.5
- hidden_gain: bfloat16 [3072], P('fsdp'), may hold values from 0.5 to 1.5
- hidden_shift: bfloat16 [3072], P('fsdp'), may hold values from -1.5 to 1.5
- head_scale: bfloat16 [12], replicated, may hold values from 0.5 to 2
- position_table: bfloat16 [1536, 12], P('fsdp'), may hold values from -4 to 4
Outputs:
- result_tokens: bfloat16 [32768, 768], P(('fsdp', 'dp'))
- input_grad: bfloat16 [32768, 768], P(('fsdp', 'dp'))
- qkv_weight_grad: float32 [768, 2304], P('fsdp', 'dp')
- query_value_bias_grad: float32 [1536], P('fsdp')
- out_weight_grad: float32 [768, 768], P('fsdp', 'dp')
- out_bias_grad: float32 [768], P('fsdp')
- up_weight_grad: float32 [768, 3072], P('fsdp', 'dp')
- up_bias_grad: float32 [3072], P('fsdp')
- down_weight_grad: float32 [3072, 768], P('fsdp', 'dp')
- down_bias_grad: float32 [768], P('fsdp')
- first_gain_grad: float32 [768], P('fsdp')
- first_shift_grad: float32 [768], P('fsdp')
- mix_gain_grad: float32 [768], P('fsdp')
- mix_shift_grad: float32 [768], P('fsdp')
- second_gain_grad: float32 [768], P('fsdp')
- second_shift_grad: float32 [768], P('fsdp')
- hidden_gain_grad: float32 [3072], P('fsdp')
- hidden_shift_grad: float32 [3072], P('fsdp')
- head_scale_grad: float32 [12], replicated
- position_table_grad: float32 [1536, 12], P('fsdp')
The draws below stay inside these ranges and needn't reach their ends.
Inputs may be any that keep to these rules, and one draw needn't show every extreme that they name: `lengths`: sequence s holds its image's patches first (64 if buckets[s] is 0, 225 if it is 1) and one or more text tokens after them; one sequence in every draw has all 256 slots live. `buckets`: 0 for an image of 64 patches on an 8 x 8 grid, 1 for 225 patches on a 15 x 15 grid.
All inputs are finite; a program needn't handle non-finite values.
Results may differ from the reference program's by a relative error of at most 0.015.
Values may be sent and summed in bfloat16 or wider, within the bound.
A program may use at most 256 MiB of HBM per device.

```python
import math
import jax
import jax.numpy as jnp
from jax import lax

D = 768
HEADS = 12
HEAD_DIM = 64
FF = 3072
SLOT = 256
TABLE = 1536
SEQS = 128
TOKENS = 32768


def draw_pair(key):
    bucket_key, text_key, pick_key = jax.random.split(key, 3)
    bucket_ids = jax.random.randint(bucket_key, (SEQS,), 0, 2)
    patches = jnp.where(bucket_ids == 0, 64, 225)
    text_count = jax.random.randint(text_key, (SEQS,), 1, SLOT - patches + 1)
    chosen = jax.random.randint(pick_key, (), 0, SEQS)
    filled = jnp.where(jnp.arange(SEQS) == chosen, SLOT, patches + text_count)
    return (bucket_ids.astype(jnp.int32), filled.astype(jnp.int32))


def draw_lengths(key, part):
    return draw_pair(key)[1]


def draw_buckets(key, part):
    return draw_pair(key)[0]


def block_scale(stream_key, dims, cuts, smallest, top_value):
    def one(axis_at, blocks):
        draws = jax.random.uniform(jax.random.fold_in(jax.random.fold_in(stream_key, 6), axis_at), (blocks,), jnp.float32, smallest / len(cuts), top_value / len(cuts))
        return jnp.repeat(jnp.exp(draws), dims[axis_at] // blocks).reshape((-1,) + (1,) * (len(dims) - axis_at - 1))

    level = one(*cuts[0])
    for cut in cuts[1:]:
        level = level * one(*cut)
    return level


def centred(rng, shape, scale, most, cuts=(), held_as=jnp.bfloat16):
    drawn = scale * jax.random.normal(rng, shape, jnp.float32)
    if cuts:
        drawn = drawn * block_scale(rng, shape, cuts, -0.22, 0.18)
    return jnp.clip(drawn, -most, most).astype(held_as)


def setup_inputs(seed: int = 0) -> dict:
    arg_keys = jax.random.split(jax.random.key(seed), 23)
    tokens = centred(arg_keys[0], (TOKENS, D), 1.0, 6.0, ((0, 32),))
    cotangent = centred(arg_keys[1], (TOKENS, D), 1.0, 6.0, ((0, 32),))
    lengths = draw_lengths(jax.random.fold_in(arg_keys[22], 71), 0)
    buckets = draw_buckets(jax.random.fold_in(arg_keys[22], 71), 0)
    qkv_weight = centred(arg_keys[4], (D, 3 * D), D ** -0.5, 0.21875, ((0, 8), (1, 4)))
    query_value_bias = centred(arg_keys[5], (2 * D,), 0.3, 1.5, ((0, 8),))
    out_weight = centred(arg_keys[6], (D, D), D ** -0.5, 0.21875, ((0, 8), (1, 4)))
    out_bias = centred(arg_keys[7], (D,), 0.3, 1.5, ((0, 8),))
    up_weight = centred(arg_keys[8], (D, FF), D ** -0.5, 0.21875, ((0, 8), (1, 4)))
    up_bias = centred(arg_keys[9], (FF,), 0.3, 1.5, ((0, 8),))
    down_weight = centred(arg_keys[10], (FF, D), FF ** -0.5, 0.109375, ((0, 8), (1, 4)))
    down_bias = centred(arg_keys[11], (D,), 0.3, 1.5, ((0, 8),))
    first_gain = jnp.clip(1.0 + 0.1 * jax.random.normal(arg_keys[12], (D,), jnp.float32), 0.5, 1.5).astype(jnp.bfloat16)
    first_shift = centred(arg_keys[13], (D,), 0.3, 1.5, ((0, 8),))
    mix_gain = jnp.clip(1.0 + 0.1 * jax.random.normal(arg_keys[14], (D,), jnp.float32), 0.5, 1.5).astype(jnp.bfloat16)
    mix_shift = centred(arg_keys[15], (D,), 0.3, 1.5, ((0, 8),))
    second_gain = jnp.clip(1.0 + 0.1 * jax.random.normal(arg_keys[16], (D,), jnp.float32), 0.5, 1.5).astype(jnp.bfloat16)
    second_shift = centred(arg_keys[17], (D,), 0.3, 1.5, ((0, 8),))
    hidden_gain = jnp.clip(1.0 + 0.1 * jax.random.normal(arg_keys[18], (FF,), jnp.float32), 0.5, 1.5).astype(jnp.bfloat16)
    hidden_shift = centred(arg_keys[19], (FF,), 0.3, 1.5, ((0, 8),))
    head_scale = jnp.clip(jnp.exp(jax.random.uniform(arg_keys[20], (HEADS,), jnp.float32, math.log(0.5), math.log(2.0))), 0.5, 2.0).astype(jnp.bfloat16)
    position_table = centred(arg_keys[21], (TABLE, HEADS), 1.0, 4.0, ((0, 8),))
    return dict(tokens=tokens, cotangent=cotangent, lengths=lengths, buckets=buckets, qkv_weight=qkv_weight, query_value_bias=query_value_bias, out_weight=out_weight, out_bias=out_bias, up_weight=up_weight, up_bias=up_bias, down_weight=down_weight, down_bias=down_bias, first_gain=first_gain, first_shift=first_shift, mix_gain=mix_gain, mix_shift=mix_shift, second_gain=second_gain, second_shift=second_shift, hidden_gain=hidden_gain, hidden_shift=hidden_shift, head_scale=head_scale, position_table=position_table)


norm_epsilon = 1e-05
masked_score = -1000000000.0

@jax.custom_vjp
def low(v):
    return lax.optimization_barrier(v.astype(jnp.bfloat16)).astype(jnp.float32)

@jax.custom_vjp
def low_back(v):
    return v

def low_keep(v):
    return (low(v), None)

def low_pass(kept, grad):
    return (grad,)

def back_keep(v):
    return (v, None)

def back_low(kept, grad):
    return (low(grad),)
low.defvjp(low_keep, low_pass)
low_back.defvjp(back_keep, back_low)

def layer_norm(values, gain, shift):
    center = values - lax.optimization_barrier(jnp.mean(values, -1, keepdims=True))
    spread = lax.optimization_barrier(jnp.mean(center * center, -1, keepdims=True))
    return center * lax.rsqrt(spread + norm_epsilon) * gain + shift

def index_map(patches, side):
    row_pos = jnp.arange(SLOT, dtype=jnp.int32)[:, None]
    col_pos = jnp.arange(SLOT, dtype=jnp.int32)[None, :]
    textual = col_pos - row_pos + SLOT - 1
    down_step = col_pos // side - row_pos // side
    across = col_pos % side - row_pos % side
    visual = (down_step + 15) * 32 + across + 15 + 2 * SLOT
    inside = (row_pos < patches) & (col_pos < patches)
    return jnp.where(inside, visual, textual).astype(jnp.int32)

def position_bias(table, buckets):
    small_grid = jnp.transpose(table[index_map(64, 8)], (2, 0, 1))
    large_grid = jnp.transpose(table[index_map(225, 15)], (2, 0, 1))
    return jnp.where((buckets == 0)[:, None, None, None], small_grid[None], large_grid[None])

def matmul(left, right):
    return jnp.dot(left, right, precision=lax.Precision.HIGHEST)

def group_layer(params, inputs, lengths, buckets):
    qkv_weight, query_value_bias, out_weight, out_bias, up_weight, up_bias, down_weight, down_bias, first_gain, first_shift, mix_gain, mix_shift, second_gain, second_shift, hidden_gain, hidden_shift, head_scale, position_table = params
    count = lengths.shape[0]
    quad = (count, SLOT, HEADS, HEAD_DIM)
    scale = HEAD_DIM ** (-0.5)
    normed = low(layer_norm(inputs, first_gain, first_shift))
    zeros = jnp.zeros((D,), jnp.float32)
    projected = matmul(normed, qkv_weight) + jnp.concatenate([query_value_bias[:D], zeros, query_value_bias[D:]])
    query = low(low_back(projected[:, :D] * scale)).reshape(quad)
    keys = low(low_back(projected[:, D:2 * D])).reshape(quad)
    values = low(low_back(projected[:, 2 * D:])).reshape(quad)
    logits = low_back(jnp.einsum('sqhd,skhd->shqk', query, keys, precision=lax.Precision.HIGHEST))
    valid = (jnp.arange(SLOT, dtype=jnp.int32)[None, :] < lengths[:, None])[:, None, None, :]
    scores = jnp.where(valid, logits + position_bias(position_table, buckets), masked_score)
    shifted = jnp.exp(scores - lax.optimization_barrier(jnp.max(scores, -1, keepdims=True)))
    weights = shifted / lax.optimization_barrier(jnp.sum(shifted, -1, keepdims=True))
    attended = low_back(jnp.einsum('shqk,skhd->sqhd', low(weights), values, precision=lax.Precision.HIGHEST))
    mixed = low(layer_norm((attended * head_scale[None, None, :, None]).reshape(-1, D), mix_gain, mix_shift))
    branch = low_back(matmul(mixed, out_weight) + out_bias)
    middle = inputs + branch
    second = low(layer_norm(middle, second_gain, second_shift))
    hidden = low_back(matmul(second, up_weight) + up_bias)
    activated = low(layer_norm(jax.nn.gelu(hidden, approximate=False), hidden_gain, hidden_shift))
    return middle + low_back(matmul(activated, down_weight) + down_bias)

def reference(tokens, cotangent, lengths, buckets, qkv_weight, query_value_bias, out_weight, out_bias, up_weight, up_bias, down_weight, down_bias, first_gain, first_shift, mix_gain, mix_shift, second_gain, second_shift, hidden_gain, hidden_shift, head_scale, position_table):
    params = tuple((entry.astype(jnp.float32) for entry in (qkv_weight, query_value_bias, out_weight, out_bias, up_weight, up_bias, down_weight, down_bias, first_gain, first_shift, mix_gain, mix_shift, second_gain, second_shift, hidden_gain, hidden_shift, head_scale, position_table)))
    groups = SEQS // 16
    inputs = tokens.astype(jnp.float32).reshape(groups, 16 * SLOT, D)
    group_lengths = lengths.reshape(groups, 16)
    group_buckets = buckets.reshape(groups, 16)

    def forward(inputs, params):
        layer = jax.checkpoint(group_layer)
        return lax.map(lambda entry: layer(params, entry[0], entry[1], entry[2]), (inputs, group_lengths, group_buckets))
    outputs, pull = jax.vjp(forward, inputs, params)
    input_grad, grads = pull(cotangent.astype(jnp.float32).reshape(groups, 16 * SLOT, D))
    return (outputs.reshape(TOKENS, D).astype(jnp.bfloat16), input_grad.reshape(TOKENS, D).astype(jnp.bfloat16), grads[0], grads[1], grads[2], grads[3], grads[4], grads[5], grads[6], grads[7], grads[8], grads[9], grads[10], grads[11], grads[12], grads[13], grads[14], grads[15], grads[16], grads[17])
```

```python
import functools

import jax
import jax.numpy as jnp
from jax import lax
from jax.experimental import pallas as pl
from jax.experimental.pallas import tpu as pltpu
from jax.sharding import PartitionSpec as P

D = 768
HEADS = 12
PAIRS = 6
HEAD_DIM = 64
FF = 3072
SLOT = 256
TABLE = 1536

EPS = 1e-05
MASKED = -1000000000.0
F32 = jnp.float32
BF16 = jnp.bfloat16
VMEM_LIMIT = 60 * 2**20


def params(**more):
    return pltpu.CompilerParams(vmem_limit_bytes=VMEM_LIMIT, **more)


def nn(left, right):
    return lax.dot_general(left, right, (((1,), (0,)), ((), ())), preferred_element_type=F32)


def nt(left, right):
    return lax.dot_general(left, right, (((1,), (1,)), ((), ())), preferred_element_type=F32)


def standardize(values):
    center = values - jnp.mean(values, -1, keepdims=True)
    inverse = lax.rsqrt(jnp.mean(center * center, -1, keepdims=True) + EPS)
    return center * inverse, inverse


def norm_back(grad, unit, inverse):
    return inverse * (
        grad
        - jnp.mean(grad, -1, keepdims=True)
        - unit * jnp.mean(grad * unit, -1, keepdims=True)
    )


def column_sum(values):
    return jnp.sum(values, 0, keepdims=True)


def split_low(values):
    high = values.astype(BF16)
    return high, (values - high.astype(F32)).astype(BF16)


def compaction(side, lanes):
    plane = lax.broadcasted_iota(jnp.int32, (1024, lanes), 0)
    lane = lax.broadcasted_iota(jnp.int32, (1024, lanes), 1)
    across = plane & 31
    return ((lane == side * (plane >> 5) + across) & (across < side)).astype(F32).astype(BF16)


def inside_grid(patches):
    row = lax.broadcasted_iota(jnp.int32, (SLOT, SLOT), 0)
    col = lax.broadcasted_iota(jnp.int32, (SLOT, SLOT), 1)
    return (row < patches) & (col < patches)


def store_tiles(ref, values):
    for k in range(ref.shape[0]):
        ref[k] = values[:, 128 * k : 128 * k + 128]


def load_tiles(ref):
    return jnp.concatenate([ref[k] for k in range(ref.shape[0])], 1)


def load_strided(ref, first, count):
    return jnp.concatenate(
        [ref[k, pl.ds(first, count, 16), :] for k in range(ref.shape[0])], 1
    )


def store_strided(ref, first, values):
    for k in range(ref.shape[0]):
        ref[k, pl.ds(first, values.shape[0], 16), :] = values[:, 128 * k : 128 * k + 128]


def bias_kernel(table_ref, out_ref, wall_small, wall_large, visual):
    plane = table_ref[:, 512:]
    shifted = [pltpu.roll(plane, (ic - 15) % 1024, 1) for ic in range(16)]
    stack = jnp.concatenate(shifted, 0).astype(BF16)
    store_tiles(wall_large, nn(stack, compaction(15, 512)))
    store_tiles(wall_small, nn(stack[:128], compaction(8, 256)))
    visual[...] = jnp.zeros_like(visual)

    def one_head(h, carry):
        line = jnp.broadcast_to(table_ref[pl.ds(h, 1), :512], (SLOT, 512))
        textual = pltpu.roll(line, 257, 1, stride=1, stride_axis=0)[:, :SLOT]
        large = load_strided(wall_large, h, 16)
        for ir in range(15):
            visual[pl.ds(ir * 15, 16), :] = pltpu.roll(large, 512 - (15 - ir) * 15, 1)[:, :SLOT]
        out_ref[1, h] = jnp.where(inside_grid(225), visual[...], textual).astype(BF16)
        small = load_strided(wall_small, h, 8)
        rows = [pltpu.roll(small, 256 - (15 - ir) * 8, 1) for ir in range(8)]
        grid = jnp.concatenate(rows + [jnp.zeros((192, SLOT), F32)], 0)
        out_ref[0, h] = jnp.where(inside_grid(64), grid, textual).astype(BF16)
        return carry

    lax.fori_loop(0, HEADS, one_head, 0)


def build_bias(table):
    return pl.pallas_call(
        bias_kernel,
        out_shape=jax.ShapeDtypeStruct((2, HEADS, SLOT, SLOT), BF16),
        scratch_shapes=[
            pltpu.VMEM((2, 128, 128), F32),
            pltpu.VMEM((4, 256, 128), F32),
            pltpu.VMEM((SLOT, SLOT), F32),
        ],
        compiler_params=params(),
        name="build_bias",
    )(table)


def table_grad_kernel(grid_ref, out_ref, wall_small, wall_large):
    wall_small[...] = jnp.zeros_like(wall_small)
    wall_large[...] = jnp.zeros_like(wall_large)
    row = lax.broadcasted_iota(jnp.int32, (SLOT, SLOT), 0)
    col = lax.broadcasted_iota(jnp.int32, (SLOT, SLOT), 1)
    flip = (row + col == SLOT - 1).astype(F32).astype(BF16)
    lane = lax.broadcasted_iota(jnp.int32, (16, SLOT), 1)

    out_ref[...] = jnp.zeros_like(out_ref)

    def one_head(h, carry):
        textual = jnp.where(inside_grid(64), 0.0, grid_ref[0, h]) + jnp.where(
            inside_grid(225), 0.0, grid_ref[1, h]
        )
        high, low = split_low(textual)
        flipped = nn(flip, high) + nn(flip, low)
        wide = jnp.concatenate([flipped, jnp.zeros((SLOT, SLOT), F32)], 1)
        out_ref[pl.ds(h, 1), :512] = column_sum(
            pltpu.roll(wide, 0, 1, stride=1, stride_axis=0)
        )
        total = jnp.zeros((16, 512), F32)
        for ir in range(15):
            part = jnp.where(lane < 225, grid_ref[1, h, pl.ds(ir * 15, 16), :], 0.0)
            part = jnp.concatenate([part, jnp.zeros((16, SLOT), F32)], 1)
            total = total + pltpu.roll(part, (15 - ir) * 15, 1)
        store_strided(wall_large, h, total)
        total = jnp.zeros((8, SLOT), F32)
        for ir in range(8):
            part = jnp.where(lane[:8] < 64, grid_ref[0, h, pl.ds(ir * 8, 8), :], 0.0)
            total = total + pltpu.roll(part, (15 - ir) * 8, 1)
        store_strided(wall_small, h, total)
        return carry

    lax.fori_loop(0, HEADS, one_head, 0)
    high, low = split_low(load_tiles(wall_large))
    spread = compaction(15, 512)
    large = nt(high, spread) + nt(low, spread)
    high, low = split_low(load_tiles(wall_small))
    spread = compaction(8, 256)
    small = nt(high, spread) + nt(low, spread)
    plane = jnp.zeros((16, 1024), F32)
    for ic in range(15):
        part = large[ic * 16 : ic * 16 + 16]
        if ic < 8:
            part = part + small[ic * 16 : ic * 16 + 16]
        plane = plane + pltpu.roll(part, 15 - ic, 1)
    out_ref[:, 512:] = plane


def table_grad(grids):
    return pl.pallas_call(
        table_grad_kernel,
        out_shape=jax.ShapeDtypeStruct((16, TABLE), F32),
        scratch_shapes=[pltpu.VMEM((2, 128, 128), F32), pltpu.VMEM((4, 256, 128), F32)],
        compiler_params=params(),
        name="table_grad",
    )(grids)


def attention_kernel(
    lengths, buckets, x_ref, vec_ref, weight_ref, qkv_bias_ref, bias_ref,
    normed_ref, qkv_ref, probs_ref, attended_ref,
):
    count = x_ref.shape[0] // SLOT

    def one_block(b, carry):
        rows = pl.ds(pl.multiple_of(b * SLOT, SLOT), SLOT)
        unit, inverse = standardize(x_ref[rows, :].astype(F32))
        normed_ref[rows, :] = (unit * vec_ref[0:1, :] + vec_ref[1:2, :]).astype(BF16)
        return carry

    lax.fori_loop(0, count, one_block, 0)

    def one_panel(n, carry):
        cols = pl.ds(pl.multiple_of(n * 256, 256), 256)
        out = nn(normed_ref[...], weight_ref[:, cols]) + qkv_bias_ref[:, cols]
        out = (out * jnp.where(n < 3, HEAD_DIM ** (-0.5), 1.0)).astype(BF16)
        qkv_ref[2 * n] = out[:, :128]
        qkv_ref[2 * n + 1] = out[:, 128:]
        return carry

    lax.fori_loop(0, 9, one_panel, 0)
    lane = lax.broadcasted_iota(jnp.int32, (SLOT, 128), 1)
    key_slot = lax.broadcasted_iota(jnp.int32, (SLOT, SLOT), 1)

    def one_unit(step, carry):
        pair = step // count
        s = step % count
        rows = pl.ds(pl.multiple_of(s * SLOT, SLOT), SLOT)
        query = qkv_ref[pair, rows, :]
        keys = qkv_ref[PAIRS + pair, rows, :]
        values = qkv_ref[2 * PAIRS + pair, rows, :]
        live = key_slot < lengths[s]
        total = jnp.zeros((SLOT, 128), F32)
        for half in range(2):
            mine = (lane >= 64 * half) & (lane < 64 * half + 64)
            logits = nt(jnp.where(mine, query, 0), keys)
            bias = bias_ref[buckets[s], 2 * pair + half].astype(F32)
            scores = jnp.where(live, logits + bias, MASKED)
            shifted = jnp.exp(scores - jnp.max(scores, -1, keepdims=True))
            probs = (shifted / jnp.sum(shifted, -1, keepdims=True)).astype(BF16)
            probs_ref[2 * pair + half, s] = probs
            total = total + nn(probs, jnp.where(mine, values, 0))
        attended_ref[rows, pl.ds(pl.multiple_of(pair * 128, 128), 128)] = total
        return carry

    lax.fori_loop(0, PAIRS * count, one_unit, 0)


def attention(lengths, buckets, tokens, vecs, weight, qkv_bias, bias):
    rows = tokens.shape[0]
    count = rows // SLOT
    smem = pl.BlockSpec(memory_space=pltpu.SMEM)
    vmem = pl.BlockSpec(memory_space=pltpu.VMEM)
    return pl.pallas_call(
        attention_kernel,
        in_specs=[smem, smem] + [vmem] * 5,
        out_shape=[
            jax.ShapeDtypeStruct((rows, D), BF16),
            jax.ShapeDtypeStruct((3 * PAIRS, rows, 128), BF16),
            jax.ShapeDtypeStruct((HEADS, count, SLOT, SLOT), BF16),
            jax.ShapeDtypeStruct((rows, D), F32),
        ],
        compiler_params=params(),
        name="attention_forward",
    )(lengths, buckets, tokens, vecs, weight, qkv_bias, bias)


PANEL = 512


def feed_kernel(
    x_ref, attended_ref, cot_ref, out_w, up_w, down_w, vec_ref, wide_ref, scale_ref,
    result_ref, mixed_ref, second_ref, act_ref, low_ref, branch_ref, middle_grad_ref,
    attended_low_ref, sums_ref, wide_sums_ref,
    gelu_ref, slope_ref, grad_ref,
):
    @pl.when(pl.program_id(0) == 0)
    def _():
        sums_ref[...] = jnp.zeros_like(sums_ref)
        wide_sums_ref[...] = jnp.zeros_like(wide_sums_ref)

    def add(row, values):
        sums_ref[row : row + 1, :] += column_sum(values)

    rows = x_ref.shape[0]
    attended = attended_ref[...]
    mix_unit, mix_inverse = standardize(attended * scale_ref[...])
    mixed = (mix_unit * vec_ref[2:3, :] + vec_ref[3:4, :]).astype(BF16)
    mixed_ref[...] = mixed
    middle = x_ref[...].astype(F32) + nn(mixed, out_w[...]) + vec_ref[6:7, :]
    second_unit, second_inverse = standardize(middle)
    second = (second_unit * vec_ref[4:5, :] + vec_ref[5:6, :]).astype(BF16)
    second_ref[...] = second
    cot = cot_ref[...]

    panels = [slice(n, n + PANEL) for n in range(0, FF, PANEL)]
    total = jnp.zeros((rows, 1), F32)
    for cols in panels:
        hidden = nn(second, up_w[:, cols]) + wide_ref[0:1, cols]
        cdf = 0.5 + 0.5 * lax.erf(hidden * 0.7071067811865476)
        gelu = hidden * cdf
        gelu_ref[:, cols] = gelu
        slope_ref[:, cols] = cdf + hidden * (jnp.exp(-0.5 * hidden * hidden) * 0.3989422804014327)
        total = total + jnp.sum(gelu, -1, keepdims=True)
    mean = total * (1.0 / FF)
    total = jnp.zeros((rows, 1), F32)
    for cols in panels:
        center = gelu_ref[:, cols] - mean
        total = total + jnp.sum(center * center, -1, keepdims=True)
    inverse = lax.rsqrt(total * (1.0 / FF) + EPS)
    result = middle + vec_ref[7:8, :]
    first = jnp.zeros((rows, 1), F32)
    second_moment = jnp.zeros((rows, 1), F32)
    for cols in panels:
        unit = (gelu_ref[:, cols] - mean) * inverse
        gelu_ref[:, cols] = unit
        act = (unit * wide_ref[1:2, cols] + wide_ref[2:3, cols]).astype(BF16)
        act_ref[:, cols] = act
        result = result + nt(act, down_w[:, cols])
        act_grad = nn(cot, down_w[:, cols])
        wide_sums_ref[1:2, cols] += column_sum(act_grad * unit)
        wide_sums_ref[2:3, cols] += column_sum(act_grad)
        grad = act_grad * wide_ref[1:2, cols]
        grad_ref[:, cols] = grad
        first = first + jnp.sum(grad, -1, keepdims=True)
        second_moment = second_moment + jnp.sum(grad * unit, -1, keepdims=True)
    result_ref[...] = result.astype(BF16)
    first = first * (1.0 / FF)
    second_moment = second_moment * (1.0 / FF)
    second_in = jnp.zeros((rows, D), F32)
    for cols in panels:
        grad = inverse * (grad_ref[:, cols] - first - gelu_ref[:, cols] * second_moment)
        low = (grad * slope_ref[:, cols]).astype(BF16)
        low_ref[:, cols] = low
        wide_sums_ref[0:1, cols] += column_sum(low.astype(F32))
        second_in = second_in + nt(low, up_w[:, cols])
    add(4, second_in * second_unit)
    add(5, second_in)
    cot_wide = cot.astype(F32)
    add(7, cot_wide)
    middle_grad = cot_wide + norm_back(second_in * vec_ref[4:5, :], second_unit, second_inverse)
    middle_grad_ref[...] = middle_grad
    branch = middle_grad.astype(BF16)
    branch_ref[...] = branch
    add(6, branch.astype(F32))
    mixed_in = nt(branch, out_w[...])
    add(2, mixed_in * mix_unit)
    add(3, mixed_in)
    grad = norm_back(mixed_in * vec_ref[2:3, :], mix_unit, mix_inverse)
    add(8, grad * attended)
    attended_low_ref[...] = (grad * scale_ref[...]).astype(BF16)


def feed_forward(tokens, attended, cotangent, out_w, up_w, down_w, vecs, wide, scales):
    rows = tokens.shape[0]
    tile = 256
    block = pl.BlockSpec((tile, D), lambda i: (i, 0))
    wide_block = pl.BlockSpec((tile, FF), lambda i: (i, 0))

    def whole(shape):
        return pl.BlockSpec(shape, lambda i: (0, 0), pipeline_mode=pl.Buffered(1))

    def held(shape):
        return pl.BlockSpec(shape, lambda i: (0, 0))

    return pl.pallas_call(
        feed_kernel,
        grid=(rows // tile,),
        in_specs=[block] * 3
        + [whole((D, D)), whole((D, FF)), whole((D, FF)), whole((8, D)), whole((8, FF)), whole((1, D))],
        out_specs=[block, block, block, wide_block, wide_block, block, block, block]
        + [held((16, D)), held((8, FF))],
        out_shape=[
            jax.ShapeDtypeStruct((rows, D), BF16),
            jax.ShapeDtypeStruct((rows, D), BF16),
            jax.ShapeDtypeStruct((rows, D), BF16),
            jax.ShapeDtypeStruct((rows, FF), BF16),
            jax.ShapeDtypeStruct((rows, FF), BF16),
            jax.ShapeDtypeStruct((rows, D), BF16),
            jax.ShapeDtypeStruct((rows, D), F32),
            jax.ShapeDtypeStruct((rows, D), BF16),
            jax.ShapeDtypeStruct((16, D), F32),
            jax.ShapeDtypeStruct((8, FF), F32),
        ],
        scratch_shapes=[pltpu.VMEM((tile, FF), F32)] * 3,
        compiler_params=params(dimension_semantics=("arbitrary",)),
        name="feed_forward",
    )(tokens, attended, cotangent, out_w, up_w, down_w, vecs, wide, scales)


def outer_kernel(left_ref, right_ref, out_ref, turned):
    @pl.when(pl.program_id(0) == 0)
    def _():
        turned[...] = left_ref[...].T

    out_ref[...] = nn(turned[...], right_ref[...]).astype(BF16)


def outer_product(left, right, panel):
    rows, width = left.shape
    cols = right.shape[1]
    return pl.pallas_call(
        outer_kernel,
        grid=(cols // panel,),
        in_specs=[
            pl.BlockSpec((rows, width), lambda i: (0, 0), pipeline_mode=pl.Buffered(1)),
            pl.BlockSpec((rows, panel), lambda i: (0, i)),
        ],
        out_specs=pl.BlockSpec((width, panel), lambda i: (0, i)),
        out_shape=jax.ShapeDtypeStruct((width, cols), BF16),
        scratch_shapes=[pltpu.VMEM((width, rows), BF16)],
        compiler_params=params(dimension_semantics=("arbitrary",)),
        name="weight_grad",
    )(left, right)


def attention_back_kernel(
    buckets, probs_ref, query_ref, keys_ref, values_ref, low_ref, normed_ref, x_ref, middle_ref,
    weight_q, weight_k, weight_v, vec_ref,
    input_grad_ref, grid_ref, weight_grad_ref, pair_ref, sums_ref,
    turned, first_in, proj_ref,
):
    count = x_ref.shape[0] // SLOT
    step = pl.program_id(0)

    @pl.when(step == 0)
    def _():
        turned[...] = normed_ref[...].T
        first_in[...] = jnp.zeros_like(first_in)

    grid_ref[...] = jnp.zeros_like(grid_ref)
    lane = lax.broadcasted_iota(jnp.int32, (SLOT, 128), 1)

    def one_sequence(s, carry):
        rows = pl.ds(pl.multiple_of(s * SLOT, SLOT), SLOT)
        query = query_ref[0, rows, :]
        keys = keys_ref[0, rows, :]
        values = values_ref[0, rows, :]
        grad = low_ref[rows, :]
        query_turned = query.T
        grad_turned = grad.T
        small = jnp.where(buckets[s] == 0, 1.0, 0.0)
        query_grad = jnp.zeros((SLOT, 128), F32)
        keys_parts = []
        values_parts = []
        for half in range(2):
            mine = (lane >= 64 * half) & (lane < 64 * half + 64)
            part = slice(64 * half, 64 * half + 64)
            low = probs_ref[half, s]
            probs = low.astype(F32)
            probs_grad = nt(jnp.where(mine, grad, 0), values)
            values_parts.append(nn(grad_turned[part], low))
            row_dot = jnp.sum(probs * probs_grad, -1, keepdims=True)
            scores_grad = probs * (probs_grad - row_dot)
            grid_ref[0, half] += scores_grad * small
            grid_ref[1, half] += scores_grad * (1.0 - small)
            scores_low = scores_grad.astype(BF16)
            query_grad = query_grad + nn(scores_low, jnp.where(mine, keys, 0))
            keys_parts.append(nn(query_turned[part], scores_low))
        proj_ref[rows, 0:128] = (query_grad * HEAD_DIM ** (-0.5)).astype(BF16)
        proj_ref[rows, 128:256] = jnp.concatenate(keys_parts, 0).T.astype(BF16)
        proj_ref[rows, 256:384] = jnp.concatenate(values_parts, 0).T.astype(BF16)
        return carry

    lax.fori_loop(0, count, one_sequence, 0)
    proj = proj_ref[...]
    weight_grad_ref[0] = nn(turned[...], proj).astype(BF16)
    pair_ref[0] = jnp.broadcast_to(column_sum(proj.astype(F32)), (8, 384))
    weights = jnp.concatenate([weight_q[...], weight_k[...], weight_v[...]], 1)
    first_in[...] += nt(proj, weights)

    @pl.when(step == PAIRS - 1)
    def _():
        sums_ref[...] = jnp.zeros_like(sums_ref)

        def one_block(b, carry):
            rows = pl.ds(pl.multiple_of(b * SLOT, SLOT), SLOT)
            unit, inverse = standardize(x_ref[rows, :].astype(F32))
            grad = first_in[rows, :]
            sums_ref[0:1, :] += column_sum(grad * unit)
            sums_ref[1:2, :] += column_sum(grad)
            back = norm_back(grad * vec_ref[0:1, :], unit, inverse)
            input_grad_ref[rows, :] = (middle_ref[rows, :] + back).astype(BF16)
            return carry

        lax.fori_loop(0, count, one_block, 0)


def attention_back(buckets, probs, qkv, attended_low, normed, tokens, middle_grad, weight, vecs):
    rows = tokens.shape[0]
    count = rows // SLOT

    def whole(shape):
        return pl.BlockSpec(shape, lambda i: (0,) * len(shape), pipeline_mode=pl.Buffered(1))

    def held(shape):
        return pl.BlockSpec(shape, lambda i: (0,) * len(shape))

    def panel(base):
        return pl.BlockSpec((1, rows, 128), lambda i: (base + i, 0, 0))

    def weight_panel(base):
        return pl.BlockSpec((D, 128), lambda i: (0, base + i))

    return pl.pallas_call(
        attention_back_kernel,
        grid=(PAIRS,),
        in_specs=[
            pl.BlockSpec(memory_space=pltpu.SMEM),
            pl.BlockSpec((2, count, SLOT, SLOT), lambda i: (i, 0, 0, 0)),
            panel(0), panel(PAIRS), panel(2 * PAIRS),
            pl.BlockSpec((rows, 128), lambda i: (0, i)),
            whole((rows, D)), whole((rows, D)), whole((rows, D)),
            weight_panel(0), weight_panel(PAIRS), weight_panel(2 * PAIRS),
            whole((8, D)),
        ],
        out_specs=[
            held((rows, D)),
            pl.BlockSpec((2, 2, SLOT, SLOT), lambda i: (0, i, 0, 0)),
            pl.BlockSpec((1, D, 384), lambda i: (i, 0, 0)),
            pl.BlockSpec((1, 8, 384), lambda i: (i, 0, 0)),
            held((8, D)),
        ],
        out_shape=[
            jax.ShapeDtypeStruct((rows, D), BF16),
            jax.ShapeDtypeStruct((2, HEADS, SLOT, SLOT), F32),
            jax.ShapeDtypeStruct((PAIRS, D, 384), BF16),
            jax.ShapeDtypeStruct((PAIRS, 8, 384), F32),
            jax.ShapeDtypeStruct((8, D), F32),
        ],
        scratch_shapes=[
            pltpu.VMEM((D, rows), BF16),
            pltpu.VMEM((rows, D), F32),
            pltpu.VMEM((rows, 384), BF16),
        ],
        compiler_params=params(dimension_semantics=("arbitrary",)),
        name="attention_backward",
    )(buckets, probs, qkv, qkv, qkv, attended_low, normed, tokens, middle_grad, weight, weight, weight, vecs)


MESH = pl.DeviceIdType.MESH
ANY = pl.ANY


class Place:
    def __init__(self):
        fsdp = lax.axis_index("fsdp")
        dp = lax.axis_index("dp")
        self.z, self.y, self.x, self.core = fsdp // 2, fsdp % 2, dp // 2, dp % 2

    def at(self, z=None, y=None, x=None, core=None):
        z = self.z if z is None else z
        y = self.y if y is None else y
        x = self.x if x is None else x
        core = self.core if core is None else core
        return (z * 2 + y, x * 2 + core)

    def greet(self):
        barrier = pltpu.get_barrier_semaphore()
        peers = [self.at(z=(self.z + k) % 4, y=self.y) for k in range(1, 4)]
        peers += [self.at(z=(self.z + k) % 4, y=1 - self.y) for k in range(4)]
        peers += [
            self.at(x=1 - self.x),
            self.at(core=1 - self.core),
            self.at(x=1 - self.x, core=1 - self.core),
        ]
        for peer in peers:
            pl.semaphore_signal(barrier, inc=1, device_id=peer, device_id_type=MESH)
        pl.semaphore_wait(barrier, len(peers))


def remote(src, dst, send, recv, peer):
    return pltpu.make_async_remote_copy(
        src_ref=src, dst_ref=dst, send_sem=send, recv_sem=recv, device_id=peer, device_id_type=MESH
    )


def rows_of(first, size):
    return pl.ds(pl.multiple_of(first * size, size), size)


def chunk(kind, ref, r, d):
    if kind == "panel":
        return ref.at[d, rows_of(r, 96), :]
    if kind == "wide":
        return ref.at[rows_of(r, 96), rows_of(d, 768)]
    return ref.at[rows_of(d, 192), rows_of(r, 384)]


class Gather:
    def __init__(self, place, kinds, pieces, fulls, send, recv, local):
        self.place, self.kinds, self.pieces, self.fulls = place, kinds, pieces, fulls
        self.send, self.recv, self.local = send, recv, local
        self.started = []

    def slot(self, w, z, y, x, core=None):
        core = self.place.core if core is None else core
        return chunk(self.kinds[w], self.fulls[w], z * 2 + y, x * 2 + core)

    def copy(self, w, index, src, dst, peer):
        return remote(src, dst, self.send.at[w, index], self.recv.at[w, index], peer)

    def start(self, made):
        made.start()
        self.started.append(made)
        return made

    def begin(self, w):
        here = self.place
        own = self.slot(w, here.z, here.y, here.x)
        keep = pltpu.make_async_copy(self.pieces[w], own, self.local.at[w])
        keep.start()
        self.keep = getattr(self, "keep", []) + [keep]
        self.along = getattr(self, "along", {})
        for k in range(1, 4):
            peer = here.at(z=(here.z + k) % 4)
            self.along[w, k] = self.start(self.copy(w, k, self.pieces[w], own, peer))

    def source(self, w, k):
        here = self.place
        if k == 0:
            return self.pieces[w]
        return self.slot(w, (here.z + 4 - k) % 4, here.y, here.x)

    def sibling(self, w, index, src, z, y, x):
        peer = self.place.at(core=1 - self.place.core)
        self.last = getattr(self, "last", [])
        self.last.append(self.start(self.copy(w, index, src, self.slot(w, z, y, x), peer)))

    def first(self, w, k):
        here = self.place
        if k:
            self.along[w, k].wait_recv()
        z = (here.z + 4 - k) % 4
        across = 1 - z // 2
        x = here.x + across * (1 - 2 * here.x)
        y = here.y + (1 - across) * (1 - 2 * here.y)
        src = self.source(w, k)
        dst = self.slot(w, z, here.y, here.x)
        self.step = getattr(self, "step", {})
        self.step[w, k] = self.start(self.copy(w, 4 + k, src, dst, here.at(x=x, y=y)))
        self.sibling(w, 16 + 4 * k, src, z, here.y, here.x)

    def second(self, w, k):
        here = self.place
        self.step[w, k].wait_recv()
        z = (here.z + 4 - k) % 4
        across = 1 - z // 2
        near_x = here.x + across * (1 - 2 * here.x)
        near_y = here.y + (1 - across) * (1 - 2 * here.y)
        far_x = here.x + (1 - across) * (1 - 2 * here.x)
        far_y = here.y + across * (1 - 2 * here.y)
        peer = here.at(x=far_x, y=far_y)
        near = self.slot(w, z, near_y, near_x)
        self.turn = getattr(self, "turn", {})
        self.turn[w, k] = [
            self.start(self.copy(w, 8 + 2 * k, self.source(w, k), self.slot(w, z, here.y, here.x), peer)),
            self.start(self.copy(w, 9 + 2 * k, near, near, peer)),
        ]
        self.sibling(w, 17 + 4 * k, near, z, near_y, near_x)

    def third(self, w, k):
        here = self.place
        z = (here.z + 4 - k) % 4
        across = 1 - z // 2
        far_x = here.x + (1 - across) * (1 - 2 * here.x)
        far_y = here.y + across * (1 - 2 * here.y)
        for i, made in enumerate(self.turn[w, k]):
            made.wait_recv()
            if i == 0:
                x, y = far_x, far_y
            else:
                x, y = 1 - here.x, 1 - here.y
            src = self.slot(w, z, y, x)
            self.sibling(w, 18 + 4 * k + i, src, z, y, x)

    def finish(self, w):
        for made in self.last:
            made.wait_recv()
        for made in self.started:
            made.wait_send()
        for made in self.keep:
            made.wait()


GATHER_KINDS = ("panel", "panel", "wide", "turned")


def gather_kernel(
    qkv_p, out_p, up_p, down_p, vec_p, table_p, qkv_f, out_f, up_f, down_f, vec_f, table_f,
    send, recv, local, vec_send, vec_recv, vec_local,
):
    place = Place()
    place.greet()
    f = place.z * 2 + place.y
    small = []
    keep = []
    for n, (piece, full) in enumerate(((vec_p, vec_f), (table_p, table_f))):
        made = pltpu.make_async_copy(piece, full.at[f], vec_local.at[n])
        made.start()
        keep.append(made)
        for k in range(1, 8):
            peer = (f + k) % 8
            made = remote(
                piece, full.at[f], vec_send.at[n, k], vec_recv.at[n, k],
                place.at(z=peer // 2, y=peer % 2),
            )
            made.start()
            small.append(made)
    gather = Gather(
        place, GATHER_KINDS, (qkv_p, out_p, up_p, down_p), (qkv_f, out_f, up_f, down_f),
        send, recv, local,
    )
    order = [(w, k) for w in range(4) for k in range(4)]
    for w in range(4):
        gather.begin(w)
    for n in range(len(order) + 2):
        if n < len(order):
            gather.first(*order[n])
        if 0 <= n - 1 < len(order):
            gather.second(*order[n - 1])
        if 0 <= n - 2 < len(order):
            gather.third(*order[n - 2])
    gather.finish(0)
    for made in small:
        made.wait()
    for made in keep:
        made.wait()


def gather_all(qkv_p, out_p, up_p, down_p, vec_p, table_p):
    return pl.pallas_call(
        gather_kernel,
        in_specs=[pl.BlockSpec(memory_space=ANY)] * 6,
        out_specs=[pl.BlockSpec(memory_space=ANY)] * 6,
        out_shape=[
            jax.ShapeDtypeStruct((4, D, 576), BF16),
            jax.ShapeDtypeStruct((4, D, 192), BF16),
            jax.ShapeDtypeStruct((D, FF), BF16),
            jax.ShapeDtypeStruct((D, FF), BF16),
            jax.ShapeDtypeStruct((8,) + vec_p.shape, BF16),
            jax.ShapeDtypeStruct((8,) + table_p.shape, BF16),
        ],
        scratch_shapes=[
            pltpu.SemaphoreType.DMA((4, 32)),
            pltpu.SemaphoreType.DMA((4, 32)),
            pltpu.SemaphoreType.DMA((4,)),
            pltpu.SemaphoreType.DMA((2, 8)),
            pltpu.SemaphoreType.DMA((2, 8)),
            pltpu.SemaphoreType.DMA((2,)),
        ],
        compiler_params=params(collective_id=1, has_side_effects=True),
        name="gather_weights",
    )(qkv_p, out_p, up_p, down_p, vec_p, table_p)


class Scatter:
    def __init__(self, place, kind, grad, acc, from_core, half, near, far, quarter, out, sems):
        self.place, self.kind, self.grad, self.acc = place, kind, grad, acc
        self.from_core, self.half, self.near, self.far = from_core, half, near, far
        self.quarter, self.out = quarter, out
        self.send, self.recv, self.local = sems
        self.started = []

    def part(self, ref, x, r, count=1):
        if self.kind == "turned":
            return ref.at[x, :, pl.ds(pl.multiple_of(r * 384, 384), count * 384)]
        return ref.at[x, pl.ds(pl.multiple_of(r * 96, 96), count * 96), :]

    def panel(self, d):
        if self.kind == "panel":
            return self.grad.at[d]
        if self.kind == "wide":
            return self.grad.at[:, rows_of(d, 768)]
        return self.grad.at[rows_of(d, 192), :]

    def copy(self, index, src, dst, peer):
        made = remote(src, dst, self.send.at[index], self.recv.at[index], peer)
        made.start()
        self.started.append(made)
        return made

    def begin(self):
        here = self.place
        peer = here.at(core=1 - here.core)
        self.keep = []
        self.core = []
        for x in range(2):
            self.core.append(
                self.copy(x, self.panel(x * 2 + 1 - here.core), self.from_core.at[x], peer)
            )
            made = pltpu.make_async_copy(
                self.panel(x * 2 + here.core), self.acc.at[x], self.local.at[x]
            )
            made.start()
            self.keep.append(made)

    def add(self, target, source):
        if self.kind == "turned":
            size = 16
        else:
            size = 32
        rows = target.shape[0]

        def step(n, carry):
            at = pl.ds(pl.multiple_of(n * size, size), size)
            target[at, :] = target[at, :] + source[at, :]
            return carry

        lax.fori_loop(0, rows // size, step, 0)

    def plane(self):
        here = self.place
        for made in self.keep:
            made.wait()
        for made in self.core:
            made.wait_recv()
        for x in range(2):
            self.add(self.acc.at[x], self.from_core.at[x])
        over_x = here.at(x=1 - here.x)
        over_y = here.at(y=1 - here.y)
        self.wait_half = [
            self.copy(2, self.part(self.acc, 1 - here.x, 0, 4), self.half, over_x)
        ]
        for x in range(2):
            for n in range(2):
                src = self.part(self.acc, x, (2 + n) * 2 + 1 - here.y)
                self.wait_half.append(
                    self.copy(3 + 2 * x + n, src, self.near.at[x, n], over_y)
                )

    def turn(self):
        here = self.place
        for made in self.wait_half:
            made.wait_recv()
        self.add(self.part(self.acc, here.x, 0, 4), self.half)
        for x in range(2):
            for n in range(2):
                self.add(self.part(self.acc, x, (2 + n) * 2 + here.y), self.near.at[x, n])
        over_x = here.at(x=1 - here.x)
        over_y = here.at(y=1 - here.y)
        self.wait_far = []
        for n in range(2):
            src = self.part(self.acc, here.x, n * 2 + 1 - here.y)
            self.wait_far.append(self.copy(7 + n, src, self.far.at[0, n], over_y))
            src = self.part(self.acc, 1 - here.x, (2 + n) * 2 + here.y)
            self.wait_far.append(self.copy(9 + n, src, self.far.at[1, n], over_x))

    def line(self):
        here = self.place
        for made in self.wait_far:
            made.wait_recv()
        for n in range(2):
            self.add(self.part(self.acc, here.x, n * 2 + here.y), self.far.at[0, n])
            self.add(self.part(self.acc, here.x, (2 + n) * 2 + here.y), self.far.at[1, n])
        self.wait_line = []
        for k in range(1, 4):
            z = (here.z + k) % 4
            src = self.part(self.acc, here.x, z * 2 + here.y)
            self.wait_line.append(self.copy(10 + k, src, self.quarter.at[k - 1], here.at(z=z)))

    def end(self):
        here = self.place
        for made in self.wait_line:
            made.wait_recv()
        total = self.part(self.acc, here.x, here.z * 2 + here.y)[...].astype(F32)
        for k in range(3):
            total = total + self.quarter[k].astype(F32)
        self.out[...] = total
        for made in self.started:
            made.wait_send()


SCATTER_PIECES = {"qkv": (96, 576), "out": (96, 192), "up": (96, 768), "down": (192, 384)}
SCATTER_KINDS = {"qkv": "panel", "out": "panel", "up": "wide", "down": "turned"}
SCATTER_ORDER = ("down", "up", "out", "qkv")


def scatter_scratch(name):
    height, width = SCATTER_PIECES[name]
    if name == "down":
        whole, half = (2, height, 8 * width), (height, 4 * width)
    else:
        whole, half = (2, 8 * height, width), (4 * height, width)
    return [
        pltpu.VMEM(whole, BF16),
        pltpu.VMEM(whole, BF16),
        pltpu.VMEM(half, BF16),
        pltpu.VMEM((2, 2, height, width), BF16),
        pltpu.VMEM((2, 2, height, width), BF16),
        pltpu.VMEM((3, height, width), BF16),
        pltpu.SemaphoreType.DMA((14,)),
        pltpu.SemaphoreType.DMA((14,)),
        pltpu.SemaphoreType.DMA((2,)),
    ]


def pack_sums(sums_ref, first_ref, wide_ref, pair_ref, table_ref, packed):
    low = first_ref[0:2, :]
    narrow = sums_ref[...]
    group = lax.broadcasted_iota(jnp.int32, (D, 128), 0) // HEAD_DIM
    pick = (group == lax.broadcasted_iota(jnp.int32, (D, 128), 1)).astype(F32).astype(BF16)
    high, rest = split_low(narrow[8:16])
    heads = (nn(high, pick) + nn(rest, pick))[0:1]
    heads = jnp.concatenate([heads, jnp.zeros((1, 64), F32)], 1)
    query = jnp.concatenate([pair_ref[n, 0:1, 0:128] for n in range(PAIRS)], 1)
    value = jnp.concatenate([pair_ref[n, 0:1, 256:384] for n in range(PAIRS)], 1)
    pair = jnp.concatenate([query, value], 1)
    for f in range(8):
        at = slice(96 * f, 96 * f + 96)
        packed[f, 0:1, :] = jnp.concatenate(
            [low[0:1, at], low[1:2, at], narrow[2:3, at], narrow[3:4, at]], 1
        )
        packed[f, 1:2, :] = jnp.concatenate([narrow[n : n + 1, at] for n in range(4, 8)], 1)
        packed[f, 2:5, :] = wide_ref[0:3, 384 * f : 384 * f + 384]
        at = slice(192 * f, 192 * f + 192)
        packed[f, 5:6, :] = jnp.concatenate([pair[:, at], heads], 1)
        for n in range(PAIRS):
            packed[f, 6 + n : 7 + n, :] = jnp.concatenate(
                [table_ref[2 * n : 2 * n + 1, at], table_ref[2 * n + 1 : 2 * n + 2, at]], 1
            )
        packed[f, 12:16, :] = jnp.zeros((4, 384), F32)


class SmallSums:
    def __init__(self, place, packed, rows, peers, sems):
        self.place, self.packed, self.rows, self.peers = place, packed, rows, peers
        self.send, self.recv = sems

    def begin(self):
        here = self.place
        f = here.z * 2 + here.y
        self.made = []
        for k in range(1, 8):
            to = (f + k) % 8
            made = remote(
                self.packed.at[to], self.rows.at[k - 1], self.send.at[k], self.recv.at[k],
                here.at(z=to // 2, y=to % 2),
            )
            made.start()
            self.made.append(made)

    def cross(self):
        here = self.place
        f = here.z * 2 + here.y
        for made in self.made:
            made.wait()
        total = self.packed[f]
        for k in range(7):
            total = total + self.rows[k]
        self.peers[0] = total
        d = here.x * 2 + here.core
        self.made = []
        for k in range(1, 4):
            to = (d + k) % 4
            made = remote(
                self.peers.at[0], self.peers.at[k], self.send.at[7 + k], self.recv.at[7 + k],
                here.at(x=to // 2, core=to % 2),
            )
            made.start()
            self.made.append(made)

    def end(self):
        for made in self.made:
            made.wait()
        return (self.peers[0] + self.peers[1]) + (self.peers[2] + self.peers[3])


def scatter_kernel(*refs):
    grads = dict(zip(SCATTER_ORDER, refs[:4]))
    sums_ref, first_ref, wide_ref, pair_ref, table_ref = refs[4:9]
    outs = dict(zip(SCATTER_ORDER, refs[9:13]))
    small_outs = refs[13:27]
    scratch = refs[27:]
    place = Place()
    place.greet()
    parts = []
    for n, name in enumerate(SCATTER_ORDER):
        own = scratch[9 * n : 9 * n + 9]
        parts.append(
            Scatter(
                place, SCATTER_KINDS[name], grads[name], *own[:6], outs[name], own[6:]
            )
        )
    packed, rows, peers, send, recv = scratch[36:]
    small = SmallSums(place, packed, rows, peers, (send, recv))
    for part in parts:
        part.begin()
    pack_sums(sums_ref, first_ref, wide_ref, pair_ref, table_ref, packed)
    small.begin()
    for n in range(len(parts) + 3):
        if n < len(parts):
            parts[n].plane()
        if 0 <= n - 1 < len(parts):
            parts[n - 1].turn()
        if 0 <= n - 2 < len(parts):
            parts[n - 2].line()
        if n == 2:
            small.cross()
        if 0 <= n - 3 < len(parts):
            parts[n - 3].end()
    total = small.end()
    for n in range(8):
        small_outs[n][...] = total[n // 4 : n // 4 + 1, 96 * (n % 4) : 96 * (n % 4) + 96]
    for n in range(3):
        small_outs[8 + n][...] = total[2 + n : 3 + n, :]
    small_outs[11][...] = total[5:6, 0:192]
    small_outs[12][...] = total[5:6, 192:204]
    small_outs[13][...] = jnp.concatenate(
        [total[6:12, 0:192], total[6:12, 192:384], jnp.zeros((4, 192), F32)], 0
    )


def scatter_all(down, up, out, qkv, sums, first, wide, pair, table):
    vmem = pl.BlockSpec(memory_space=pltpu.VMEM)
    scratch = []
    for name in SCATTER_ORDER:
        scratch += scatter_scratch(name)
    small = [(1, 96)] * 8 + [(1, 384)] * 3 + [(1, 192), (1, 12), (16, 192)]
    shapes = [SCATTER_PIECES[name] for name in SCATTER_ORDER] + small
    return pl.pallas_call(
        scatter_kernel,
        in_specs=[pl.BlockSpec(memory_space=ANY)] * 4 + [vmem] * 5,
        out_specs=[vmem] * len(shapes),
        out_shape=[jax.ShapeDtypeStruct(shape, F32) for shape in shapes],
        scratch_shapes=scratch
        + [
            pltpu.VMEM((8, 16, 384), F32),
            pltpu.VMEM((7, 16, 384), F32),
            pltpu.VMEM((4, 16, 384), F32),
            pltpu.SemaphoreType.DMA((11,)),
            pltpu.SemaphoreType.DMA((11,)),
        ],
        compiler_params=params(collective_id=2, has_side_effects=True),
        name="scatter_grads",
    )(down, up, out, qkv, sums, first, wide, pair, table)


def gather_matrix(piece):
    rows = lax.all_gather(piece, "fsdp", axis=0, tiled=True)
    return lax.all_gather(rows, "dp", axis=1, tiled=True)


def scatter_matrix(grad):
    part = lax.psum_scatter(grad, "dp", scatter_dimension=1, tiled=True).astype(F32)
    return lax.psum_scatter(part, "fsdp", scatter_dimension=0, tiled=True)


def body(
    tokens, cotangent, lengths, buckets, qkv_weight, query_value_bias, out_weight, out_bias,
    up_weight, up_bias, down_weight, down_bias, first_gain, first_shift, mix_gain, mix_shift,
    second_gain, second_shift, hidden_gain, hidden_shift, head_scale, position_table,
):
    parts = lax.axis_size("fsdp")
    own_kernels = (parts, lax.axis_size("dp")) == (8, 4)
    narrow = [
        first_gain, first_shift, mix_gain, mix_shift, second_gain, second_shift, out_bias, down_bias,
    ]
    wide = [up_bias, hidden_gain, hidden_shift]
    a = D // parts
    b = FF // parts
    packed = jnp.concatenate(
        [jnp.pad(jnp.stack(narrow), ((0, 0), (0, b - a))), jnp.stack(wide)]
        + [jnp.pad(query_value_bias, (0, b - 2 * a))[None], jnp.zeros((4, b), BF16)]
    )
    if own_kernels:
        qkv_full, out_full, up_full, down_full, gathered, table = gather_all(
            qkv_weight, out_weight, up_weight, down_weight.T, packed, position_table
        )
        qkv_full = qkv_full.transpose(1, 0, 2).reshape(D, 3 * D)
        out_full = out_full.transpose(1, 0, 2).reshape(D, D)
    else:
        gathered = lax.all_gather(packed, "fsdp", axis=0)
        table = lax.all_gather(position_table, "fsdp", axis=0)
        qkv_full = gather_matrix(qkv_weight)
        out_full = gather_matrix(out_weight)
        up_full = gather_matrix(up_weight)
        down_full = gather_matrix(down_weight).T
    gathered = gathered.astype(F32)
    vecs = gathered[:, :8, :a].transpose(1, 0, 2).reshape(8, D)
    wides = jnp.pad(gathered[:, 8:11].transpose(1, 0, 2).reshape(3, FF), ((0, 5), (0, 0)))
    pair = gathered[:, 11, : 2 * a].reshape(1, 2 * D)
    table = jnp.pad(table.astype(F32).reshape(TABLE, HEADS).T, ((0, 4), (0, 0)))
    qkv_bias = jnp.concatenate([pair[:, :D], jnp.zeros((1, D), F32), pair[:, D:]], 1)
    scales = jnp.repeat(head_scale.astype(F32), HEAD_DIM)[None]

    bias = build_bias(table)
    normed, qkv, probs, attended = attention(
        lengths, buckets, tokens, vecs, qkv_full, qkv_bias, bias
    )
    (
        result, mixed, second, act, low, branch, middle_grad, attended_low, sums, wide_sums,
    ) = feed_forward(tokens, attended, cotangent, out_full, up_full, down_full, vecs, wides, scales)
    down_grad = outer_product(cotangent, act, 512)
    up_grad = outer_product(second, low, 512)
    out_grad = outer_product(mixed, branch, 256)
    input_grad, grids, qkv_grad, pair_sums, first_sums = attention_back(
        buckets, probs, qkv, attended_low, normed, tokens, middle_grad, qkv_full, vecs
    )
    table_sums = table_grad(grids)
    qkv_natural = qkv_grad.reshape(PAIRS, D, 3, 128).transpose(1, 2, 0, 3).reshape(D, 3 * D)

    if own_kernels:
        owned = scatter_all(
            down_grad, up_grad, out_grad.reshape(D, 4, 192).transpose(1, 0, 2),
            qkv_natural.reshape(D, 4, 576).transpose(1, 0, 2),
            sums, first_sums, wide_sums, pair_sums, table_sums,
        )
        down_owned, up_owned, out_owned, qkv_owned = owned[0].T, owned[1], owned[2], owned[3]
        narrow_owned = [part.reshape(-1) for part in owned[4:12]]
        wide_owned = [part.reshape(-1) for part in owned[12:15]]
        pair_owned = owned[15].reshape(-1)
        scale_grad = owned[16].reshape(-1)
        table_owned = owned[17][:HEADS].reshape(2, PAIRS, -1).transpose(2, 1, 0).reshape(-1, HEADS)
    else:
        qkv_owned = scatter_matrix(qkv_natural)
        out_owned = scatter_matrix(out_grad)
        up_owned = scatter_matrix(up_grad)
        down_owned = scatter_matrix(down_grad.T)
        pair_grad = pair_sums[:, 0].reshape(PAIRS, 3, 128).transpose(1, 0, 2).reshape(3, D)
        pair_grad = jnp.concatenate([pair_grad[0], pair_grad[2]])
        narrow_sums = jnp.concatenate([first_sums[:2], sums[2:8]], 0)
        packed = jnp.concatenate(
            [
                narrow_sums.reshape(8, parts, a).transpose(1, 0, 2).reshape(parts, -1),
                wide_sums[:3].reshape(3, parts, b).transpose(1, 0, 2).reshape(parts, -1),
                pair_grad.reshape(parts, -1),
                table_sums[:HEADS].T.reshape(parts, -1),
            ],
            1,
        )
        owned = lax.psum(lax.psum_scatter(packed, "fsdp", scatter_dimension=0, tiled=True), "dp")[0]
        scale_grad = lax.psum(sums[8].reshape(HEADS, HEAD_DIM).sum(1), ("fsdp", "dp"))
        narrow_owned = owned[: 8 * a].reshape(8, a)
        edge = 8 * a
        wide_owned = owned[edge : edge + 3 * b].reshape(3, b)
        edge += 3 * b
        pair_owned = owned[edge : edge + 2 * a]
        edge += 2 * a
        table_owned = owned[edge:].reshape(TABLE // parts, HEADS)
    return (
        result, input_grad, qkv_owned, pair_owned, out_owned, narrow_owned[6], up_owned,
        wide_owned[0], down_owned, narrow_owned[7], narrow_owned[0], narrow_owned[1],
        narrow_owned[2], narrow_owned[3], narrow_owned[4], narrow_owned[5], wide_owned[1],
        wide_owned[2], scale_grad, table_owned,
    )


def solution(mesh):
    tokens = P(("fsdp", "dp"), None)
    sequences = P(("fsdp", "dp"))
    matrix = P("fsdp", "dp")
    vector = P("fsdp")
    table = P("fsdp", None)
    in_specs = (
        tokens, tokens, sequences, sequences, matrix, vector, matrix, vector, matrix, vector,
        matrix, vector, vector, vector, vector, vector, vector, vector, vector, vector, P(), table,
    )
    out_specs = (
        tokens, tokens, matrix, vector, matrix, vector, matrix, vector, matrix, vector, vector,
        vector, vector, vector, vector, vector, vector, vector, P(), table,
    )
    return jax.shard_map(body, mesh=mesh, in_specs=in_specs, out_specs=out_specs, check_vma=False)
```

```python
import functools

import jax
import jax.numpy as jnp
from jax import lax
from jax.experimental import pallas as pl
from jax.experimental.pallas import tpu as pltpu
from jax.sharding import PartitionSpec as P

D = 768
HEADS = 12
PAIRS = 6
HEAD_DIM = 64
FF = 3072
SLOT = 256
TABLE = 1536

EPS = 1e-05
MASKED = -1000000000.0
F32 = jnp.float32
BF16 = jnp.bfloat16
VMEM_LIMIT = 60 * 2**20


def params(**more):
    return pltpu.CompilerParams(vmem_limit_bytes=VMEM_LIMIT, **more)


def nn(left, right):
    return lax.dot_general(left, right, (((1,), (0,)), ((), ())), preferred_element_type=F32)


def nt(left, right):
    return lax.dot_general(left, right, (((1,), (1,)), ((), ())), preferred_element_type=F32)


def standardize(values):
    center = values - jnp.mean(values, -1, keepdims=True)
    inverse = lax.rsqrt(jnp.mean(center * center, -1, keepdims=True) + EPS)
    return center * inverse, inverse


def norm_back(grad, unit, inverse):
    return inverse * (
        grad
        - jnp.mean(grad, -1, keepdims=True)
        - unit * jnp.mean(grad * unit, -1, keepdims=True)
    )


def column_sum(values):
    return jnp.sum(values, 0, keepdims=True)


def split_low(values):
    high = values.astype(BF16)
    return high, (values - high.astype(F32)).astype(BF16)


def compaction(side, lanes):
    plane = lax.broadcasted_iota(jnp.int32, (1024, lanes), 0)
    lane = lax.broadcasted_iota(jnp.int32, (1024, lanes), 1)
    across = plane & 31
    return ((lane == side * (plane >> 5) + across) & (across < side)).astype(F32).astype(BF16)


def inside_grid(patches):
    row = lax.broadcasted_iota(jnp.int32, (SLOT, SLOT), 0)
    col = lax.broadcasted_iota(jnp.int32, (SLOT, SLOT), 1)
    return (row < patches) & (col < patches)


def store_tiles(ref, values):
    for k in range(ref.shape[0]):
        ref[k] = values[:, 128 * k : 128 * k + 128]


def load_tiles(ref):
    return jnp.concatenate([ref[k] for k in range(ref.shape[0])], 1)


def load_strided(ref, first, count):
    return jnp.concatenate(
        [ref[k, pl.ds(first, count, 16), :] for k in range(ref.shape[0])], 1
    )


def store_strided(ref, first, values):
    for k in range(ref.shape[0]):
        ref[k, pl.ds(first, values.shape[0], 16), :] = values[:, 128 * k : 128 * k + 128]


def bias_walls(table_ref, wall_small, wall_large, visual):
    plane = table_ref[:, 512:]
    shifted = [pltpu.roll(plane, (ic - 15) % 1024, 1) for ic in range(16)]
    stack = jnp.concatenate(shifted, 0).astype(BF16)
    store_tiles(wall_large, nn(stack, compaction(15, 512)))
    store_tiles(wall_small, nn(stack[:128], compaction(8, 256)))
    visual[...] = jnp.zeros_like(visual)


def bias_head(table_ref, out_ref, wall_small, wall_large, visual, h, carry):
    line = jnp.broadcast_to(table_ref[pl.ds(h, 1), :512], (SLOT, 512))
    textual = pltpu.roll(line, 257, 1, stride=1, stride_axis=0)[:, :SLOT]
    large = load_strided(wall_large, h, 16)
    for ir in range(15):
        visual[pl.ds(ir * 15, 16), :] = pltpu.roll(large, 512 - (15 - ir) * 15, 1)[:, :SLOT]
    out_ref[1, h] = jnp.where(inside_grid(225), visual[...], textual).astype(BF16)
    small = load_strided(wall_small, h, 8)
    rows = [pltpu.roll(small, 256 - (15 - ir) * 8, 1) for ir in range(8)]
    grid = jnp.concatenate(rows + [jnp.zeros((192, SLOT), F32)], 0)
    out_ref[0, h] = jnp.where(inside_grid(64), grid, textual).astype(BF16)
    return carry


def bias_kernel(table_ref, out_ref, wall_small, wall_large, visual):
    bias_walls(table_ref, wall_small, wall_large, visual)
    one_head = functools.partial(bias_head, table_ref, out_ref, wall_small, wall_large, visual)
    lax.fori_loop(0, HEADS, one_head, 0)


def build_bias(table):
    return pl.pallas_call(
        bias_kernel,
        out_shape=jax.ShapeDtypeStruct((2, HEADS, SLOT, SLOT), BF16),
        scratch_shapes=[
            pltpu.VMEM((2, 128, 128), F32),
            pltpu.VMEM((4, 256, 128), F32),
            pltpu.VMEM((SLOT, SLOT), F32),
        ],
        compiler_params=params(),
        name="build_bias",
    )(table)


def table_grad_start(out_ref, wall_small, wall_large):
    wall_small[...] = jnp.zeros_like(wall_small)
    wall_large[...] = jnp.zeros_like(wall_large)
    out_ref[...] = jnp.zeros_like(out_ref)


def table_grad_head(grid_ref, out_ref, wall_small, wall_large, h, carry):
    row = lax.broadcasted_iota(jnp.int32, (SLOT, SLOT), 0)
    col = lax.broadcasted_iota(jnp.int32, (SLOT, SLOT), 1)
    flip = (row + col == SLOT - 1).astype(F32).astype(BF16)
    lane = lax.broadcasted_iota(jnp.int32, (16, SLOT), 1)
    textual = jnp.where(inside_grid(64), 0.0, grid_ref[0, h]) + jnp.where(
        inside_grid(225), 0.0, grid_ref[1, h]
    )
    high, low = split_low(textual)
    flipped = nn(flip, high) + nn(flip, low)
    wide = jnp.concatenate([flipped, jnp.zeros((SLOT, SLOT), F32)], 1)
    out_ref[pl.ds(h, 1), :512] = column_sum(pltpu.roll(wide, 0, 1, stride=1, stride_axis=0))
    total = jnp.zeros((16, 512), F32)
    for ir in range(15):
        part = jnp.where(lane < 225, grid_ref[1, h, pl.ds(ir * 15, 16), :], 0.0)
        part = jnp.concatenate([part, jnp.zeros((16, SLOT), F32)], 1)
        total = total + pltpu.roll(part, (15 - ir) * 15, 1)
    store_strided(wall_large, h, total)
    total = jnp.zeros((8, SLOT), F32)
    for ir in range(8):
        part = jnp.where(lane[:8] < 64, grid_ref[0, h, pl.ds(ir * 8, 8), :], 0.0)
        total = total + pltpu.roll(part, (15 - ir) * 8, 1)
    store_strided(wall_small, h, total)
    return carry


def table_grad_end(out_ref, wall_small, wall_large):
    high, low = split_low(load_tiles(wall_large))
    spread = compaction(15, 512)
    large = nt(high, spread) + nt(low, spread)
    high, low = split_low(load_tiles(wall_small))
    spread = compaction(8, 256)
    small = nt(high, spread) + nt(low, spread)
    plane = jnp.zeros((16, 1024), F32)
    for ic in range(15):
        part = large[ic * 16 : ic * 16 + 16]
        if ic < 8:
            part = part + small[ic * 16 : ic * 16 + 16]
        plane = plane + pltpu.roll(part, 15 - ic, 1)
    out_ref[:, 512:] = plane


def table_grad_kernel(grid_ref, out_ref, wall_small, wall_large):
    table_grad_start(out_ref, wall_small, wall_large)
    one_head = functools.partial(table_grad_head, grid_ref, out_ref, wall_small, wall_large)
    lax.fori_loop(0, HEADS, one_head, 0)
    table_grad_end(out_ref, wall_small, wall_large)


def table_grad(grids):
    return pl.pallas_call(
        table_grad_kernel,
        out_shape=jax.ShapeDtypeStruct((16, TABLE), F32),
        scratch_shapes=[pltpu.VMEM((2, 128, 128), F32), pltpu.VMEM((4, 256, 128), F32)],
        compiler_params=params(),
        name="table_grad",
    )(grids)


def by_head(pair, axis):
    first = lax.broadcasted_iota(jnp.int32, pair.shape, 1) < HEAD_DIM
    return jnp.concatenate([jnp.where(first, pair, 0), jnp.where(first, 0, pair)], axis)


def attend(query, keys, values, bias, live):
    logits = nt(by_head(query, 0), keys)
    probs = []
    for half in range(2):
        rows = slice(SLOT * half, SLOT * half + SLOT)
        scores = jnp.where(live, logits[rows] + bias[half].astype(F32), MASKED)
        shifted = jnp.exp(scores - jnp.max(scores, -1, keepdims=True))
        probs.append((shifted * (1.0 / jnp.sum(shifted, -1, keepdims=True))).astype(BF16))
    return probs, nn(jnp.concatenate(probs, 1), by_head(values, 0))


def attend_back(query, keys, values, grad, probs):
    probs_grads = nt(by_head(grad, 0), values)
    grad_turned = grad.T
    query_turned = query.T
    keys_parts = []
    values_parts = []
    scores_grads = []
    lows = []
    for half in range(2):
        part = slice(HEAD_DIM * half, HEAD_DIM * half + HEAD_DIM)
        wide = probs[half].astype(F32)
        probs_grad = probs_grads[SLOT * half : SLOT * half + SLOT]
        values_parts.append(nn(grad_turned[part], probs[half]))
        scores_grad = wide * (probs_grad - jnp.sum(wide * probs_grad, -1, keepdims=True))
        scores_grads.append(scores_grad)
        lows.append(scores_grad.astype(BF16))
        keys_parts.append(nn(query_turned[part], lows[half]))
    query_grad = nn(jnp.concatenate(lows, 1), by_head(keys, 0)) * HEAD_DIM ** (-0.5)
    keys_grad = jnp.concatenate(keys_parts, 0).T
    values_grad = jnp.concatenate(values_parts, 0).T
    return query_grad.astype(BF16), keys_grad.astype(BF16), values_grad.astype(BF16), scores_grads


def attention_kernel(
    lengths, buckets, x_ref, vec_ref, weight_ref, qkv_bias_ref, bias_ref,
    normed_ref, qkv_ref, probs_ref, attended_ref,
):
    count = x_ref.shape[0] // SLOT

    def one_block(b, carry):
        rows = pl.ds(pl.multiple_of(b * SLOT, SLOT), SLOT)
        unit, inverse = standardize(x_ref[rows, :].astype(F32))
        normed_ref[rows, :] = (unit * vec_ref[0:1, :] + vec_ref[1:2, :]).astype(BF16)
        return carry

    lax.fori_loop(0, count, one_block, 0)

    def one_panel(n, carry):
        cols = pl.ds(pl.multiple_of(n * 256, 256), 256)
        out = nn(normed_ref[...], weight_ref[:, cols]) + qkv_bias_ref[:, cols]
        out = (out * jnp.where(n < 3, HEAD_DIM ** (-0.5), 1.0)).astype(BF16)
        qkv_ref[2 * n] = out[:, :128]
        qkv_ref[2 * n + 1] = out[:, 128:]
        return carry

    lax.fori_loop(0, 9, one_panel, 0)
    key_slot = lax.broadcasted_iota(jnp.int32, (SLOT, SLOT), 1)

    def one_unit(step, carry):
        pair = step // count
        s = step % count
        rows = pl.ds(pl.multiple_of(s * SLOT, SLOT), SLOT)
        bias = [bias_ref[buckets[s], 2 * pair + half] for half in range(2)]
        probs, out = attend(
            qkv_ref[pair, rows, :], qkv_ref[PAIRS + pair, rows, :], qkv_ref[2 * PAIRS + pair, rows, :],
            bias, key_slot < lengths[s],
        )
        for half in range(2):
            probs_ref[2 * pair + half, s] = probs[half]
        attended_ref[rows, pl.ds(pl.multiple_of(pair * 128, 128), 128)] = out
        return carry

    lax.fori_loop(0, PAIRS * count, one_unit, 0)


def attention(lengths, buckets, tokens, vecs, weight, qkv_bias, bias):
    rows = tokens.shape[0]
    count = rows // SLOT
    smem = pl.BlockSpec(memory_space=pltpu.SMEM)
    vmem = pl.BlockSpec(memory_space=pltpu.VMEM)
    return pl.pallas_call(
        attention_kernel,
        in_specs=[smem, smem] + [vmem] * 5,
        out_shape=[
            jax.ShapeDtypeStruct((rows, D), BF16),
            jax.ShapeDtypeStruct((3 * PAIRS, rows, 128), BF16),
            jax.ShapeDtypeStruct((HEADS, count, SLOT, SLOT), BF16),
            jax.ShapeDtypeStruct((rows, D), F32),
        ],
        compiler_params=params(),
        name="attention_forward",
    )(lengths, buckets, tokens, vecs, weight, qkv_bias, bias)


PANEL = 512


def feed_kernel(*refs):
    @pl.when(pl.program_id(0) == 0)
    def _():
        for ref in refs[17:19]:
            ref[...] = jnp.zeros_like(ref)

    feed_block(*refs, lambda: None)


def feed_block(
    x_ref, attended_ref, cot_ref, out_w, up_w, down_w, vec_ref, wide_ref, scale_ref,
    result_ref, mixed_ref, second_ref, act_ref, low_ref, branch_ref, middle_grad_ref,
    attended_low_ref, sums_ref, wide_sums_ref,
    gelu_ref, slope_ref, grad_ref, before_down,
):
    def add(row, values):
        sums_ref[row : row + 1, :] += column_sum(values)

    rows = x_ref.shape[0]
    attended = attended_ref[...]
    mix_unit, mix_inverse = standardize(attended * scale_ref[...])
    mixed = (mix_unit * vec_ref[2:3, :] + vec_ref[3:4, :]).astype(BF16)
    mixed_ref[...] = mixed
    middle = x_ref[...].astype(F32) + nn(mixed, out_w[...]) + vec_ref[6:7, :]
    second_unit, second_inverse = standardize(middle)
    second = (second_unit * vec_ref[4:5, :] + vec_ref[5:6, :]).astype(BF16)
    second_ref[...] = second
    cot = cot_ref[...]

    panels = [slice(n, n + PANEL) for n in range(0, FF, PANEL)]
    total = jnp.zeros((rows, 1), F32)
    for cols in panels:
        hidden = nn(second, up_w[:, cols]) + wide_ref[0:1, cols]
        cdf = 0.5 + 0.5 * lax.erf(hidden * 0.7071067811865476)
        gelu = hidden * cdf
        gelu_ref[:, cols] = gelu
        slope_ref[:, cols] = cdf + hidden * (jnp.exp(-0.5 * hidden * hidden) * 0.3989422804014327)
        total = total + jnp.sum(gelu, -1, keepdims=True)
    mean = total * (1.0 / FF)
    total = jnp.zeros((rows, 1), F32)
    for cols in panels:
        center = gelu_ref[:, cols] - mean
        total = total + jnp.sum(center * center, -1, keepdims=True)
    inverse = lax.rsqrt(total * (1.0 / FF) + EPS)
    before_down()
    result = middle + vec_ref[7:8, :]
    first = jnp.zeros((rows, 1), F32)
    second_moment = jnp.zeros((rows, 1), F32)
    for cols in panels:
        unit = (gelu_ref[:, cols] - mean) * inverse
        gelu_ref[:, cols] = unit
        act = (unit * wide_ref[1:2, cols] + wide_ref[2:3, cols]).astype(BF16)
        act_ref[:, cols] = act
        result = result + nt(act, down_w[:, cols])
        act_grad = nn(cot, down_w[:, cols])
        wide_sums_ref[1:2, cols] += column_sum(act_grad * unit)
        wide_sums_ref[2:3, cols] += column_sum(act_grad)
        grad = act_grad * wide_ref[1:2, cols]
        grad_ref[:, cols] = grad
        first = first + jnp.sum(grad, -1, keepdims=True)
        second_moment = second_moment + jnp.sum(grad * unit, -1, keepdims=True)
    result_ref[...] = result.astype(BF16)
    first = first * (1.0 / FF)
    second_moment = second_moment * (1.0 / FF)
    second_in = jnp.zeros((rows, D), F32)
    for cols in panels:
        grad = inverse * (grad_ref[:, cols] - first - gelu_ref[:, cols] * second_moment)
        low = (grad * slope_ref[:, cols]).astype(BF16)
        low_ref[:, cols] = low
        wide_sums_ref[0:1, cols] += column_sum(low.astype(F32))
        second_in = second_in + nt(low, up_w[:, cols])
    add(4, second_in * second_unit)
    add(5, second_in)
    cot_wide = cot.astype(F32)
    add(7, cot_wide)
    middle_grad = cot_wide + norm_back(second_in * vec_ref[4:5, :], second_unit, second_inverse)
    middle_grad_ref[...] = middle_grad
    branch = middle_grad.astype(BF16)
    branch_ref[...] = branch
    add(6, branch.astype(F32))
    mixed_in = nt(branch, out_w[...])
    add(2, mixed_in * mix_unit)
    add(3, mixed_in)
    grad = norm_back(mixed_in * vec_ref[2:3, :], mix_unit, mix_inverse)
    add(8, grad * attended)
    attended_low_ref[...] = (grad * scale_ref[...]).astype(BF16)


def feed_forward(tokens, attended, cotangent, out_w, up_w, down_w, vecs, wide, scales):
    rows = tokens.shape[0]
    tile = 256
    block = pl.BlockSpec((tile, D), lambda i: (i, 0))
    wide_block = pl.BlockSpec((tile, FF), lambda i: (i, 0))

    def whole(shape):
        return pl.BlockSpec(shape, lambda i: (0, 0), pipeline_mode=pl.Buffered(1))

    def held(shape):
        return pl.BlockSpec(shape, lambda i: (0, 0))

    return pl.pallas_call(
        feed_kernel,
        grid=(rows // tile,),
        in_specs=[block] * 3
        + [whole((D, D)), whole((D, FF)), whole((D, FF)), whole((8, D)), whole((8, FF)), whole((1, D))],
        out_specs=[block, block, block, wide_block, wide_block, block, block, block]
        + [held((16, D)), held((8, FF))],
        out_shape=[
            jax.ShapeDtypeStruct((rows, D), BF16),
            jax.ShapeDtypeStruct((rows, D), BF16),
            jax.ShapeDtypeStruct((rows, D), BF16),
            jax.ShapeDtypeStruct((rows, FF), BF16),
            jax.ShapeDtypeStruct((rows, FF), BF16),
            jax.ShapeDtypeStruct((rows, D), BF16),
            jax.ShapeDtypeStruct((rows, D), F32),
            jax.ShapeDtypeStruct((rows, D), BF16),
            jax.ShapeDtypeStruct((16, D), F32),
            jax.ShapeDtypeStruct((8, FF), F32),
        ],
        scratch_shapes=[pltpu.VMEM((tile, FF), F32)] * 3,
        compiler_params=params(dimension_semantics=("arbitrary",)),
        name="feed_forward",
    )(tokens, attended, cotangent, out_w, up_w, down_w, vecs, wide, scales)


def outer_kernel(left_ref, right_ref, out_ref, turned):
    @pl.when(pl.program_id(0) == 0)
    def _():
        turned[...] = left_ref[...].T

    out_ref[...] = nn(turned[...], right_ref[...]).astype(BF16)


def outer_product(left, right, panel):
    rows, width = left.shape
    cols = right.shape[1]
    return pl.pallas_call(
        outer_kernel,
        grid=(cols // panel,),
        in_specs=[
            pl.BlockSpec((rows, width), lambda i: (0, 0), pipeline_mode=pl.Buffered(1)),
            pl.BlockSpec((rows, panel), lambda i: (0, i)),
        ],
        out_specs=pl.BlockSpec((width, panel), lambda i: (0, i)),
        out_shape=jax.ShapeDtypeStruct((width, cols), BF16),
        scratch_shapes=[pltpu.VMEM((width, rows), BF16)],
        compiler_params=params(dimension_semantics=("arbitrary",)),
        name="weight_grad",
    )(left, right)


def attention_back_kernel(
    buckets, probs_ref, query_ref, keys_ref, values_ref, low_ref, normed_ref, x_ref, middle_ref,
    weight_q, weight_k, weight_v, vec_ref,
    input_grad_ref, grid_ref, weight_grad_ref, pair_ref, sums_ref,
    turned, first_in, proj_ref,
):
    count = x_ref.shape[0] // SLOT
    step = pl.program_id(0)

    @pl.when(step == 0)
    def _():
        turned[...] = normed_ref[...].T
        first_in[...] = jnp.zeros_like(first_in)

    grid_ref[...] = jnp.zeros_like(grid_ref)

    def one_sequence(s, carry):
        rows = pl.ds(pl.multiple_of(s * SLOT, SLOT), SLOT)
        query_grad, keys_grad, values_grad, scores_grads = attend_back(
            query_ref[0, rows, :], keys_ref[0, rows, :], values_ref[0, rows, :], low_ref[rows, :],
            [probs_ref[half, s] for half in range(2)],
        )
        small = jnp.where(buckets[s] == 0, 1.0, 0.0)
        for half in range(2):
            grid_ref[0, half] += scores_grads[half] * small
            grid_ref[1, half] += scores_grads[half] * (1.0 - small)
        proj_ref[rows, 0:128] = query_grad
        proj_ref[rows, 128:256] = keys_grad
        proj_ref[rows, 256:384] = values_grad
        return carry

    lax.fori_loop(0, count, one_sequence, 0)
    proj = proj_ref[...]
    weight_grad_ref[0] = nn(turned[...], proj).astype(BF16)
    pair_ref[0] = jnp.broadcast_to(column_sum(proj.astype(F32)), (8, 384))
    weights = jnp.concatenate([weight_q[...], weight_k[...], weight_v[...]], 1)
    first_in[...] += nt(proj, weights)

    @pl.when(step == PAIRS - 1)
    def _():
        sums_ref[...] = jnp.zeros_like(sums_ref)

        def one_block(b, carry):
            rows = pl.ds(pl.multiple_of(b * SLOT, SLOT), SLOT)
            unit, inverse = standardize(x_ref[rows, :].astype(F32))
            grad = first_in[rows, :]
            sums_ref[0:1, :] += column_sum(grad * unit)
            sums_ref[1:2, :] += column_sum(grad)
            back = norm_back(grad * vec_ref[0:1, :], unit, inverse)
            input_grad_ref[rows, :] = (middle_ref[rows, :] + back).astype(BF16)
            return carry

        lax.fori_loop(0, count, one_block, 0)


def attention_back(buckets, probs, qkv, attended_low, normed, tokens, middle_grad, weight, vecs):
    rows = tokens.shape[0]
    count = rows // SLOT

    def whole(shape):
        return pl.BlockSpec(shape, lambda i: (0,) * len(shape), pipeline_mode=pl.Buffered(1))

    def held(shape):
        return pl.BlockSpec(shape, lambda i: (0,) * len(shape))

    def panel(base):
        return pl.BlockSpec((1, rows, 128), lambda i: (base + i, 0, 0))

    def weight_panel(base):
        return pl.BlockSpec((D, 128), lambda i: (0, base + i))

    return pl.pallas_call(
        attention_back_kernel,
        grid=(PAIRS,),
        in_specs=[
            pl.BlockSpec(memory_space=pltpu.SMEM),
            pl.BlockSpec((2, count, SLOT, SLOT), lambda i: (i, 0, 0, 0)),
            panel(0), panel(PAIRS), panel(2 * PAIRS),
            pl.BlockSpec((rows, 128), lambda i: (0, i)),
            whole((rows, D)), whole((rows, D)), whole((rows, D)),
            weight_panel(0), weight_panel(PAIRS), weight_panel(2 * PAIRS),
            whole((8, D)),
        ],
        out_specs=[
            held((rows, D)),
            pl.BlockSpec((2, 2, SLOT, SLOT), lambda i: (0, i, 0, 0)),
            pl.BlockSpec((1, D, 384), lambda i: (i, 0, 0)),
            pl.BlockSpec((1, 8, 384), lambda i: (i, 0, 0)),
            held((8, D)),
        ],
        out_shape=[
            jax.ShapeDtypeStruct((rows, D), BF16),
            jax.ShapeDtypeStruct((2, HEADS, SLOT, SLOT), F32),
            jax.ShapeDtypeStruct((PAIRS, D, 384), BF16),
            jax.ShapeDtypeStruct((PAIRS, 8, 384), F32),
            jax.ShapeDtypeStruct((8, D), F32),
        ],
        scratch_shapes=[
            pltpu.VMEM((D, rows), BF16),
            pltpu.VMEM((rows, D), F32),
            pltpu.VMEM((rows, 384), BF16),
        ],
        compiler_params=params(dimension_semantics=("arbitrary",)),
        name="attention_backward",
    )(buckets, probs, qkv, qkv, qkv, attended_low, normed, tokens, middle_grad, weight, weight, weight, vecs)


MESH = pl.DeviceIdType.MESH
ANY = pl.ANY


class Place:
    def __init__(self):
        fsdp = lax.axis_index("fsdp")
        dp = lax.axis_index("dp")
        self.z, self.y, self.x, self.core = fsdp // 2, fsdp % 2, dp // 2, dp % 2

    def at(self, z=None, y=None, x=None, core=None):
        z = self.z if z is None else z
        y = self.y if y is None else y
        x = self.x if x is None else x
        core = self.core if core is None else core
        return (z * 2 + y, x * 2 + core)

    def greet(self):
        barrier = pltpu.get_barrier_semaphore()
        peers = [self.at(z=(self.z + k) % 4, y=self.y) for k in range(1, 4)]
        peers += [self.at(z=(self.z + k) % 4, y=1 - self.y) for k in range(4)]
        peers += [
            self.at(x=1 - self.x),
            self.at(core=1 - self.core),
            self.at(x=1 - self.x, core=1 - self.core),
        ]
        for peer in peers:
            pl.semaphore_signal(barrier, inc=1, device_id=peer, device_id_type=MESH)
        pl.semaphore_wait(barrier, len(peers))


def remote(src, dst, send, recv, peer):
    return pltpu.make_async_remote_copy(
        src_ref=src, dst_ref=dst, send_sem=send, recv_sem=recv, device_id=peer, device_id_type=MESH
    )


def rows_of(first, size):
    return pl.ds(pl.multiple_of(first * size, size), size)


def chunk(kind, ref, r, d):
    if kind == "panel":
        return ref.at[d, rows_of(r, 96), :]
    if kind == "wide":
        return ref.at[rows_of(r, 96), rows_of(d, 768)]
    return ref.at[rows_of(d, 192), rows_of(r, 384)]


class Gather:
    def __init__(self, place, pieces, fulls, send, recv, local):
        self.place, self.pieces, self.fulls = place, pieces, fulls
        self.send, self.recv, self.local = send, recv, local
        self.made = {}

    def slot(self, w, z, y, x):
        return chunk(GATHER_KINDS[w], self.fulls[w], z * 2 + y, x * 2 + self.place.core)

    def copy(self, w, index, src, dst, peer):
        self.made[w, index] = remote(src, dst, self.send.at[w, index], self.recv.at[w, index], peer)
        return self.made[w, index]

    def sources(self, w, k):
        here = self.place
        over_x = (k + GATHER_TURN[w]) % 2 == 0
        near = (here.y, 1 - here.x) if over_x else (1 - here.y, here.x)
        far = (1 - here.y, here.x) if over_x else (here.y, 1 - here.x)
        upper = here.z // 2
        depth = here.z + upper * (3 - 2 * here.z)
        z = k - depth if k == 1 else k
        z = z + upper * (3 - 2 * z) if k else here.z
        return z, near, far

    def plan(self, w):
        here = self.place
        own = self.slot(w, here.z, here.y, here.x)
        self.made[w, "keep"] = pltpu.make_async_copy(self.pieces[w], own, self.local.at[w])
        sibling = here.at(core=1 - here.core)
        pair = here.at(z=here.z + 1 - 2 * (here.z % 2))
        across = here.at(z=3 - here.z)
        for k in range(4):
            z, near, far = self.sources(w, k)
            mine = self.slot(w, z, here.y, here.x)
            src = mine if k else self.pieces[w]
            if k == 0:
                self.copy(w, 1, src, mine, pair)
                self.copy(w, 2, src, mine, across)
            elif k == 1:
                self.copy(w, 3, src, mine, across)
            else:
                self.made[w, "on", k] = remote(
                    src, mine, self.send.at[w, 30 + k], self.recv.at[w, k], pair
                )
            self.copy(w, 4 + k, src, mine, here.at(y=near[0], x=near[1]))
            passed = self.slot(w, z, *near)
            self.copy(w, 8 + 2 * k, src, mine, here.at(y=far[0], x=far[1]))
            self.copy(w, 9 + 2 * k, passed, passed, here.at(y=far[0], x=far[1]))
            third = self.slot(w, z, *far)
            fourth = self.slot(w, z, 1 - here.y, 1 - here.x)
            for n, part in enumerate((src, passed, third, fourth)):
                dst = mine if n == 0 else part
                self.copy(w, 16 + 4 * k + n, part, dst, sibling)

    def when_middle(self, act):
        pl.when(self.place.z * (3 - self.place.z) > 0)(act)

    def begin(self, w):
        self.made[w, "keep"].start()
        self.made[w, 1].start()
        self.when_middle(lambda: self.made[w, 2].start())

    def first(self, w, k):
        if k:
            self.made[w, k].wait_recv()
            on = self.made[w, 3] if k == 1 else self.made[w, "on", k]
            self.when_middle(lambda: on.start())
        self.made[w, 4 + k].start()
        self.made[w, 16 + 4 * k].start()

    def second(self, w, k):
        self.made[w, 4 + k].wait_recv()
        self.made[w, 8 + 2 * k].start()
        self.made[w, 9 + 2 * k].start()
        self.made[w, 17 + 4 * k].start()

    def third(self, w, k):
        for n in range(2):
            self.made[w, 8 + 2 * k + n].wait_recv()
            self.made[w, 18 + 4 * k + n].start()

    def finish(self, w):
        for n in range(16):
            self.made[w, 16 + n].wait_recv()
        for n in [1] + list(range(4, 32)):
            self.made[w, n].wait_send()

        def passed_on():
            for made in (self.made[w, 2], self.made[w, 3], self.made[w, "on", 2], self.made[w, "on", 3]):
                made.wait_send()

        self.when_middle(passed_on)
        self.made[w, "keep"].wait()


MIXED, UP, DOWN = range(3)
GATHER_TURN = (0, 1, 0)
GATHER_KINDS = ("panel", "wide", "turned")


def lined(ref, row, width):
    return jnp.concatenate([ref[f, row : row + 1, :width].astype(F32) for f in range(8)], 1)


def forward_kernel(
    lengths, buckets, x_ref, cot_ref, scale_ref, qkv_p, out_p, up_p, down_p, vec_p,
    normed_ref, qkv_ref, probs_ref, result_ref, mixed_ref, second_ref, act_ref, low_ref, branch_ref,
    middle_grad_ref, attended_low_ref, sums_ref, wide_sums_ref, vec_ref, qkv_out,
    mixed_p, down_t, qkv_w, up_w, down_w, vec_f, out_w, bias_ref, wide_ref, qkv_bias_ref, table_ref,
    wall_small, wall_large, visual, attended_ref, gelu_ref, slope_ref, grad_ref,
    send, recv, local, small_send, small_recv, small_local, qkv_sem,
):
    step = pl.program_id(0)
    count = pl.num_programs(0) // 2
    place = Place()
    gather = Gather(place, (mixed_p, up_p, down_t), (qkv_w, up_w, down_w), send, recv, local)
    for w in range(3):
        gather.plan(w)
    f = place.z * 2 + place.y
    small = [pltpu.make_async_copy(vec_p, vec_f.at[f], small_local)]
    for k in range(1, 8):
        peer = (f + k) % 8
        small.append(
            remote(
                vec_p, vec_f.at[f], small_send.at[k], small_recv.at[k],
                place.at(z=peer // 2, y=peer % 2),
            )
        )
    keep_qkv = pltpu.make_async_copy(qkv_w, qkv_out, qkv_sem)

    @pl.when(step == 0)
    def _():
        mixed_p[:, :576] = qkv_p[...]
        mixed_p[:, 576:] = out_p[...]
        place.greet()
        for made in small:
            made.start()
        gather.begin(MIXED)
        gather.first(MIXED, 0)
        gather.first(UP, 0)
        down_t[...] = down_p[...].T
        gather.first(DOWN, 0)
        for made in small:
            made.wait()
        for n in range(8):
            vec_ref[n : n + 1, :] = lined(vec_f, n, 96)
        for n in range(3):
            wide_ref[n : n + 1, :] = lined(vec_f, 8 + n, 384)
        pair = lined(vec_f, 11, 192)
        qkv_bias_ref[0:1, :] = jnp.concatenate([pair[:, :D], jnp.zeros((1, D), F32), pair[:, D:]], 1)
        lane = lax.broadcasted_iota(jnp.int32, (1, 3 * D), 1)
        qkv_bias_ref[1:2, :] = jnp.where(lane < D, HEAD_DIM ** (-0.5), 1.0)
        table_ref[...] = jnp.concatenate([vec_f[n, 16:32, :192].astype(F32) for n in range(8)], 1)
        bias_walls(table_ref, wall_small, wall_large, visual)
        heads = functools.partial(bias_head, table_ref, bias_ref, wall_small, wall_large, visual)
        gather.first(MIXED, 1)
        gather.begin(UP)
        gather.second(MIXED, 0)
        gather.second(UP, 0)
        gather.first(MIXED, 2)
        gather.second(DOWN, 0)
        lax.fori_loop(0, 2, heads, 0)
        gather.first(MIXED, 3)
        gather.begin(DOWN)
        gather.second(MIXED, 1)
        gather.third(MIXED, 0)
        lax.fori_loop(2, 4, heads, 0)
        gather.second(MIXED, 2)
        gather.first(UP, 1)
        gather.third(UP, 0)
        lax.fori_loop(4, 6, heads, 0)
        gather.second(MIXED, 3)
        gather.third(DOWN, 0)
        gather.third(MIXED, 1)
        gather.first(UP, 2)
        lax.fori_loop(6, 8, heads, 0)
        gather.second(UP, 1)
        gather.first(UP, 3)
        gather.third(MIXED, 2)
        gather.first(DOWN, 1)
        lax.fori_loop(8, HEADS, heads, 0)
        gather.second(UP, 2)
        gather.third(MIXED, 3)
        gather.finish(MIXED)
        keep_qkv.start()
        sums_ref[...] = jnp.zeros_like(sums_ref)
        wide_sums_ref[...] = jnp.zeros_like(wide_sums_ref)

    schedule = [
        [("first", DOWN, 2)],
        [("second", UP, 3)],
        [("third", UP, 1), ("first", DOWN, 3)],
        [("second", DOWN, 1)],
        [("third", UP, 2)],
        [("second", DOWN, 2)],
        [("third", UP, 3)],
        [("second", DOWN, 3)],
        [("third", DOWN, 1)],
        [],
        [("third", DOWN, 2)],
        [],
    ]

    def progress(spot):
        for s in range(count):
            todo = schedule[3 * s + spot]
            if todo:

                @pl.when(step == s)
                def _(todo=todo):
                    for name, w, k in todo:
                        getattr(gather, name)(w, k)

    @pl.when(step < count)
    def _():
        rows = pl.ds(pl.multiple_of(step * SLOT, SLOT), SLOT)
        progress(0)
        unit, inverse = standardize(x_ref[...].astype(F32))
        normed = (unit * vec_ref[0:1, :] + vec_ref[1:2, :]).astype(BF16)
        normed_ref[...] = normed
        for d in range(4):
            cols = slice(576 * d, 576 * d + 576)
            out = (nn(normed, qkv_w[d, :, :576]) + qkv_bias_ref[0:1, cols]) * qkv_bias_ref[1:2, cols]
            qkv_ref[:, cols] = out.astype(BF16)
        live = lax.broadcasted_iota(jnp.int32, (SLOT, SLOT), 1) < lengths[step]
        bucket = buckets[step]
        for pair in range(PAIRS):
            if pair % 3 == 0:
                progress(1 + pair // 3)
            query = qkv_ref[:, 128 * pair : 128 * pair + 128]
            keys = qkv_ref[:, D + 128 * pair : D + 128 * pair + 128]
            values = qkv_ref[:, 2 * D + 128 * pair : 2 * D + 128 * pair + 128]
            bias = [bias_ref[bucket, 2 * pair + half] for half in range(2)]
            probs, out = attend(query, keys, values, bias, live)
            for half in range(2):
                probs_ref[2 * pair + half, 0] = probs[half]
            attended_ref[rows, 128 * pair : 128 * pair + 128] = out

    @pl.when(step == count)
    def _():
        gather.finish(UP)
        gather.third(DOWN, 3)
        for d in range(4):
            out_w[:, 192 * d : 192 * d + 192] = qkv_w[d, :, 576:]

    @pl.when(step >= count)
    def _():
        rows = pl.ds(pl.multiple_of((step - count) * SLOT, SLOT), SLOT)

        def wait_down():
            @pl.when(step == count)
            def _():
                gather.finish(DOWN)

        feed_block(
            x_ref, attended_ref.at[rows, :], cot_ref, out_w, up_w, down_w, vec_ref, wide_ref, scale_ref,
            result_ref, mixed_ref, second_ref, act_ref, low_ref, branch_ref, middle_grad_ref,
            attended_low_ref, sums_ref, wide_sums_ref, gelu_ref, slope_ref, grad_ref, wait_down,
        )

    @pl.when(step == 2 * count - 1)
    def _():
        keep_qkv.wait()


def forward(lengths, buckets, tokens, cotangent, scales, qkv_p, out_p, up_p, down_p, vec_p):
    rows = tokens.shape[0]
    count = rows // SLOT
    smem = pl.BlockSpec(memory_space=pltpu.SMEM)

    def early(shape):
        return pl.BlockSpec(shape, lambda i: (jnp.minimum(i, count - 1),) + (0,) * (len(shape) - 1))

    def late(shape):
        return pl.BlockSpec(shape, lambda i: (jnp.maximum(i - count, 0),) + (0,) * (len(shape) - 1))

    def held(shape):
        return pl.BlockSpec(shape, lambda i: (0,) * len(shape))

    block = (SLOT, D)
    wide = (SLOT, FF)
    return pl.pallas_call(
        forward_kernel,
        grid=(2 * count,),
        in_specs=[
            smem, smem, pl.BlockSpec(block, lambda i: (i % count, 0)), late(block), held((1, D)),
        ]
        + [held((96, 576)), held((96, 192)), pl.BlockSpec(memory_space=ANY), held((384, 192))]
        + [pl.BlockSpec(memory_space=ANY)],
        out_specs=[
            early(block), early((SLOT, 3 * D)),
            pl.BlockSpec((HEADS, 1, SLOT, SLOT), lambda i: (0, jnp.minimum(i, count - 1), 0, 0)),
            late(block), late(block), late(block), late(wide), late(wide), late(block), late(block),
            late(block), held((16, D)), held((8, FF)), held((8, D)), pl.BlockSpec(memory_space=ANY),
        ],
        out_shape=[
            jax.ShapeDtypeStruct((rows, D), BF16),
            jax.ShapeDtypeStruct((rows, 3 * D), BF16),
            jax.ShapeDtypeStruct((HEADS, count, SLOT, SLOT), BF16),
            jax.ShapeDtypeStruct((rows, D), BF16),
            jax.ShapeDtypeStruct((rows, D), BF16),
            jax.ShapeDtypeStruct((rows, D), BF16),
            jax.ShapeDtypeStruct((rows, FF), BF16),
            jax.ShapeDtypeStruct((rows, FF), BF16),
            jax.ShapeDtypeStruct((rows, D), BF16),
            jax.ShapeDtypeStruct((rows, D), F32),
            jax.ShapeDtypeStruct((rows, D), BF16),
            jax.ShapeDtypeStruct((16, D), F32),
            jax.ShapeDtypeStruct((8, FF), F32),
            jax.ShapeDtypeStruct((8, D), F32),
            jax.ShapeDtypeStruct((4, D, D), BF16),
        ],
        scratch_shapes=[
            pltpu.VMEM((96, D), BF16),
            pltpu.VMEM((192, 384), BF16),
            pltpu.VMEM((4, D, D), BF16),
            pltpu.VMEM((D, FF), BF16),
            pltpu.VMEM((D, FF), BF16),
            pltpu.VMEM((8,) + vec_p.shape, BF16),
            pltpu.VMEM((D, D), BF16),
            pltpu.VMEM((2, HEADS, SLOT, SLOT), BF16),
            pltpu.VMEM((8, FF), F32),
            pltpu.VMEM((8, 3 * D), F32),
            pltpu.VMEM((16, TABLE), F32),
            pltpu.VMEM((2, 128, 128), F32),
            pltpu.VMEM((4, 256, 128), F32),
            pltpu.VMEM((SLOT, SLOT), F32),
            pltpu.VMEM((rows, D), F32),
            pltpu.VMEM(wide, F32),
            pltpu.VMEM(wide, F32),
            pltpu.VMEM(wide, F32),
            pltpu.SemaphoreType.DMA((3, 34)),
            pltpu.SemaphoreType.DMA((3, 32)),
            pltpu.SemaphoreType.DMA((3,)),
            pltpu.SemaphoreType.DMA((8,)),
            pltpu.SemaphoreType.DMA((8,)),
            pltpu.SemaphoreType.DMA,
            pltpu.SemaphoreType.DMA,
        ],
        compiler_params=params(
            collective_id=1, has_side_effects=True, dimension_semantics=("arbitrary",)
        ),
        name="forward",
    )(lengths, buckets, tokens, cotangent, scales, qkv_p, out_p, up_p, down_p, vec_p)


ORDER = (1, 2, 3, 0)


class Scatter:
    def __init__(self, place, kind, grad, out, buffers):
        self.place, self.kind, self.grad, self.out = place, kind, grad, out
        self.cores, self.over_x, self.over_y, self.far, self.quarter, self.send, self.recv = buffers
        self.made = {}
        here = place
        for k in range(4):
            z = (here.z + k) % 4
            mine = 2 * here.x + here.core
            other = 2 * (1 - here.x) + here.core
            for x in range(2):
                self.copy(
                    k, x, self.block(2 * x + 1 - here.core, z), self.cores.at[k, x],
                    here.at(core=1 - here.core),
                )
            if k % 2 == 0:
                self.copy(k, 2, self.block(other, z), self.over_x.at[k // 2], here.at(x=1 - here.x))
                self.copy(
                    k, 4, self.part(mine, z, 1 - here.y), self.far.at[k], here.at(y=1 - here.y)
                )
            else:
                for x in range(2):
                    self.copy(
                        k, 2 + x, self.part(2 * x + here.core, z, 1 - here.y),
                        self.over_y.at[k // 2, x], here.at(y=1 - here.y),
                    )
                self.copy(k, 4, self.part(other, z, here.y), self.far.at[k], here.at(x=1 - here.x))
            if k:
                self.copy(k, 5, self.part(mine, z, here.y), self.quarter.at[k - 1], here.at(z=z))

    def block(self, d, z):
        if self.kind == "panel":
            return self.grad.at[d, rows_of(z, 192), :]
        if self.kind == "wide":
            return self.grad.at[rows_of(z, 192), rows_of(d, 768)]
        return self.grad.at[rows_of(d, 192), rows_of(z, 768)]

    def part(self, d, z, y):
        if self.kind == "panel":
            return self.grad.at[d, rows_of(2 * z + y, 96), :]
        if self.kind == "wide":
            return self.grad.at[rows_of(2 * z + y, 96), rows_of(d, 768)]
        return self.grad.at[rows_of(d, 192), rows_of(2 * z + y, 384)]

    def copy(self, k, index, src, dst, peer):
        self.made[k, index] = remote(src, dst, self.send.at[k, index], self.recv.at[k, index], peer)

    def add(self, target, source):
        for first in range(0, target.shape[0], 48):
            at = pl.ds(first, 48)
            target[at, :] = target[at, :] + source[at, :]

    def core(self, k):
        for x in range(2):
            self.made[k, x].start()

    def plane(self, k):
        here = self.place
        z = (here.z + k) % 4
        for x in range(2):
            self.made[k, x].wait_recv()
            self.add(self.block(2 * x + here.core, z), self.cores.at[k, x])
        self.made[k, 2].start()
        if k % 2:
            self.made[k, 3].start()

    def turn(self, k):
        here = self.place
        z = (here.z + k) % 4
        self.made[k, 2].wait_recv()
        if k % 2 == 0:
            self.add(self.block(2 * here.x + here.core, z), self.over_x.at[k // 2])
        else:
            self.made[k, 3].wait_recv()
            for x in range(2):
                self.add(self.part(2 * x + here.core, z, here.y), self.over_y.at[k // 2, x])
        self.made[k, 4].start()

    def line(self, k):
        here = self.place
        self.made[k, 4].wait_recv()
        self.add(self.part(2 * here.x + here.core, (here.z + k) % 4, here.y), self.far.at[k])
        if k:
            self.made[k, 5].start()

    def end(self):
        here = self.place
        for k in range(1, 4):
            self.made[k, 5].wait_recv()
        total = self.part(2 * here.x + here.core, here.z, here.y)[...].astype(F32)
        for k in range(3):
            total = total + self.quarter[k].astype(F32)
        self.out[...] = total.T if self.kind == "turned" else total
        for made in self.made.values():
            made.wait_send()


def scatter_scratch(kind, width):
    half = (192, width // 2) if kind == "turned" else (96, width)
    return [
        pltpu.VMEM((4, 2, 192, width), BF16),
        pltpu.VMEM((2, 192, width), BF16),
        pltpu.VMEM((2, 2) + half, BF16),
        pltpu.VMEM((4,) + half, BF16),
        pltpu.VMEM((3,) + half, BF16),
        pltpu.SemaphoreType.DMA((4, 6)),
        pltpu.SemaphoreType.DMA((4, 6)),
    ]


BACK_SCHEDULE = {
    2: [("down", "plane", 0)],
    3: [("down", "plane", 1)],
    4: [("down", "plane", 2)],
    5: [("down", "plane", 3), ("down", "turn", 0)],
    6: [("down", "turn", 1)],
    7: [("down", "line", 0)],
    8: [("down", "turn", 2), ("down", "turn", 3), ("down", "line", 1)],
    9: [("up", "plane", 0), ("up", "plane", 1), ("down", "line", 2)],
    10: [("down", "line", 3), ("up", "plane", 2), ("up", "plane", 3)],
    11: [("up", "turn", 0), ("up", "turn", 1), ("out", "plane", 0), ("out", "plane", 1)],
    12: [("up", "line", 0), ("up", "turn", 2), ("out", "plane", 2), ("out", "plane", 3)],
    13: [("up", "line", 1), ("up", "turn", 3), ("out", "turn", 0), ("out", "turn", 1)],
    14: [("up", "line", 2), ("up", "line", 3), ("out", "turn", 2), ("out", "turn", 3)],
}


def backward_kernel(
    buckets, cot_ref, act_ref, second_ref, low_ref, mixed_ref, branch_ref,
    probs_ref, query_ref, keys_ref, values_ref, attended_low_ref,
    query_grad_ref, keys_grad_ref, values_grad_ref, grid_ref, down_out, up_out, out_out,
    turned, down_ref, up_ref, out_ref, *buffers,
):
    step = pl.program_id(0)
    place = Place()
    parts = {
        "down": Scatter(place, "turned", down_ref, down_out, buffers[0:7]),
        "up": Scatter(place, "wide", up_ref, up_out, buffers[7:14]),
        "out": Scatter(place, "panel", out_ref, out_out, buffers[14:21]),
    }

    @pl.when(step == 0)
    def _():
        place.greet()

    for at, todo in BACK_SCHEDULE.items():

        @pl.when(step == at)
        def _(todo=todo):
            for name, event, n in todo:
                getattr(parts[name], event)(ORDER[n])

    @pl.when(step < 4)
    def _():
        @pl.when(step == 0)
        def _():
            turned[...] = cot_ref[...].T

        z = (place.z + 1 + step) % 4
        down_ref[:, rows_of(z, 768)] = nn(turned[...], act_ref[...]).astype(BF16)
        for n in range(4):

            @pl.when(step == n)
            def _(n=n):
                parts["down"].core(ORDER[n])

    @pl.when((step >= 4) & (step < 8))
    def _():
        @pl.when(step == 4)
        def _():
            turned[...] = second_ref[...].T

        up_ref[:, rows_of(step - 4, 768)] = nn(turned[...], low_ref[...]).astype(BF16)

        @pl.when(step == 7)
        def _():
            for k in ORDER:
                parts["up"].core(k)

    @pl.when(step == 8)
    def _():
        turned[...] = mixed_ref[...].T
        for d in range(4):
            out_ref[d] = nn(turned[...], branch_ref[:, 192 * d : 192 * d + 192]).astype(BF16)
        for k in ORDER:
            parts["out"].core(k)

    @pl.when(step >= 9)
    def _():
        count = query_ref.shape[0] // SLOT
        for s in range(count):
            rows = slice(s * SLOT, s * SLOT + SLOT)
            query_grad, keys_grad, values_grad, scores_grads = attend_back(
                query_ref[rows, :], keys_ref[rows, :], values_ref[rows, :], attended_low_ref[rows, :],
                [probs_ref[half, s] for half in range(2)],
            )
            query_grad_ref[rows, :] = query_grad
            keys_grad_ref[rows, :] = keys_grad
            values_grad_ref[rows, :] = values_grad
            small = jnp.where(buckets[s] == 0, 1.0, 0.0)
            for half in range(2):
                if s == 0:
                    grid_ref[0, half] = scores_grads[half] * small
                    grid_ref[1, half] = scores_grads[half] * (1.0 - small)
                else:
                    grid_ref[0, half] += scores_grads[half] * small
                    grid_ref[1, half] += scores_grads[half] * (1.0 - small)

    @pl.when(step == 14)
    def _():
        parts["down"].end()
        for k in ORDER:
            parts["out"].line(k)
        parts["up"].end()
        parts["out"].end()


def backward(buckets, cotangent, act, second, low, mixed, branch, probs, qkv, attended_low):
    rows = cotangent.shape[0]
    count = rows // SLOT

    def whole(shape):
        return pl.BlockSpec(shape, lambda i: (0,) * len(shape), pipeline_mode=pl.Buffered(1))

    def held(shape):
        return pl.BlockSpec(shape, lambda i: (0,) * len(shape))

    def pair(i):
        return jnp.clip(i - 9, 0, PAIRS - 1)

    def panel(base):
        return pl.BlockSpec((rows, 128), lambda i: (0, base + pair(i)))

    def act_panel(i):
        return (0, (lax.axis_index("fsdp") // 2 + 1 + jnp.minimum(i, 3)) % 4)

    return pl.pallas_call(
        backward_kernel,
        grid=(15,),
        in_specs=[
            pl.BlockSpec(memory_space=pltpu.SMEM),
            whole((rows, D)),
            pl.BlockSpec((rows, D), act_panel),
            whole((rows, D)),
            pl.BlockSpec((rows, D), lambda i: (0, jnp.clip(i - 4, 0, 3))),
            whole((rows, D)), whole((rows, D)),
            pl.BlockSpec((2, count, SLOT, SLOT), lambda i: (pair(i), 0, 0, 0)),
            panel(0), panel(PAIRS), panel(2 * PAIRS), panel(0),
        ],
        out_specs=[
            panel(0), panel(0), panel(0),
            pl.BlockSpec((2, 2, SLOT, SLOT), lambda i: (0, pair(i), 0, 0)),
            held((384, 192)), held((96, 768)), held((96, 192)),
        ],
        out_shape=[jax.ShapeDtypeStruct((rows, D), BF16)] * 3
        + [
            jax.ShapeDtypeStruct((2, HEADS, SLOT, SLOT), F32),
            jax.ShapeDtypeStruct((384, 192), F32),
            jax.ShapeDtypeStruct((96, 768), F32),
            jax.ShapeDtypeStruct((96, 192), F32),
        ],
        scratch_shapes=[
            pltpu.VMEM((D, rows), BF16),
            pltpu.VMEM((D, FF), BF16),
            pltpu.VMEM((D, FF), BF16),
            pltpu.VMEM((4, D, 192), BF16),
        ]
        + scatter_scratch("turned", 768) + scatter_scratch("wide", 768) + scatter_scratch("panel", 192),
        compiler_params=params(
            collective_id=2, has_side_effects=True, dimension_semantics=("arbitrary",)
        ),
        name="backward",
    )(buckets, cotangent, act, second, low, mixed, branch, probs, qkv, qkv, qkv, attended_low)


def pack_sums(sums_ref, first_ref, wide_ref, pair, table_ref, packed):
    low = first_ref[0:2, :]
    narrow = sums_ref[...]
    group = lax.broadcasted_iota(jnp.int32, (D, 128), 0) // HEAD_DIM
    pick = (group == lax.broadcasted_iota(jnp.int32, (D, 128), 1)).astype(F32).astype(BF16)
    high, rest = split_low(narrow[8:16])
    heads = (nn(high, pick) + nn(rest, pick))[0:1]
    heads = jnp.concatenate([heads, jnp.zeros((1, 64), F32)], 1)
    for f in range(8):
        at = slice(96 * f, 96 * f + 96)
        packed[f, 0:1, :] = jnp.concatenate(
            [low[0:1, at], low[1:2, at], narrow[2:3, at], narrow[3:4, at]], 1
        )
        packed[f, 1:2, :] = jnp.concatenate([narrow[n : n + 1, at] for n in range(4, 8)], 1)
        packed[f, 2:5, :] = wide_ref[0:3, 384 * f : 384 * f + 384]
        at = slice(192 * f, 192 * f + 192)
        packed[f, 5:6, :] = jnp.concatenate([pair[:, at], heads], 1)
        for n in range(PAIRS):
            packed[f, 6 + n : 7 + n, :] = jnp.concatenate(
                [table_ref[2 * n : 2 * n + 1, at], table_ref[2 * n + 1 : 2 * n + 2, at]], 1
            )
        packed[f, 12:16, :] = jnp.zeros((4, 384), F32)


class SmallSums:
    def __init__(self, place, packed, rows, peers, sems):
        self.place, self.packed, self.rows, self.peers = place, packed, rows, peers
        self.send, self.recv = sems

    def begin(self):
        here = self.place
        f = here.z * 2 + here.y
        self.made = []
        for k in range(1, 8):
            to = (f + k) % 8
            made = remote(
                self.packed.at[to], self.rows.at[k - 1], self.send.at[k], self.recv.at[k],
                here.at(z=to // 2, y=to % 2),
            )
            made.start()
            self.made.append(made)

    def cross(self):
        here = self.place
        f = here.z * 2 + here.y
        for made in self.made:
            made.wait()
        total = self.packed[f]
        for k in range(7):
            total = total + self.rows[k]
        self.peers[0] = total
        d = here.x * 2 + here.core
        self.made = []
        for k in range(1, 4):
            to = (d + k) % 4
            made = remote(
                self.peers.at[0], self.peers.at[k], self.send.at[7 + k], self.recv.at[7 + k],
                here.at(x=to // 2, core=to % 2),
            )
            made.start()
            self.made.append(made)

    def end(self):
        for made in self.made:
            made.wait()
        return (self.peers[0] + self.peers[1]) + (self.peers[2] + self.peers[3])


def finish_kernel(
    query_grad, keys_grad, values_grad, normed_ref, vec_ref, sums_ref, wide_ref, x_hbm, middle_hbm,
    weight_hbm, grid_hbm, *rest,
):
    input_grad_ref, qkv_out = rest[:2]
    small_outs = rest[2:16]
    (
        x_ref, middle_ref, weight_ref, grid_ref, qkv_ref, first_in, table_ref, first_ref,
        wall_small, wall_large, packed, gathered, peers, small_send, small_recv, local,
    ) = rest[16:32]
    place = Place()
    loads = [
        pltpu.make_async_copy(src, dst, local.at[n])
        for n, (src, dst) in enumerate(
            ((grid_hbm, grid_ref), (weight_hbm, weight_ref), (x_hbm, x_ref), (middle_hbm, middle_ref))
        )
    ]
    for made in loads:
        made.start()
    place.greet()
    qkv = Scatter(place, "panel", qkv_ref, qkv_out, rest[32:39])
    small = SmallSums(place, packed, gathered, peers, (small_send, small_recv))
    count = normed_ref.shape[0] // SLOT

    def panel(d, rows=slice(None)):
        if d == 0:
            return query_grad[rows, 0:576]
        if d == 1:
            return jnp.concatenate([query_grad[rows, 576:768], keys_grad[rows, 0:384]], 1)
        if d == 2:
            return jnp.concatenate([keys_grad[rows, 384:768], values_grad[rows, 0:192]], 1)
        return values_grad[rows, 192:768]

    turned = normed_ref[...].T
    for d in range(4):
        qkv_ref[d] = nn(turned, panel(d)).astype(BF16)
    for k in ORDER:
        qkv.core(k)
    table_grad_start(table_ref, wall_small, wall_large)
    heads = functools.partial(table_grad_head, grid_ref, table_ref, wall_small, wall_large)
    loads[1].wait()
    first_in[...] = nt(panel(0), weight_ref[0, :, :576])
    qkv.plane(ORDER[0])
    qkv.plane(ORDER[1])
    for d in range(1, 4):
        first_in[...] += nt(panel(d), weight_ref[d, :, :576])
    qkv.plane(ORDER[2])
    qkv.plane(ORDER[3])
    loads[0].wait()
    lax.fori_loop(0, 6, heads, 0)
    qkv.turn(ORDER[0])
    qkv.turn(ORDER[1])
    loads[2].wait()
    loads[3].wait()
    first_ref[...] = jnp.zeros_like(first_ref)

    def one_block(b, carry):
        rows = pl.ds(pl.multiple_of(b * SLOT, SLOT), SLOT)
        unit, inverse = standardize(x_ref[rows, :].astype(F32))
        grad = first_in[rows, :]
        first_ref[0:1, :] += column_sum(grad * unit)
        first_ref[1:2, :] += column_sum(grad)
        back = norm_back(grad * vec_ref[0:1, :], unit, inverse)
        input_grad_ref[rows, :] = (middle_ref[rows, :] + back).astype(BF16)
        return carry

    lax.fori_loop(0, count, one_block, 0)
    lax.fori_loop(6, HEADS, heads, 0)
    qkv.turn(ORDER[2])
    qkv.turn(ORDER[3])
    table_grad_end(table_ref, wall_small, wall_large)
    pair = jnp.concatenate(
        [column_sum(query_grad[...].astype(F32)), column_sum(values_grad[...].astype(F32))], 1
    )
    pack_sums(sums_ref, first_ref, wide_ref, pair, table_ref, packed)
    small.begin()
    for k in ORDER:
        qkv.line(k)
    small.cross()
    qkv.end()
    total = small.end()
    for n in range(8):
        small_outs[n][...] = total[n // 4 : n // 4 + 1, 96 * (n % 4) : 96 * (n % 4) + 96]
    for n in range(3):
        small_outs[8 + n][...] = total[2 + n : 3 + n, :]
    small_outs[11][...] = total[5:6, 0:192]
    small_outs[12][...] = total[5:6, 192:204]
    spread = jnp.concatenate([total[6:12, 0:192], total[6:12, 192:384], jnp.zeros((4, 192), F32)], 0)
    spread = jnp.concatenate([spread, jnp.zeros((112, 192), F32)], 0).T
    source = lax.broadcasted_iota(jnp.int32, (128, 128), 0)
    head = lax.broadcasted_iota(jnp.int32, (128, 128), 1)
    pick = (source == head // 2 + PAIRS * (head % 2)) & (head < HEADS)
    pick = pick.astype(F32).astype(BF16)
    high = spread.astype(BF16)
    rest_part = spread - high.astype(F32)
    middle = rest_part.astype(BF16)
    low = (rest_part - middle.astype(F32)).astype(BF16)
    ordered = nn(high, pick) + nn(middle, pick) + nn(low, pick)
    small_outs[13][...] = ordered[:, :HEADS]


def finish(query_grad, keys_grad, values_grad, normed, vecs, sums, wide, tokens, middle_grad, weight, grids):
    rows = tokens.shape[0]
    vmem = pl.BlockSpec(memory_space=pltpu.VMEM)
    any_space = pl.BlockSpec(memory_space=ANY)
    small = [(1, 96)] * 8 + [(1, 384)] * 3 + [(1, 192), (1, 12), (192, HEADS)]
    shapes = [jax.ShapeDtypeStruct((rows, D), BF16), jax.ShapeDtypeStruct((96, 576), F32)]
    shapes += [jax.ShapeDtypeStruct(shape, F32) for shape in small]
    return pl.pallas_call(
        finish_kernel,
        in_specs=[vmem] * 7 + [any_space] * 4,
        out_specs=[vmem] * len(shapes),
        out_shape=shapes,
        scratch_shapes=[
            pltpu.VMEM((rows, D), BF16),
            pltpu.VMEM((rows, D), F32),
            pltpu.VMEM((4, D, D), BF16),
            pltpu.VMEM((2, HEADS, SLOT, SLOT), F32),
            pltpu.VMEM((4, D, 576), BF16),
            pltpu.VMEM((rows, D), F32),
            pltpu.VMEM((16, TABLE), F32),
            pltpu.VMEM((8, D), F32),
            pltpu.VMEM((2, 128, 128), F32),
            pltpu.VMEM((4, 256, 128), F32),
            pltpu.VMEM((8, 16, 384), F32),
            pltpu.VMEM((7, 16, 384), F32),
            pltpu.VMEM((4, 16, 384), F32),
            pltpu.SemaphoreType.DMA((11,)),
            pltpu.SemaphoreType.DMA((11,)),
            pltpu.SemaphoreType.DMA((4,)),
        ]
        + scatter_scratch("panel", 576),
        compiler_params=params(collective_id=3, has_side_effects=True),
        name="finish",
    )(query_grad, keys_grad, values_grad, normed, vecs, sums, wide, tokens, middle_grad, weight, grids)


def gather_matrix(piece):
    rows = lax.all_gather(piece, "fsdp", axis=0, tiled=True)
    return lax.all_gather(rows, "dp", axis=1, tiled=True)


def scatter_matrix(grad):
    part = lax.psum_scatter(grad, "dp", scatter_dimension=1, tiled=True).astype(F32)
    return lax.psum_scatter(part, "fsdp", scatter_dimension=0, tiled=True)


def body(
    tokens, cotangent, lengths, buckets, qkv_weight, query_value_bias, out_weight, out_bias,
    up_weight, up_bias, down_weight, down_bias, first_gain, first_shift, mix_gain, mix_shift,
    second_gain, second_shift, hidden_gain, hidden_shift, head_scale, position_table,
):
    parts = lax.axis_size("fsdp")
    own_kernels = (parts, lax.axis_size("dp")) == (8, 4)
    narrow = [
        first_gain, first_shift, mix_gain, mix_shift, second_gain, second_shift, out_bias, down_bias,
    ]
    wide = [up_bias, hidden_gain, hidden_shift]
    a = D // parts
    b = FF // parts
    packed = jnp.concatenate(
        [jnp.pad(jnp.stack(narrow), ((0, 0), (0, b - a))), jnp.stack(wide)]
        + [jnp.pad(query_value_bias, (0, b - 2 * a))[None], jnp.zeros((4, b), BF16)]
        + [jnp.pad(position_table.T, ((0, 4), (0, b - 2 * a)))]
    )
    scales = jnp.repeat(head_scale.astype(F32), HEAD_DIM)[None]
    if own_kernels:
        (
            normed, qkv, probs, result, mixed, second, act, low, branch, middle_grad, attended_low,
            sums, wide_sums, vecs, qkv_full,
        ) = forward(
            lengths, buckets, tokens, cotangent, scales, qkv_weight, out_weight, up_weight,
            down_weight, packed,
        )
        query_grad, keys_grad, values_grad, grids, down_owned, up_owned, out_owned = backward(
            buckets, cotangent, act, second, low, mixed, branch, probs, qkv, attended_low
        )
        owned = finish(
            query_grad, keys_grad, values_grad, normed, vecs, sums, wide_sums, tokens, middle_grad,
            qkv_full, grids,
        )
        input_grad, qkv_owned = owned[:2]
        narrow_owned = [part.reshape(-1) for part in owned[2:10]]
        wide_owned = [part.reshape(-1) for part in owned[10:13]]
        pair_owned = owned[13].reshape(-1)
        scale_grad = owned[14].reshape(-1)
        table_owned = owned[15]
    else:
        gathered = lax.all_gather(packed, "fsdp", axis=0)
        qkv_full = gather_matrix(qkv_weight)
        out_full = gather_matrix(out_weight)
        up_full = gather_matrix(up_weight)
        down_full = gather_matrix(down_weight).T
        gathered = gathered.astype(F32)
        vecs = gathered[:, :8, :a].transpose(1, 0, 2).reshape(8, D)
        wides = jnp.pad(gathered[:, 8:11].transpose(1, 0, 2).reshape(3, FF), ((0, 5), (0, 0)))
        pair = gathered[:, 11, : 2 * a].reshape(1, 2 * D)
        table = gathered[:, 16:, : 2 * a].transpose(1, 0, 2).reshape(16, TABLE)
        qkv_bias = jnp.concatenate([pair[:, :D], jnp.zeros((1, D), F32), pair[:, D:]], 1)

        bias = build_bias(table)
        normed, qkv, probs, attended = attention(
            lengths, buckets, tokens, vecs, qkv_full, qkv_bias, bias
        )
        (
            result, mixed, second, act, low, branch, middle_grad, attended_low, sums, wide_sums,
        ) = feed_forward(tokens, attended, cotangent, out_full, up_full, down_full, vecs, wides, scales)
        down_grad = outer_product(cotangent, act, 512)
        up_grad = outer_product(second, low, 512)
        out_grad = outer_product(mixed, branch, 256)
        input_grad, grids, qkv_grad, pair_sums, first_sums = attention_back(
            buckets, probs, qkv, attended_low, normed, tokens, middle_grad, qkv_full, vecs
        )
        table_sums = table_grad(grids)
        qkv_natural = qkv_grad.reshape(PAIRS, D, 3, 128).transpose(1, 2, 0, 3).reshape(D, 3 * D)

        qkv_owned = scatter_matrix(qkv_natural)
        out_owned = scatter_matrix(out_grad)
        up_owned = scatter_matrix(up_grad)
        down_owned = scatter_matrix(down_grad.T)
        pair_grad = pair_sums[:, 0].reshape(PAIRS, 3, 128).transpose(1, 0, 2).reshape(3, D)
        pair_grad = jnp.concatenate([pair_grad[0], pair_grad[2]])
        narrow_sums = jnp.concatenate([first_sums[:2], sums[2:8]], 0)
        packed = jnp.concatenate(
            [
                narrow_sums.reshape(8, parts, a).transpose(1, 0, 2).reshape(parts, -1),
                wide_sums[:3].reshape(3, parts, b).transpose(1, 0, 2).reshape(parts, -1),
                pair_grad.reshape(parts, -1),
                table_sums[:HEADS].T.reshape(parts, -1),
            ],
            1,
        )
        owned = lax.psum(lax.psum_scatter(packed, "fsdp", scatter_dimension=0, tiled=True), "dp")[0]
        scale_grad = lax.psum(sums[8].reshape(HEADS, HEAD_DIM).sum(1), ("fsdp", "dp"))
        narrow_owned = owned[: 8 * a].reshape(8, a)
        edge = 8 * a
        wide_owned = owned[edge : edge + 3 * b].reshape(3, b)
        edge += 3 * b
        pair_owned = owned[edge : edge + 2 * a]
        edge += 2 * a
        table_owned = owned[edge:].reshape(TABLE // parts, HEADS)
    return (
        result, input_grad, qkv_owned, pair_owned, out_owned, narrow_owned[6], up_owned,
        wide_owned[0], down_owned, narrow_owned[7], narrow_owned[0], narrow_owned[1],
        narrow_owned[2], narrow_owned[3], narrow_owned[4], narrow_owned[5], wide_owned[1],
        wide_owned[2], scale_grad, table_owned,
    )


def solution(mesh):
    tokens = P(("fsdp", "dp"), None)
    sequences = P(("fsdp", "dp"))
    matrix = P("fsdp", "dp")
    vector = P("fsdp")
    table = P("fsdp", None)
    in_specs = (
        tokens, tokens, sequences, sequences, matrix, vector, matrix, vector, matrix, vector,
        matrix, vector, vector, vector, vector, vector, vector, vector, vector, vector, P(), table,
    )
    out_specs = (
        tokens, tokens, matrix, vector, matrix, vector, matrix, vector, matrix, vector, vector,
        vector, vector, vector, vector, vector, vector, vector, P(), table,
    )
    return jax.shard_map(body, mesh=mesh, in_specs=in_specs, out_specs=out_specs, check_vma=False)
```

```python
import functools

import jax
import jax.numpy as jnp
from jax import lax
from jax.experimental import pallas as pl
from jax.experimental.pallas import tpu as pltpu
from jax.sharding import PartitionSpec as P

D = 768
HEADS = 12
PAIRS = 6
HEAD_DIM = 64
FF = 3072
SLOT = 256
TABLE = 1536

EPS = 1e-05
MASKED = -1000000000.0
F32 = jnp.float32
BF16 = jnp.bfloat16
VMEM_LIMIT = 60 * 2**20
BACK_LIMIT = 60 * 2**20


def params(**more):
    return pltpu.CompilerParams(vmem_limit_bytes=VMEM_LIMIT, **more)


def nn(left, right):
    return lax.dot_general(left, right, (((1,), (0,)), ((), ())), preferred_element_type=F32)


def nt(left, right):
    return lax.dot_general(left, right, (((1,), (1,)), ((), ())), preferred_element_type=F32)


def standardize(values):
    center = values - jnp.mean(values, -1, keepdims=True)
    inverse = lax.rsqrt(jnp.mean(center * center, -1, keepdims=True) + EPS)
    return center * inverse, inverse


def norm_back(grad, unit, inverse):
    return inverse * (
        grad
        - jnp.mean(grad, -1, keepdims=True)
        - unit * jnp.mean(grad * unit, -1, keepdims=True)
    )


def column_sum(values):
    return jnp.sum(values, 0, keepdims=True)


def tall_sum(ref):
    def some(n, total):
        return total + column_sum(ref[rows_of(n, 64), :].astype(F32))

    return lax.fori_loop(0, ref.shape[0] // 64, some, jnp.zeros((1, ref.shape[1]), F32))


def split_low(values):
    high = values.astype(BF16)
    return high, (values - high.astype(F32)).astype(BF16)


def compaction(side, lanes):
    plane = lax.broadcasted_iota(jnp.int32, (1024, lanes), 0)
    lane = lax.broadcasted_iota(jnp.int32, (1024, lanes), 1)
    across = plane & 31
    return ((lane == side * (plane >> 5) + across) & (across < side)).astype(F32).astype(BF16)


def inside_grid(patches):
    row = lax.broadcasted_iota(jnp.int32, (SLOT, SLOT), 0)
    col = lax.broadcasted_iota(jnp.int32, (SLOT, SLOT), 1)
    return (row < patches) & (col < patches)


def store_tiles(ref, values):
    for k in range(ref.shape[0]):
        ref[k] = values[:, 128 * k : 128 * k + 128]


def load_tiles(ref):
    return jnp.concatenate([ref[k] for k in range(ref.shape[0])], 1)


def load_strided(ref, first, count):
    return jnp.concatenate(
        [ref[k, pl.ds(first, count, 16), :] for k in range(ref.shape[0])], 1
    )


def store_strided(ref, first, values):
    for k in range(ref.shape[0]):
        ref[k, pl.ds(first, values.shape[0], 16), :] = values[:, 128 * k : 128 * k + 128]


def bias_walls(table_ref, wall_small, wall_large, visual):
    plane = table_ref[:, 512:]
    shifted = [pltpu.roll(plane, (ic - 15) % 1024, 1) for ic in range(16)]
    stack = jnp.concatenate(shifted, 0).astype(BF16)
    store_tiles(wall_large, nn(stack, compaction(15, 512)))
    store_tiles(wall_small, nn(stack[:128], compaction(8, 256)))
    visual[...] = jnp.zeros_like(visual)


def bias_head(table_ref, out_ref, wall_small, wall_large, visual, h, carry):
    line = jnp.broadcast_to(table_ref[pl.ds(h, 1), :512], (SLOT, 512))
    textual = pltpu.roll(line, 257, 1, stride=1, stride_axis=0)[:, :SLOT]
    large = load_strided(wall_large, h, 16)
    for ir in range(15):
        visual[pl.ds(ir * 15, 16), :] = pltpu.roll(large, 512 - (15 - ir) * 15, 1)[:, :SLOT]
    out_ref[1, h] = jnp.where(inside_grid(225), visual[...], textual).astype(BF16)
    small = load_strided(wall_small, h, 8)
    rows = [pltpu.roll(small, 256 - (15 - ir) * 8, 1) for ir in range(8)]
    grid = jnp.concatenate(rows + [jnp.zeros((192, SLOT), F32)], 0)
    out_ref[0, h] = jnp.where(inside_grid(64), grid, textual).astype(BF16)
    return carry


def bias_kernel(table_ref, out_ref, wall_small, wall_large, visual):
    bias_walls(table_ref, wall_small, wall_large, visual)
    one_head = functools.partial(bias_head, table_ref, out_ref, wall_small, wall_large, visual)
    lax.fori_loop(0, HEADS, one_head, 0)


def build_bias(table):
    return pl.pallas_call(
        bias_kernel,
        out_shape=jax.ShapeDtypeStruct((2, HEADS, SLOT, SLOT), BF16),
        scratch_shapes=[
            pltpu.VMEM((2, 128, 128), F32),
            pltpu.VMEM((4, 256, 128), F32),
            pltpu.VMEM((SLOT, SLOT), F32),
        ],
        compiler_params=params(),
        name="build_bias",
    )(table)


def table_grad_start(out_ref, wall_small, wall_large):
    wall_small[...] = jnp.zeros_like(wall_small)
    wall_large[...] = jnp.zeros_like(wall_large)
    out_ref[...] = jnp.zeros_like(out_ref)


def table_grad_head(grid_ref, out_ref, wall_small, wall_large, h, slot):
    row = lax.broadcasted_iota(jnp.int32, (SLOT, SLOT), 0)
    col = lax.broadcasted_iota(jnp.int32, (SLOT, SLOT), 1)
    flip = (row + col == SLOT - 1).astype(F32).astype(BF16)
    lane = lax.broadcasted_iota(jnp.int32, (16, SLOT), 1)
    textual = jnp.where(inside_grid(64), 0.0, grid_ref[0, slot]) + jnp.where(
        inside_grid(225), 0.0, grid_ref[1, slot]
    )
    high, low = split_low(textual)
    flipped = nn(flip, high) + nn(flip, low)
    wide = jnp.concatenate([flipped, jnp.zeros((SLOT, SLOT), F32)], 1)
    out_ref[pl.ds(h, 1), :512] = column_sum(pltpu.roll(wide, 0, 1, stride=1, stride_axis=0))
    total = jnp.zeros((16, 512), F32)
    for ir in range(15):
        part = jnp.where(lane < 225, grid_ref[1, slot, pl.ds(ir * 15, 16), :], 0.0)
        part = jnp.concatenate([part, jnp.zeros((16, SLOT), F32)], 1)
        total = total + pltpu.roll(part, (15 - ir) * 15, 1)
    store_strided(wall_large, h, total)
    total = jnp.zeros((8, SLOT), F32)
    for ir in range(8):
        part = jnp.where(lane[:8] < 64, grid_ref[0, slot, pl.ds(ir * 8, 8), :], 0.0)
        total = total + pltpu.roll(part, (15 - ir) * 8, 1)
    store_strided(wall_small, h, total)


def table_grad_end(out_ref, wall_small, wall_large):
    high, low = split_low(load_tiles(wall_large))
    spread = compaction(15, 512)
    large = nt(high, spread) + nt(low, spread)
    high, low = split_low(load_tiles(wall_small))
    spread = compaction(8, 256)
    small = nt(high, spread) + nt(low, spread)
    plane = jnp.zeros((16, 1024), F32)
    for ic in range(15):
        part = large[ic * 16 : ic * 16 + 16]
        if ic < 8:
            part = part + small[ic * 16 : ic * 16 + 16]
        plane = plane + pltpu.roll(part, 15 - ic, 1)
    out_ref[:, 512:] = plane


def table_grad_kernel(grid_ref, out_ref, wall_small, wall_large):
    table_grad_start(out_ref, wall_small, wall_large)

    def one_head(h, carry):
        table_grad_head(grid_ref, out_ref, wall_small, wall_large, h, h)
        return carry

    lax.fori_loop(0, HEADS, one_head, 0)
    table_grad_end(out_ref, wall_small, wall_large)


def table_grad(grids):
    return pl.pallas_call(
        table_grad_kernel,
        out_shape=jax.ShapeDtypeStruct((16, TABLE), F32),
        scratch_shapes=[pltpu.VMEM((2, 128, 128), F32), pltpu.VMEM((4, 256, 128), F32)],
        compiler_params=params(),
        name="table_grad",
    )(grids)


def by_head(pair, axis):
    first = lax.broadcasted_iota(jnp.int32, pair.shape, 1) < HEAD_DIM
    return jnp.concatenate([jnp.where(first, pair, 0), jnp.where(first, 0, pair)], axis)


def attend(query, keys, values, bias, live):
    logits = nt(by_head(query, 0), keys)
    probs = []
    for half in range(2):
        rows = slice(SLOT * half, SLOT * half + SLOT)
        scores = jnp.where(live, logits[rows] + bias[half].astype(F32), MASKED)
        shifted = jnp.exp(scores - jnp.max(scores, -1, keepdims=True))
        probs.append((shifted * (1.0 / jnp.sum(shifted, -1, keepdims=True))).astype(BF16))
    return probs, nn(jnp.concatenate(probs, 1), by_head(values, 0))


def attend_back(query, keys, values, grad, probs):
    probs_grads = nt(by_head(grad, 0), values)
    grad_turned = grad.T
    query_turned = query.T
    keys_parts = []
    values_parts = []
    scores_grads = []
    lows = []
    for half in range(2):
        part = slice(HEAD_DIM * half, HEAD_DIM * half + HEAD_DIM)
        wide = probs[half].astype(F32)
        probs_grad = probs_grads[SLOT * half : SLOT * half + SLOT]
        values_parts.append(nn(grad_turned[part], probs[half]))
        scores_grad = wide * (probs_grad - jnp.sum(wide * probs_grad, -1, keepdims=True))
        scores_grads.append(scores_grad)
        lows.append(scores_grad.astype(BF16))
        keys_parts.append(nn(query_turned[part], lows[half]))
    query_grad = nn(jnp.concatenate(lows, 1), by_head(keys, 0)) * HEAD_DIM ** (-0.5)
    keys_grad = jnp.concatenate(keys_parts, 0).T
    values_grad = jnp.concatenate(values_parts, 0).T
    return query_grad.astype(BF16), keys_grad.astype(BF16), values_grad.astype(BF16), scores_grads


def attention_kernel(
    lengths, buckets, x_ref, vec_ref, weight_ref, qkv_bias_ref, bias_ref,
    normed_ref, qkv_ref, probs_ref, attended_ref,
):
    count = x_ref.shape[0] // SLOT

    def one_block(b, carry):
        rows = pl.ds(pl.multiple_of(b * SLOT, SLOT), SLOT)
        unit, inverse = standardize(x_ref[rows, :].astype(F32))
        normed_ref[rows, :] = (unit * vec_ref[0:1, :] + vec_ref[1:2, :]).astype(BF16)
        return carry

    lax.fori_loop(0, count, one_block, 0)

    def one_panel(n, carry):
        cols = pl.ds(pl.multiple_of(n * 256, 256), 256)
        out = nn(normed_ref[...], weight_ref[:, cols]) + qkv_bias_ref[:, cols]
        out = (out * jnp.where(n < 3, HEAD_DIM ** (-0.5), 1.0)).astype(BF16)
        qkv_ref[2 * n] = out[:, :128]
        qkv_ref[2 * n + 1] = out[:, 128:]
        return carry

    lax.fori_loop(0, 9, one_panel, 0)
    key_slot = lax.broadcasted_iota(jnp.int32, (SLOT, SLOT), 1)

    def one_unit(step, carry):
        pair = step // count
        s = step % count
        rows = pl.ds(pl.multiple_of(s * SLOT, SLOT), SLOT)
        bias = [bias_ref[buckets[s], 2 * pair + half] for half in range(2)]
        probs, out = attend(
            qkv_ref[pair, rows, :], qkv_ref[PAIRS + pair, rows, :], qkv_ref[2 * PAIRS + pair, rows, :],
            bias, key_slot < lengths[s],
        )
        for half in range(2):
            probs_ref[2 * pair + half, s] = probs[half]
        attended_ref[rows, pl.ds(pl.multiple_of(pair * 128, 128), 128)] = out
        return carry

    lax.fori_loop(0, PAIRS * count, one_unit, 0)


def attention(lengths, buckets, tokens, vecs, weight, qkv_bias, bias):
    rows = tokens.shape[0]
    count = rows // SLOT
    smem = pl.BlockSpec(memory_space=pltpu.SMEM)
    vmem = pl.BlockSpec(memory_space=pltpu.VMEM)
    return pl.pallas_call(
        attention_kernel,
        in_specs=[smem, smem] + [vmem] * 5,
        out_shape=[
            jax.ShapeDtypeStruct((rows, D), BF16),
            jax.ShapeDtypeStruct((3 * PAIRS, rows, 128), BF16),
            jax.ShapeDtypeStruct((HEADS, count, SLOT, SLOT), BF16),
            jax.ShapeDtypeStruct((rows, D), F32),
        ],
        compiler_params=params(),
        name="attention_forward",
    )(lengths, buckets, tokens, vecs, weight, qkv_bias, bias)


PANEL = 512


def feed_kernel(*refs):
    @pl.when(pl.program_id(0) == 0)
    def _():
        for ref in refs[17:19]:
            ref[...] = jnp.zeros_like(ref)

    feed_block(*refs, lambda: None)


def feed_block(
    x_ref, attended_ref, cot_ref, out_w, up_w, down_w, vec_ref, wide_ref, scale_ref,
    result_ref, mixed_ref, second_ref, act_ref, low_ref, branch_ref, middle_grad_ref,
    attended_low_ref, sums_ref, wide_sums_ref,
    gelu_ref, slope_ref, grad_ref, before_down,
):
    def add(row, values):
        sums_ref[row : row + 1, :] += column_sum(values)

    rows = x_ref.shape[0]
    attended = attended_ref[...]
    mix_unit, mix_inverse = standardize(attended * scale_ref[...])
    mixed = (mix_unit * vec_ref[2:3, :] + vec_ref[3:4, :]).astype(BF16)
    mixed_ref[...] = mixed
    middle = x_ref[...].astype(F32) + nn(mixed, out_w[...]) + vec_ref[6:7, :]
    second_unit, second_inverse = standardize(middle)
    second = (second_unit * vec_ref[4:5, :] + vec_ref[5:6, :]).astype(BF16)
    second_ref[...] = second
    cot = cot_ref[...]

    panels = [slice(n, n + PANEL) for n in range(0, FF, PANEL)]
    total = jnp.zeros((rows, 1), F32)
    for cols in panels:
        hidden = nn(second, up_w[:, cols]) + wide_ref[0:1, cols]
        cdf = 0.5 + 0.5 * lax.erf(hidden * 0.7071067811865476)
        gelu = hidden * cdf
        gelu_ref[:, cols] = gelu
        slope_ref[:, cols] = cdf + hidden * (jnp.exp(-0.5 * hidden * hidden) * 0.3989422804014327)
        total = total + jnp.sum(gelu, -1, keepdims=True)
    mean = total * (1.0 / FF)
    total = jnp.zeros((rows, 1), F32)
    for cols in panels:
        center = gelu_ref[:, cols] - mean
        total = total + jnp.sum(center * center, -1, keepdims=True)
    inverse = lax.rsqrt(total * (1.0 / FF) + EPS)
    before_down()
    result = middle + vec_ref[7:8, :]
    first = jnp.zeros((rows, 1), F32)
    second_moment = jnp.zeros((rows, 1), F32)
    for cols in panels:
        unit = (gelu_ref[:, cols] - mean) * inverse
        gelu_ref[:, cols] = unit
        act = (unit * wide_ref[1:2, cols] + wide_ref[2:3, cols]).astype(BF16)
        act_ref[:, cols] = act
        result = result + nt(act, down_w[:, cols])
        act_grad = nn(cot, down_w[:, cols])
        wide_sums_ref[1:2, cols] += column_sum(act_grad * unit)
        wide_sums_ref[2:3, cols] += column_sum(act_grad)
        grad = act_grad * wide_ref[1:2, cols]
        grad_ref[:, cols] = grad
        first = first + jnp.sum(grad, -1, keepdims=True)
        second_moment = second_moment + jnp.sum(grad * unit, -1, keepdims=True)
    result_ref[...] = result.astype(BF16)
    first = first * (1.0 / FF)
    second_moment = second_moment * (1.0 / FF)
    second_in = jnp.zeros((rows, D), F32)
    for cols in panels:
        grad = inverse * (grad_ref[:, cols] - first - gelu_ref[:, cols] * second_moment)
        low = (grad * slope_ref[:, cols]).astype(BF16)
        low_ref[:, cols] = low
        wide_sums_ref[0:1, cols] += column_sum(low.astype(F32))
        second_in = second_in + nt(low, up_w[:, cols])
    add(4, second_in * second_unit)
    add(5, second_in)
    cot_wide = cot.astype(F32)
    add(7, cot_wide)
    middle_grad = cot_wide + norm_back(second_in * vec_ref[4:5, :], second_unit, second_inverse)
    middle_grad_ref[...] = middle_grad
    branch = middle_grad.astype(BF16)
    branch_ref[...] = branch
    add(6, branch.astype(F32))
    mixed_in = nt(branch, out_w[...])
    add(2, mixed_in * mix_unit)
    add(3, mixed_in)
    grad = norm_back(mixed_in * vec_ref[2:3, :], mix_unit, mix_inverse)
    add(8, grad * attended)
    attended_low_ref[...] = (grad * scale_ref[...]).astype(BF16)


def feed_forward(tokens, attended, cotangent, out_w, up_w, down_w, vecs, wide, scales):
    rows = tokens.shape[0]
    tile = 256
    block = pl.BlockSpec((tile, D), lambda i: (i, 0))
    wide_block = pl.BlockSpec((tile, FF), lambda i: (i, 0))

    def whole(shape):
        return pl.BlockSpec(shape, lambda i: (0, 0), pipeline_mode=pl.Buffered(1))

    def held(shape):
        return pl.BlockSpec(shape, lambda i: (0, 0))

    return pl.pallas_call(
        feed_kernel,
        grid=(rows // tile,),
        in_specs=[block] * 3
        + [whole((D, D)), whole((D, FF)), whole((D, FF)), whole((8, D)), whole((8, FF)), whole((1, D))],
        out_specs=[block, block, block, wide_block, wide_block, block, block, block]
        + [held((16, D)), held((8, FF))],
        out_shape=[
            jax.ShapeDtypeStruct((rows, D), BF16),
            jax.ShapeDtypeStruct((rows, D), BF16),
            jax.ShapeDtypeStruct((rows, D), BF16),
            jax.ShapeDtypeStruct((rows, FF), BF16),
            jax.ShapeDtypeStruct((rows, FF), BF16),
            jax.ShapeDtypeStruct((rows, D), BF16),
            jax.ShapeDtypeStruct((rows, D), F32),
            jax.ShapeDtypeStruct((rows, D), BF16),
            jax.ShapeDtypeStruct((16, D), F32),
            jax.ShapeDtypeStruct((8, FF), F32),
        ],
        scratch_shapes=[pltpu.VMEM((tile, FF), F32)] * 3,
        compiler_params=params(dimension_semantics=("arbitrary",)),
        name="feed_forward",
    )(tokens, attended, cotangent, out_w, up_w, down_w, vecs, wide, scales)


def outer_kernel(left_ref, right_ref, out_ref, turned):
    @pl.when(pl.program_id(0) == 0)
    def _():
        turned[...] = left_ref[...].T

    out_ref[...] = nn(turned[...], right_ref[...]).astype(BF16)


def outer_product(left, right, panel):
    rows, width = left.shape
    cols = right.shape[1]
    return pl.pallas_call(
        outer_kernel,
        grid=(cols // panel,),
        in_specs=[
            pl.BlockSpec((rows, width), lambda i: (0, 0), pipeline_mode=pl.Buffered(1)),
            pl.BlockSpec((rows, panel), lambda i: (0, i)),
        ],
        out_specs=pl.BlockSpec((width, panel), lambda i: (0, i)),
        out_shape=jax.ShapeDtypeStruct((width, cols), BF16),
        scratch_shapes=[pltpu.VMEM((width, rows), BF16)],
        compiler_params=params(dimension_semantics=("arbitrary",)),
        name="weight_grad",
    )(left, right)


def attention_back_kernel(
    buckets, probs_ref, query_ref, keys_ref, values_ref, low_ref, normed_ref, x_ref, middle_ref,
    weight_q, weight_k, weight_v, vec_ref,
    input_grad_ref, grid_ref, weight_grad_ref, pair_ref, sums_ref,
    turned, first_in, proj_ref,
):
    count = x_ref.shape[0] // SLOT
    step = pl.program_id(0)

    @pl.when(step == 0)
    def _():
        turned[...] = normed_ref[...].T
        first_in[...] = jnp.zeros_like(first_in)

    grid_ref[...] = jnp.zeros_like(grid_ref)

    def one_sequence(s, carry):
        rows = pl.ds(pl.multiple_of(s * SLOT, SLOT), SLOT)
        query_grad, keys_grad, values_grad, scores_grads = attend_back(
            query_ref[0, rows, :], keys_ref[0, rows, :], values_ref[0, rows, :], low_ref[rows, :],
            [probs_ref[half, s] for half in range(2)],
        )
        small = jnp.where(buckets[s] == 0, 1.0, 0.0)
        for half in range(2):
            grid_ref[0, half] += scores_grads[half] * small
            grid_ref[1, half] += scores_grads[half] * (1.0 - small)
        proj_ref[rows, 0:128] = query_grad
        proj_ref[rows, 128:256] = keys_grad
        proj_ref[rows, 256:384] = values_grad
        return carry

    lax.fori_loop(0, count, one_sequence, 0)
    proj = proj_ref[...]
    weight_grad_ref[0] = nn(turned[...], proj).astype(BF16)
    pair_ref[0] = jnp.broadcast_to(column_sum(proj.astype(F32)), (8, 384))
    weights = jnp.concatenate([weight_q[...], weight_k[...], weight_v[...]], 1)
    first_in[...] += nt(proj, weights)

    @pl.when(step == PAIRS - 1)
    def _():
        sums_ref[...] = jnp.zeros_like(sums_ref)

        def one_block(b, carry):
            rows = pl.ds(pl.multiple_of(b * SLOT, SLOT), SLOT)
            unit, inverse = standardize(x_ref[rows, :].astype(F32))
            grad = first_in[rows, :]
            sums_ref[0:1, :] += column_sum(grad * unit)
            sums_ref[1:2, :] += column_sum(grad)
            back = norm_back(grad * vec_ref[0:1, :], unit, inverse)
            input_grad_ref[rows, :] = (middle_ref[rows, :] + back).astype(BF16)
            return carry

        lax.fori_loop(0, count, one_block, 0)


def attention_back(buckets, probs, qkv, attended_low, normed, tokens, middle_grad, weight, vecs):
    rows = tokens.shape[0]
    count = rows // SLOT

    def whole(shape):
        return pl.BlockSpec(shape, lambda i: (0,) * len(shape), pipeline_mode=pl.Buffered(1))

    def held(shape):
        return pl.BlockSpec(shape, lambda i: (0,) * len(shape))

    def panel(base):
        return pl.BlockSpec((1, rows, 128), lambda i: (base + i, 0, 0))

    def weight_panel(base):
        return pl.BlockSpec((D, 128), lambda i: (0, base + i))

    return pl.pallas_call(
        attention_back_kernel,
        grid=(PAIRS,),
        in_specs=[
            pl.BlockSpec(memory_space=pltpu.SMEM),
            pl.BlockSpec((2, count, SLOT, SLOT), lambda i: (i, 0, 0, 0)),
            panel(0), panel(PAIRS), panel(2 * PAIRS),
            pl.BlockSpec((rows, 128), lambda i: (0, i)),
            whole((rows, D)), whole((rows, D)), whole((rows, D)),
            weight_panel(0), weight_panel(PAIRS), weight_panel(2 * PAIRS),
            whole((8, D)),
        ],
        out_specs=[
            held((rows, D)),
            pl.BlockSpec((2, 2, SLOT, SLOT), lambda i: (0, i, 0, 0)),
            pl.BlockSpec((1, D, 384), lambda i: (i, 0, 0)),
            pl.BlockSpec((1, 8, 384), lambda i: (i, 0, 0)),
            held((8, D)),
        ],
        out_shape=[
            jax.ShapeDtypeStruct((rows, D), BF16),
            jax.ShapeDtypeStruct((2, HEADS, SLOT, SLOT), F32),
            jax.ShapeDtypeStruct((PAIRS, D, 384), BF16),
            jax.ShapeDtypeStruct((PAIRS, 8, 384), F32),
            jax.ShapeDtypeStruct((8, D), F32),
        ],
        scratch_shapes=[
            pltpu.VMEM((D, rows), BF16),
            pltpu.VMEM((rows, D), F32),
            pltpu.VMEM((rows, 384), BF16),
        ],
        compiler_params=params(dimension_semantics=("arbitrary",)),
        name="attention_backward",
    )(buckets, probs, qkv, qkv, qkv, attended_low, normed, tokens, middle_grad, weight, weight, weight, vecs)


MESH = pl.DeviceIdType.MESH
ANY = pl.ANY


class Place:
    def __init__(self):
        fsdp = lax.axis_index("fsdp")
        dp = lax.axis_index("dp")
        self.z, self.y, self.x, self.core = fsdp // 2, fsdp % 2, dp // 2, dp % 2

    def at(self, z=None, y=None, x=None, core=None):
        z = self.z if z is None else z
        y = self.y if y is None else y
        x = self.x if x is None else x
        core = self.core if core is None else core
        return (z * 2 + y, x * 2 + core)

    def greet(self):
        barrier = pltpu.get_barrier_semaphore()
        peers = [self.at(z=(self.z + k) % 4, y=self.y) for k in range(1, 4)]
        peers += [self.at(z=(self.z + k) % 4, y=1 - self.y) for k in range(4)]
        peers += [
            self.at(x=1 - self.x),
            self.at(core=1 - self.core),
            self.at(x=1 - self.x, core=1 - self.core),
        ]
        for peer in peers:
            pl.semaphore_signal(barrier, inc=1, device_id=peer, device_id_type=MESH)

    def meet(self):
        pl.semaphore_wait(pltpu.get_barrier_semaphore(), 10)


def remote(src, dst, send, recv, peer):
    return pltpu.make_async_remote_copy(
        src_ref=src, dst_ref=dst, send_sem=send, recv_sem=recv, device_id=peer, device_id_type=MESH
    )


def rows_of(first, size):
    return pl.ds(pl.multiple_of(first * size, size), size)


def chunk(kind, ref, r, d):
    if kind == "panel":
        return ref.at[d, rows_of(r, 96), :]
    if kind == "wide":
        return ref.at[rows_of(r, 96), rows_of(d, 768)]
    return ref.at[rows_of(d, 192), rows_of(r, 384)]


class Gather:
    def __init__(self, place, pieces, fulls, send, recv, local):
        self.place, self.pieces, self.fulls = place, pieces, fulls
        self.send, self.recv, self.local = send, recv, local
        self.made = {}

    def slot(self, w, z, y, x):
        return chunk(GATHER_KINDS[w], self.fulls[w], z * 2 + y, x * 2 + self.place.core)

    def copy(self, w, index, src, dst, peer):
        self.made[w, index] = remote(src, dst, self.send.at[w, index], self.recv.at[w, index], peer)
        return self.made[w, index]

    def sources(self, w, k):
        here = self.place
        over_x = (k + GATHER_TURN[w]) % 2 == 0
        near = (here.y, 1 - here.x) if over_x else (1 - here.y, here.x)
        far = (1 - here.y, here.x) if over_x else (here.y, 1 - here.x)
        upper = here.z // 2
        depth = here.z + upper * (3 - 2 * here.z)
        z = k - depth if k == 1 else k
        z = z + upper * (3 - 2 * z) if k else here.z
        return z, near, far

    def plan(self, w):
        here = self.place
        own = self.slot(w, here.z, here.y, here.x)
        self.made[w, "keep"] = pltpu.make_async_copy(self.pieces[w], own, self.local.at[w])
        sibling = here.at(core=1 - here.core)
        pair = here.at(z=here.z + 1 - 2 * (here.z % 2))
        across = here.at(z=3 - here.z)
        for k in range(4):
            z, near, far = self.sources(w, k)
            mine = self.slot(w, z, here.y, here.x)
            src = mine if k else self.pieces[w]
            if k == 0:
                self.copy(w, 1, src, mine, pair)
                self.copy(w, 2, src, mine, across)
            elif k == 1:
                self.copy(w, 3, src, mine, across)
            else:
                self.made[w, "on", k] = remote(
                    src, mine, self.send.at[w, 30 + k], self.recv.at[w, k], pair
                )
            self.copy(w, 4 + k, src, mine, here.at(y=near[0], x=near[1]))
            passed = self.slot(w, z, *near)
            self.copy(w, 8 + 2 * k, src, mine, here.at(y=far[0], x=far[1]))
            self.copy(w, 9 + 2 * k, passed, passed, here.at(y=far[0], x=far[1]))
            third = self.slot(w, z, *far)
            fourth = self.slot(w, z, 1 - here.y, 1 - here.x)
            for n, part in enumerate((src, passed, third, fourth)):
                dst = mine if n == 0 else part
                self.copy(w, 16 + 4 * k + n, part, dst, sibling)

    def when_middle(self, act):
        pl.when(self.place.z * (3 - self.place.z) > 0)(act)

    def begin(self, w):
        self.made[w, "keep"].start()
        self.made[w, 1].start()
        self.when_middle(lambda: self.made[w, 2].start())

    def first(self, w, k):
        if k:
            self.made[w, k].wait_recv()
            on = self.made[w, 3] if k == 1 else self.made[w, "on", k]
            self.when_middle(lambda: on.start())
        self.made[w, 4 + k].start()
        self.made[w, 16 + 4 * k].start()

    def second(self, w, k):
        self.made[w, 4 + k].wait_recv()
        self.made[w, 8 + 2 * k].start()
        self.made[w, 9 + 2 * k].start()
        self.made[w, 17 + 4 * k].start()

    def third(self, w, k):
        for n in range(2):
            self.made[w, 8 + 2 * k + n].wait_recv()
            self.made[w, 18 + 4 * k + n].start()

    def finish(self, w):
        for n in range(16):
            self.made[w, 16 + n].wait_recv()
        for n in [1] + list(range(4, 32)):
            self.made[w, n].wait_send()

        def passed_on():
            for made in (self.made[w, 2], self.made[w, 3], self.made[w, "on", 2], self.made[w, "on", 3]):
                made.wait_send()

        self.when_middle(passed_on)
        self.made[w, "keep"].wait()


MIXED, UP, DOWN = range(3)
GATHER_TURN = (0, 1, 0)
GATHER_KINDS = ("wide", "wide", "turned")


def lined(ref, row, width):
    return jnp.concatenate([ref[f, row : row + 1, :width].astype(F32) for f in range(8)], 1)


def forward_kernel(
    lengths, buckets, x_ref, cot_ref, qkv_p, out_p, up_p, down_t, table_p, head_scale, *refs,
):
    vectors = refs[:12]
    (
    normed_ref, qkv_ref, probs_ref, result_ref, mixed_ref, second_ref, act_ref, low_ref, branch_ref,
    middle_grad_ref, attended_low_ref, sums_ref, wide_sums_ref, vec_ref, qkv_out,
    mixed_p, scale_ref, vec_wide, vec_p, qkv_w, up_w, down_w, vec_f, out_w, bias_ref, wide_ref, qkv_bias_ref, table_ref,
    wall_small, wall_large, visual, attended_ref, gelu_ref, slope_ref, grad_ref,
    send, recv, local, small_send, small_recv, small_local, qkv_sem,
    ) = refs[12:]
    step = pl.program_id(0)
    count = pl.num_programs(0) // 2
    place = Place()
    gather = Gather(place, (mixed_p, up_p, down_t), (qkv_w, up_w, down_w), send, recv, local)
    for w in range(3):
        gather.plan(w)
    f = place.z * 2 + place.y
    small = [pltpu.make_async_copy(vec_p, vec_f.at[f], small_local)]
    for k in range(1, 8):
        peer = (f + k) % 8
        small.append(
            remote(
                vec_p, vec_f.at[f], small_send.at[k], small_recv.at[k],
                place.at(z=peer // 2, y=peer % 2),
            )
        )
    keep_qkv = pltpu.make_async_copy(qkv_w, qkv_out, qkv_sem)

    @pl.when(step == 0)
    def _():
        place.greet()
        vec_wide[...] = jnp.zeros_like(vec_wide)
        for n, vector in enumerate(vectors):
            size = vector.shape[0]
            vec_wide[n : n + 1, :size] = vector[...].astype(F32).reshape(1, size)
        vec_wide[16 : 16 + HEADS, :192] = table_p[...].astype(F32)
        vec_wide[12:13, :HEADS] = head_scale[...].astype(F32).reshape(1, HEADS)
        vec_p[...] = vec_wide[...].astype(BF16)
        head = lax.broadcasted_iota(jnp.int32, (128, D), 0)
        spread = (head == lax.broadcasted_iota(jnp.int32, (128, D), 1) // HEAD_DIM).astype(F32)
        scale_ref[...] = nn(vec_p[...], jnp.concatenate([spread, jnp.zeros((256, D), F32)], 0).astype(BF16))[8:16]
        mixed_p[:, :576] = qkv_p[...]
        mixed_p[:, 576:] = out_p[...]
        place.meet()
        for made in small:
            made.start()
        gather.begin(MIXED)
        gather.first(MIXED, 0)
        gather.first(UP, 0)
        gather.first(DOWN, 0)
        for made in small:
            made.wait()
        for n in range(8):
            vec_ref[n : n + 1, :] = lined(vec_f, n, 96)
        for n in range(3):
            wide_ref[n : n + 1, :] = lined(vec_f, 8 + n, 384)
        pair = lined(vec_f, 11, 192)
        qkv_bias_ref[0:1, :] = jnp.concatenate([pair[:, :D], jnp.zeros((1, D), F32), pair[:, D:]], 1)
        lane = lax.broadcasted_iota(jnp.int32, (1, 3 * D), 1)
        qkv_bias_ref[1:2, :] = jnp.where(lane < D, HEAD_DIM ** (-0.5), 1.0)
        table_ref[...] = jnp.concatenate([vec_f[n, 16:32, :192].astype(F32) for n in range(8)], 1)
        bias_walls(table_ref, wall_small, wall_large, visual)
        heads = functools.partial(bias_head, table_ref, bias_ref, wall_small, wall_large, visual)
        gather.first(MIXED, 1)
        gather.begin(UP)
        gather.second(MIXED, 0)
        gather.second(UP, 0)
        gather.first(MIXED, 2)
        gather.second(DOWN, 0)
        lax.fori_loop(0, 2, heads, 0)
        gather.first(MIXED, 3)
        gather.begin(DOWN)
        gather.second(MIXED, 1)
        gather.third(MIXED, 0)
        lax.fori_loop(2, 4, heads, 0)
        gather.second(MIXED, 2)
        gather.first(UP, 1)
        gather.third(UP, 0)
        lax.fori_loop(4, 6, heads, 0)
        gather.second(MIXED, 3)
        gather.third(DOWN, 0)
        gather.third(MIXED, 1)
        gather.first(UP, 2)
        lax.fori_loop(6, 8, heads, 0)
        gather.second(UP, 1)
        gather.first(UP, 3)
        gather.third(MIXED, 2)
        gather.first(DOWN, 1)
        lax.fori_loop(8, HEADS, heads, 0)
        gather.second(UP, 2)
        gather.third(MIXED, 3)
        gather.finish(MIXED)
        keep_qkv.start()
        sums_ref[...] = jnp.zeros_like(sums_ref)
        wide_sums_ref[...] = jnp.zeros_like(wide_sums_ref)

    schedule = [
        [("first", DOWN, 2)],
        [("second", UP, 3)],
        [("third", UP, 1), ("first", DOWN, 3)],
        [("second", DOWN, 1)],
        [("third", UP, 2)],
        [("second", DOWN, 2)],
        [("third", UP, 3)],
        [("second", DOWN, 3)],
        [("third", DOWN, 1)],
        [],
        [("third", DOWN, 2)],
        [],
    ]

    def progress(spot):
        for s in range(count):
            todo = schedule[3 * s + spot]
            if todo:

                @pl.when(step == s)
                def _(todo=todo):
                    for name, w, k in todo:
                        getattr(gather, name)(w, k)

    @pl.when(step < count)
    def _():
        rows = pl.ds(pl.multiple_of(step * SLOT, SLOT), SLOT)
        progress(0)
        unit, inverse = standardize(x_ref[...].astype(F32))
        normed = (unit * vec_ref[0:1, :] + vec_ref[1:2, :]).astype(BF16)
        normed_ref[...] = normed
        for d in range(4):
            cols = slice(576 * d, 576 * d + 576)
            out = (nn(normed, qkv_w[:, 768 * d : 768 * d + 576]) + qkv_bias_ref[0:1, cols]) * qkv_bias_ref[1:2, cols]
            qkv_ref[:, cols] = out.astype(BF16)
        live = lax.broadcasted_iota(jnp.int32, (SLOT, SLOT), 1) < lengths[step]
        bucket = buckets[step]
        for pair in range(PAIRS):
            if pair % 3 == 0:
                progress(1 + pair // 3)
            query = qkv_ref[:, 128 * pair : 128 * pair + 128]
            keys = qkv_ref[:, D + 128 * pair : D + 128 * pair + 128]
            values = qkv_ref[:, 2 * D + 128 * pair : 2 * D + 128 * pair + 128]
            bias = [bias_ref[bucket, 2 * pair + half] for half in range(2)]
            probs, out = attend(query, keys, values, bias, live)
            for half in range(2):
                probs_ref[2 * pair + half, 0] = probs[half]
            attended_ref[rows, 128 * pair : 128 * pair + 128] = out

    @pl.when(step == count)
    def _():
        gather.finish(UP)
        gather.third(DOWN, 3)
        for d in range(4):
            out_w[:, 192 * d : 192 * d + 192] = qkv_w[:, 768 * d + 576 : 768 * d + 768]

    @pl.when(step >= count)
    def _():
        rows = pl.ds(pl.multiple_of((step - count) * SLOT, SLOT), SLOT)

        def wait_down():
            @pl.when(step == count)
            def _():
                gather.finish(DOWN)

        feed_block(
            x_ref, attended_ref.at[rows, :], cot_ref, out_w, up_w, down_w, vec_ref, wide_ref,
            scale_ref.at[4:5, :],
            result_ref, mixed_ref, second_ref, act_ref, low_ref, branch_ref, middle_grad_ref,
            attended_low_ref, sums_ref, wide_sums_ref, gelu_ref, slope_ref, grad_ref, wait_down,
        )

    @pl.when(step == 2 * count - 1)
    def _():
        keep_qkv.wait()


def forward(lengths, buckets, tokens, cotangent, qkv_p, out_p, up_p, down_p, table_p, head_scale, vectors):
    rows = tokens.shape[0]
    count = rows // SLOT
    smem = pl.BlockSpec(memory_space=pltpu.SMEM)

    def early(shape):
        return pl.BlockSpec(shape, lambda i: (jnp.minimum(i, count - 1),) + (0,) * (len(shape) - 1))

    def late(shape):
        return pl.BlockSpec(shape, lambda i: (jnp.maximum(i - count, 0),) + (0,) * (len(shape) - 1))

    def held(shape):
        return pl.BlockSpec(shape, lambda i: (0,) * len(shape))

    block = (SLOT, D)
    wide = (SLOT, FF)
    return pl.pallas_call(
        forward_kernel,
        grid=(2 * count,),
        in_specs=[
            smem, smem, pl.BlockSpec(block, lambda i: (i % count, 0)), late(block),
            held((96, 576)), held((96, 192)), pl.BlockSpec(memory_space=ANY),
            pl.BlockSpec(memory_space=ANY), held((HEADS, 192)), held((HEADS,)),
        ]
        + [held(vector.shape) for vector in vectors],
        out_specs=[
            early(block), early((SLOT, 3 * D)),
            pl.BlockSpec((HEADS, 1, SLOT, SLOT), lambda i: (0, jnp.minimum(i, count - 1), 0, 0)),
            late(block), late(block), late(block), late(wide), late(wide), late(block), late(block),
            late(block), held((16, D)), held((8, FF)), held((8, D)), pl.BlockSpec(memory_space=ANY),
        ],
        out_shape=[
            jax.ShapeDtypeStruct((rows, D), BF16),
            jax.ShapeDtypeStruct((rows, 3 * D), BF16),
            jax.ShapeDtypeStruct((HEADS, count, SLOT, SLOT), BF16),
            jax.ShapeDtypeStruct((rows, D), BF16),
            jax.ShapeDtypeStruct((rows, D), BF16),
            jax.ShapeDtypeStruct((rows, D), BF16),
            jax.ShapeDtypeStruct((rows, FF), BF16),
            jax.ShapeDtypeStruct((rows, FF), BF16),
            jax.ShapeDtypeStruct((rows, D), BF16),
            jax.ShapeDtypeStruct((rows, D), F32),
            jax.ShapeDtypeStruct((rows, D), BF16),
            jax.ShapeDtypeStruct((16, D), F32),
            jax.ShapeDtypeStruct((8, FF), F32),
            jax.ShapeDtypeStruct((8, D), F32),
            jax.ShapeDtypeStruct((D, FF), BF16),
        ],
        scratch_shapes=[
            pltpu.VMEM((96, D), BF16),
            pltpu.VMEM((8, D), F32),
            pltpu.VMEM((32, 384), F32),
            pltpu.VMEM((32, 384), BF16),
            pltpu.VMEM((D, FF), BF16),
            pltpu.VMEM((D, FF), BF16),
            pltpu.VMEM((D, FF), BF16),
            pltpu.VMEM((8, 32, 384), BF16),
            pltpu.VMEM((D, D), BF16),
            pltpu.VMEM((2, HEADS, SLOT, SLOT), BF16),
            pltpu.VMEM((8, FF), F32),
            pltpu.VMEM((8, 3 * D), F32),
            pltpu.VMEM((16, TABLE), F32),
            pltpu.VMEM((2, 128, 128), F32),
            pltpu.VMEM((4, 256, 128), F32),
            pltpu.VMEM((SLOT, SLOT), F32),
            pltpu.VMEM((rows, D), F32),
            pltpu.VMEM(wide, F32),
            pltpu.VMEM(wide, F32),
            pltpu.VMEM(wide, F32),
            pltpu.SemaphoreType.DMA((3, 34)),
            pltpu.SemaphoreType.DMA((3, 32)),
            pltpu.SemaphoreType.DMA((3,)),
            pltpu.SemaphoreType.DMA((8,)),
            pltpu.SemaphoreType.DMA((8,)),
            pltpu.SemaphoreType.DMA,
            pltpu.SemaphoreType.DMA,
        ],
        compiler_params=params(
            collective_id=1, has_side_effects=True, dimension_semantics=("arbitrary",)
        ),
        name="forward",
    )(lengths, buckets, tokens, cotangent, qkv_p, out_p, up_p, down_p, table_p, head_scale, *vectors)


ORDER = (1, 2, 3, 0)


class Scatter:
    def __init__(self, place, kind, grad, out, buffers):
        self.place, self.kind, self.grad, self.out = place, kind, grad, out
        self.cores, self.over_x, self.over_y, self.far, self.quarter, self.send, self.recv = buffers
        self.made = {}
        here = place
        for k in range(4):
            z = (here.z + k) % 4
            mine = 2 * here.x + here.core
            other = 2 * (1 - here.x) + here.core
            for x in range(2):
                self.copy(
                    k, x, self.block(2 * x + 1 - here.core, z), self.from_core(k, x),
                    here.at(core=1 - here.core),
                )
            if k % 2 == 0:
                self.copy(k, 2, self.block(other, z), self.over_x.at[k // 2], here.at(x=1 - here.x))
                self.copy(
                    k, 4, self.part(mine, z, 1 - here.y), self.far.at[k], here.at(y=1 - here.y)
                )
            else:
                for x in range(2):
                    self.copy(
                        k, 2 + x, self.part(2 * x + here.core, z, 1 - here.y),
                        self.over_y.at[k // 2, x], here.at(y=1 - here.y),
                    )
                self.copy(k, 4, self.part(other, z, here.y), self.far.at[k], here.at(x=1 - here.x))
            if k:
                self.copy(k, 5, self.part(mine, z, here.y), self.quarter.at[k - 1], here.at(z=z))

    def from_core(self, k, x):
        return self.cores.at[k, x, :, : self.over_x.shape[-1]]

    def block(self, d, z):
        if self.kind == "panel":
            return self.grad.at[d, rows_of(z, 192), :]
        if self.kind == "wide":
            return self.grad.at[rows_of(z, 192), rows_of(d, 768)]
        return self.grad.at[rows_of(d, 192), rows_of(z, 768)]

    def part(self, d, z, y):
        if self.kind == "panel":
            return self.grad.at[d, rows_of(2 * z + y, 96), :]
        if self.kind == "wide":
            return self.grad.at[rows_of(2 * z + y, 96), rows_of(d, 768)]
        return self.grad.at[rows_of(d, 192), rows_of(2 * z + y, 384)]

    def copy(self, k, index, src, dst, peer):
        self.made[k, index] = remote(src, dst, self.send.at[k, index], self.recv.at[k, index], peer)

    def add(self, target, source):
        def some(n, carry):
            at = rows_of(n, 16)
            target[at, :] = target[at, :] + source[at, :]
            return carry

        lax.fori_loop(0, target.shape[0] // 16, some, 0)

    def core(self, k):
        for x in range(2):
            self.made[k, x].start()

    def plane(self, k):
        here = self.place
        z = (here.z + k) % 4
        for x in range(2):
            self.made[k, x].wait_recv()
            self.add(self.block(2 * x + here.core, z), self.from_core(k, x))
        self.made[k, 2].start()
        if k % 2:
            self.made[k, 3].start()

    def turn(self, k):
        here = self.place
        z = (here.z + k) % 4
        self.made[k, 2].wait_recv()
        if k % 2 == 0:
            self.add(self.block(2 * here.x + here.core, z), self.over_x.at[k // 2])
        else:
            self.made[k, 3].wait_recv()
            for x in range(2):
                self.add(self.part(2 * x + here.core, z, here.y), self.over_y.at[k // 2, x])
        self.made[k, 4].start()

    def line(self, k):
        here = self.place
        self.made[k, 4].wait_recv()
        self.add(self.part(2 * here.x + here.core, (here.z + k) % 4, here.y), self.far.at[k])
        if k:
            self.made[k, 5].start()

    def end(self):
        here = self.place
        for k in range(1, 4):
            self.made[k, 5].wait_recv()
        total = self.part(2 * here.x + here.core, here.z, here.y)[...].astype(F32)
        for k in range(3):
            total = total + self.quarter[k].astype(F32)
        self.out[...] = total[:, : self.out.shape[1]]
        for made in self.made.values():
            made.wait_send()


def scatter_scratch(kind, width):
    half = (192, width // 2) if kind == "turned" else (96, width)
    return [
        pltpu.VMEM((4, 2, 192, width), BF16),
        pltpu.VMEM((2, 192, width), BF16),
        pltpu.VMEM((2, 2) + half, BF16),
        pltpu.VMEM((4,) + half, BF16),
        pltpu.VMEM((3,) + half, BF16),
        pltpu.SemaphoreType.DMA((4, 6)),
        pltpu.SemaphoreType.DMA((4, 6)),
    ]


def pack_sums(sums_ref, first_ref, wide_ref, pair, table_ref, packed):
    low = first_ref[0:2, :]
    narrow = sums_ref[...]
    group = lax.broadcasted_iota(jnp.int32, (D, 128), 0) // HEAD_DIM
    pick = (group == lax.broadcasted_iota(jnp.int32, (D, 128), 1)).astype(F32).astype(BF16)
    high, rest = split_low(narrow[8:16])
    heads = (nn(high, pick) + nn(rest, pick))[0:1]
    heads = jnp.concatenate([heads, jnp.zeros((1, 64), F32)], 1)
    for f in range(8):
        at = slice(96 * f, 96 * f + 96)
        packed[f, 0:1, :] = jnp.concatenate(
            [low[0:1, at], low[1:2, at], narrow[2:3, at], narrow[3:4, at]], 1
        )
        packed[f, 1:2, :] = jnp.concatenate([narrow[n : n + 1, at] for n in range(4, 8)], 1)
        packed[f, 2:5, :] = wide_ref[0:3, 384 * f : 384 * f + 384]
        at = slice(192 * f, 192 * f + 192)
        packed[f, 5:6, :] = jnp.concatenate([pair[:, at], heads], 1)
        for n in range(PAIRS):
            packed[f, 6 + n : 7 + n, :] = jnp.concatenate(
                [table_ref[2 * n : 2 * n + 1, at], table_ref[2 * n + 1 : 2 * n + 2, at]], 1
            )
        packed[f, 12:16, :] = jnp.zeros((4, 384), F32)


class SmallSums:
    def __init__(self, place, packed, rows, peers, sems):
        self.place, self.packed, self.rows, self.peers = place, packed, rows, peers
        self.send, self.recv = sems

    def begin(self):
        here = self.place
        f = here.z * 2 + here.y
        self.made = []
        for k in range(1, 8):
            to = (f + k) % 8
            made = remote(
                self.packed.at[to], self.rows.at[k - 1], self.send.at[k], self.recv.at[k],
                here.at(z=to // 2, y=to % 2),
            )
            made.start()
            self.made.append(made)

    def cross(self):
        here = self.place
        f = here.z * 2 + here.y
        for made in self.made:
            made.wait()
        total = self.packed[f]
        for k in range(7):
            total = total + self.rows[k]
        self.peers[0] = total
        d = here.x * 2 + here.core
        self.made = []
        for k in range(1, 4):
            to = (d + k) % 4
            made = remote(
                self.peers.at[0], self.peers.at[k], self.send.at[7 + k], self.recv.at[7 + k],
                here.at(x=to // 2, core=to % 2),
            )
            made.start()
            self.made.append(made)

    def end(self):
        for made in self.made:
            made.wait()
        return (self.peers[0] + self.peers[1]) + (self.peers[2] + self.peers[3])


BACK_SCHEDULE = {
    3: [("down", "plane", 0)],
    4: [("down", "plane", 1)],
    5: [("down", "plane", 2)],
    6: [("down", "plane", 3)],
    7: [("down", "turn", 0)],
    8: [("down", "turn", 1)],
    10: [("down", "turn", 2), ("up", "plane", 0)],
    11: [("down", "line", 1), ("down", "turn", 3), ("up", "plane", 1), ("up", "plane", 2)],
    12: [("up", "plane", 3), ("out", "plane", 0), ("out", "plane", 1), ("out", "plane", 2), ("out", "plane", 3)],
    13: [("down", "line", 0)],
    14: [("down", "line", 2)],
    15: [("up", "turn", 0)],
    17: [("down", "line", 3)],
    18: [("up", "turn", 1)],
    22: [("up", "turn", 2), ("qkv", "plane", 0)],
    23: [("up", "turn", 3), ("out", "turn", 0), ("qkv", "plane", 1), ("qkv", "plane", 2)],
    24: [("out", "turn", 1), ("out", "turn", 2), ("qkv", "plane", 3)],
    25: [("out", "turn", 3)],
}
BACK_DRAIN = [
    ("up", "line", 1),
    ("up", "line", 0),
    ("up", "line", 2),
    ("qkv", "turn", 0),
    ("out", "line", 0),
    ("up", "line", 3),
    ("qkv", "turn", 1),
    ("out", "line", 2),
    ("qkv", "turn", 2),
    ("out", "line", 1),
    ("out", "line", 3),
    ("qkv", "turn", 3),
    ("qkv", "line", 1),
    ("qkv", "line", 0),
    ("qkv", "line", 3),
    ("qkv", "line", 2),
]


def backward_kernel(
    buckets, cot_hbm, act_ref, second_hbm, low_ref, mixed_hbm, branch_hbm, normed_hbm,
    probs_ref, query_ref, keys_ref, values_ref, attended_low_ref, vec_ref, sums_ref, wide_ref,
    x_hbm, middle_hbm, weight_hbm,
    input_grad_ref, down_out, up_out, out_out, qkv_out, total_ref,
    left, turned, middle_ref, first_in, proj, grid_ref, down_ref, up_ref, out_ref, qkv_ref,
    table_ref, first_ref, wall_small, wall_large, packed, gathered, peers, small_send, small_recv,
    loading, middle_sem, *buffers,
):
    step = pl.program_id(0)
    place = Place()
    parts = {
        "down": Scatter(place, "turned", down_ref, down_out, buffers[0:7]),
        "up": Scatter(place, "wide", up_ref, up_out, buffers[7:14]),
        "out": Scatter(place, "panel", out_ref, out_out, buffers[14:21]),
        "qkv": Scatter(place, "panel", qkv_ref, qkv_out, buffers[0:1] + buffers[21:27]),
    }
    small = SmallSums(place, packed, gathered, peers, (small_send, small_recv))
    count = query_ref.shape[0] // SLOT

    def load(n, src, dst):
        return pltpu.make_async_copy(src, dst, loading.at[n])

    load_cot = load(0, cot_hbm, left.at[0])
    load_second = load(1, second_hbm, left.at[1])
    load_mixed = load(2, mixed_hbm, left.at[0])
    load_branch = load(3, branch_hbm, left.at[1])
    load_normed = load(4, normed_hbm, left.at[0])
    load_x = load(5, x_hbm, left.at[1])

    def load_middle(b):
        n = b % 2
        return pltpu.make_async_copy(middle_hbm.at[rows_of(b, SLOT), :], middle_ref.at[n], middle_sem.at[n])

    load_weight = load(7, weight_hbm, down_ref)

    def progress(at):
        for name, event, n in BACK_SCHEDULE.get(at, []):
            getattr(parts[name], event)(ORDER[n])

    def down_panel():
        z = (place.z + 1 + step) % 4
        down_ref[:, rows_of(z, 768)] = nn(turned[...], act_ref[...]).astype(BF16)

    @pl.when(step == 0)
    def _():
        place.greet()
        load_cot.start()
        load_second.start()
        place.meet()

    for at in BACK_SCHEDULE:
        if at < 23:
            pl.when(step == at)(functools.partial(progress, at))

    @pl.when(step < 4)
    def _():
        @pl.when(step == 0)
        def _():
            load_cot.wait()
            turned[...] = left[0].T
            load_mixed.start()

        down_panel()
        for n in range(4):
            pl.when(step == n)(functools.partial(parts["down"].core, ORDER[n]))

    @pl.when((step >= 4) & (step < 8))
    def _():
        @pl.when(step == 4)
        def _():
            load_second.wait()
            turned[...] = left[1].T
            load_branch.start()

        up_ref[:, rows_of(step - 4, 768)] = nn(turned[...], low_ref[...]).astype(BF16)

        @pl.when(step == 7)
        def _():
            for k in ORDER:
                parts["up"].core(k)

    @pl.when(step == 8)
    def _():
        load_mixed.wait()
        turned[...] = left[0].T
        load_normed.start()
        load_branch.wait()
        for d in range(4):
            out_ref[d] = nn(turned[...], left[1, :, 192 * d : 192 * d + 192]).astype(BF16)
        for k in ORDER:
            parts["out"].core(k)
        load_x.start()
        table_grad_start(table_ref, wall_small, wall_large)

    @pl.when((step >= 9) & (step < 15))
    def _():
        pair = step - 9
        cols = rows_of(pair, 128)
        for s in range(count):
            rows = slice(s * SLOT, s * SLOT + SLOT)
            query_grad, keys_grad, values_grad, scores_grads = attend_back(
                query_ref[rows, :], keys_ref[rows, :], values_ref[rows, :], attended_low_ref[rows, :],
                [probs_ref[half, s] for half in range(2)],
            )
            proj[0, rows, cols] = query_grad
            proj[1, rows, cols] = keys_grad
            proj[2, rows, cols] = values_grad
            chosen = jnp.where(buckets[s] == 0, 1.0, 0.0)
            for half in range(2):
                if s == 0:
                    grid_ref[0, half] = scores_grads[half] * chosen
                    grid_ref[1, half] = scores_grads[half] * (1.0 - chosen)
                else:
                    grid_ref[0, half] += scores_grads[half] * chosen
                    grid_ref[1, half] += scores_grads[half] * (1.0 - chosen)
        for half in range(2):
            table_grad_head(grid_ref, table_ref, wall_small, wall_large, 2 * pair + half, half)

    def lay_panel(d):
        def lay(pieces):
            at = 0
            for n, first, last in pieces:
                left[0, :, at : at + last - first] = proj[n, :, first:last]
                at += last - first

        cuts = (
            [(0, 0, 576)], [(0, 576, 768), (1, 0, 384)], [(1, 384, 768), (2, 0, 192)], [(2, 192, 768)],
        )
        for n, pieces in enumerate(cuts):
            pl.when(d == n)(functools.partial(lay, pieces))

    @pl.when((step >= 15) & (step < 19))
    def _():
        @pl.when(step == 15)
        def _():
            load_normed.wait()
            turned[...] = left[0].T

        lay_panel(step - 15)
        grad = nn(turned[...], left[0, :, :576]).astype(BF16)
        qkv_ref[step - 15] = jnp.concatenate([grad, jnp.zeros((D, 64), BF16)], 1)

        @pl.when(step == 18)
        def _():
            for k in ORDER:
                parts["qkv"].core(k)

    @pl.when(step == 19)
    def _():
        parts["down"].end()
        load_weight.start()

    @pl.when((step >= 19) & (step < 23))
    def _():
        lay_panel(step - 19)

        @pl.when(step == 19)
        def _():
            load_weight.wait()
            first_in[...] = jnp.zeros_like(first_in)

        first_in[...] += nt(left[0, :, :576], down_ref[:, pl.ds(pl.multiple_of(768 * (step - 19), 768), 576)])

    @pl.when(step == 23)
    def _():
        progress(23)
        load_middle(0).start()
        load_x.wait()
        first_ref[...] = jnp.zeros_like(first_ref)

        def one_block(b, carry):
            rows = pl.ds(pl.multiple_of(b * SLOT, SLOT), SLOT)
            unit, inverse = standardize(left[1, rows, :].astype(F32))
            grad = first_in[rows, :]
            first_ref[0:1, :] += column_sum(grad * unit)
            first_ref[1:2, :] += column_sum(grad)
            back = norm_back(grad * vec_ref[0:1, :], unit, inverse)

            @pl.when(b + 1 < count)
            def _():
                load_middle(b + 1).start()

            load_middle(b).wait()
            input_grad_ref[rows, :] = (middle_ref[b % 2] + back).astype(BF16)
            return carry

        lax.fori_loop(0, count, one_block, 0)
        progress(24)
        table_grad_end(table_ref, wall_small, wall_large)
        pair = jnp.concatenate([tall_sum(proj.at[0]), tall_sum(proj.at[2])], 1)
        progress(25)
        pack_sums(sums_ref, first_ref, wide_ref, pair, table_ref, packed)
        small.begin()
        for n, (name, event, k) in enumerate(BACK_DRAIN):
            if n == len(BACK_DRAIN) // 2:
                small.cross()
            getattr(parts[name], event)(ORDER[k])
        parts["up"].end()
        parts["out"].end()
        total_ref[...] = small.end()
        parts["qkv"].end()


def backward(
    buckets, cotangent, act, second, low, mixed, branch, normed, probs, qkv, attended_low, vecs,
    sums, wide, tokens, middle_grad, weight,
):
    rows = cotangent.shape[0]
    count = rows // SLOT
    any_space = pl.BlockSpec(memory_space=ANY)

    def held(shape):
        return pl.BlockSpec(shape, lambda i: (0,) * len(shape))

    def pair(i):
        return jnp.clip(i - 9, 0, PAIRS - 1)

    def panel(base):
        return pl.BlockSpec((rows, 128), lambda i: (0, base + pair(i)))

    def act_panel(i):
        return (0, (lax.axis_index("fsdp") // 2 + 1 + jnp.minimum(i, 3)) % 4)

    outs = [(192, 384), (96, 768), (96, 192), (96, 576), (16, 384)]
    return pl.pallas_call(
        backward_kernel,
        grid=(24,),
        in_specs=[
            pl.BlockSpec(memory_space=pltpu.SMEM),
            any_space,
            pl.BlockSpec((rows, D), act_panel),
            any_space,
            pl.BlockSpec((rows, D), lambda i: (0, jnp.clip(i - 4, 0, 3))),
            any_space, any_space, any_space,
            pl.BlockSpec((2, count, SLOT, SLOT), lambda i: (pair(i), 0, 0, 0)),
            panel(0), panel(PAIRS), panel(2 * PAIRS), panel(0),
            held((8, D)), held((16, D)), held((8, FF)),
            any_space, any_space, any_space,
        ],
        out_specs=[held((rows, D))] + [held(shape) for shape in outs],
        out_shape=[jax.ShapeDtypeStruct((rows, D), BF16)]
        + [jax.ShapeDtypeStruct(shape, F32) for shape in outs],
        scratch_shapes=[
            pltpu.VMEM((2, rows, D), BF16),
            pltpu.VMEM((D, rows), BF16),
            pltpu.VMEM((2, SLOT, D), F32),
            pltpu.VMEM((rows, D), F32),
            pltpu.VMEM((3, rows, D), BF16),
            pltpu.VMEM((2, 2, SLOT, SLOT), F32),
            pltpu.VMEM((D, FF), BF16),
            pltpu.VMEM((D, FF), BF16),
            pltpu.VMEM((4, D, 192), BF16),
            pltpu.VMEM((4, D, 640), BF16),
            pltpu.VMEM((16, TABLE), F32),
            pltpu.VMEM((8, D), F32),
            pltpu.VMEM((2, 128, 128), F32),
            pltpu.VMEM((4, 256, 128), F32),
            pltpu.VMEM((8, 16, 384), F32),
            pltpu.VMEM((7, 16, 384), F32),
            pltpu.VMEM((4, 16, 384), F32),
            pltpu.SemaphoreType.DMA((11,)),
            pltpu.SemaphoreType.DMA((11,)),
            pltpu.SemaphoreType.DMA((8,)),
            pltpu.SemaphoreType.DMA((2,)),
        ]
        + scatter_scratch("turned", 768) + scatter_scratch("wide", 768)
        + scatter_scratch("panel", 192) + scatter_scratch("panel", 640)[1:],
        compiler_params=pltpu.CompilerParams(
            collective_id=2, has_side_effects=True, dimension_semantics=("arbitrary",),
            vmem_limit_bytes=BACK_LIMIT,
        ),
        name="backward",
    )(
        buckets, cotangent, act, second, low, mixed, branch, normed, probs, qkv, qkv, qkv,
        attended_low, vecs, sums, wide, tokens, middle_grad, weight,
    )


def emit_kernel(count, total_ref, *refs):
    sources = refs[:count]
    targets = refs[count : 2 * count]
    small = refs[2 * count : 2 * count + 14]
    held = refs[2 * count + 14 : -2]
    into, out = refs[-2:]
    loads = [
        pltpu.make_async_copy(src, dst, into.at[n]) for n, (src, dst) in enumerate(zip(sources, held))
    ]
    made = [
        pltpu.make_async_copy(src, dst, out.at[n]) for n, (src, dst) in enumerate(zip(held, targets))
    ]
    for each in loads:
        each.start()
    for load, each in zip(loads, made):
        load.wait()
        each.start()
    total = total_ref[...]
    for n in range(8):
        at = 96 * (n % 4)
        small[n][...] = total[n // 4 : n // 4 + 1, at : at + 96].reshape(96)
    for n in range(3):
        small[8 + n][...] = total[2 + n : 3 + n, :].reshape(384)
    small[11][...] = total[5:6, 0:192].reshape(192)
    small[12][...] = total[5:6, 192:204].reshape(HEADS)
    for n in range(PAIRS):
        small[13][2 * n : 2 * n + 1, :] = total[6 + n : 7 + n, 0:192]
        small[13][2 * n + 1 : 2 * n + 2, :] = total[6 + n : 7 + n, 192:384]
    for each in made:
        each.wait()


def emit(total, *large):
    vmem = pl.BlockSpec(memory_space=pltpu.VMEM)
    any_space = pl.BlockSpec(memory_space=ANY)
    small = [(96,)] * 8 + [(384,)] * 3 + [(192,), (HEADS,), (HEADS, 192)]
    return pl.pallas_call(
        functools.partial(emit_kernel, len(large)),
        in_specs=[vmem] + [any_space] * len(large),
        out_specs=[any_space] * len(large) + [vmem] * len(small),
        out_shape=[jax.ShapeDtypeStruct(part.shape, part.dtype) for part in large]
        + [jax.ShapeDtypeStruct(shape, F32) for shape in small],
        scratch_shapes=[pltpu.VMEM(part.shape, part.dtype) for part in large]
        + [pltpu.SemaphoreType.DMA((len(large),))] * 2,
        compiler_params=params(),
        name="emit",
    )(total, *large)


def gather_matrix(piece):
    rows = lax.all_gather(piece, "fsdp", axis=0, tiled=True)
    return lax.all_gather(rows, "dp", axis=1, tiled=True)


def scatter_matrix(grad):
    part = lax.psum_scatter(grad, "dp", scatter_dimension=1, tiled=True).astype(F32)
    return lax.psum_scatter(part, "fsdp", scatter_dimension=0, tiled=True)


def body(
    tokens, cotangent, lengths, buckets, qkv_weight, query_value_bias, out_weight, out_bias,
    up_weight, up_bias, down_weight, down_bias, first_gain, first_shift, mix_gain, mix_shift,
    second_gain, second_shift, hidden_gain, hidden_shift, head_scale, position_table,
):
    parts = lax.axis_size("fsdp")
    own_kernels = (parts, lax.axis_size("dp")) == (8, 4)
    narrow = [
        first_gain, first_shift, mix_gain, mix_shift, second_gain, second_shift, out_bias, down_bias,
    ]
    wide = [up_bias, hidden_gain, hidden_shift]
    a = D // parts
    b = FF // parts
    if own_kernels:
        (
            normed, qkv, probs, result, mixed, second, act, low, branch, middle_grad, attended_low,
            sums, wide_sums, vecs, qkv_full,
        ) = forward(
            lengths, buckets, tokens, cotangent, qkv_weight, out_weight, up_weight, down_weight.T,
            position_table.T, head_scale, narrow + wide + [query_value_bias],
        )
        input_grad, down_owned, up_owned, out_owned, qkv_owned, total = backward(
            buckets, cotangent, act, second, low, mixed, branch, normed, probs, qkv, attended_low,
            vecs, sums, wide_sums, tokens, middle_grad, qkv_full,
        )
        result, input_grad, qkv_owned, out_owned, up_owned, down_owned, *small = emit(
            total, result, input_grad, qkv_owned, out_owned, up_owned, down_owned
        )
        down_owned = down_owned.T
        narrow_owned = small[:8]
        wide_owned = small[8:11]
        pair_owned, scale_grad, table_owned = small[11], small[12], small[13].T
    else:
        packed = jnp.concatenate(
            [jnp.pad(jnp.stack(narrow), ((0, 0), (0, b - a))), jnp.stack(wide)]
            + [jnp.pad(query_value_bias, (0, b - 2 * a))[None], jnp.zeros((4, b), BF16)]
            + [jnp.pad(position_table.T, ((0, 4), (0, b - 2 * a)))]
        )
        scales = jnp.repeat(head_scale.astype(F32), HEAD_DIM)[None]
        gathered = lax.all_gather(packed, "fsdp", axis=0)
        qkv_full = gather_matrix(qkv_weight)
        out_full = gather_matrix(out_weight)
        up_full = gather_matrix(up_weight)
        down_full = gather_matrix(down_weight).T
        gathered = gathered.astype(F32)
        vecs = gathered[:, :8, :a].transpose(1, 0, 2).reshape(8, D)
        wides = jnp.pad(gathered[:, 8:11].transpose(1, 0, 2).reshape(3, FF), ((0, 5), (0, 0)))
        pair = gathered[:, 11, : 2 * a].reshape(1, 2 * D)
        table = gathered[:, 16:, : 2 * a].transpose(1, 0, 2).reshape(16, TABLE)
        qkv_bias = jnp.concatenate([pair[:, :D], jnp.zeros((1, D), F32), pair[:, D:]], 1)

        bias = build_bias(table)
        normed, qkv, probs, attended = attention(
            lengths, buckets, tokens, vecs, qkv_full, qkv_bias, bias
        )
        (
            result, mixed, second, act, low, branch, middle_grad, attended_low, sums, wide_sums,
        ) = feed_forward(tokens, attended, cotangent, out_full, up_full, down_full, vecs, wides, scales)
        down_grad = outer_product(cotangent, act, 512)
        up_grad = outer_product(second, low, 512)
        out_grad = outer_product(mixed, branch, 256)
        input_grad, grids, qkv_grad, pair_sums, first_sums = attention_back(
            buckets, probs, qkv, attended_low, normed, tokens, middle_grad, qkv_full, vecs
        )
        table_sums = table_grad(grids)
        qkv_natural = qkv_grad.reshape(PAIRS, D, 3, 128).transpose(1, 2, 0, 3).reshape(D, 3 * D)

        qkv_owned = scatter_matrix(qkv_natural)
        out_owned = scatter_matrix(out_grad)
        up_owned = scatter_matrix(up_grad)
        down_owned = scatter_matrix(down_grad.T)
        pair_grad = pair_sums[:, 0].reshape(PAIRS, 3, 128).transpose(1, 0, 2).reshape(3, D)
        pair_grad = jnp.concatenate([pair_grad[0], pair_grad[2]])
        narrow_sums = jnp.concatenate([first_sums[:2], sums[2:8]], 0)
        packed = jnp.concatenate(
            [
                narrow_sums.reshape(8, parts, a).transpose(1, 0, 2).reshape(parts, -1),
                wide_sums[:3].reshape(3, parts, b).transpose(1, 0, 2).reshape(parts, -1),
                pair_grad.reshape(parts, -1),
                table_sums[:HEADS].T.reshape(parts, -1),
            ],
            1,
        )
        owned = lax.psum(lax.psum_scatter(packed, "fsdp", scatter_dimension=0, tiled=True), "dp")[0]
        scale_grad = lax.psum(sums[8].reshape(HEADS, HEAD_DIM).sum(1), ("fsdp", "dp"))
        narrow_owned = owned[: 8 * a].reshape(8, a)
        edge = 8 * a
        wide_owned = owned[edge : edge + 3 * b].reshape(3, b)
        edge += 3 * b
        pair_owned = owned[edge : edge + 2 * a]
        edge += 2 * a
        table_owned = owned[edge:].reshape(TABLE // parts, HEADS)
    return (
        result, input_grad, qkv_owned, pair_owned, out_owned, narrow_owned[6], up_owned,
        wide_owned[0], down_owned, narrow_owned[7], narrow_owned[0], narrow_owned[1],
        narrow_owned[2], narrow_owned[3], narrow_owned[4], narrow_owned[5], wide_owned[1],
        wide_owned[2], scale_grad, table_owned,
    )


def solution(mesh):
    tokens = P(("fsdp", "dp"), None)
    sequences = P(("fsdp", "dp"))
    matrix = P("fsdp", "dp")
    vector = P("fsdp")
    table = P("fsdp", None)
    in_specs = (
        tokens, tokens, sequences, sequences, matrix, vector, matrix, vector, matrix, vector,
        matrix, vector, vector, vector, vector, vector, vector, vector, vector, vector, P(), table,
    )
    out_specs = (
        tokens, tokens, matrix, vector, matrix, vector, matrix, vector, matrix, vector, vector,
        vector, vector, vector, vector, vector, vector, vector, P(), table,
    )
    return jax.shard_map(body, mesh=mesh, in_specs=in_specs, out_specs=out_specs, check_vma=False)
```

```python
import functools

import jax
import jax.numpy as jnp
from jax import lax
from jax.experimental import pallas as pl
from jax.experimental.pallas import tpu as pltpu
from jax.sharding import PartitionSpec as P

D = 768
HEADS = 12
PAIRS = 6
HEAD_DIM = 64
FF = 3072
SLOT = 256
TABLE = 1536

EPS = 1e-05
MASKED = -1000000000.0
F32 = jnp.float32
BF16 = jnp.bfloat16
VMEM_LIMIT = 60 * 2**20
BACK_LIMIT = 60 * 2**20


def params(**more):
    return pltpu.CompilerParams(vmem_limit_bytes=VMEM_LIMIT, **more)


def nn(left, right):
    return lax.dot_general(left, right, (((1,), (0,)), ((), ())), preferred_element_type=F32)


def nt(left, right):
    return lax.dot_general(left, right, (((1,), (1,)), ((), ())), preferred_element_type=F32)


def standardize(values):
    center = values - jnp.mean(values, -1, keepdims=True)
    inverse = lax.rsqrt(jnp.mean(center * center, -1, keepdims=True) + EPS)
    return center * inverse, inverse


def norm_back(grad, unit, inverse):
    return inverse * (
        grad
        - jnp.mean(grad, -1, keepdims=True)
        - unit * jnp.mean(grad * unit, -1, keepdims=True)
    )


def column_sum(values):
    return jnp.sum(values, 0, keepdims=True)


def tall_sum(ref):
    def some(n, total):
        return total + column_sum(ref[rows_of(n, 64), :].astype(F32))

    return lax.fori_loop(0, ref.shape[0] // 64, some, jnp.zeros((1, ref.shape[1]), F32))


def split_low(values):
    high = values.astype(BF16)
    return high, (values - high.astype(F32)).astype(BF16)


def compaction(side, lanes):
    plane = lax.broadcasted_iota(jnp.int32, (1024, lanes), 0)
    lane = lax.broadcasted_iota(jnp.int32, (1024, lanes), 1)
    across = plane & 31
    return ((lane == side * (plane >> 5) + across) & (across < side)).astype(F32).astype(BF16)


def inside_grid(patches):
    row = lax.broadcasted_iota(jnp.int32, (SLOT, SLOT), 0)
    col = lax.broadcasted_iota(jnp.int32, (SLOT, SLOT), 1)
    return (row < patches) & (col < patches)


def store_tiles(ref, values):
    for k in range(ref.shape[0]):
        ref[k] = values[:, 128 * k : 128 * k + 128]


def load_tiles(ref):
    return jnp.concatenate([ref[k] for k in range(ref.shape[0])], 1)


def load_strided(ref, first, count):
    return jnp.concatenate(
        [ref[k, pl.ds(first, count, 16), :] for k in range(ref.shape[0])], 1
    )


def store_strided(ref, first, values):
    for k in range(ref.shape[0]):
        ref[k, pl.ds(first, values.shape[0], 16), :] = values[:, 128 * k : 128 * k + 128]


def bias_walls(table_ref, wall_small, wall_large, visual):
    plane = table_ref[:, 512:]
    shifted = [pltpu.roll(plane, (ic - 15) % 1024, 1) for ic in range(16)]
    stack = jnp.concatenate(shifted, 0).astype(BF16)
    store_tiles(wall_large, nn(stack, compaction(15, 512)))
    store_tiles(wall_small, nn(stack[:128], compaction(8, 256)))
    visual[...] = jnp.zeros_like(visual)


def bias_head(table_ref, out_ref, wall_small, wall_large, visual, h, carry):
    line = jnp.broadcast_to(table_ref[pl.ds(h, 1), :512], (SLOT, 512))
    textual = pltpu.roll(line, 257, 1, stride=1, stride_axis=0)[:, :SLOT]
    large = load_strided(wall_large, h, 16)
    for ir in range(15):
        visual[pl.ds(ir * 15, 16), :] = pltpu.roll(large, 512 - (15 - ir) * 15, 1)[:, :SLOT]
    out_ref[1, h] = jnp.where(inside_grid(225), visual[...], textual).astype(BF16)
    small = load_strided(wall_small, h, 8)
    rows = [pltpu.roll(small, 256 - (15 - ir) * 8, 1) for ir in range(8)]
    grid = jnp.concatenate(rows + [jnp.zeros((192, SLOT), F32)], 0)
    out_ref[0, h] = jnp.where(inside_grid(64), grid, textual).astype(BF16)
    return carry


def bias_kernel(table_ref, out_ref, wall_small, wall_large, visual):
    bias_walls(table_ref, wall_small, wall_large, visual)
    one_head = functools.partial(bias_head, table_ref, out_ref, wall_small, wall_large, visual)
    lax.fori_loop(0, HEADS, one_head, 0)


def build_bias(table):
    return pl.pallas_call(
        bias_kernel,
        out_shape=jax.ShapeDtypeStruct((2, HEADS, SLOT, SLOT), BF16),
        scratch_shapes=[
            pltpu.VMEM((2, 128, 128), F32),
            pltpu.VMEM((4, 256, 128), F32),
            pltpu.VMEM((SLOT, SLOT), F32),
        ],
        compiler_params=params(),
        name="build_bias",
    )(table)


def table_grad_start(out_ref, wall_small, wall_large):
    wall_small[...] = jnp.zeros_like(wall_small)
    wall_large[...] = jnp.zeros_like(wall_large)
    out_ref[...] = jnp.zeros_like(out_ref)


def table_grad_head(grid_ref, out_ref, wall_small, wall_large, h, slot):
    row = lax.broadcasted_iota(jnp.int32, (SLOT, SLOT), 0)
    col = lax.broadcasted_iota(jnp.int32, (SLOT, SLOT), 1)
    flip = (row + col == SLOT - 1).astype(F32).astype(BF16)
    lane = lax.broadcasted_iota(jnp.int32, (16, SLOT), 1)
    textual = jnp.where(inside_grid(64), 0.0, grid_ref[0, slot]) + jnp.where(
        inside_grid(225), 0.0, grid_ref[1, slot]
    )
    high, low = split_low(textual)
    flipped = nn(flip, high) + nn(flip, low)
    wide = jnp.concatenate([flipped, jnp.zeros((SLOT, SLOT), F32)], 1)
    out_ref[pl.ds(h, 1), :512] = column_sum(pltpu.roll(wide, 0, 1, stride=1, stride_axis=0))
    total = jnp.zeros((16, 512), F32)
    for ir in range(15):
        part = jnp.where(lane < 225, grid_ref[1, slot, pl.ds(ir * 15, 16), :], 0.0)
        part = jnp.concatenate([part, jnp.zeros((16, SLOT), F32)], 1)
        total = total + pltpu.roll(part, (15 - ir) * 15, 1)
    store_strided(wall_large, h, total)
    total = jnp.zeros((8, SLOT), F32)
    for ir in range(8):
        part = jnp.where(lane[:8] < 64, grid_ref[0, slot, pl.ds(ir * 8, 8), :], 0.0)
        total = total + pltpu.roll(part, (15 - ir) * 8, 1)
    store_strided(wall_small, h, total)


def table_grad_end(out_ref, wall_small, wall_large):
    high, low = split_low(load_tiles(wall_large))
    spread = compaction(15, 512)
    large = nt(high, spread) + nt(low, spread)
    high, low = split_low(load_tiles(wall_small))
    spread = compaction(8, 256)
    small = nt(high, spread) + nt(low, spread)
    plane = jnp.zeros((16, 1024), F32)
    for ic in range(15):
        part = large[ic * 16 : ic * 16 + 16]
        if ic < 8:
            part = part + small[ic * 16 : ic * 16 + 16]
        plane = plane + pltpu.roll(part, 15 - ic, 1)
    out_ref[:, 512:] = plane


def table_grad_kernel(grid_ref, out_ref, wall_small, wall_large):
    table_grad_start(out_ref, wall_small, wall_large)

    def one_head(h, carry):
        table_grad_head(grid_ref, out_ref, wall_small, wall_large, h, h)
        return carry

    lax.fori_loop(0, HEADS, one_head, 0)
    table_grad_end(out_ref, wall_small, wall_large)


def table_grad(grids):
    return pl.pallas_call(
        table_grad_kernel,
        out_shape=jax.ShapeDtypeStruct((16, TABLE), F32),
        scratch_shapes=[pltpu.VMEM((2, 128, 128), F32), pltpu.VMEM((4, 256, 128), F32)],
        compiler_params=params(),
        name="table_grad",
    )(grids)


def by_head(pair, axis):
    first = lax.broadcasted_iota(jnp.int32, pair.shape, 1) < HEAD_DIM
    return jnp.concatenate([jnp.where(first, pair, 0), jnp.where(first, 0, pair)], axis)


def attend(query, keys, values, bias, live):
    logits = nt(by_head(query, 0), keys)
    probs = []
    for half in range(2):
        rows = slice(SLOT * half, SLOT * half + SLOT)
        scores = jnp.where(live, logits[rows] + bias[half].astype(F32), MASKED)
        shifted = jnp.exp(scores - jnp.max(scores, -1, keepdims=True))
        probs.append((shifted * (1.0 / jnp.sum(shifted, -1, keepdims=True))).astype(BF16))
    return probs, nn(jnp.concatenate(probs, 1), by_head(values, 0))


def attend_back(query, keys, values, grad, probs):
    probs_grads = nt(by_head(grad, 0), values)
    grad_turned = grad.T
    query_turned = query.T
    keys_parts = []
    values_parts = []
    scores_grads = []
    lows = []
    for half in range(2):
        part = slice(HEAD_DIM * half, HEAD_DIM * half + HEAD_DIM)
        wide = probs[half].astype(F32)
        probs_grad = probs_grads[SLOT * half : SLOT * half + SLOT]
        values_parts.append(nn(grad_turned[part], probs[half]))
        scores_grad = wide * (probs_grad - jnp.sum(wide * probs_grad, -1, keepdims=True))
        scores_grads.append(scores_grad)
        lows.append(scores_grad.astype(BF16))
        keys_parts.append(nn(query_turned[part], lows[half]))
    query_grad = nn(jnp.concatenate(lows, 1), by_head(keys, 0)) * HEAD_DIM ** (-0.5)
    keys_grad = jnp.concatenate(keys_parts, 0).T
    values_grad = jnp.concatenate(values_parts, 0).T
    return query_grad.astype(BF16), keys_grad.astype(BF16), values_grad.astype(BF16), scores_grads


def attention_kernel(
    lengths, buckets, x_ref, vec_ref, weight_ref, qkv_bias_ref, bias_ref,
    normed_ref, qkv_ref, probs_ref, attended_ref,
):
    count = x_ref.shape[0] // SLOT

    def one_block(b, carry):
        rows = pl.ds(pl.multiple_of(b * SLOT, SLOT), SLOT)
        unit, inverse = standardize(x_ref[rows, :].astype(F32))
        normed_ref[rows, :] = (unit * vec_ref[0:1, :] + vec_ref[1:2, :]).astype(BF16)
        return carry

    lax.fori_loop(0, count, one_block, 0)

    def one_panel(n, carry):
        cols = pl.ds(pl.multiple_of(n * 256, 256), 256)
        out = nn(normed_ref[...], weight_ref[:, cols]) + qkv_bias_ref[:, cols]
        out = (out * jnp.where(n < 3, HEAD_DIM ** (-0.5), 1.0)).astype(BF16)
        qkv_ref[2 * n] = out[:, :128]
        qkv_ref[2 * n + 1] = out[:, 128:]
        return carry

    lax.fori_loop(0, 9, one_panel, 0)
    key_slot = lax.broadcasted_iota(jnp.int32, (SLOT, SLOT), 1)

    def one_unit(step, carry):
        pair = step // count
        s = step % count
        rows = pl.ds(pl.multiple_of(s * SLOT, SLOT), SLOT)
        bias = [bias_ref[buckets[s], 2 * pair + half] for half in range(2)]
        probs, out = attend(
            qkv_ref[pair, rows, :], qkv_ref[PAIRS + pair, rows, :], qkv_ref[2 * PAIRS + pair, rows, :],
            bias, key_slot < lengths[s],
        )
        for half in range(2):
            probs_ref[2 * pair + half, s] = probs[half]
        attended_ref[rows, pl.ds(pl.multiple_of(pair * 128, 128), 128)] = out
        return carry

    lax.fori_loop(0, PAIRS * count, one_unit, 0)


def attention(lengths, buckets, tokens, vecs, weight, qkv_bias, bias):
    rows = tokens.shape[0]
    count = rows // SLOT
    smem = pl.BlockSpec(memory_space=pltpu.SMEM)
    vmem = pl.BlockSpec(memory_space=pltpu.VMEM)
    return pl.pallas_call(
        attention_kernel,
        in_specs=[smem, smem] + [vmem] * 5,
        out_shape=[
            jax.ShapeDtypeStruct((rows, D), BF16),
            jax.ShapeDtypeStruct((3 * PAIRS, rows, 128), BF16),
            jax.ShapeDtypeStruct((HEADS, count, SLOT, SLOT), BF16),
            jax.ShapeDtypeStruct((rows, D), F32),
        ],
        compiler_params=params(),
        name="attention_forward",
    )(lengths, buckets, tokens, vecs, weight, qkv_bias, bias)


PANEL = 512


def feed_kernel(*refs):
    @pl.when(pl.program_id(0) == 0)
    def _():
        for ref in refs[17:19]:
            ref[...] = jnp.zeros_like(ref)

    feed_block(*refs, lambda: None)


def feed_block(
    x_ref, attended_ref, cot_ref, out_w, up_w, down_w, vec_ref, wide_ref, scale_ref,
    result_ref, mixed_ref, second_ref, act_ref, low_ref, branch_ref, middle_grad_ref,
    attended_low_ref, sums_ref, wide_sums_ref,
    gelu_ref, slope_ref, grad_ref, before_down,
):
    def add(row, values):
        sums_ref[row : row + 1, :] += column_sum(values)

    rows = x_ref.shape[0]
    attended = attended_ref[...]
    mix_unit, mix_inverse = standardize(attended * scale_ref[...])
    mixed = (mix_unit * vec_ref[2:3, :] + vec_ref[3:4, :]).astype(BF16)
    mixed_ref[...] = mixed
    middle = x_ref[...].astype(F32) + nn(mixed, out_w[...]) + vec_ref[6:7, :]
    second_unit, second_inverse = standardize(middle)
    second = (second_unit * vec_ref[4:5, :] + vec_ref[5:6, :]).astype(BF16)
    second_ref[...] = second
    cot = cot_ref[...]

    panels = [slice(n, n + PANEL) for n in range(0, FF, PANEL)]
    total = jnp.zeros((rows, 1), F32)
    for cols in panels:
        hidden = nn(second, up_w[:, cols]) + wide_ref[0:1, cols]
        cdf = 0.5 + 0.5 * lax.erf(hidden * 0.7071067811865476)
        gelu = hidden * cdf
        gelu_ref[:, cols] = gelu
        slope_ref[:, cols] = cdf + hidden * (jnp.exp(-0.5 * hidden * hidden) * 0.3989422804014327)
        total = total + jnp.sum(gelu, -1, keepdims=True)
    mean = total * (1.0 / FF)
    total = jnp.zeros((rows, 1), F32)
    for cols in panels:
        center = gelu_ref[:, cols] - mean
        total = total + jnp.sum(center * center, -1, keepdims=True)
    inverse = lax.rsqrt(total * (1.0 / FF) + EPS)
    before_down()
    result = middle + vec_ref[7:8, :]
    first = jnp.zeros((rows, 1), F32)
    second_moment = jnp.zeros((rows, 1), F32)
    for cols in panels:
        unit = (gelu_ref[:, cols] - mean) * inverse
        gelu_ref[:, cols] = unit
        act = (unit * wide_ref[1:2, cols] + wide_ref[2:3, cols]).astype(BF16)
        act_ref[:, cols] = act
        result = result + nt(act, down_w[:, cols])
        act_grad = nn(cot, down_w[:, cols])
        wide_sums_ref[1:2, cols] += column_sum(act_grad * unit)
        wide_sums_ref[2:3, cols] += column_sum(act_grad)
        grad = act_grad * wide_ref[1:2, cols]
        grad_ref[:, cols] = grad
        first = first + jnp.sum(grad, -1, keepdims=True)
        second_moment = second_moment + jnp.sum(grad * unit, -1, keepdims=True)
    result_ref[...] = result.astype(BF16)
    first = first * (1.0 / FF)
    second_moment = second_moment * (1.0 / FF)
    second_in = jnp.zeros((rows, D), F32)
    for cols in panels:
        grad = inverse * (grad_ref[:, cols] - first - gelu_ref[:, cols] * second_moment)
        low = (grad * slope_ref[:, cols]).astype(BF16)
        low_ref[:, cols] = low
        wide_sums_ref[0:1, cols] += column_sum(low.astype(F32))
        second_in = second_in + nt(low, up_w[:, cols])
    add(4, second_in * second_unit)
    add(5, second_in)
    cot_wide = cot.astype(F32)
    add(7, cot_wide)
    middle_grad = cot_wide + norm_back(second_in * vec_ref[4:5, :], second_unit, second_inverse)
    middle_grad_ref[...] = middle_grad
    branch = middle_grad.astype(BF16)
    branch_ref[...] = branch
    add(6, branch.astype(F32))
    mixed_in = nt(branch, out_w[...])
    add(2, mixed_in * mix_unit)
    add(3, mixed_in)
    grad = norm_back(mixed_in * vec_ref[2:3, :], mix_unit, mix_inverse)
    add(8, grad * attended)
    attended_low_ref[...] = (grad * scale_ref[...]).astype(BF16)


def feed_forward(tokens, attended, cotangent, out_w, up_w, down_w, vecs, wide, scales):
    rows = tokens.shape[0]
    tile = 256
    block = pl.BlockSpec((tile, D), lambda i: (i, 0))
    wide_block = pl.BlockSpec((tile, FF), lambda i: (i, 0))

    def whole(shape):
        return pl.BlockSpec(shape, lambda i: (0, 0), pipeline_mode=pl.Buffered(1))

    def held(shape):
        return pl.BlockSpec(shape, lambda i: (0, 0))

    return pl.pallas_call(
        feed_kernel,
        grid=(rows // tile,),
        in_specs=[block] * 3
        + [whole((D, D)), whole((D, FF)), whole((D, FF)), whole((8, D)), whole((8, FF)), whole((1, D))],
        out_specs=[block, block, block, wide_block, wide_block, block, block, block]
        + [held((16, D)), held((8, FF))],
        out_shape=[
            jax.ShapeDtypeStruct((rows, D), BF16),
            jax.ShapeDtypeStruct((rows, D), BF16),
            jax.ShapeDtypeStruct((rows, D), BF16),
            jax.ShapeDtypeStruct((rows, FF), BF16),
            jax.ShapeDtypeStruct((rows, FF), BF16),
            jax.ShapeDtypeStruct((rows, D), BF16),
            jax.ShapeDtypeStruct((rows, D), F32),
            jax.ShapeDtypeStruct((rows, D), BF16),
            jax.ShapeDtypeStruct((16, D), F32),
            jax.ShapeDtypeStruct((8, FF), F32),
        ],
        scratch_shapes=[pltpu.VMEM((tile, FF), F32)] * 3,
        compiler_params=params(dimension_semantics=("arbitrary",)),
        name="feed_forward",
    )(tokens, attended, cotangent, out_w, up_w, down_w, vecs, wide, scales)


def outer_kernel(left_ref, right_ref, out_ref, turned):
    @pl.when(pl.program_id(0) == 0)
    def _():
        turned[...] = left_ref[...].T

    out_ref[...] = nn(turned[...], right_ref[...]).astype(BF16)


def outer_product(left, right, panel):
    rows, width = left.shape
    cols = right.shape[1]
    return pl.pallas_call(
        outer_kernel,
        grid=(cols // panel,),
        in_specs=[
            pl.BlockSpec((rows, width), lambda i: (0, 0), pipeline_mode=pl.Buffered(1)),
            pl.BlockSpec((rows, panel), lambda i: (0, i)),
        ],
        out_specs=pl.BlockSpec((width, panel), lambda i: (0, i)),
        out_shape=jax.ShapeDtypeStruct((width, cols), BF16),
        scratch_shapes=[pltpu.VMEM((width, rows), BF16)],
        compiler_params=params(dimension_semantics=("arbitrary",)),
        name="weight_grad",
    )(left, right)


def attention_back_kernel(
    buckets, probs_ref, query_ref, keys_ref, values_ref, low_ref, normed_ref, x_ref, middle_ref,
    weight_q, weight_k, weight_v, vec_ref,
    input_grad_ref, grid_ref, weight_grad_ref, pair_ref, sums_ref,
    turned, first_in, proj_ref,
):
    count = x_ref.shape[0] // SLOT
    step = pl.program_id(0)

    @pl.when(step == 0)
    def _():
        turned[...] = normed_ref[...].T
        first_in[...] = jnp.zeros_like(first_in)

    grid_ref[...] = jnp.zeros_like(grid_ref)

    def one_sequence(s, carry):
        rows = pl.ds(pl.multiple_of(s * SLOT, SLOT), SLOT)
        query_grad, keys_grad, values_grad, scores_grads = attend_back(
            query_ref[0, rows, :], keys_ref[0, rows, :], values_ref[0, rows, :], low_ref[rows, :],
            [probs_ref[half, s] for half in range(2)],
        )
        small = jnp.where(buckets[s] == 0, 1.0, 0.0)
        for half in range(2):
            grid_ref[0, half] += scores_grads[half] * small
            grid_ref[1, half] += scores_grads[half] * (1.0 - small)
        proj_ref[rows, 0:128] = query_grad
        proj_ref[rows, 128:256] = keys_grad
        proj_ref[rows, 256:384] = values_grad
        return carry

    lax.fori_loop(0, count, one_sequence, 0)
    proj = proj_ref[...]
    weight_grad_ref[0] = nn(turned[...], proj).astype(BF16)
    pair_ref[0] = jnp.broadcast_to(column_sum(proj.astype(F32)), (8, 384))
    weights = jnp.concatenate([weight_q[...], weight_k[...], weight_v[...]], 1)
    first_in[...] += nt(proj, weights)

    @pl.when(step == PAIRS - 1)
    def _():
        sums_ref[...] = jnp.zeros_like(sums_ref)

        def one_block(b, carry):
            rows = pl.ds(pl.multiple_of(b * SLOT, SLOT), SLOT)
            unit, inverse = standardize(x_ref[rows, :].astype(F32))
            grad = first_in[rows, :]
            sums_ref[0:1, :] += column_sum(grad * unit)
            sums_ref[1:2, :] += column_sum(grad)
            back = norm_back(grad * vec_ref[0:1, :], unit, inverse)
            input_grad_ref[rows, :] = (middle_ref[rows, :] + back).astype(BF16)
            return carry

        lax.fori_loop(0, count, one_block, 0)


def attention_back(buckets, probs, qkv, attended_low, normed, tokens, middle_grad, weight, vecs):
    rows = tokens.shape[0]
    count = rows // SLOT

    def whole(shape):
        return pl.BlockSpec(shape, lambda i: (0,) * len(shape), pipeline_mode=pl.Buffered(1))

    def held(shape):
        return pl.BlockSpec(shape, lambda i: (0,) * len(shape))

    def panel(base):
        return pl.BlockSpec((1, rows, 128), lambda i: (base + i, 0, 0))

    def weight_panel(base):
        return pl.BlockSpec((D, 128), lambda i: (0, base + i))

    return pl.pallas_call(
        attention_back_kernel,
        grid=(PAIRS,),
        in_specs=[
            pl.BlockSpec(memory_space=pltpu.SMEM),
            pl.BlockSpec((2, count, SLOT, SLOT), lambda i: (i, 0, 0, 0)),
            panel(0), panel(PAIRS), panel(2 * PAIRS),
            pl.BlockSpec((rows, 128), lambda i: (0, i)),
            whole((rows, D)), whole((rows, D)), whole((rows, D)),
            weight_panel(0), weight_panel(PAIRS), weight_panel(2 * PAIRS),
            whole((8, D)),
        ],
        out_specs=[
            held((rows, D)),
            pl.BlockSpec((2, 2, SLOT, SLOT), lambda i: (0, i, 0, 0)),
            pl.BlockSpec((1, D, 384), lambda i: (i, 0, 0)),
            pl.BlockSpec((1, 8, 384), lambda i: (i, 0, 0)),
            held((8, D)),
        ],
        out_shape=[
            jax.ShapeDtypeStruct((rows, D), BF16),
            jax.ShapeDtypeStruct((2, HEADS, SLOT, SLOT), F32),
            jax.ShapeDtypeStruct((PAIRS, D, 384), BF16),
            jax.ShapeDtypeStruct((PAIRS, 8, 384), F32),
            jax.ShapeDtypeStruct((8, D), F32),
        ],
        scratch_shapes=[
            pltpu.VMEM((D, rows), BF16),
            pltpu.VMEM((rows, D), F32),
            pltpu.VMEM((rows, 384), BF16),
        ],
        compiler_params=params(dimension_semantics=("arbitrary",)),
        name="attention_backward",
    )(buckets, probs, qkv, qkv, qkv, attended_low, normed, tokens, middle_grad, weight, weight, weight, vecs)


MESH = pl.DeviceIdType.MESH
ANY = pl.ANY


class Place:
    def __init__(self):
        fsdp = lax.axis_index("fsdp")
        dp = lax.axis_index("dp")
        self.z, self.y, self.x, self.core = fsdp // 2, fsdp % 2, dp // 2, dp % 2

    def at(self, z=None, y=None, x=None, core=None):
        z = self.z if z is None else z
        y = self.y if y is None else y
        x = self.x if x is None else x
        core = self.core if core is None else core
        return (z * 2 + y, x * 2 + core)

    def greet(self):
        barrier = pltpu.get_barrier_semaphore()
        peers = [self.at(z=(self.z + k) % 4, y=self.y) for k in range(1, 4)]
        peers += [self.at(z=(self.z + k) % 4, y=1 - self.y) for k in range(4)]
        peers += [
            self.at(x=1 - self.x),
            self.at(core=1 - self.core),
            self.at(x=1 - self.x, core=1 - self.core),
        ]
        for peer in peers:
            pl.semaphore_signal(barrier, inc=1, device_id=peer, device_id_type=MESH)

    def meet(self):
        pl.semaphore_wait(pltpu.get_barrier_semaphore(), 10)


def remote(src, dst, send, recv, peer):
    return pltpu.make_async_remote_copy(
        src_ref=src, dst_ref=dst, send_sem=send, recv_sem=recv, device_id=peer, device_id_type=MESH
    )


def rows_of(first, size):
    return pl.ds(pl.multiple_of(first * size, size), size)


def chunk(kind, ref, r, d):
    if kind == "panel":
        return ref.at[d, rows_of(r, 96), :]
    if kind == "wide":
        return ref.at[rows_of(r, 96), rows_of(d, 768)]
    return ref.at[rows_of(d, 192), rows_of(r, 384)]


class Gather:
    def __init__(self, place, pieces, fulls, send, recv, local):
        self.place, self.pieces, self.fulls = place, pieces, fulls
        self.send, self.recv, self.local = send, recv, local
        self.made = {}

    def slot(self, w, z, y, x):
        return chunk(GATHER_KINDS[w], self.fulls[w], z * 2 + y, x * 2 + self.place.core)

    def copy(self, w, index, src, dst, peer):
        self.made[w, index] = remote(src, dst, self.send.at[w, index], self.recv.at[w, index], peer)
        return self.made[w, index]

    def sources(self, w, k):
        here = self.place
        over_x = (k + GATHER_TURN[w]) % 2 == 0
        near = (here.y, 1 - here.x) if over_x else (1 - here.y, here.x)
        far = (1 - here.y, here.x) if over_x else (here.y, 1 - here.x)
        upper = here.z // 2
        depth = here.z + upper * (3 - 2 * here.z)
        z = k - depth if k == 1 else k
        z = z + upper * (3 - 2 * z) if k else here.z
        return z, near, far

    def plan(self, w):
        here = self.place
        own = self.slot(w, here.z, here.y, here.x)
        self.made[w, "keep"] = pltpu.make_async_copy(self.pieces[w], own, self.local.at[w])
        sibling = here.at(core=1 - here.core)
        pair = here.at(z=here.z + 1 - 2 * (here.z % 2))
        across = here.at(z=3 - here.z)
        for k in range(4):
            z, near, far = self.sources(w, k)
            mine = self.slot(w, z, here.y, here.x)
            src = mine if k else self.pieces[w]
            if k == 0:
                self.copy(w, 1, src, mine, pair)
                self.copy(w, 2, src, mine, across)
            elif k == 1:
                self.copy(w, 3, src, mine, across)
            else:
                self.made[w, "on", k] = remote(
                    src, mine, self.send.at[w, 30 + k], self.recv.at[w, k], pair
                )
            self.copy(w, 4 + k, src, mine, here.at(y=near[0], x=near[1]))
            passed = self.slot(w, z, *near)
            self.copy(w, 8 + 2 * k, src, mine, here.at(y=far[0], x=far[1]))
            self.copy(w, 9 + 2 * k, passed, passed, here.at(y=far[0], x=far[1]))
            third = self.slot(w, z, *far)
            fourth = self.slot(w, z, 1 - here.y, 1 - here.x)
            for n, part in enumerate((src, passed, third, fourth)):
                dst = mine if n == 0 else part
                self.copy(w, 16 + 4 * k + n, part, dst, sibling)

    def when_middle(self, act):
        pl.when(self.place.z * (3 - self.place.z) > 0)(act)

    def begin(self, w, k=0):
        self.made[w, "keep"].start()
        self.made[w, 1].start()
        self.when_middle(lambda: self.made[w, 2].start())

    def relay(self, w, k):
        def on():
            self.made[w, k].wait_recv()
            (self.made[w, 3] if k == 1 else self.made[w, "on", k]).start()

        self.when_middle(on)

    def first(self, w, k):
        if k:
            pl.when(self.place.z * (3 - self.place.z) == 0)(self.made[w, k].wait_recv)
        self.made[w, 4 + k].start()
        self.made[w, 16 + 4 * k].start()

    def second(self, w, k):
        self.made[w, 4 + k].wait_recv()
        self.made[w, 8 + 2 * k].start()
        self.made[w, 9 + 2 * k].start()
        self.made[w, 17 + 4 * k].start()

    def third(self, w, k):
        for n in range(2):
            self.made[w, 8 + 2 * k + n].wait_recv()
            self.made[w, 18 + 4 * k + n].start()

    def finish(self, w):
        for n in range(16):
            self.made[w, 16 + n].wait_recv()
        for n in [1] + list(range(4, 32)):
            self.made[w, n].wait_send()

        def passed_on():
            for made in (self.made[w, 2], self.made[w, 3], self.made[w, "on", 2], self.made[w, "on", 3]):
                made.wait_send()

        self.when_middle(passed_on)
        self.made[w, "keep"].wait()


MIXED, UP, DOWN = range(3)
GATHER_TURN = (0, 1, 0)
GATHER_KINDS = ("wide", "wide", "turned")


GATHER_SCHEDULE = [
    [("begin", MIXED, 0), ("first", MIXED, 0), ("first", UP, 0)],
    [("first", DOWN, 0)],
    [("begin", DOWN, 0)],
    [],
    [],
    [("second", MIXED, 0), ("relay", MIXED, 1), ("first", MIXED, 1), ("relay", MIXED, 2), ("second", UP, 0)],
    [
        ("begin", UP, 0),
        ("relay", DOWN, 1),
        ("first", DOWN, 1),
        ("first", MIXED, 2),
        ("relay", MIXED, 3),
        ("relay", UP, 1),
        ("third", MIXED, 0),
        ("first", UP, 1),
        ("relay", UP, 2),
        ("second", MIXED, 1),
        ("first", MIXED, 3),
        ("second", MIXED, 2),
        ("relay", DOWN, 3),
        ("first", UP, 2),
        ("second", UP, 1),
        ("relay", UP, 3),
        ("second", MIXED, 3),
        ("first", DOWN, 3),
        ("first", UP, 3),
        ("third", MIXED, 1),
        ("third", MIXED, 2),
        ("second", UP, 2),
        ("third", MIXED, 3),
    ],
    [],
    [],
    [("third", UP, 1)],
    [("second", UP, 3), ("relay", DOWN, 2), ("second", DOWN, 1)],
    [],
    [("third", UP, 0), ("third", UP, 2), ("second", DOWN, 0)],
    [],
    [("first", DOWN, 2)],
    [],
    [("third", UP, 3), ("second", DOWN, 3)],
    [("third", DOWN, 1)],
    [],
    [("second", DOWN, 2)],
    [("third", DOWN, 0), ("third", DOWN, 3), ("third", DOWN, 2)],
]


def lined(ref, row, width):
    return jnp.concatenate([ref[f, row : row + 1, :width].astype(F32) for f in range(8)], 1)


def forward_kernel(
    lengths, buckets, x_ref, cot_ref, qkv_p, out_p, up_p, down_t, table_p, head_scale, *refs,
):
    vectors = refs[:12]
    (
    normed_ref, qkv_ref, probs_ref, result_ref, mixed_ref, second_ref, act_ref, low_ref, branch_ref,
    middle_grad_ref, attended_low_ref, sums_ref, wide_sums_ref, vec_ref, qkv_out,
    mixed_p, scale_ref, vec_wide, vec_p, qkv_w, up_w, down_w, vec_f, out_w, bias_ref, wide_ref, qkv_bias_ref, table_ref,
    wall_small, wall_large, visual, attended_ref, gelu_ref, slope_ref, grad_ref,
    send, recv, local, small_send, small_recv, small_local, qkv_sem,
    ) = refs[12:]
    step = pl.program_id(0)
    count = pl.num_programs(0) // 2
    place = Place()
    gather = Gather(place, (mixed_p, up_p, down_t), (qkv_w, up_w, down_w), send, recv, local)
    for w in range(3):
        gather.plan(w)
    f = place.z * 2 + place.y
    small = [pltpu.make_async_copy(vec_p, vec_f.at[f], small_local)]
    for k in range(1, 8):
        peer = (f + k) % 8
        small.append(
            remote(
                vec_p, vec_f.at[f], small_send.at[k], small_recv.at[k],
                place.at(z=peer // 2, y=peer % 2),
            )
        )
    keep_qkv = pltpu.make_async_copy(qkv_w, qkv_out, qkv_sem)

    def follow(point):
        for name, w, k in GATHER_SCHEDULE[point]:
            getattr(gather, name)(w, k)

    @pl.when(step == 0)
    def _():
        place.greet()
        vec_wide[...] = jnp.zeros_like(vec_wide)
        for n, vector in enumerate(vectors):
            size = vector.shape[0]
            vec_wide[n : n + 1, :size] = vector[...].astype(F32).reshape(1, size)
        vec_wide[16 : 16 + HEADS, :192] = table_p[...].astype(F32)
        vec_wide[12:13, :HEADS] = head_scale[...].astype(F32).reshape(1, HEADS)
        vec_p[...] = vec_wide[...].astype(BF16)
        head = lax.broadcasted_iota(jnp.int32, (128, D), 0)
        spread = (head == lax.broadcasted_iota(jnp.int32, (128, D), 1) // HEAD_DIM).astype(F32)
        scale_ref[...] = nn(vec_p[...], jnp.concatenate([spread, jnp.zeros((256, D), F32)], 0).astype(BF16))[8:16]
        mixed_p[:, :576] = qkv_p[...]
        mixed_p[:, 576:] = out_p[...]
        place.meet()
        for made in small:
            made.start()
        follow(0)
        for made in small:
            made.wait()
        for n in range(8):
            vec_ref[n : n + 1, :] = lined(vec_f, n, 96)
        for n in range(3):
            wide_ref[n : n + 1, :] = lined(vec_f, 8 + n, 384)
        pair = lined(vec_f, 11, 192)
        qkv_bias_ref[0:1, :] = jnp.concatenate([pair[:, :D], jnp.zeros((1, D), F32), pair[:, D:]], 1)
        lane = lax.broadcasted_iota(jnp.int32, (1, 3 * D), 1)
        qkv_bias_ref[1:2, :] = jnp.where(lane < D, HEAD_DIM ** (-0.5), 1.0)
        table_ref[...] = jnp.concatenate([vec_f[n, 16:32, :192].astype(F32) for n in range(8)], 1)
        bias_walls(table_ref, wall_small, wall_large, visual)
        heads = functools.partial(bias_head, table_ref, bias_ref, wall_small, wall_large, visual)
        for n, last in enumerate((2, 4, 6, 9, HEADS)):
            follow(1 + n)
            lax.fori_loop((0, 2, 4, 6, 9)[n], last, heads, 0)
        follow(6)
        gather.finish(MIXED)
        keep_qkv.start()
        sums_ref[...] = jnp.zeros_like(sums_ref)
        wide_sums_ref[...] = jnp.zeros_like(wide_sums_ref)

    def progress(spot):
        for s in range(count):
            if GATHER_SCHEDULE[7 + 3 * s + spot]:
                pl.when(step == s)(functools.partial(follow, 7 + 3 * s + spot))

    @pl.when(step < count)
    def _():
        rows = pl.ds(pl.multiple_of(step * SLOT, SLOT), SLOT)
        progress(0)
        unit, inverse = standardize(x_ref[...].astype(F32))
        normed = (unit * vec_ref[0:1, :] + vec_ref[1:2, :]).astype(BF16)
        normed_ref[...] = normed
        for d in range(4):
            cols = slice(576 * d, 576 * d + 576)
            out = (nn(normed, qkv_w[:, 768 * d : 768 * d + 576]) + qkv_bias_ref[0:1, cols]) * qkv_bias_ref[1:2, cols]
            qkv_ref[:, cols] = out.astype(BF16)
        live = lax.broadcasted_iota(jnp.int32, (SLOT, SLOT), 1) < lengths[step]
        bucket = buckets[step]
        for pair in range(PAIRS):
            if pair % 3 == 0:
                progress(1 + pair // 3)
            query = qkv_ref[:, 128 * pair : 128 * pair + 128]
            keys = qkv_ref[:, D + 128 * pair : D + 128 * pair + 128]
            values = qkv_ref[:, 2 * D + 128 * pair : 2 * D + 128 * pair + 128]
            bias = [bias_ref[bucket, 2 * pair + half] for half in range(2)]
            probs, out = attend(query, keys, values, bias, live)
            for half in range(2):
                probs_ref[2 * pair + half, 0] = probs[half]
            attended_ref[rows, 128 * pair : 128 * pair + 128] = out

    @pl.when(step == count)
    def _():
        follow(7 + 3 * count)
        gather.finish(UP)
        for d in range(4):
            out_w[:, 192 * d : 192 * d + 192] = qkv_w[:, 768 * d + 576 : 768 * d + 768]

    @pl.when(step >= count)
    def _():
        rows = pl.ds(pl.multiple_of((step - count) * SLOT, SLOT), SLOT)

        def wait_down():
            @pl.when(step == count)
            def _():
                follow(8 + 3 * count)
                gather.finish(DOWN)

        feed_block(
            x_ref, attended_ref.at[rows, :], cot_ref, out_w, up_w, down_w, vec_ref, wide_ref,
            scale_ref.at[4:5, :],
            result_ref, mixed_ref, second_ref, act_ref, low_ref, branch_ref, middle_grad_ref,
            attended_low_ref, sums_ref, wide_sums_ref, gelu_ref, slope_ref, grad_ref, wait_down,
        )

    @pl.when(step == 2 * count - 1)
    def _():
        keep_qkv.wait()


def forward(lengths, buckets, tokens, cotangent, qkv_p, out_p, up_p, down_p, table_p, head_scale, vectors):
    rows = tokens.shape[0]
    count = rows // SLOT
    smem = pl.BlockSpec(memory_space=pltpu.SMEM)

    def early(shape):
        return pl.BlockSpec(shape, lambda i: (jnp.minimum(i, count - 1),) + (0,) * (len(shape) - 1))

    def late(shape):
        return pl.BlockSpec(shape, lambda i: (jnp.maximum(i - count, 0),) + (0,) * (len(shape) - 1))

    def held(shape):
        return pl.BlockSpec(shape, lambda i: (0,) * len(shape))

    block = (SLOT, D)
    wide = (SLOT, FF)
    return pl.pallas_call(
        forward_kernel,
        grid=(2 * count,),
        in_specs=[
            smem, smem, pl.BlockSpec(block, lambda i: (i % count, 0)), late(block),
            held((96, 576)), held((96, 192)), pl.BlockSpec(memory_space=ANY),
            pl.BlockSpec(memory_space=ANY), held((HEADS, 192)), held((HEADS,)),
        ]
        + [held(vector.shape) for vector in vectors],
        out_specs=[
            early(block), early((SLOT, 3 * D)),
            pl.BlockSpec((HEADS, 1, SLOT, SLOT), lambda i: (0, jnp.minimum(i, count - 1), 0, 0)),
            late(block), late(block), late(block), late(wide), late(wide), late(block), late(block),
            late(block), held((16, D)), held((8, FF)), held((8, D)), pl.BlockSpec(memory_space=ANY),
        ],
        out_shape=[
            jax.ShapeDtypeStruct((rows, D), BF16),
            jax.ShapeDtypeStruct((rows, 3 * D), BF16),
            jax.ShapeDtypeStruct((HEADS, count, SLOT, SLOT), BF16),
            jax.ShapeDtypeStruct((rows, D), BF16),
            jax.ShapeDtypeStruct((rows, D), BF16),
            jax.ShapeDtypeStruct((rows, D), BF16),
            jax.ShapeDtypeStruct((rows, FF), BF16),
            jax.ShapeDtypeStruct((rows, FF), BF16),
            jax.ShapeDtypeStruct((rows, D), BF16),
            jax.ShapeDtypeStruct((rows, D), F32),
            jax.ShapeDtypeStruct((rows, D), BF16),
            jax.ShapeDtypeStruct((16, D), F32),
            jax.ShapeDtypeStruct((8, FF), F32),
            jax.ShapeDtypeStruct((8, D), F32),
            jax.ShapeDtypeStruct((D, FF), BF16),
        ],
        scratch_shapes=[
            pltpu.VMEM((96, D), BF16),
            pltpu.VMEM((8, D), F32),
            pltpu.VMEM((32, 384), F32),
            pltpu.VMEM((32, 384), BF16),
            pltpu.VMEM((D, FF), BF16),
            pltpu.VMEM((D, FF), BF16),
            pltpu.VMEM((D, FF), BF16),
            pltpu.VMEM((8, 32, 384), BF16),
            pltpu.VMEM((D, D), BF16),
            pltpu.VMEM((2, HEADS, SLOT, SLOT), BF16),
            pltpu.VMEM((8, FF), F32),
            pltpu.VMEM((8, 3 * D), F32),
            pltpu.VMEM((16, TABLE), F32),
            pltpu.VMEM((2, 128, 128), F32),
            pltpu.VMEM((4, 256, 128), F32),
            pltpu.VMEM((SLOT, SLOT), F32),
            pltpu.VMEM((rows, D), F32),
            pltpu.VMEM(wide, F32),
            pltpu.VMEM(wide, F32),
            pltpu.VMEM(wide, F32),
            pltpu.SemaphoreType.DMA((3, 34)),
            pltpu.SemaphoreType.DMA((3, 32)),
            pltpu.SemaphoreType.DMA((3,)),
            pltpu.SemaphoreType.DMA((8,)),
            pltpu.SemaphoreType.DMA((8,)),
            pltpu.SemaphoreType.DMA,
            pltpu.SemaphoreType.DMA,
        ],
        compiler_params=params(
            collective_id=1, has_side_effects=True, dimension_semantics=("arbitrary",)
        ),
        name="forward",
    )(lengths, buckets, tokens, cotangent, qkv_p, out_p, up_p, down_p, table_p, head_scale, *vectors)


ORDER = (1, 2, 3, 0)


class Scatter:
    def __init__(self, place, kind, grad, out, buffers):
        self.place, self.kind, self.grad, self.out = place, kind, grad, out
        self.cores, self.over_x, self.over_y, self.far, self.quarter, self.send, self.recv = buffers
        self.made = {}
        here = place
        for k in range(4):
            z = (here.z + k) % 4
            mine = 2 * here.x + here.core
            other = 2 * (1 - here.x) + here.core
            for x in range(2):
                self.copy(
                    k, x, self.block(2 * x + 1 - here.core, z), self.from_core(k, x),
                    here.at(core=1 - here.core),
                )
            if k % 2 == 0:
                self.copy(k, 2, self.block(other, z), self.over_x.at[k // 2], here.at(x=1 - here.x))
                self.copy(
                    k, 4, self.part(mine, z, 1 - here.y), self.far.at[k], here.at(y=1 - here.y)
                )
            else:
                for x in range(2):
                    self.copy(
                        k, 2 + x, self.part(2 * x + here.core, z, 1 - here.y),
                        self.over_y.at[k // 2, x], here.at(y=1 - here.y),
                    )
                self.copy(k, 4, self.part(other, z, here.y), self.far.at[k], here.at(x=1 - here.x))
            if k:
                self.copy(k, 5, self.part(mine, z, here.y), self.quarter.at[k - 1], here.at(z=z))

    def from_core(self, k, x):
        return self.cores.at[k, x, :, : self.over_x.shape[-1]]

    def block(self, d, z):
        if self.kind == "panel":
            return self.grad.at[d, rows_of(z, 192), :]
        if self.kind == "wide":
            return self.grad.at[rows_of(z, 192), rows_of(d, 768)]
        return self.grad.at[rows_of(d, 192), rows_of(z, 768)]

    def part(self, d, z, y):
        if self.kind == "panel":
            return self.grad.at[d, rows_of(2 * z + y, 96), :]
        if self.kind == "wide":
            return self.grad.at[rows_of(2 * z + y, 96), rows_of(d, 768)]
        return self.grad.at[rows_of(d, 192), rows_of(2 * z + y, 384)]

    def copy(self, k, index, src, dst, peer):
        self.made[k, index] = remote(src, dst, self.send.at[k, index], self.recv.at[k, index], peer)

    def add(self, target, source):
        def some(n, carry):
            at = rows_of(n, 16)
            target[at, :] = target[at, :] + source[at, :]
            return carry

        lax.fori_loop(0, target.shape[0] // 16, some, 0)

    def core(self, k):
        for x in range(2):
            self.made[k, x].start()

    def plane(self, k):
        here = self.place
        z = (here.z + k) % 4
        for x in range(2):
            self.made[k, x].wait_recv()
            self.add(self.block(2 * x + here.core, z), self.from_core(k, x))
        self.made[k, 2].start()
        if k % 2:
            self.made[k, 3].start()

    def turn(self, k):
        here = self.place
        z = (here.z + k) % 4
        self.made[k, 2].wait_recv()
        if k % 2 == 0:
            self.add(self.block(2 * here.x + here.core, z), self.over_x.at[k // 2])
        else:
            self.made[k, 3].wait_recv()
            for x in range(2):
                self.add(self.part(2 * x + here.core, z, here.y), self.over_y.at[k // 2, x])
        self.made[k, 4].start()

    def line(self, k):
        here = self.place
        self.made[k, 4].wait_recv()
        self.add(self.part(2 * here.x + here.core, (here.z + k) % 4, here.y), self.far.at[k])
        if k:
            self.made[k, 5].start()

    def end(self):
        here = self.place
        for k in range(1, 4):
            self.made[k, 5].wait_recv()
        total = self.part(2 * here.x + here.core, here.z, here.y)[...].astype(F32)
        for k in range(3):
            total = total + self.quarter[k].astype(F32)
        self.out[...] = total[:, : self.out.shape[1]]
        for made in self.made.values():
            made.wait_send()


def scatter_scratch(kind, width):
    half = (192, width // 2) if kind == "turned" else (96, width)
    return [
        pltpu.VMEM((4, 2, 192, width), BF16),
        pltpu.VMEM((2, 192, width), BF16),
        pltpu.VMEM((2, 2) + half, BF16),
        pltpu.VMEM((4,) + half, BF16),
        pltpu.VMEM((3,) + half, BF16),
        pltpu.SemaphoreType.DMA((4, 6)),
        pltpu.SemaphoreType.DMA((4, 6)),
    ]


def pack_sums(sums_ref, first_ref, wide_ref, pair, table_ref, packed):
    low = first_ref[0:2, :]
    narrow = sums_ref[...]
    group = lax.broadcasted_iota(jnp.int32, (D, 128), 0) // HEAD_DIM
    pick = (group == lax.broadcasted_iota(jnp.int32, (D, 128), 1)).astype(F32).astype(BF16)
    high, rest = split_low(narrow[8:16])
    heads = (nn(high, pick) + nn(rest, pick))[0:1]
    heads = jnp.concatenate([heads, jnp.zeros((1, 64), F32)], 1)
    for f in range(8):
        at = slice(96 * f, 96 * f + 96)
        packed[f, 0:1, :] = jnp.concatenate(
            [low[0:1, at], low[1:2, at], narrow[2:3, at], narrow[3:4, at]], 1
        )
        packed[f, 1:2, :] = jnp.concatenate([narrow[n : n + 1, at] for n in range(4, 8)], 1)
        packed[f, 2:5, :] = wide_ref[0:3, 384 * f : 384 * f + 384]
        at = slice(192 * f, 192 * f + 192)
        packed[f, 5:6, :] = jnp.concatenate([pair[:, at], heads], 1)
        for n in range(PAIRS):
            packed[f, 6 + n : 7 + n, :] = jnp.concatenate(
                [table_ref[2 * n : 2 * n + 1, at], table_ref[2 * n + 1 : 2 * n + 2, at]], 1
            )
        packed[f, 12:16, :] = jnp.zeros((4, 384), F32)


class SmallSums:
    def __init__(self, place, packed, rows, peers, sems):
        self.place, self.packed, self.rows, self.peers = place, packed, rows, peers
        self.send, self.recv = sems

    def begin(self):
        here = self.place
        f = here.z * 2 + here.y
        self.made = []
        for k in range(1, 8):
            to = (f + k) % 8
            made = remote(
                self.packed.at[to], self.rows.at[k - 1], self.send.at[k], self.recv.at[k],
                here.at(z=to // 2, y=to % 2),
            )
            made.start()
            self.made.append(made)

    def cross(self):
        here = self.place
        f = here.z * 2 + here.y
        for made in self.made:
            made.wait()
        total = self.packed[f]
        for k in range(7):
            total = total + self.rows[k]
        self.peers[0] = total
        d = here.x * 2 + here.core
        self.made = []
        for k in range(1, 4):
            to = (d + k) % 4
            made = remote(
                self.peers.at[0], self.peers.at[k], self.send.at[7 + k], self.recv.at[7 + k],
                here.at(x=to // 2, core=to % 2),
            )
            made.start()
            self.made.append(made)

    def end(self):
        for made in self.made:
            made.wait()
        return (self.peers[0] + self.peers[1]) + (self.peers[2] + self.peers[3])


BACK_SCHEDULE = {
    3: [("down", "plane", 0)],
    4: [("down", "plane", 1), ("down", "plane", 2)],
    5: [("down", "plane", 3)],
    6: [("down", "turn", 0)],
    7: [("down", "turn", 1)],
    8: [("down", "turn", 2)],
    10: [("down", "turn", 3), ("down", "line", 1), ("up", "plane", 0), ("up", "plane", 1), ("up", "plane", 2)],
    11: [
        ("down", "line", 0),
        ("up", "plane", 3),
        ("out", "plane", 0),
        ("out", "plane", 1),
        ("out", "plane", 2),
        ("down", "line", 2),
        ("out", "plane", 3),
    ],
    12: [("down", "line", 3)],
    14: [("up", "turn", 0), ("up", "turn", 1)],
    16: [("up", "turn", 2), ("up", "turn", 3)],
    17: [("out", "turn", 0), ("out", "turn", 1), ("out", "turn", 3)],
    18: [("up", "line", 0), ("out", "turn", 2), ("up", "line", 1)],
    19: [("up", "line", 2), ("up", "line", 3), ("out", "line", 0)],
    20: [("out", "line", 1), ("out", "line", 2), ("out", "line", 3), ("qkv", "plane", 0), ("qkv", "plane", 1)],
    21: [("qkv", "plane", 2), ("qkv", "plane", 3)],
}
BACK_DRAIN = [
    ("qkv", "turn", 0),
    ("qkv", "turn", 1),
    ("qkv", "turn", 2),
    ("qkv", "turn", 3),
    ("qkv", "line", 1),
    ("qkv", "line", 0),
    ("qkv", "line", 3),
    ("qkv", "line", 2),
]


def backward_kernel(
    buckets, cot_hbm, act_ref, second_hbm, low_ref, mixed_hbm, branch_hbm, normed_hbm,
    probs_ref, query_ref, keys_ref, values_ref, attended_low_ref, vec_ref, sums_ref, wide_ref,
    x_hbm, middle_hbm, weight_hbm,
    input_grad_ref, down_out, up_out, out_out, qkv_out, total_ref,
    left, turned, middle_ref, first_in, proj, grid_ref, down_ref, up_ref, out_ref, qkv_ref,
    table_ref, first_ref, wall_small, wall_large, packed, gathered, peers, small_send, small_recv,
    loading, middle_sem, *buffers,
):
    step = pl.program_id(0)
    place = Place()
    parts = {
        "down": Scatter(place, "turned", down_ref, down_out, buffers[0:7]),
        "up": Scatter(place, "wide", up_ref, up_out, buffers[7:14]),
        "out": Scatter(place, "panel", out_ref, out_out, buffers[14:21]),
        "qkv": Scatter(place, "panel", qkv_ref, qkv_out, buffers[0:1] + buffers[21:27]),
    }
    small = SmallSums(place, packed, gathered, peers, (small_send, small_recv))
    count = query_ref.shape[0] // SLOT

    def load(n, src, dst):
        return pltpu.make_async_copy(src, dst, loading.at[n])

    load_cot = load(0, cot_hbm, left.at[0])
    load_second = load(1, second_hbm, left.at[1])
    load_mixed = load(2, mixed_hbm, left.at[0])
    load_branch = load(3, branch_hbm, left.at[1])
    load_normed = load(4, normed_hbm, left.at[0])
    load_x = load(5, x_hbm, left.at[1])

    def load_middle(b):
        n = b % 2
        return pltpu.make_async_copy(middle_hbm.at[rows_of(b, SLOT), :], middle_ref.at[n], middle_sem.at[n])

    load_weight = load(7, weight_hbm, down_ref)

    def progress(at):
        for name, event, n in BACK_SCHEDULE.get(at, []):
            getattr(parts[name], event)(ORDER[n])

    def down_panel():
        z = (place.z + 1 + step) % 4
        down_ref[:, rows_of(z, 768)] = nn(turned[...], act_ref[...]).astype(BF16)

    @pl.when(step == 0)
    def _():
        place.greet()
        load_cot.start()
        load_second.start()
        place.meet()

    for at in BACK_SCHEDULE:
        if at < 19:
            pl.when(step == at)(functools.partial(progress, at))

    @pl.when(step < 4)
    def _():
        @pl.when(step == 0)
        def _():
            load_cot.wait()
            turned[...] = left[0].T
            load_mixed.start()

        down_panel()
        for n in range(4):
            pl.when(step == n)(functools.partial(parts["down"].core, ORDER[n]))

    @pl.when((step >= 4) & (step < 8))
    def _():
        @pl.when(step == 4)
        def _():
            load_second.wait()
            turned[...] = left[1].T
            load_branch.start()

        up_ref[:, rows_of(step - 4, 768)] = nn(turned[...], low_ref[...]).astype(BF16)

        @pl.when(step == 7)
        def _():
            for k in ORDER:
                parts["up"].core(k)

    @pl.when(step == 8)
    def _():
        load_mixed.wait()
        turned[...] = left[0].T
        load_normed.start()
        load_branch.wait()
        for d in range(4):
            out_ref[d] = nn(turned[...], left[1, :, 192 * d : 192 * d + 192]).astype(BF16)
        for k in ORDER:
            parts["out"].core(k)
        load_x.start()
        table_grad_start(table_ref, wall_small, wall_large)

    @pl.when((step >= 9) & (step < 15))
    def _():
        pair = step - 9
        cols = rows_of(pair, 128)
        for s in range(count):
            rows = slice(s * SLOT, s * SLOT + SLOT)
            query_grad, keys_grad, values_grad, scores_grads = attend_back(
                query_ref[rows, :], keys_ref[rows, :], values_ref[rows, :], attended_low_ref[rows, :],
                [probs_ref[half, s] for half in range(2)],
            )
            proj[0, rows, cols] = query_grad
            proj[1, rows, cols] = keys_grad
            proj[2, rows, cols] = values_grad
            chosen = jnp.where(buckets[s] == 0, 1.0, 0.0)
            for half in range(2):
                if s == 0:
                    grid_ref[0, half] = scores_grads[half] * chosen
                    grid_ref[1, half] = scores_grads[half] * (1.0 - chosen)
                else:
                    grid_ref[0, half] += scores_grads[half] * chosen
                    grid_ref[1, half] += scores_grads[half] * (1.0 - chosen)
        for half in range(2):
            table_grad_head(grid_ref, table_ref, wall_small, wall_large, 2 * pair + half, half)

    def lay_panel(d):
        def lay(pieces):
            at = 0
            for n, first, last in pieces:
                left[0, :, at : at + last - first] = proj[n, :, first:last]
                at += last - first

        cuts = (
            [(0, 0, 576)], [(0, 576, 768), (1, 0, 384)], [(1, 384, 768), (2, 0, 192)], [(2, 192, 768)],
        )
        for n, pieces in enumerate(cuts):
            pl.when(d == n)(functools.partial(lay, pieces))

    @pl.when((step >= 15) & (step < 19))
    def _():
        @pl.when(step == 15)
        def _():
            parts["down"].end()
            load_weight.start()
            load_normed.wait()
            turned[...] = left[0].T
            first_in[...] = jnp.zeros_like(first_in)

        d = step - 15
        lay_panel(d)
        grad = nn(turned[...], left[0, :, :576]).astype(BF16)
        qkv_ref[d] = jnp.concatenate([grad, jnp.zeros((D, 64), BF16)], 1)

        @pl.when(step == 15)
        def _():
            load_weight.wait()

        @pl.when(step == 18)
        def _():
            for k in ORDER:
                parts["qkv"].core(k)

        first_in[...] += nt(left[0, :, :576], down_ref[:, pl.ds(pl.multiple_of(768 * d, 768), 576)])

    @pl.when(step == 19)
    def _():
        progress(19)
        load_middle(0).start()
        load_x.wait()
        first_ref[...] = jnp.zeros_like(first_ref)

        def one_block(b, carry):
            rows = pl.ds(pl.multiple_of(b * SLOT, SLOT), SLOT)
            unit, inverse = standardize(left[1, rows, :].astype(F32))
            grad = first_in[rows, :]
            first_ref[0:1, :] += column_sum(grad * unit)
            first_ref[1:2, :] += column_sum(grad)
            back = norm_back(grad * vec_ref[0:1, :], unit, inverse)

            @pl.when(b + 1 < count)
            def _():
                load_middle(b + 1).start()

            load_middle(b).wait()
            input_grad_ref[rows, :] = (middle_ref[b % 2] + back).astype(BF16)
            return carry

        lax.fori_loop(0, count, one_block, 0)
        progress(20)
        table_grad_end(table_ref, wall_small, wall_large)
        pair = jnp.concatenate([tall_sum(proj.at[0]), tall_sum(proj.at[2])], 1)
        progress(21)
        pack_sums(sums_ref, first_ref, wide_ref, pair, table_ref, packed)
        small.begin()
        for n, (name, event, k) in enumerate(BACK_DRAIN):
            if n == len(BACK_DRAIN) // 2:
                small.cross()
            getattr(parts[name], event)(ORDER[k])
        parts["up"].end()
        parts["out"].end()
        total_ref[...] = small.end()
        parts["qkv"].end()


def backward(
    buckets, cotangent, act, second, low, mixed, branch, normed, probs, qkv, attended_low, vecs,
    sums, wide, tokens, middle_grad, weight,
):
    rows = cotangent.shape[0]
    count = rows // SLOT
    any_space = pl.BlockSpec(memory_space=ANY)

    def held(shape):
        return pl.BlockSpec(shape, lambda i: (0,) * len(shape))

    def pair(i):
        return jnp.clip(i - 9, 0, PAIRS - 1)

    def panel(base):
        return pl.BlockSpec((rows, 128), lambda i: (0, base + pair(i)))

    def act_panel(i):
        return (0, (lax.axis_index("fsdp") // 2 + 1 + jnp.minimum(i, 3)) % 4)

    outs = [(192, 384), (96, 768), (96, 192), (96, 576), (16, 384)]
    return pl.pallas_call(
        backward_kernel,
        grid=(20,),
        in_specs=[
            pl.BlockSpec(memory_space=pltpu.SMEM),
            any_space,
            pl.BlockSpec((rows, D), act_panel),
            any_space,
            pl.BlockSpec((rows, D), lambda i: (0, jnp.clip(i - 4, 0, 3))),
            any_space, any_space, any_space,
            pl.BlockSpec((2, count, SLOT, SLOT), lambda i: (pair(i), 0, 0, 0)),
            panel(0), panel(PAIRS), panel(2 * PAIRS), panel(0),
            held((8, D)), held((16, D)), held((8, FF)),
            any_space, any_space, any_space,
        ],
        out_specs=[held((rows, D))] + [held(shape) for shape in outs],
        out_shape=[jax.ShapeDtypeStruct((rows, D), BF16)]
        + [jax.ShapeDtypeStruct(shape, F32) for shape in outs],
        scratch_shapes=[
            pltpu.VMEM((2, rows, D), BF16),
            pltpu.VMEM((D, rows), BF16),
            pltpu.VMEM((2, SLOT, D), F32),
            pltpu.VMEM((rows, D), F32),
            pltpu.VMEM((3, rows, D), BF16),
            pltpu.VMEM((2, 2, SLOT, SLOT), F32),
            pltpu.VMEM((D, FF), BF16),
            pltpu.VMEM((D, FF), BF16),
            pltpu.VMEM((4, D, 192), BF16),
            pltpu.VMEM((4, D, 640), BF16),
            pltpu.VMEM((16, TABLE), F32),
            pltpu.VMEM((8, D), F32),
            pltpu.VMEM((2, 128, 128), F32),
            pltpu.VMEM((4, 256, 128), F32),
            pltpu.VMEM((8, 16, 384), F32),
            pltpu.VMEM((7, 16, 384), F32),
            pltpu.VMEM((4, 16, 384), F32),
            pltpu.SemaphoreType.DMA((11,)),
            pltpu.SemaphoreType.DMA((11,)),
            pltpu.SemaphoreType.DMA((8,)),
            pltpu.SemaphoreType.DMA((2,)),
        ]
        + scatter_scratch("turned", 768) + scatter_scratch("wide", 768)
        + scatter_scratch("panel", 192) + scatter_scratch("panel", 640)[1:],
        compiler_params=pltpu.CompilerParams(
            collective_id=2, has_side_effects=True, dimension_semantics=("arbitrary",),
            vmem_limit_bytes=BACK_LIMIT,
        ),
        name="backward",
    )(
        buckets, cotangent, act, second, low, mixed, branch, normed, probs, qkv, qkv, qkv,
        attended_low, vecs, sums, wide, tokens, middle_grad, weight,
    )


def emit_kernel(count, total_ref, *refs):
    sources = refs[:count]
    targets = refs[count : 2 * count]
    small = refs[2 * count : 2 * count + 14]
    held = refs[2 * count + 14 : -2]
    into, out = refs[-2:]
    loads = [
        pltpu.make_async_copy(src, dst, into.at[n]) for n, (src, dst) in enumerate(zip(sources, held))
    ]
    made = [
        pltpu.make_async_copy(src, dst, out.at[n]) for n, (src, dst) in enumerate(zip(held, targets))
    ]
    for each in loads:
        each.start()
    for load, each in zip(loads, made):
        load.wait()
        each.start()
    total = total_ref[...]
    for n in range(8):
        at = 96 * (n % 4)
        small[n][...] = total[n // 4 : n // 4 + 1, at : at + 96].reshape(96)
    for n in range(3):
        small[8 + n][...] = total[2 + n : 3 + n, :].reshape(384)
    small[11][...] = total[5:6, 0:192].reshape(192)
    small[12][...] = total[5:6, 192:204].reshape(HEADS)
    for n in range(PAIRS):
        small[13][2 * n : 2 * n + 1, :] = total[6 + n : 7 + n, 0:192]
        small[13][2 * n + 1 : 2 * n + 2, :] = total[6 + n : 7 + n, 192:384]
    for each in made:
        each.wait()


def emit(total, *large):
    vmem = pl.BlockSpec(memory_space=pltpu.VMEM)
    any_space = pl.BlockSpec(memory_space=ANY)
    small = [(96,)] * 8 + [(384,)] * 3 + [(192,), (HEADS,), (HEADS, 192)]
    return pl.pallas_call(
        functools.partial(emit_kernel, len(large)),
        in_specs=[vmem] + [any_space] * len(large),
        out_specs=[any_space] * len(large) + [vmem] * len(small),
        out_shape=[jax.ShapeDtypeStruct(part.shape, part.dtype) for part in large]
        + [jax.ShapeDtypeStruct(shape, F32) for shape in small],
        scratch_shapes=[pltpu.VMEM(part.shape, part.dtype) for part in large]
        + [pltpu.SemaphoreType.DMA((len(large),))] * 2,
        compiler_params=params(),
        name="emit",
    )(total, *large)


def gather_matrix(piece):
    rows = lax.all_gather(piece, "fsdp", axis=0, tiled=True)
    return lax.all_gather(rows, "dp", axis=1, tiled=True)


def scatter_matrix(grad):
    part = lax.psum_scatter(grad, "dp", scatter_dimension=1, tiled=True).astype(F32)
    return lax.psum_scatter(part, "fsdp", scatter_dimension=0, tiled=True)


def body(
    tokens, cotangent, lengths, buckets, qkv_weight, query_value_bias, out_weight, out_bias,
    up_weight, up_bias, down_weight, down_bias, first_gain, first_shift, mix_gain, mix_shift,
    second_gain, second_shift, hidden_gain, hidden_shift, head_scale, position_table,
):
    parts = lax.axis_size("fsdp")
    own_kernels = (parts, lax.axis_size("dp")) == (8, 4)
    narrow = [
        first_gain, first_shift, mix_gain, mix_shift, second_gain, second_shift, out_bias, down_bias,
    ]
    wide = [up_bias, hidden_gain, hidden_shift]
    a = D // parts
    b = FF // parts
    if own_kernels:
        (
            normed, qkv, probs, result, mixed, second, act, low, branch, middle_grad, attended_low,
            sums, wide_sums, vecs, qkv_full,
        ) = forward(
            lengths, buckets, tokens, cotangent, qkv_weight, out_weight, up_weight, down_weight.T,
            position_table.T, head_scale, narrow + wide + [query_value_bias],
        )
        input_grad, down_owned, up_owned, out_owned, qkv_owned, total = backward(
            buckets, cotangent, act, second, low, mixed, branch, normed, probs, qkv, attended_low,
            vecs, sums, wide_sums, tokens, middle_grad, qkv_full,
        )
        result, input_grad, qkv_owned, out_owned, up_owned, down_owned, *small = emit(
            total, result, input_grad, qkv_owned, out_owned, up_owned, down_owned
        )
        down_owned = down_owned.T
        narrow_owned = small[:8]
        wide_owned = small[8:11]
        pair_owned, scale_grad, table_owned = small[11], small[12], small[13].T
    else:
        packed = jnp.concatenate(
            [jnp.pad(jnp.stack(narrow), ((0, 0), (0, b - a))), jnp.stack(wide)]
            + [jnp.pad(query_value_bias, (0, b - 2 * a))[None], jnp.zeros((4, b), BF16)]
            + [jnp.pad(position_table.T, ((0, 4), (0, b - 2 * a)))]
        )
        scales = jnp.repeat(head_scale.astype(F32), HEAD_DIM)[None]
        gathered = lax.all_gather(packed, "fsdp", axis=0)
        qkv_full = gather_matrix(qkv_weight)
        out_full = gather_matrix(out_weight)
        up_full = gather_matrix(up_weight)
        down_full = gather_matrix(down_weight).T
        gathered = gathered.astype(F32)
        vecs = gathered[:, :8, :a].transpose(1, 0, 2).reshape(8, D)
        wides = jnp.pad(gathered[:, 8:11].transpose(1, 0, 2).reshape(3, FF), ((0, 5), (0, 0)))
        pair = gathered[:, 11, : 2 * a].reshape(1, 2 * D)
        table = gathered[:, 16:, : 2 * a].transpose(1, 0, 2).reshape(16, TABLE)
        qkv_bias = jnp.concatenate([pair[:, :D], jnp.zeros((1, D), F32), pair[:, D:]], 1)

        bias = build_bias(table)
        normed, qkv, probs, attended = attention(
            lengths, buckets, tokens, vecs, qkv_full, qkv_bias, bias
        )
        (
            result, mixed, second, act, low, branch, middle_grad, attended_low, sums, wide_sums,
        ) = feed_forward(tokens, attended, cotangent, out_full, up_full, down_full, vecs, wides, scales)
        down_grad = outer_product(cotangent, act, 512)
        up_grad = outer_product(second, low, 512)
        out_grad = outer_product(mixed, branch, 256)
        input_grad, grids, qkv_grad, pair_sums, first_sums = attention_back(
            buckets, probs, qkv, attended_low, normed, tokens, middle_grad, qkv_full, vecs
        )
        table_sums = table_grad(grids)
        qkv_natural = qkv_grad.reshape(PAIRS, D, 3, 128).transpose(1, 2, 0, 3).reshape(D, 3 * D)

        qkv_owned = scatter_matrix(qkv_natural)
        out_owned = scatter_matrix(out_grad)
        up_owned = scatter_matrix(up_grad)
        down_owned = scatter_matrix(down_grad.T)
        pair_grad = pair_sums[:, 0].reshape(PAIRS, 3, 128).transpose(1, 0, 2).reshape(3, D)
        pair_grad = jnp.concatenate([pair_grad[0], pair_grad[2]])
        narrow_sums = jnp.concatenate([first_sums[:2], sums[2:8]], 0)
        packed = jnp.concatenate(
            [
                narrow_sums.reshape(8, parts, a).transpose(1, 0, 2).reshape(parts, -1),
                wide_sums[:3].reshape(3, parts, b).transpose(1, 0, 2).reshape(parts, -1),
                pair_grad.reshape(parts, -1),
                table_sums[:HEADS].T.reshape(parts, -1),
            ],
            1,
        )
        owned = lax.psum(lax.psum_scatter(packed, "fsdp", scatter_dimension=0, tiled=True), "dp")[0]
        scale_grad = lax.psum(sums[8].reshape(HEADS, HEAD_DIM).sum(1), ("fsdp", "dp"))
        narrow_owned = owned[: 8 * a].reshape(8, a)
        edge = 8 * a
        wide_owned = owned[edge : edge + 3 * b].reshape(3, b)
        edge += 3 * b
        pair_owned = owned[edge : edge + 2 * a]
        edge += 2 * a
        table_owned = owned[edge:].reshape(TABLE // parts, HEADS)
    return (
        result, input_grad, qkv_owned, pair_owned, out_owned, narrow_owned[6], up_owned,
        wide_owned[0], down_owned, narrow_owned[7], narrow_owned[0], narrow_owned[1],
        narrow_owned[2], narrow_owned[3], narrow_owned[4], narrow_owned[5], wide_owned[1],
        wide_owned[2], scale_grad, table_owned,
    )


def solution(mesh):
    tokens = P(("fsdp", "dp"), None)
    sequences = P(("fsdp", "dp"))
    matrix = P("fsdp", "dp")
    vector = P("fsdp")
    table = P("fsdp", None)
    in_specs = (
        tokens, tokens, sequences, sequences, matrix, vector, matrix, vector, matrix, vector,
        matrix, vector, vector, vector, vector, vector, vector, vector, vector, vector, P(), table,
    )
    out_specs = (
        tokens, tokens, matrix, vector, matrix, vector, matrix, vector, matrix, vector, vector,
        vector, vector, vector, vector, vector, vector, vector, P(), table,
    )
    return jax.shard_map(body, mesh=mesh, in_specs=in_specs, out_specs=out_specs, check_vma=False)
```

```python
import functools

import jax
import jax.numpy as jnp
from jax import lax
from jax.experimental import pallas as pl
from jax.experimental.pallas import tpu as pltpu
from jax.sharding import PartitionSpec as P

D = 768
HEADS = 12
PAIRS = 6
HEAD_DIM = 64
FF = 3072
SLOT = 256
TABLE = 1536

EPS = 1e-05
MASKED = -1000000000.0
F32 = jnp.float32
BF16 = jnp.bfloat16
VMEM_LIMIT = 60 * 2**20
BACK_LIMIT = 60 * 2**20


def params(**more):
    return pltpu.CompilerParams(vmem_limit_bytes=VMEM_LIMIT, **more)


def nn(left, right):
    return lax.dot_general(left, right, (((1,), (0,)), ((), ())), preferred_element_type=F32)


def nt(left, right):
    return lax.dot_general(left, right, (((1,), (1,)), ((), ())), preferred_element_type=F32)


def standardize(values):
    center = values - jnp.mean(values, -1, keepdims=True)
    inverse = lax.rsqrt(jnp.mean(center * center, -1, keepdims=True) + EPS)
    return center * inverse, inverse


def norm_back(grad, unit, inverse):
    return inverse * (
        grad
        - jnp.mean(grad, -1, keepdims=True)
        - unit * jnp.mean(grad * unit, -1, keepdims=True)
    )


def column_sum(values):
    return jnp.sum(values, 0, keepdims=True)


def tall_sum(ref):
    def some(n, total):
        return total + column_sum(ref[rows_of(n, 64), :].astype(F32))

    return lax.fori_loop(0, ref.shape[0] // 64, some, jnp.zeros((1, ref.shape[1]), F32))


def split_low(values):
    high = values.astype(BF16)
    return high, (values - high.astype(F32)).astype(BF16)


def compaction(side, lanes):
    plane = lax.broadcasted_iota(jnp.int32, (1024, lanes), 0)
    lane = lax.broadcasted_iota(jnp.int32, (1024, lanes), 1)
    across = plane & 31
    return ((lane == side * (plane >> 5) + across) & (across < side)).astype(F32).astype(BF16)


def inside_grid(patches):
    row = lax.broadcasted_iota(jnp.int32, (SLOT, SLOT), 0)
    col = lax.broadcasted_iota(jnp.int32, (SLOT, SLOT), 1)
    return (row < patches) & (col < patches)


def store_tiles(ref, values):
    for k in range(ref.shape[0]):
        ref[k] = values[:, 128 * k : 128 * k + 128]


def load_tiles(ref):
    return jnp.concatenate([ref[k] for k in range(ref.shape[0])], 1)


def load_strided(ref, first, count):
    return jnp.concatenate(
        [ref[k, pl.ds(first, count, 16), :] for k in range(ref.shape[0])], 1
    )


def store_strided(ref, first, values):
    for k in range(ref.shape[0]):
        ref[k, pl.ds(first, values.shape[0], 16), :] = values[:, 128 * k : 128 * k + 128]


def bias_walls(table_ref, wall_small, wall_large, visual):
    plane = table_ref[:, 512:]
    shifted = [pltpu.roll(plane, (ic - 15) % 1024, 1) for ic in range(16)]
    stack = jnp.concatenate(shifted, 0).astype(BF16)
    store_tiles(wall_large, nn(stack, compaction(15, 512)))
    store_tiles(wall_small, nn(stack[:128], compaction(8, 256)))
    visual[...] = jnp.zeros_like(visual)


def bias_head(table_ref, out_ref, wall_small, wall_large, visual, h, carry):
    line = jnp.broadcast_to(table_ref[pl.ds(h, 1), :512], (SLOT, 512))
    textual = pltpu.roll(line, 257, 1, stride=1, stride_axis=0)[:, :SLOT]
    large = load_strided(wall_large, h, 16)
    for ir in range(15):
        visual[pl.ds(ir * 15, 16), :] = pltpu.roll(large, 512 - (15 - ir) * 15, 1)[:, :SLOT]
    out_ref[1, h] = jnp.where(inside_grid(225), visual[...], textual).astype(BF16)
    small = load_strided(wall_small, h, 8)
    rows = [pltpu.roll(small, 256 - (15 - ir) * 8, 1) for ir in range(8)]
    grid = jnp.concatenate(rows + [jnp.zeros((192, SLOT), F32)], 0)
    out_ref[0, h] = jnp.where(inside_grid(64), grid, textual).astype(BF16)
    return carry


def bias_kernel(table_ref, out_ref, wall_small, wall_large, visual):
    bias_walls(table_ref, wall_small, wall_large, visual)
    one_head = functools.partial(bias_head, table_ref, out_ref, wall_small, wall_large, visual)
    lax.fori_loop(0, HEADS, one_head, 0)


def build_bias(table):
    return pl.pallas_call(
        bias_kernel,
        out_shape=jax.ShapeDtypeStruct((2, HEADS, SLOT, SLOT), BF16),
        scratch_shapes=[
            pltpu.VMEM((2, 128, 128), F32),
            pltpu.VMEM((4, 256, 128), F32),
            pltpu.VMEM((SLOT, SLOT), F32),
        ],
        compiler_params=params(),
        name="build_bias",
    )(table)


def table_grad_start(out_ref, wall_small, wall_large):
    wall_small[...] = jnp.zeros_like(wall_small)
    wall_large[...] = jnp.zeros_like(wall_large)
    out_ref[...] = jnp.zeros_like(out_ref)


def table_grad_head(grid_ref, out_ref, wall_small, wall_large, h, slot):
    row = lax.broadcasted_iota(jnp.int32, (SLOT, SLOT), 0)
    col = lax.broadcasted_iota(jnp.int32, (SLOT, SLOT), 1)
    flip = (row + col == SLOT - 1).astype(F32).astype(BF16)
    lane = lax.broadcasted_iota(jnp.int32, (16, SLOT), 1)
    textual = jnp.where(inside_grid(64), 0.0, grid_ref[0, slot]) + jnp.where(
        inside_grid(225), 0.0, grid_ref[1, slot]
    )
    high, low = split_low(textual)
    flipped = nn(flip, high) + nn(flip, low)
    wide = jnp.concatenate([flipped, jnp.zeros((SLOT, SLOT), F32)], 1)
    out_ref[pl.ds(h, 1), :512] = column_sum(pltpu.roll(wide, 0, 1, stride=1, stride_axis=0))
    total = jnp.zeros((16, 512), F32)
    for ir in range(15):
        part = jnp.where(lane < 225, grid_ref[1, slot, pl.ds(ir * 15, 16), :], 0.0)
        part = jnp.concatenate([part, jnp.zeros((16, SLOT), F32)], 1)
        total = total + pltpu.roll(part, (15 - ir) * 15, 1)
    store_strided(wall_large, h, total)
    total = jnp.zeros((8, SLOT), F32)
    for ir in range(8):
        part = jnp.where(lane[:8] < 64, grid_ref[0, slot, pl.ds(ir * 8, 8), :], 0.0)
        total = total + pltpu.roll(part, (15 - ir) * 8, 1)
    store_strided(wall_small, h, total)


def table_grad_end(out_ref, wall_small, wall_large):
    high, low = split_low(load_tiles(wall_large))
    spread = compaction(15, 512)
    large = nt(high, spread) + nt(low, spread)
    high, low = split_low(load_tiles(wall_small))
    spread = compaction(8, 256)
    small = nt(high, spread) + nt(low, spread)
    plane = jnp.zeros((16, 1024), F32)
    for ic in range(15):
        part = large[ic * 16 : ic * 16 + 16]
        if ic < 8:
            part = part + small[ic * 16 : ic * 16 + 16]
        plane = plane + pltpu.roll(part, 15 - ic, 1)
    out_ref[:, 512:] = plane


def table_grad_kernel(grid_ref, out_ref, wall_small, wall_large):
    table_grad_start(out_ref, wall_small, wall_large)

    def one_head(h, carry):
        table_grad_head(grid_ref, out_ref, wall_small, wall_large, h, h)
        return carry

    lax.fori_loop(0, HEADS, one_head, 0)
    table_grad_end(out_ref, wall_small, wall_large)


def table_grad(grids):
    return pl.pallas_call(
        table_grad_kernel,
        out_shape=jax.ShapeDtypeStruct((16, TABLE), F32),
        scratch_shapes=[pltpu.VMEM((2, 128, 128), F32), pltpu.VMEM((4, 256, 128), F32)],
        compiler_params=params(),
        name="table_grad",
    )(grids)


def by_head(pair, axis):
    first = lax.broadcasted_iota(jnp.int32, pair.shape, 1) < HEAD_DIM
    return jnp.concatenate([jnp.where(first, pair, 0), jnp.where(first, 0, pair)], axis)


def attend(query, keys, values, bias, live):
    logits = nt(by_head(query, 0), keys)
    probs = []
    for half in range(2):
        rows = slice(SLOT * half, SLOT * half + SLOT)
        scores = jnp.where(live, logits[rows] + bias[half].astype(F32), MASKED)
        shifted = jnp.exp(scores - jnp.max(scores, -1, keepdims=True))
        probs.append((shifted * (1.0 / jnp.sum(shifted, -1, keepdims=True))).astype(BF16))
    return probs, nn(jnp.concatenate(probs, 1), by_head(values, 0))


def attend_back(query, keys, values, grad, probs):
    probs_grads = nt(by_head(grad, 0), values)
    grad_turned = grad.T
    query_turned = query.T
    keys_parts = []
    values_parts = []
    scores_grads = []
    lows = []
    for half in range(2):
        part = slice(HEAD_DIM * half, HEAD_DIM * half + HEAD_DIM)
        wide = probs[half].astype(F32)
        probs_grad = probs_grads[SLOT * half : SLOT * half + SLOT]
        values_parts.append(nn(grad_turned[part], probs[half]))
        scores_grad = wide * (probs_grad - jnp.sum(wide * probs_grad, -1, keepdims=True))
        scores_grads.append(scores_grad)
        lows.append(scores_grad.astype(BF16))
        keys_parts.append(nn(query_turned[part], lows[half]))
    query_grad = nn(jnp.concatenate(lows, 1), by_head(keys, 0)) * HEAD_DIM ** (-0.5)
    keys_grad = jnp.concatenate(keys_parts, 0).T
    values_grad = jnp.concatenate(values_parts, 0).T
    return query_grad.astype(BF16), keys_grad.astype(BF16), values_grad.astype(BF16), scores_grads


def attention_kernel(
    lengths, buckets, x_ref, vec_ref, weight_ref, qkv_bias_ref, bias_ref,
    normed_ref, qkv_ref, probs_ref, attended_ref,
):
    count = x_ref.shape[0] // SLOT

    def one_block(b, carry):
        rows = pl.ds(pl.multiple_of(b * SLOT, SLOT), SLOT)
        unit, inverse = standardize(x_ref[rows, :].astype(F32))
        normed_ref[rows, :] = (unit * vec_ref[0:1, :] + vec_ref[1:2, :]).astype(BF16)
        return carry

    lax.fori_loop(0, count, one_block, 0)

    def one_panel(n, carry):
        cols = pl.ds(pl.multiple_of(n * 256, 256), 256)
        out = nn(normed_ref[...], weight_ref[:, cols]) + qkv_bias_ref[:, cols]
        out = (out * jnp.where(n < 3, HEAD_DIM ** (-0.5), 1.0)).astype(BF16)
        qkv_ref[2 * n] = out[:, :128]
        qkv_ref[2 * n + 1] = out[:, 128:]
        return carry

    lax.fori_loop(0, 9, one_panel, 0)
    key_slot = lax.broadcasted_iota(jnp.int32, (SLOT, SLOT), 1)

    def one_unit(step, carry):
        pair = step // count
        s = step % count
        rows = pl.ds(pl.multiple_of(s * SLOT, SLOT), SLOT)
        bias = [bias_ref[buckets[s], 2 * pair + half] for half in range(2)]
        probs, out = attend(
            qkv_ref[pair, rows, :], qkv_ref[PAIRS + pair, rows, :], qkv_ref[2 * PAIRS + pair, rows, :],
            bias, key_slot < lengths[s],
        )
        for half in range(2):
            probs_ref[2 * pair + half, s] = probs[half]
        attended_ref[rows, pl.ds(pl.multiple_of(pair * 128, 128), 128)] = out
        return carry

    lax.fori_loop(0, PAIRS * count, one_unit, 0)


def attention(lengths, buckets, tokens, vecs, weight, qkv_bias, bias):
    rows = tokens.shape[0]
    count = rows // SLOT
    smem = pl.BlockSpec(memory_space=pltpu.SMEM)
    vmem = pl.BlockSpec(memory_space=pltpu.VMEM)
    return pl.pallas_call(
        attention_kernel,
        in_specs=[smem, smem] + [vmem] * 5,
        out_shape=[
            jax.ShapeDtypeStruct((rows, D), BF16),
            jax.ShapeDtypeStruct((3 * PAIRS, rows, 128), BF16),
            jax.ShapeDtypeStruct((HEADS, count, SLOT, SLOT), BF16),
            jax.ShapeDtypeStruct((rows, D), F32),
        ],
        compiler_params=params(),
        name="attention_forward",
    )(lengths, buckets, tokens, vecs, weight, qkv_bias, bias)


PANEL = 512


def feed_kernel(*refs):
    @pl.when(pl.program_id(0) == 0)
    def _():
        for ref in refs[17:19]:
            ref[...] = jnp.zeros_like(ref)

    feed_block(*refs, lambda: None)


def feed_block(
    x_ref, attended_ref, cot_ref, out_w, up_w, down_w, vec_ref, wide_ref, scale_ref,
    result_ref, mixed_ref, second_ref, act_ref, low_ref, branch_ref, middle_grad_ref,
    attended_low_ref, sums_ref, wide_sums_ref,
    gelu_ref, slope_ref, grad_ref, before_down,
):
    def add(row, values):
        sums_ref[row : row + 1, :] += column_sum(values)

    rows = x_ref.shape[0]
    attended = attended_ref[...]
    mix_unit, mix_inverse = standardize(attended * scale_ref[...])
    mixed = (mix_unit * vec_ref[2:3, :] + vec_ref[3:4, :]).astype(BF16)
    mixed_ref[...] = mixed
    middle = x_ref[...].astype(F32) + nn(mixed, out_w[...]) + vec_ref[6:7, :]
    second_unit, second_inverse = standardize(middle)
    second = (second_unit * vec_ref[4:5, :] + vec_ref[5:6, :]).astype(BF16)
    second_ref[...] = second
    cot = cot_ref[...]

    panels = [slice(n, n + PANEL) for n in range(0, FF, PANEL)]
    total = jnp.zeros((rows, 1), F32)
    for cols in panels:
        hidden = nn(second, up_w[:, cols]) + wide_ref[0:1, cols]
        cdf = 0.5 + 0.5 * lax.erf(hidden * 0.7071067811865476)
        gelu = hidden * cdf
        gelu_ref[:, cols] = gelu
        slope_ref[:, cols] = cdf + hidden * (jnp.exp(-0.5 * hidden * hidden) * 0.3989422804014327)
        total = total + jnp.sum(gelu, -1, keepdims=True)
    mean = total * (1.0 / FF)
    total = jnp.zeros((rows, 1), F32)
    for cols in panels:
        center = gelu_ref[:, cols] - mean
        total = total + jnp.sum(center * center, -1, keepdims=True)
    inverse = lax.rsqrt(total * (1.0 / FF) + EPS)
    before_down()
    result = middle + vec_ref[7:8, :]
    first = jnp.zeros((rows, 1), F32)
    second_moment = jnp.zeros((rows, 1), F32)
    for cols in panels:
        unit = (gelu_ref[:, cols] - mean) * inverse
        gelu_ref[:, cols] = unit
        act = (unit * wide_ref[1:2, cols] + wide_ref[2:3, cols]).astype(BF16)
        act_ref[:, cols] = act
        result = result + nt(act, down_w[:, cols])
        act_grad = nn(cot, down_w[:, cols])
        wide_sums_ref[1:2, cols] += column_sum(act_grad * unit)
        wide_sums_ref[2:3, cols] += column_sum(act_grad)
        grad = act_grad * wide_ref[1:2, cols]
        grad_ref[:, cols] = grad
        first = first + jnp.sum(grad, -1, keepdims=True)
        second_moment = second_moment + jnp.sum(grad * unit, -1, keepdims=True)
    result_ref[...] = result.astype(BF16)
    first = first * (1.0 / FF)
    second_moment = second_moment * (1.0 / FF)
    second_in = jnp.zeros((rows, D), F32)
    for cols in panels:
        grad = inverse * (grad_ref[:, cols] - first - gelu_ref[:, cols] * second_moment)
        low = (grad * slope_ref[:, cols]).astype(BF16)
        low_ref[:, cols] = low
        wide_sums_ref[0:1, cols] += column_sum(low.astype(F32))
        second_in = second_in + nt(low, up_w[:, cols])
    add(4, second_in * second_unit)
    add(5, second_in)
    cot_wide = cot.astype(F32)
    add(7, cot_wide)
    middle_grad = cot_wide + norm_back(second_in * vec_ref[4:5, :], second_unit, second_inverse)
    middle_grad_ref[...] = middle_grad
    branch = middle_grad.astype(BF16)
    branch_ref[...] = branch
    add(6, branch.astype(F32))
    mixed_in = nt(branch, out_w[...])
    add(2, mixed_in * mix_unit)
    add(3, mixed_in)
    grad = norm_back(mixed_in * vec_ref[2:3, :], mix_unit, mix_inverse)
    add(8, grad * attended)
    attended_low_ref[...] = (grad * scale_ref[...]).astype(BF16)


def feed_forward(tokens, attended, cotangent, out_w, up_w, down_w, vecs, wide, scales):
    rows = tokens.shape[0]
    tile = 256
    block = pl.BlockSpec((tile, D), lambda i: (i, 0))
    wide_block = pl.BlockSpec((tile, FF), lambda i: (i, 0))

    def whole(shape):
        return pl.BlockSpec(shape, lambda i: (0, 0), pipeline_mode=pl.Buffered(1))

    def held(shape):
        return pl.BlockSpec(shape, lambda i: (0, 0))

    return pl.pallas_call(
        feed_kernel,
        grid=(rows // tile,),
        in_specs=[block] * 3
        + [whole((D, D)), whole((D, FF)), whole((D, FF)), whole((8, D)), whole((8, FF)), whole((1, D))],
        out_specs=[block, block, block, wide_block, wide_block, block, block, block]
        + [held((16, D)), held((8, FF))],
        out_shape=[
            jax.ShapeDtypeStruct((rows, D), BF16),
            jax.ShapeDtypeStruct((rows, D), BF16),
            jax.ShapeDtypeStruct((rows, D), BF16),
            jax.ShapeDtypeStruct((rows, FF), BF16),
            jax.ShapeDtypeStruct((rows, FF), BF16),
            jax.ShapeDtypeStruct((rows, D), BF16),
            jax.ShapeDtypeStruct((rows, D), F32),
            jax.ShapeDtypeStruct((rows, D), BF16),
            jax.ShapeDtypeStruct((16, D), F32),
            jax.ShapeDtypeStruct((8, FF), F32),
        ],
        scratch_shapes=[pltpu.VMEM((tile, FF), F32)] * 3,
        compiler_params=params(dimension_semantics=("arbitrary",)),
        name="feed_forward",
    )(tokens, attended, cotangent, out_w, up_w, down_w, vecs, wide, scales)


def outer_kernel(left_ref, right_ref, out_ref, turned):
    @pl.when(pl.program_id(0) == 0)
    def _():
        turned[...] = left_ref[...].T

    out_ref[...] = nn(turned[...], right_ref[...]).astype(BF16)


def outer_product(left, right, panel):
    rows, width = left.shape
    cols = right.shape[1]
    return pl.pallas_call(
        outer_kernel,
        grid=(cols // panel,),
        in_specs=[
            pl.BlockSpec((rows, width), lambda i: (0, 0), pipeline_mode=pl.Buffered(1)),
            pl.BlockSpec((rows, panel), lambda i: (0, i)),
        ],
        out_specs=pl.BlockSpec((width, panel), lambda i: (0, i)),
        out_shape=jax.ShapeDtypeStruct((width, cols), BF16),
        scratch_shapes=[pltpu.VMEM((width, rows), BF16)],
        compiler_params=params(dimension_semantics=("arbitrary",)),
        name="weight_grad",
    )(left, right)


def attention_back_kernel(
    buckets, probs_ref, query_ref, keys_ref, values_ref, low_ref, normed_ref, x_ref, middle_ref,
    weight_q, weight_k, weight_v, vec_ref,
    input_grad_ref, grid_ref, weight_grad_ref, pair_ref, sums_ref,
    turned, first_in, proj_ref,
):
    count = x_ref.shape[0] // SLOT
    step = pl.program_id(0)

    @pl.when(step == 0)
    def _():
        turned[...] = normed_ref[...].T
        first_in[...] = jnp.zeros_like(first_in)

    grid_ref[...] = jnp.zeros_like(grid_ref)

    def one_sequence(s, carry):
        rows = pl.ds(pl.multiple_of(s * SLOT, SLOT), SLOT)
        query_grad, keys_grad, values_grad, scores_grads = attend_back(
            query_ref[0, rows, :], keys_ref[0, rows, :], values_ref[0, rows, :], low_ref[rows, :],
            [probs_ref[half, s] for half in range(2)],
        )
        small = jnp.where(buckets[s] == 0, 1.0, 0.0)
        for half in range(2):
            grid_ref[0, half] += scores_grads[half] * small
            grid_ref[1, half] += scores_grads[half] * (1.0 - small)
        proj_ref[rows, 0:128] = query_grad
        proj_ref[rows, 128:256] = keys_grad
        proj_ref[rows, 256:384] = values_grad
        return carry

    lax.fori_loop(0, count, one_sequence, 0)
    proj = proj_ref[...]
    weight_grad_ref[0] = nn(turned[...], proj).astype(BF16)
    pair_ref[0] = jnp.broadcast_to(column_sum(proj.astype(F32)), (8, 384))
    weights = jnp.concatenate([weight_q[...], weight_k[...], weight_v[...]], 1)
    first_in[...] += nt(proj, weights)

    @pl.when(step == PAIRS - 1)
    def _():
        sums_ref[...] = jnp.zeros_like(sums_ref)

        def one_block(b, carry):
            rows = pl.ds(pl.multiple_of(b * SLOT, SLOT), SLOT)
            unit, inverse = standardize(x_ref[rows, :].astype(F32))
            grad = first_in[rows, :]
            sums_ref[0:1, :] += column_sum(grad * unit)
            sums_ref[1:2, :] += column_sum(grad)
            back = norm_back(grad * vec_ref[0:1, :], unit, inverse)
            input_grad_ref[rows, :] = (middle_ref[rows, :] + back).astype(BF16)
            return carry

        lax.fori_loop(0, count, one_block, 0)


def attention_back(buckets, probs, qkv, attended_low, normed, tokens, middle_grad, weight, vecs):
    rows = tokens.shape[0]
    count = rows // SLOT

    def whole(shape):
        return pl.BlockSpec(shape, lambda i: (0,) * len(shape), pipeline_mode=pl.Buffered(1))

    def held(shape):
        return pl.BlockSpec(shape, lambda i: (0,) * len(shape))

    def panel(base):
        return pl.BlockSpec((1, rows, 128), lambda i: (base + i, 0, 0))

    def weight_panel(base):
        return pl.BlockSpec((D, 128), lambda i: (0, base + i))

    return pl.pallas_call(
        attention_back_kernel,
        grid=(PAIRS,),
        in_specs=[
            pl.BlockSpec(memory_space=pltpu.SMEM),
            pl.BlockSpec((2, count, SLOT, SLOT), lambda i: (i, 0, 0, 0)),
            panel(0), panel(PAIRS), panel(2 * PAIRS),
            pl.BlockSpec((rows, 128), lambda i: (0, i)),
            whole((rows, D)), whole((rows, D)), whole((rows, D)),
            weight_panel(0), weight_panel(PAIRS), weight_panel(2 * PAIRS),
            whole((8, D)),
        ],
        out_specs=[
            held((rows, D)),
            pl.BlockSpec((2, 2, SLOT, SLOT), lambda i: (0, i, 0, 0)),
            pl.BlockSpec((1, D, 384), lambda i: (i, 0, 0)),
            pl.BlockSpec((1, 8, 384), lambda i: (i, 0, 0)),
            held((8, D)),
        ],
        out_shape=[
            jax.ShapeDtypeStruct((rows, D), BF16),
            jax.ShapeDtypeStruct((2, HEADS, SLOT, SLOT), F32),
            jax.ShapeDtypeStruct((PAIRS, D, 384), BF16),
            jax.ShapeDtypeStruct((PAIRS, 8, 384), F32),
            jax.ShapeDtypeStruct((8, D), F32),
        ],
        scratch_shapes=[
            pltpu.VMEM((D, rows), BF16),
            pltpu.VMEM((rows, D), F32),
            pltpu.VMEM((rows, 384), BF16),
        ],
        compiler_params=params(dimension_semantics=("arbitrary",)),
        name="attention_backward",
    )(buckets, probs, qkv, qkv, qkv, attended_low, normed, tokens, middle_grad, weight, weight, weight, vecs)


MESH = pl.DeviceIdType.MESH
ANY = pl.ANY


class Place:
    def __init__(self):
        fsdp = lax.axis_index("fsdp")
        dp = lax.axis_index("dp")
        self.z, self.y, self.x, self.core = fsdp // 2, fsdp % 2, dp // 2, dp % 2

    def at(self, z=None, y=None, x=None, core=None):
        z = self.z if z is None else z
        y = self.y if y is None else y
        x = self.x if x is None else x
        core = self.core if core is None else core
        return (z * 2 + y, x * 2 + core)

    def greet(self):
        barrier = pltpu.get_barrier_semaphore()
        peers = [self.at(z=(self.z + k) % 4, y=self.y) for k in range(1, 4)]
        peers += [self.at(z=(self.z + k) % 4, y=1 - self.y) for k in range(4)]
        peers += [
            self.at(x=1 - self.x),
            self.at(core=1 - self.core),
            self.at(x=1 - self.x, core=1 - self.core),
        ]
        for peer in peers:
            pl.semaphore_signal(barrier, inc=1, device_id=peer, device_id_type=MESH)

    def meet(self):
        pl.semaphore_wait(pltpu.get_barrier_semaphore(), 10)


def remote(src, dst, send, recv, peer):
    return pltpu.make_async_remote_copy(
        src_ref=src, dst_ref=dst, send_sem=send, recv_sem=recv, device_id=peer, device_id_type=MESH
    )


def rows_of(first, size):
    return pl.ds(pl.multiple_of(first * size, size), size)


def chunk(kind, ref, r, d):
    if kind == "panel":
        return ref.at[d, rows_of(r, 96), :]
    if kind == "wide":
        return ref.at[rows_of(r, 96), rows_of(d, 768)]
    return ref.at[rows_of(d, 192), rows_of(r, 384)]


class Gather:
    def __init__(self, place, pieces, fulls, send, recv, local):
        self.place, self.pieces, self.fulls = place, pieces, fulls
        self.send, self.recv, self.local = send, recv, local
        self.made = {}

    def slot(self, w, z, y, x):
        return chunk(GATHER_KINDS[w], self.fulls[w], z * 2 + y, x * 2 + self.place.core)

    def copy(self, w, index, src, dst, peer):
        self.made[w, index] = remote(src, dst, self.send.at[w, index], self.recv.at[w, index], peer)
        return self.made[w, index]

    def sources(self, w, k):
        here = self.place
        over_x = (k + GATHER_TURN[w]) % 2 == 0
        near = (here.y, 1 - here.x) if over_x else (1 - here.y, here.x)
        far = (1 - here.y, here.x) if over_x else (here.y, 1 - here.x)
        upper = here.z // 2
        depth = here.z + upper * (3 - 2 * here.z)
        z = k - depth if k == 1 else k
        z = z + upper * (3 - 2 * z) if k else here.z
        return z, near, far

    def plan(self, w):
        here = self.place
        own = self.slot(w, here.z, here.y, here.x)
        self.made[w, "keep"] = pltpu.make_async_copy(self.pieces[w], own, self.local.at[w])
        sibling = here.at(core=1 - here.core)
        pair = here.at(z=here.z + 1 - 2 * (here.z % 2))
        across = here.at(z=3 - here.z)
        for k in range(4):
            z, near, far = self.sources(w, k)
            mine = self.slot(w, z, here.y, here.x)
            src = mine if k else self.pieces[w]
            if k == 0:
                self.copy(w, 1, src, mine, pair)
                self.copy(w, 2, src, mine, across)
            elif k == 1:
                self.copy(w, 3, src, mine, across)
            else:
                self.made[w, "on", k] = remote(
                    src, mine, self.send.at[w, 30 + k], self.recv.at[w, k], pair
                )
            self.copy(w, 4 + k, src, mine, here.at(y=near[0], x=near[1]))
            passed = self.slot(w, z, *near)
            self.copy(w, 8 + 2 * k, src, mine, here.at(y=far[0], x=far[1]))
            self.copy(w, 9 + 2 * k, passed, passed, here.at(y=far[0], x=far[1]))
            third = self.slot(w, z, *far)
            fourth = self.slot(w, z, 1 - here.y, 1 - here.x)
            for n, part in enumerate((src, passed, third, fourth)):
                dst = mine if n == 0 else part
                self.copy(w, 16 + 4 * k + n, part, dst, sibling)

    def when_middle(self, act):
        pl.when(self.place.z * (3 - self.place.z) > 0)(act)

    def begin(self, w, k=0):
        self.made[w, "keep"].start()
        self.made[w, 1].start()
        self.when_middle(lambda: self.made[w, 2].start())

    def relay(self, w, k):
        def on():
            self.made[w, k].wait_recv()
            (self.made[w, 3] if k == 1 else self.made[w, "on", k]).start()

        self.when_middle(on)

    def first(self, w, k):
        if k:
            pl.when(self.place.z * (3 - self.place.z) == 0)(self.made[w, k].wait_recv)
        self.made[w, 4 + k].start()
        self.made[w, 16 + 4 * k].start()

    def second(self, w, k):
        self.made[w, 4 + k].wait_recv()
        self.made[w, 8 + 2 * k].start()
        self.made[w, 9 + 2 * k].start()
        self.made[w, 17 + 4 * k].start()

    def third(self, w, k):
        for n in range(2):
            self.made[w, 8 + 2 * k + n].wait_recv()
            self.made[w, 18 + 4 * k + n].start()

    def finish(self, w):
        for n in range(16):
            self.made[w, 16 + n].wait_recv()
        for n in [1] + list(range(4, 32)):
            self.made[w, n].wait_send()

        def passed_on():
            for made in (self.made[w, 2], self.made[w, 3], self.made[w, "on", 2], self.made[w, "on", 3]):
                made.wait_send()

        self.when_middle(passed_on)
        self.made[w, "keep"].wait()


MIXED, UP, DOWN = range(3)
GATHER_TURN = (0, 1, 0)
GATHER_KINDS = ("wide", "wide", "turned")


GATHER_SCHEDULE = [
    [("begin", MIXED, 0), ("first", MIXED, 0), ("first", UP, 0)],
    [("first", DOWN, 0)],
    [("begin", DOWN, 0)],
    [],
    [],
    [("second", MIXED, 0), ("relay", MIXED, 1), ("first", MIXED, 1), ("relay", MIXED, 2), ("second", UP, 0)],
    [
        ("begin", UP, 0),
        ("relay", DOWN, 1),
        ("first", DOWN, 1),
        ("first", MIXED, 2),
        ("relay", MIXED, 3),
        ("relay", UP, 1),
        ("third", MIXED, 0),
        ("first", UP, 1),
        ("relay", UP, 2),
        ("second", MIXED, 1),
        ("first", MIXED, 3),
        ("second", MIXED, 2),
        ("relay", DOWN, 3),
        ("first", UP, 2),
        ("second", UP, 1),
        ("relay", UP, 3),
        ("second", MIXED, 3),
        ("first", DOWN, 3),
        ("first", UP, 3),
        ("third", MIXED, 1),
        ("third", MIXED, 2),
        ("second", UP, 2),
        ("third", MIXED, 3),
    ],
    [],
    [],
    [("third", UP, 1)],
    [("second", UP, 3), ("relay", DOWN, 2), ("second", DOWN, 1)],
    [],
    [("third", UP, 0), ("third", UP, 2), ("second", DOWN, 0)],
    [],
    [("first", DOWN, 2)],
    [],
    [("third", UP, 3), ("second", DOWN, 3)],
    [("third", DOWN, 1)],
    [],
    [("second", DOWN, 2)],
    [("third", DOWN, 0), ("third", DOWN, 3), ("third", DOWN, 2)],
]


def lined(ref, row, width):
    return jnp.concatenate([ref[f, row : row + 1, :width].astype(F32) for f in range(8)], 1)


def forward_kernel(
    lengths, buckets, x_ref, cot_ref, qkv_p, out_p, up_p, down_t, table_p, head_scale, *refs,
):
    vectors = refs[:12]
    (
    normed_ref, qkv_ref, probs_ref, result_ref, mixed_ref, second_ref, act_ref, low_ref, branch_ref,
    middle_grad_ref, attended_low_ref, sums_ref, wide_sums_ref, vec_ref, qkv_out,
    mixed_p, scale_ref, vec_wide, vec_p, qkv_w, up_w, down_w, vec_f, out_w, bias_ref, wide_ref, qkv_bias_ref, table_ref,
    wall_small, wall_large, visual, attended_ref, gelu_ref, slope_ref, grad_ref,
    send, recv, local, small_send, small_recv, small_local, qkv_sem,
    ) = refs[12:]
    step = pl.program_id(0)
    count = pl.num_programs(0) // 2
    place = Place()
    gather = Gather(place, (mixed_p, up_p, down_t), (qkv_w, up_w, down_w), send, recv, local)
    for w in range(3):
        gather.plan(w)
    f = place.z * 2 + place.y
    small = [pltpu.make_async_copy(vec_p, vec_f.at[f], small_local)]
    for k in range(1, 8):
        peer = (f + k) % 8
        small.append(
            remote(
                vec_p, vec_f.at[f], small_send.at[k], small_recv.at[k],
                place.at(z=peer // 2, y=peer % 2),
            )
        )
    keep_qkv = pltpu.make_async_copy(qkv_w, qkv_out, qkv_sem)

    def follow(point):
        for name, w, k in GATHER_SCHEDULE[point]:
            getattr(gather, name)(w, k)

    @pl.when(step == 0)
    def _():
        place.greet()
        vec_wide[...] = jnp.zeros_like(vec_wide)
        for n, vector in enumerate(vectors):
            size = vector.shape[0]
            vec_wide[n : n + 1, :size] = vector[...].astype(F32).reshape(1, size)
        vec_wide[16 : 16 + HEADS, :192] = table_p[...].astype(F32)
        vec_wide[12:13, :HEADS] = head_scale[...].astype(F32).reshape(1, HEADS)
        vec_p[...] = vec_wide[...].astype(BF16)
        head = lax.broadcasted_iota(jnp.int32, (128, D), 0)
        spread = (head == lax.broadcasted_iota(jnp.int32, (128, D), 1) // HEAD_DIM).astype(F32)
        scale_ref[...] = nn(vec_p[...], jnp.concatenate([spread, jnp.zeros((256, D), F32)], 0).astype(BF16))[8:16]
        mixed_p[:, :576] = qkv_p[...]
        mixed_p[:, 576:] = out_p[...]
        place.meet()
        for made in small:
            made.start()
        follow(0)
        for made in small:
            made.wait()
        for n in range(8):
            vec_ref[n : n + 1, :] = lined(vec_f, n, 96)
        for n in range(3):
            wide_ref[n : n + 1, :] = lined(vec_f, 8 + n, 384)
        pair = lined(vec_f, 11, 192)
        qkv_bias_ref[0:1, :] = jnp.concatenate([pair[:, :D], jnp.zeros((1, D), F32), pair[:, D:]], 1)
        lane = lax.broadcasted_iota(jnp.int32, (1, 3 * D), 1)
        qkv_bias_ref[1:2, :] = jnp.where(lane < D, HEAD_DIM ** (-0.5), 1.0)
        table_ref[...] = jnp.concatenate([vec_f[n, 16:32, :192].astype(F32) for n in range(8)], 1)
        bias_walls(table_ref, wall_small, wall_large, visual)
        heads = functools.partial(bias_head, table_ref, bias_ref, wall_small, wall_large, visual)
        for n, last in enumerate((2, 4, 6, 9, HEADS)):
            follow(1 + n)
            lax.fori_loop((0, 2, 4, 6, 9)[n], last, heads, 0)
        follow(6)
        gather.finish(MIXED)
        keep_qkv.start()
        sums_ref[...] = jnp.zeros_like(sums_ref)
        wide_sums_ref[...] = jnp.zeros_like(wide_sums_ref)

    def progress(spot):
        for s in range(count):
            if GATHER_SCHEDULE[7 + 3 * s + spot]:
                pl.when(step == s)(functools.partial(follow, 7 + 3 * s + spot))

    @pl.when(step < count)
    def _():
        rows = pl.ds(pl.multiple_of(step * SLOT, SLOT), SLOT)
        progress(0)
        unit, inverse = standardize(x_ref[...].astype(F32))
        normed = (unit * vec_ref[0:1, :] + vec_ref[1:2, :]).astype(BF16)
        normed_ref[...] = normed
        for d in range(4):
            cols = slice(576 * d, 576 * d + 576)
            out = (nn(normed, qkv_w[:, 768 * d : 768 * d + 576]) + qkv_bias_ref[0:1, cols]) * qkv_bias_ref[1:2, cols]
            qkv_ref[:, cols] = out.astype(BF16)
        live = lax.broadcasted_iota(jnp.int32, (SLOT, SLOT), 1) < lengths[step]
        bucket = buckets[step]
        for pair in range(PAIRS):
            if pair % 3 == 0:
                progress(1 + pair // 3)
            query = qkv_ref[:, 128 * pair : 128 * pair + 128]
            keys = qkv_ref[:, D + 128 * pair : D + 128 * pair + 128]
            values = qkv_ref[:, 2 * D + 128 * pair : 2 * D + 128 * pair + 128]
            bias = [bias_ref[bucket, 2 * pair + half] for half in range(2)]
            probs, out = attend(query, keys, values, bias, live)
            for half in range(2):
                probs_ref[2 * pair + half, 0] = probs[half]
            attended_ref[rows, 128 * pair : 128 * pair + 128] = out

    @pl.when(step == count)
    def _():
        follow(7 + 3 * count)
        gather.finish(UP)
        for d in range(4):
            out_w[:, 192 * d : 192 * d + 192] = qkv_w[:, 768 * d + 576 : 768 * d + 768]

    @pl.when(step >= count)
    def _():
        rows = pl.ds(pl.multiple_of((step - count) * SLOT, SLOT), SLOT)

        def wait_down():
            @pl.when(step == count)
            def _():
                follow(8 + 3 * count)
                gather.finish(DOWN)

        feed_block(
            x_ref, attended_ref.at[rows, :], cot_ref, out_w, up_w, down_w, vec_ref, wide_ref,
            scale_ref.at[4:5, :],
            result_ref, mixed_ref, second_ref, act_ref, low_ref, branch_ref, middle_grad_ref,
            attended_low_ref, sums_ref, wide_sums_ref, gelu_ref, slope_ref, grad_ref, wait_down,
        )

    @pl.when(step == 2 * count - 1)
    def _():
        keep_qkv.wait()


def forward(lengths, buckets, tokens, cotangent, qkv_p, out_p, up_p, down_p, table_p, head_scale, vectors):
    rows = tokens.shape[0]
    count = rows // SLOT
    smem = pl.BlockSpec(memory_space=pltpu.SMEM)

    def early(shape):
        return pl.BlockSpec(shape, lambda i: (jnp.minimum(i, count - 1),) + (0,) * (len(shape) - 1))

    def late(shape):
        return pl.BlockSpec(shape, lambda i: (jnp.maximum(i - count, 0),) + (0,) * (len(shape) - 1))

    def held(shape):
        return pl.BlockSpec(shape, lambda i: (0,) * len(shape))

    block = (SLOT, D)
    wide = (SLOT, FF)
    return pl.pallas_call(
        forward_kernel,
        grid=(2 * count,),
        in_specs=[
            smem, smem, pl.BlockSpec(block, lambda i: (i % count, 0)), late(block),
            held((96, 576)), held((96, 192)), pl.BlockSpec(memory_space=ANY),
            pl.BlockSpec(memory_space=ANY), held((HEADS, 192)), held((HEADS,)),
        ]
        + [held(vector.shape) for vector in vectors],
        out_specs=[
            early(block), early((SLOT, 3 * D)),
            pl.BlockSpec((HEADS, 1, SLOT, SLOT), lambda i: (0, jnp.minimum(i, count - 1), 0, 0)),
            late(block), late(block), late(block), late(wide), late(wide), late(block), late(block),
            late(block), held((16, D)), held((8, FF)), held((8, D)), pl.BlockSpec(memory_space=ANY),
        ],
        out_shape=[
            jax.ShapeDtypeStruct((rows, D), BF16),
            jax.ShapeDtypeStruct((rows, 3 * D), BF16),
            jax.ShapeDtypeStruct((HEADS, count, SLOT, SLOT), BF16),
            jax.ShapeDtypeStruct((rows, D), BF16),
            jax.ShapeDtypeStruct((rows, D), BF16),
            jax.ShapeDtypeStruct((rows, D), BF16),
            jax.ShapeDtypeStruct((rows, FF), BF16),
            jax.ShapeDtypeStruct((rows, FF), BF16),
            jax.ShapeDtypeStruct((rows, D), BF16),
            jax.ShapeDtypeStruct((rows, D), F32),
            jax.ShapeDtypeStruct((rows, D), BF16),
            jax.ShapeDtypeStruct((16, D), F32),
            jax.ShapeDtypeStruct((8, FF), F32),
            jax.ShapeDtypeStruct((8, D), F32),
            jax.ShapeDtypeStruct((D, FF), BF16),
        ],
        scratch_shapes=[
            pltpu.VMEM((96, D), BF16),
            pltpu.VMEM((8, D), F32),
            pltpu.VMEM((32, 384), F32),
            pltpu.VMEM((32, 384), BF16),
            pltpu.VMEM((D, FF), BF16),
            pltpu.VMEM((D, FF), BF16),
            pltpu.VMEM((D, FF), BF16),
            pltpu.VMEM((8, 32, 384), BF16),
            pltpu.VMEM((D, D), BF16),
            pltpu.VMEM((2, HEADS, SLOT, SLOT), BF16),
            pltpu.VMEM((8, FF), F32),
            pltpu.VMEM((8, 3 * D), F32),
            pltpu.VMEM((16, TABLE), F32),
            pltpu.VMEM((2, 128, 128), F32),
            pltpu.VMEM((4, 256, 128), F32),
            pltpu.VMEM((SLOT, SLOT), F32),
            pltpu.VMEM((rows, D), F32),
            pltpu.VMEM(wide, F32),
            pltpu.VMEM(wide, F32),
            pltpu.VMEM(wide, F32),
            pltpu.SemaphoreType.DMA((3, 34)),
            pltpu.SemaphoreType.DMA((3, 32)),
            pltpu.SemaphoreType.DMA((3,)),
            pltpu.SemaphoreType.DMA((8,)),
            pltpu.SemaphoreType.DMA((8,)),
            pltpu.SemaphoreType.DMA,
            pltpu.SemaphoreType.DMA,
        ],
        compiler_params=params(
            collective_id=1, has_side_effects=True, dimension_semantics=("arbitrary",)
        ),
        name="forward",
    )(lengths, buckets, tokens, cotangent, qkv_p, out_p, up_p, down_p, table_p, head_scale, *vectors)


ORDER = (1, 2, 3, 0)


class Scatter:
    def __init__(self, place, kind, grad, out, buffers, flip=0, offset=0):
        self.place, self.kind, self.grad, self.out = place, kind, grad, out
        self.flip, self.offset = flip, offset
        self.cores, self.over_x, self.over_y, self.far, self.quarter, self.send, self.recv = buffers
        self.made = {}
        here = place
        for k in range(4):
            z = (here.z + k) % 4
            mine = 2 * here.x + here.core
            other = 2 * (1 - here.x) + here.core
            for x in range(2):
                self.copy(
                    k, x, self.block(2 * x + 1 - here.core, z), self.from_core(k, x),
                    here.at(core=1 - here.core),
                )
            if self.x_first(k):
                self.copy(k, 2, self.block(other, z), self.over_x.at[k // 2], here.at(x=1 - here.x))
                self.copy(
                    k, 4, self.part(mine, z, 1 - here.y), self.far.at[k], here.at(y=1 - here.y)
                )
            else:
                for x in range(2):
                    self.copy(
                        k, 2 + x, self.part(2 * x + here.core, z, 1 - here.y),
                        self.over_y.at[k // 2, x], here.at(y=1 - here.y),
                    )
                self.copy(k, 4, self.part(other, z, here.y), self.far.at[k], here.at(x=1 - here.x))
            if k:
                self.copy(k, 5, self.part(mine, z, here.y), self.quarter.at[k - 1], here.at(z=z))

    def x_first(self, k):
        return (k + self.flip) % 2 == 0

    def from_core(self, k, x):
        return self.cores.at[k, x, :, self.offset : self.offset + self.over_x.shape[-1]]

    def block(self, d, z):
        if self.kind == "panel":
            return self.grad.at[d, rows_of(z, 192), :]
        if self.kind == "wide":
            return self.grad.at[rows_of(z, 192), rows_of(d, 768)]
        return self.grad.at[rows_of(d, 192), rows_of(z, 768)]

    def part(self, d, z, y):
        if self.kind == "panel":
            return self.grad.at[d, rows_of(2 * z + y, 96), :]
        if self.kind == "wide":
            return self.grad.at[rows_of(2 * z + y, 96), rows_of(d, 768)]
        return self.grad.at[rows_of(d, 192), rows_of(2 * z + y, 384)]

    def copy(self, k, index, src, dst, peer):
        self.made[k, index] = remote(src, dst, self.send.at[k, index], self.recv.at[k, index], peer)

    def add(self, target, source):
        def some(n, carry):
            at = rows_of(n, 16)
            target[at, :] = target[at, :] + source[at, :]
            return carry

        lax.fori_loop(0, target.shape[0] // 16, some, 0)

    def core(self, k):
        for x in range(2):
            self.made[k, x].start()

    def plane(self, k):
        here = self.place
        z = (here.z + k) % 4
        for x in range(2):
            self.made[k, x].wait_recv()
            self.add(self.block(2 * x + here.core, z), self.from_core(k, x))
        self.made[k, 2].start()
        if not self.x_first(k):
            self.made[k, 3].start()

    def turn(self, k):
        here = self.place
        z = (here.z + k) % 4
        self.made[k, 2].wait_recv()
        if self.x_first(k):
            self.add(self.block(2 * here.x + here.core, z), self.over_x.at[k // 2])
        else:
            self.made[k, 3].wait_recv()
            for x in range(2):
                self.add(self.part(2 * x + here.core, z, here.y), self.over_y.at[k // 2, x])
        self.made[k, 4].start()

    def line(self, k):
        here = self.place
        self.made[k, 4].wait_recv()
        self.add(self.part(2 * here.x + here.core, (here.z + k) % 4, here.y), self.far.at[k])
        if k:
            self.made[k, 5].start()

    def end(self):
        here = self.place
        for k in range(1, 4):
            self.made[k, 5].wait_recv()
        total = self.part(2 * here.x + here.core, here.z, here.y)[...].astype(F32)
        for k in range(3):
            total = total + self.quarter[k].astype(F32)
        self.out[...] = total[:, : self.out.shape[1]]
        for made in self.made.values():
            made.wait_send()


def scatter_scratch(kind, width):
    half = (192, width // 2) if kind == "turned" else (96, width)
    return [
        pltpu.VMEM((4, 2, 192, width), BF16),
        pltpu.VMEM((2, 192, width), BF16),
        pltpu.VMEM((2, 2) + half, BF16),
        pltpu.VMEM((4,) + half, BF16),
        pltpu.VMEM((3,) + half, BF16),
        pltpu.SemaphoreType.DMA((4, 6)),
        pltpu.SemaphoreType.DMA((4, 6)),
    ]


def pack_sums(sums_ref, first_ref, wide_ref, pair, table_ref, packed):
    low = first_ref[0:2, :]
    narrow = sums_ref[...]
    group = lax.broadcasted_iota(jnp.int32, (D, 128), 0) // HEAD_DIM
    pick = (group == lax.broadcasted_iota(jnp.int32, (D, 128), 1)).astype(F32).astype(BF16)
    high, rest = split_low(narrow[8:16])
    heads = (nn(high, pick) + nn(rest, pick))[0:1]
    heads = jnp.concatenate([heads, jnp.zeros((1, 64), F32)], 1)
    for f in range(8):
        at = slice(96 * f, 96 * f + 96)
        packed[f, 0:1, :] = jnp.concatenate(
            [low[0:1, at], low[1:2, at], narrow[2:3, at], narrow[3:4, at]], 1
        )
        packed[f, 1:2, :] = jnp.concatenate([narrow[n : n + 1, at] for n in range(4, 8)], 1)
        packed[f, 2:5, :] = wide_ref[0:3, 384 * f : 384 * f + 384]
        at = slice(192 * f, 192 * f + 192)
        packed[f, 5:6, :] = jnp.concatenate([pair[:, at], heads], 1)
        for n in range(PAIRS):
            packed[f, 6 + n : 7 + n, :] = jnp.concatenate(
                [table_ref[2 * n : 2 * n + 1, at], table_ref[2 * n + 1 : 2 * n + 2, at]], 1
            )
        packed[f, 12:16, :] = jnp.zeros((4, 384), F32)


class SmallSums:
    def __init__(self, place, packed, rows, peers, sems):
        self.place, self.packed, self.rows, self.peers = place, packed, rows, peers
        self.send, self.recv = sems

    def begin(self):
        here = self.place
        f = here.z * 2 + here.y
        self.made = []
        for k in range(1, 8):
            to = (f + k) % 8
            made = remote(
                self.packed.at[to], self.rows.at[k - 1], self.send.at[k], self.recv.at[k],
                here.at(z=to // 2, y=to % 2),
            )
            made.start()
            self.made.append(made)

    def cross(self):
        here = self.place
        f = here.z * 2 + here.y
        for made in self.made:
            made.wait()
        total = self.packed[f]
        for k in range(7):
            total = total + self.rows[k]
        self.peers[0] = total
        d = here.x * 2 + here.core
        self.made = []
        for k in range(1, 4):
            to = (d + k) % 4
            made = remote(
                self.peers.at[0], self.peers.at[k], self.send.at[7 + k], self.recv.at[7 + k],
                here.at(x=to // 2, core=to % 2),
            )
            made.start()
            self.made.append(made)

    def end(self):
        for made in self.made:
            made.wait()
        return (self.peers[0] + self.peers[1]) + (self.peers[2] + self.peers[3])


BACK_SCHEDULE = {
    3: [("down", "plane", 0)],
    4: [("down", "plane", 1)],
    5: [("down", "plane", 2)],
    6: [("down", "plane", 3), ("down", "turn", 0)],
    7: [("down", "turn", 1)],
    10: [
        ("up", "plane", 0),
        ("down", "turn", 3),
        ("down", "turn", 2),
        ("down", "line", 1),
        ("up", "plane", 1),
        ("up", "plane", 2),
    ],
    11: [("down", "line", 0)],
    12: [("down", "line", 2)],
    13: [("up", "turn", 0), ("up", "plane", 3)],
    14: [("out", "plane", 0), ("out", "plane", 1)],
    15: [("up", "turn", 1), ("down", "line", 3)],
    16: [("out", "plane", 3), ("out", "plane", 2), ("up", "line", 0)],
    17: [("up", "turn", 2)],
    18: [("up", "turn", 3), ("up", "line", 1)],
    19: [("out", "turn", 3), ("out", "turn", 2), ("out", "turn", 1), ("out", "turn", 0)],
    20: [("qkv0", "plane", 2), ("qkv0", "plane", 1), ("up", "line", 2), ("qkv0", "plane", 0)],
    21: [("qkv1", "plane", 0), ("qkv1", "plane", 1)],
}
BACK_DRAIN = [
    ("qkv0", "turn", 2),
    ("qkv0", "turn", 1),
    ("out", "line", 2),
    ("out", "line", 3),
    ("out", "line", 0),
    ("qkv0", "plane", 3),
    ("qkv0", "turn", 0),
    ("qkv0", "line", 2),
    ("qkv1", "turn", 0),
    ("out", "line", 1),
    ("qkv1", "plane", 2),
    ("qkv1", "turn", 1),
    ("qkv1", "plane", 3),
    ("qkv0", "line", 1),
    ("qkv0", "turn", 3),
    ("qkv0", "line", 0),
    ("qkv1", "line", 0),
    ("qkv1", "turn", 2),
    ("qkv1", "turn", 3),
    ("qkv1", "line", 1),
    ("up", "line", 3),
    ("qkv0", "line", 3),
    ("qkv1", "line", 2),
    ("qkv1", "line", 3),
]


def backward_kernel(
    buckets, cot_hbm, act_ref, second_hbm, low_ref, mixed_hbm, branch_hbm, normed_hbm,
    probs_ref, query_ref, keys_ref, values_ref, attended_low_ref, vec_ref, sums_ref, wide_ref,
    x_hbm, middle_hbm, weight_hbm,
    input_grad_ref, down_out, up_out, out_out, qkv_out, total_ref,
    left, turned, middle_ref, first_in, proj, grid_ref, down_ref, up_ref, out_ref, qkv_a, qkv_b,
    table_ref, first_ref, wall_small, wall_large, packed, gathered, peers, small_send, small_recv,
    loading, middle_sem, *buffers,
):
    step = pl.program_id(0)
    place = Place()
    parts = {
        "down": Scatter(place, "turned", down_ref, down_out, buffers[0:7]),
        "up": Scatter(place, "wide", up_ref, up_out, buffers[7:14]),
        "out": Scatter(place, "panel", out_ref, out_out, buffers[14:21]),
        "qkv0": Scatter(place, "panel", qkv_a, qkv_out.at[:, 0:256], buffers[0:1] + buffers[21:27]),
        "qkv1": Scatter(
            place, "panel", qkv_b, qkv_out.at[:, 256:576], buffers[0:1] + buffers[27:33], 1, 256
        ),
    }
    small = SmallSums(place, packed, gathered, peers, (small_send, small_recv))
    count = query_ref.shape[0] // SLOT

    def load(n, src, dst):
        return pltpu.make_async_copy(src, dst, loading.at[n])

    load_cot = load(0, cot_hbm, left.at[0])
    load_second = load(1, second_hbm, left.at[1])
    load_mixed = load(2, mixed_hbm, left.at[0])
    load_branch = load(3, branch_hbm, left.at[1])
    load_normed = load(4, normed_hbm, left.at[0])
    load_x = load(5, x_hbm, left.at[1])

    def load_middle(b):
        n = b % 2
        return pltpu.make_async_copy(middle_hbm.at[rows_of(b, SLOT), :], middle_ref.at[n], middle_sem.at[n])

    load_weight = load(7, weight_hbm, down_ref)

    def progress(at):
        for name, event, n in BACK_SCHEDULE.get(at, []):
            getattr(parts[name], event)(ORDER[n])

    def down_panel():
        z = (place.z + 1 + step) % 4
        down_ref[:, rows_of(z, 768)] = nn(turned[...], act_ref[...]).astype(BF16)

    @pl.when(step == 0)
    def _():
        place.greet()
        load_cot.start()
        load_second.start()
        place.meet()

    for at in BACK_SCHEDULE:
        if at < 19:
            pl.when(step == at)(functools.partial(progress, at))

    @pl.when(step < 4)
    def _():
        @pl.when(step == 0)
        def _():
            load_cot.wait()
            turned[...] = left[0].T
            load_mixed.start()

        down_panel()
        for n in range(4):
            pl.when(step == n)(functools.partial(parts["down"].core, ORDER[n]))

    @pl.when((step >= 4) & (step < 8))
    def _():
        @pl.when(step == 4)
        def _():
            load_second.wait()
            turned[...] = left[1].T
            load_branch.start()

        up_ref[:, rows_of(step - 4, 768)] = nn(turned[...], low_ref[...]).astype(BF16)

        @pl.when(step == 7)
        def _():
            for k in ORDER:
                parts["up"].core(k)

    @pl.when(step == 8)
    def _():
        load_mixed.wait()
        turned[...] = left[0].T
        load_normed.start()
        load_branch.wait()
        for d in range(4):
            out_ref[d] = nn(turned[...], left[1, :, 192 * d : 192 * d + 192]).astype(BF16)
        for k in ORDER:
            parts["out"].core(k)
        load_x.start()
        table_grad_start(table_ref, wall_small, wall_large)

    @pl.when((step >= 9) & (step < 15))
    def _():
        pair = step - 9
        cols = rows_of(pair, 128)
        for s in range(count):
            rows = slice(s * SLOT, s * SLOT + SLOT)
            query_grad, keys_grad, values_grad, scores_grads = attend_back(
                query_ref[rows, :], keys_ref[rows, :], values_ref[rows, :], attended_low_ref[rows, :],
                [probs_ref[half, s] for half in range(2)],
            )
            proj[0, rows, cols] = query_grad
            proj[1, rows, cols] = keys_grad
            proj[2, rows, cols] = values_grad
            chosen = jnp.where(buckets[s] == 0, 1.0, 0.0)
            for half in range(2):
                if s == 0:
                    grid_ref[0, half] = scores_grads[half] * chosen
                    grid_ref[1, half] = scores_grads[half] * (1.0 - chosen)
                else:
                    grid_ref[0, half] += scores_grads[half] * chosen
                    grid_ref[1, half] += scores_grads[half] * (1.0 - chosen)
        for half in range(2):
            table_grad_head(grid_ref, table_ref, wall_small, wall_large, 2 * pair + half, half)

    def lay_panel(d):
        def lay(pieces):
            at = 0
            for n, first, last in pieces:
                left[0, :, at : at + last - first] = proj[n, :, first:last]
                at += last - first

        cuts = (
            [(0, 0, 576)], [(0, 576, 768), (1, 0, 384)], [(1, 384, 768), (2, 0, 192)], [(2, 192, 768)],
        )
        for n, pieces in enumerate(cuts):
            pl.when(d == n)(functools.partial(lay, pieces))

    @pl.when((step >= 15) & (step < 19))
    def _():
        @pl.when(step == 15)
        def _():
            parts["down"].end()
            load_weight.start()
            load_normed.wait()
            turned[...] = left[0].T
            first_in[...] = jnp.zeros_like(first_in)

        d = step - 15
        lay_panel(d)
        grad = nn(turned[...], left[0, :, :576]).astype(BF16)
        qkv_a[d] = grad[:, :256]
        qkv_b[d] = jnp.concatenate([grad[:, 256:], jnp.zeros((D, 64), BF16)], 1)

        @pl.when(step == 15)
        def _():
            load_weight.wait()

        @pl.when(step == 18)
        def _():
            for k in ORDER:
                parts["qkv0"].core(k)
                parts["qkv1"].core(k)

        first_in[...] += nt(left[0, :, :576], down_ref[:, pl.ds(pl.multiple_of(768 * d, 768), 576)])

    @pl.when(step == 19)
    def _():
        progress(19)
        load_middle(0).start()
        load_x.wait()
        first_ref[...] = jnp.zeros_like(first_ref)

        def one_block(b, carry):
            rows = pl.ds(pl.multiple_of(b * SLOT, SLOT), SLOT)
            unit, inverse = standardize(left[1, rows, :].astype(F32))
            grad = first_in[rows, :]
            first_ref[0:1, :] += column_sum(grad * unit)
            first_ref[1:2, :] += column_sum(grad)
            back = norm_back(grad * vec_ref[0:1, :], unit, inverse)

            @pl.when(b + 1 < count)
            def _():
                load_middle(b + 1).start()

            load_middle(b).wait()
            input_grad_ref[rows, :] = (middle_ref[b % 2] + back).astype(BF16)
            return carry

        lax.fori_loop(0, count, one_block, 0)
        progress(20)
        table_grad_end(table_ref, wall_small, wall_large)
        pair = jnp.concatenate([tall_sum(proj.at[0]), tall_sum(proj.at[2])], 1)
        progress(21)
        pack_sums(sums_ref, first_ref, wide_ref, pair, table_ref, packed)
        small.begin()
        for n, (name, event, k) in enumerate(BACK_DRAIN):
            if n == len(BACK_DRAIN) // 2:
                small.cross()
            getattr(parts[name], event)(ORDER[k])
        parts["up"].end()
        parts["out"].end()
        total_ref[...] = small.end()
        parts["qkv0"].end()
        parts["qkv1"].end()


def backward(
    buckets, cotangent, act, second, low, mixed, branch, normed, probs, qkv, attended_low, vecs,
    sums, wide, tokens, middle_grad, weight,
):
    rows = cotangent.shape[0]
    count = rows // SLOT
    any_space = pl.BlockSpec(memory_space=ANY)

    def held(shape):
        return pl.BlockSpec(shape, lambda i: (0,) * len(shape))

    def pair(i):
        return jnp.clip(i - 9, 0, PAIRS - 1)

    def panel(base):
        return pl.BlockSpec((rows, 128), lambda i: (0, base + pair(i)))

    def act_panel(i):
        return (0, (lax.axis_index("fsdp") // 2 + 1 + jnp.minimum(i, 3)) % 4)

    outs = [(192, 384), (96, 768), (96, 192), (96, 576), (16, 384)]
    return pl.pallas_call(
        backward_kernel,
        grid=(20,),
        in_specs=[
            pl.BlockSpec(memory_space=pltpu.SMEM),
            any_space,
            pl.BlockSpec((rows, D), act_panel),
            any_space,
            pl.BlockSpec((rows, D), lambda i: (0, jnp.clip(i - 4, 0, 3))),
            any_space, any_space, any_space,
            pl.BlockSpec((2, count, SLOT, SLOT), lambda i: (pair(i), 0, 0, 0)),
            panel(0), panel(PAIRS), panel(2 * PAIRS), panel(0),
            held((8, D)), held((16, D)), held((8, FF)),
            any_space, any_space, any_space,
        ],
        out_specs=[held((rows, D))] + [held(shape) for shape in outs],
        out_shape=[jax.ShapeDtypeStruct((rows, D), BF16)]
        + [jax.ShapeDtypeStruct(shape, F32) for shape in outs],
        scratch_shapes=[
            pltpu.VMEM((2, rows, D), BF16),
            pltpu.VMEM((D, rows), BF16),
            pltpu.VMEM((2, SLOT, D), F32),
            pltpu.VMEM((rows, D), F32),
            pltpu.VMEM((3, rows, D), BF16),
            pltpu.VMEM((2, 2, SLOT, SLOT), F32),
            pltpu.VMEM((D, FF), BF16),
            pltpu.VMEM((D, FF), BF16),
            pltpu.VMEM((4, D, 192), BF16),
            pltpu.VMEM((4, D, 256), BF16),
            pltpu.VMEM((4, D, 384), BF16),
            pltpu.VMEM((16, TABLE), F32),
            pltpu.VMEM((8, D), F32),
            pltpu.VMEM((2, 128, 128), F32),
            pltpu.VMEM((4, 256, 128), F32),
            pltpu.VMEM((8, 16, 384), F32),
            pltpu.VMEM((7, 16, 384), F32),
            pltpu.VMEM((4, 16, 384), F32),
            pltpu.SemaphoreType.DMA((11,)),
            pltpu.SemaphoreType.DMA((11,)),
            pltpu.SemaphoreType.DMA((8,)),
            pltpu.SemaphoreType.DMA((2,)),
        ]
        + scatter_scratch("turned", 768) + scatter_scratch("wide", 768)
        + scatter_scratch("panel", 192) + scatter_scratch("panel", 256)[1:]
        + scatter_scratch("panel", 384)[1:],
        compiler_params=pltpu.CompilerParams(
            collective_id=2, has_side_effects=True, dimension_semantics=("arbitrary",),
            vmem_limit_bytes=BACK_LIMIT,
        ),
        name="backward",
    )(
        buckets, cotangent, act, second, low, mixed, branch, normed, probs, qkv, qkv, qkv,
        attended_low, vecs, sums, wide, tokens, middle_grad, weight,
    )


def emit_kernel(count, total_ref, *refs):
    sources = refs[:count]
    targets = refs[count : 2 * count]
    small = refs[2 * count : 2 * count + 14]
    held = refs[2 * count + 14 : -2]
    into, out = refs[-2:]
    loads = [
        pltpu.make_async_copy(src, dst, into.at[n]) for n, (src, dst) in enumerate(zip(sources, held))
    ]
    made = [
        pltpu.make_async_copy(src, dst, out.at[n]) for n, (src, dst) in enumerate(zip(held, targets))
    ]
    for each in loads:
        each.start()
    for load, each in zip(loads, made):
        load.wait()
        each.start()
    total = total_ref[...]
    for n in range(8):
        at = 96 * (n % 4)
        small[n][...] = total[n // 4 : n // 4 + 1, at : at + 96].reshape(96)
    for n in range(3):
        small[8 + n][...] = total[2 + n : 3 + n, :].reshape(384)
    small[11][...] = total[5:6, 0:192].reshape(192)
    small[12][...] = total[5:6, 192:204].reshape(HEADS)
    for n in range(PAIRS):
        small[13][2 * n : 2 * n + 1, :] = total[6 + n : 7 + n, 0:192]
        small[13][2 * n + 1 : 2 * n + 2, :] = total[6 + n : 7 + n, 192:384]
    for each in made:
        each.wait()


def emit(total, *large):
    vmem = pl.BlockSpec(memory_space=pltpu.VMEM)
    any_space = pl.BlockSpec(memory_space=ANY)
    small = [(96,)] * 8 + [(384,)] * 3 + [(192,), (HEADS,), (HEADS, 192)]
    return pl.pallas_call(
        functools.partial(emit_kernel, len(large)),
        in_specs=[vmem] + [any_space] * len(large),
        out_specs=[any_space] * len(large) + [vmem] * len(small),
        out_shape=[jax.ShapeDtypeStruct(part.shape, part.dtype) for part in large]
        + [jax.ShapeDtypeStruct(shape, F32) for shape in small],
        scratch_shapes=[pltpu.VMEM(part.shape, part.dtype) for part in large]
        + [pltpu.SemaphoreType.DMA((len(large),))] * 2,
        compiler_params=params(),
        name="emit",
    )(total, *large)


def gather_matrix(piece):
    rows = lax.all_gather(piece, "fsdp", axis=0, tiled=True)
    return lax.all_gather(rows, "dp", axis=1, tiled=True)


def scatter_matrix(grad):
    part = lax.psum_scatter(grad, "dp", scatter_dimension=1, tiled=True).astype(F32)
    return lax.psum_scatter(part, "fsdp", scatter_dimension=0, tiled=True)


def body(
    tokens, cotangent, lengths, buckets, qkv_weight, query_value_bias, out_weight, out_bias,
    up_weight, up_bias, down_weight, down_bias, first_gain, first_shift, mix_gain, mix_shift,
    second_gain, second_shift, hidden_gain, hidden_shift, head_scale, position_table,
):
    parts = lax.axis_size("fsdp")
    own_kernels = (parts, lax.axis_size("dp")) == (8, 4)
    narrow = [
        first_gain, first_shift, mix_gain, mix_shift, second_gain, second_shift, out_bias, down_bias,
    ]
    wide = [up_bias, hidden_gain, hidden_shift]
    a = D // parts
    b = FF // parts
    if own_kernels:
        (
            normed, qkv, probs, result, mixed, second, act, low, branch, middle_grad, attended_low,
            sums, wide_sums, vecs, qkv_full,
        ) = forward(
            lengths, buckets, tokens, cotangent, qkv_weight, out_weight, up_weight, down_weight.T,
            position_table.T, head_scale, narrow + wide + [query_value_bias],
        )
        input_grad, down_owned, up_owned, out_owned, qkv_owned, total = backward(
            buckets, cotangent, act, second, low, mixed, branch, normed, probs, qkv, attended_low,
            vecs, sums, wide_sums, tokens, middle_grad, qkv_full,
        )
        result, input_grad, qkv_owned, out_owned, up_owned, down_owned, *small = emit(
            total, result, input_grad, qkv_owned, out_owned, up_owned, down_owned
        )
        down_owned = down_owned.T
        narrow_owned = small[:8]
        wide_owned = small[8:11]
        pair_owned, scale_grad, table_owned = small[11], small[12], small[13].T
    else:
        packed = jnp.concatenate(
            [jnp.pad(jnp.stack(narrow), ((0, 0), (0, b - a))), jnp.stack(wide)]
            + [jnp.pad(query_value_bias, (0, b - 2 * a))[None], jnp.zeros((4, b), BF16)]
            + [jnp.pad(position_table.T, ((0, 4), (0, b - 2 * a)))]
        )
        scales = jnp.repeat(head_scale.astype(F32), HEAD_DIM)[None]
        gathered = lax.all_gather(packed, "fsdp", axis=0)
        qkv_full = gather_matrix(qkv_weight)
        out_full = gather_matrix(out_weight)
        up_full = gather_matrix(up_weight)
        down_full = gather_matrix(down_weight).T
        gathered = gathered.astype(F32)
        vecs = gathered[:, :8, :a].transpose(1, 0, 2).reshape(8, D)
        wides = jnp.pad(gathered[:, 8:11].transpose(1, 0, 2).reshape(3, FF), ((0, 5), (0, 0)))
        pair = gathered[:, 11, : 2 * a].reshape(1, 2 * D)
        table = gathered[:, 16:, : 2 * a].transpose(1, 0, 2).reshape(16, TABLE)
        qkv_bias = jnp.concatenate([pair[:, :D], jnp.zeros((1, D), F32), pair[:, D:]], 1)

        bias = build_bias(table)
        normed, qkv, probs, attended = attention(
            lengths, buckets, tokens, vecs, qkv_full, qkv_bias, bias
        )
        (
            result, mixed, second, act, low, branch, middle_grad, attended_low, sums, wide_sums,
        ) = feed_forward(tokens, attended, cotangent, out_full, up_full, down_full, vecs, wides, scales)
        down_grad = outer_product(cotangent, act, 512)
        up_grad = outer_product(second, low, 512)
        out_grad = outer_product(mixed, branch, 256)
        input_grad, grids, qkv_grad, pair_sums, first_sums = attention_back(
            buckets, probs, qkv, attended_low, normed, tokens, middle_grad, qkv_full, vecs
        )
        table_sums = table_grad(grids)
        qkv_natural = qkv_grad.reshape(PAIRS, D, 3, 128).transpose(1, 2, 0, 3).reshape(D, 3 * D)

        qkv_owned = scatter_matrix(qkv_natural)
        out_owned = scatter_matrix(out_grad)
        up_owned = scatter_matrix(up_grad)
        down_owned = scatter_matrix(down_grad.T)
        pair_grad = pair_sums[:, 0].reshape(PAIRS, 3, 128).transpose(1, 0, 2).reshape(3, D)
        pair_grad = jnp.concatenate([pair_grad[0], pair_grad[2]])
        narrow_sums = jnp.concatenate([first_sums[:2], sums[2:8]], 0)
        packed = jnp.concatenate(
            [
                narrow_sums.reshape(8, parts, a).transpose(1, 0, 2).reshape(parts, -1),
                wide_sums[:3].reshape(3, parts, b).transpose(1, 0, 2).reshape(parts, -1),
                pair_grad.reshape(parts, -1),
                table_sums[:HEADS].T.reshape(parts, -1),
            ],
            1,
        )
        owned = lax.psum(lax.psum_scatter(packed, "fsdp", scatter_dimension=0, tiled=True), "dp")[0]
        scale_grad = lax.psum(sums[8].reshape(HEADS, HEAD_DIM).sum(1), ("fsdp", "dp"))
        narrow_owned = owned[: 8 * a].reshape(8, a)
        edge = 8 * a
        wide_owned = owned[edge : edge + 3 * b].reshape(3, b)
        edge += 3 * b
        pair_owned = owned[edge : edge + 2 * a]
        edge += 2 * a
        table_owned = owned[edge:].reshape(TABLE // parts, HEADS)
    return (
        result, input_grad, qkv_owned, pair_owned, out_owned, narrow_owned[6], up_owned,
        wide_owned[0], down_owned, narrow_owned[7], narrow_owned[0], narrow_owned[1],
        narrow_owned[2], narrow_owned[3], narrow_owned[4], narrow_owned[5], wide_owned[1],
        wide_owned[2], scale_grad, table_owned,
    )


def solution(mesh):
    tokens = P(("fsdp", "dp"), None)
    sequences = P(("fsdp", "dp"))
    matrix = P("fsdp", "dp")
    vector = P("fsdp")
    table = P("fsdp", None)
    in_specs = (
        tokens, tokens, sequences, sequences, matrix, vector, matrix, vector, matrix, vector,
        matrix, vector, vector, vector, vector, vector, vector, vector, vector, vector, P(), table,
    )
    out_specs = (
        tokens, tokens, matrix, vector, matrix, vector, matrix, vector, matrix, vector, vector,
        vector, vector, vector, vector, vector, vector, vector, P(), table,
    )
    return jax.shard_map(body, mesh=mesh, in_specs=in_specs, out_specs=out_specs, check_vma=False)
```

```python
import functools

import jax
import jax.numpy as jnp
from jax import lax
from jax.experimental import pallas as pl
from jax.experimental.pallas import tpu as pltpu
from jax.sharding import PartitionSpec as P

D = 768
HEADS = 12
PAIRS = 6
HEAD_DIM = 64
FF = 3072
SLOT = 256
TABLE = 1536

EPS = 1e-05
MASKED = -1000000000.0
F32 = jnp.float32
BF16 = jnp.bfloat16
VMEM_LIMIT = 60 * 2**20
BACK_LIMIT = 60 * 2**20


def params(**more):
    return pltpu.CompilerParams(vmem_limit_bytes=VMEM_LIMIT, **more)


def nn(left, right):
    return lax.dot_general(left, right, (((1,), (0,)), ((), ())), preferred_element_type=F32)


def nt(left, right):
    return lax.dot_general(left, right, (((1,), (1,)), ((), ())), preferred_element_type=F32)


def standardize(values):
    center = values - jnp.mean(values, -1, keepdims=True)
    inverse = lax.rsqrt(jnp.mean(center * center, -1, keepdims=True) + EPS)
    return center * inverse, inverse


def norm_back(grad, unit, inverse):
    return inverse * (
        grad
        - jnp.mean(grad, -1, keepdims=True)
        - unit * jnp.mean(grad * unit, -1, keepdims=True)
    )


def column_sum(values):
    return jnp.sum(values, 0, keepdims=True)


def tall_sum(ref):
    def some(n, total):
        return total + column_sum(ref[rows_of(n, 64), :].astype(F32))

    return lax.fori_loop(0, ref.shape[0] // 64, some, jnp.zeros((1, ref.shape[1]), F32))


def split_low(values):
    high = values.astype(BF16)
    return high, (values - high.astype(F32)).astype(BF16)


def compaction(side, lanes):
    plane = lax.broadcasted_iota(jnp.int32, (1024, lanes), 0)
    lane = lax.broadcasted_iota(jnp.int32, (1024, lanes), 1)
    across = plane & 31
    return ((lane == side * (plane >> 5) + across) & (across < side)).astype(F32).astype(BF16)


def inside_grid(patches):
    row = lax.broadcasted_iota(jnp.int32, (SLOT, SLOT), 0)
    col = lax.broadcasted_iota(jnp.int32, (SLOT, SLOT), 1)
    return (row < patches) & (col < patches)


def store_tiles(ref, values):
    for k in range(ref.shape[0]):
        ref[k] = values[:, 128 * k : 128 * k + 128]


def load_tiles(ref):
    return jnp.concatenate([ref[k] for k in range(ref.shape[0])], 1)


def load_strided(ref, first, count):
    return jnp.concatenate(
        [ref[k, pl.ds(first, count, 16), :] for k in range(ref.shape[0])], 1
    )


def store_strided(ref, first, values):
    for k in range(ref.shape[0]):
        ref[k, pl.ds(first, values.shape[0], 16), :] = values[:, 128 * k : 128 * k + 128]


def bias_walls(table_ref, wall_small, wall_large, visual):
    plane = table_ref[:, 512:]
    shifted = [pltpu.roll(plane, (ic - 15) % 1024, 1) for ic in range(16)]
    stack = jnp.concatenate(shifted, 0).astype(BF16)
    store_tiles(wall_large, nn(stack, compaction(15, 512)))
    store_tiles(wall_small, nn(stack[:128], compaction(8, 256)))
    visual[...] = jnp.zeros_like(visual)


def bias_head(table_ref, out_ref, wall_small, wall_large, visual, h, carry):
    line = jnp.broadcast_to(table_ref[pl.ds(h, 1), :512], (SLOT, 512))
    textual = pltpu.roll(line, 257, 1, stride=1, stride_axis=0)[:, :SLOT]
    large = load_strided(wall_large, h, 16)
    for ir in range(15):
        visual[pl.ds(ir * 15, 16), :] = pltpu.roll(large, 512 - (15 - ir) * 15, 1)[:, :SLOT]
    out_ref[1, h] = jnp.where(inside_grid(225), visual[...], textual).astype(BF16)
    small = load_strided(wall_small, h, 8)
    rows = [pltpu.roll(small, 256 - (15 - ir) * 8, 1) for ir in range(8)]
    grid = jnp.concatenate(rows + [jnp.zeros((192, SLOT), F32)], 0)
    out_ref[0, h] = jnp.where(inside_grid(64), grid, textual).astype(BF16)
    return carry


def bias_kernel(table_ref, out_ref, wall_small, wall_large, visual):
    bias_walls(table_ref, wall_small, wall_large, visual)
    one_head = functools.partial(bias_head, table_ref, out_ref, wall_small, wall_large, visual)
    lax.fori_loop(0, HEADS, one_head, 0)


def build_bias(table):
    return pl.pallas_call(
        bias_kernel,
        out_shape=jax.ShapeDtypeStruct((2, HEADS, SLOT, SLOT), BF16),
        scratch_shapes=[
            pltpu.VMEM((2, 128, 128), F32),
            pltpu.VMEM((4, 256, 128), F32),
            pltpu.VMEM((SLOT, SLOT), F32),
        ],
        compiler_params=params(),
        name="build_bias",
    )(table)


def table_grad_start(out_ref, wall_small, wall_large):
    wall_small[...] = jnp.zeros_like(wall_small)
    wall_large[...] = jnp.zeros_like(wall_large)
    out_ref[...] = jnp.zeros_like(out_ref)


def table_grad_head(grid_ref, out_ref, wall_small, wall_large, h, slot):
    row = lax.broadcasted_iota(jnp.int32, (SLOT, SLOT), 0)
    col = lax.broadcasted_iota(jnp.int32, (SLOT, SLOT), 1)
    flip = (row + col == SLOT - 1).astype(F32).astype(BF16)
    lane = lax.broadcasted_iota(jnp.int32, (16, SLOT), 1)
    textual = jnp.where(inside_grid(64), 0.0, grid_ref[0, slot]) + jnp.where(
        inside_grid(225), 0.0, grid_ref[1, slot]
    )
    high, low = split_low(textual)
    flipped = nn(flip, high) + nn(flip, low)
    wide = jnp.concatenate([flipped, jnp.zeros((SLOT, SLOT), F32)], 1)
    out_ref[pl.ds(h, 1), :512] = column_sum(pltpu.roll(wide, 0, 1, stride=1, stride_axis=0))
    total = jnp.zeros((16, 512), F32)
    for ir in range(15):
        part = jnp.where(lane < 225, grid_ref[1, slot, pl.ds(ir * 15, 16), :], 0.0)
        part = jnp.concatenate([part, jnp.zeros((16, SLOT), F32)], 1)
        total = total + pltpu.roll(part, (15 - ir) * 15, 1)
    store_strided(wall_large, h, total)
    total = jnp.zeros((8, SLOT), F32)
    for ir in range(8):
        part = jnp.where(lane[:8] < 64, grid_ref[0, slot, pl.ds(ir * 8, 8), :], 0.0)
        total = total + pltpu.roll(part, (15 - ir) * 8, 1)
    store_strided(wall_small, h, total)


def table_grad_end(out_ref, wall_small, wall_large):
    high, low = split_low(load_tiles(wall_large))
    spread = compaction(15, 512)
    large = nt(high, spread) + nt(low, spread)
    high, low = split_low(load_tiles(wall_small))
    spread = compaction(8, 256)
    small = nt(high, spread) + nt(low, spread)
    plane = jnp.zeros((16, 1024), F32)
    for ic in range(15):
        part = large[ic * 16 : ic * 16 + 16]
        if ic < 8:
            part = part + small[ic * 16 : ic * 16 + 16]
        plane = plane + pltpu.roll(part, 15 - ic, 1)
    out_ref[:, 512:] = plane


def table_grad_kernel(grid_ref, out_ref, wall_small, wall_large):
    table_grad_start(out_ref, wall_small, wall_large)

    def one_head(h, carry):
        table_grad_head(grid_ref, out_ref, wall_small, wall_large, h, h)
        return carry

    lax.fori_loop(0, HEADS, one_head, 0)
    table_grad_end(out_ref, wall_small, wall_large)


def table_grad(grids):
    return pl.pallas_call(
        table_grad_kernel,
        out_shape=jax.ShapeDtypeStruct((16, TABLE), F32),
        scratch_shapes=[pltpu.VMEM((2, 128, 128), F32), pltpu.VMEM((4, 256, 128), F32)],
        compiler_params=params(),
        name="table_grad",
    )(grids)


def by_head(pair, axis):
    first = lax.broadcasted_iota(jnp.int32, pair.shape, 1) < HEAD_DIM
    return jnp.concatenate([jnp.where(first, pair, 0), jnp.where(first, 0, pair)], axis)


def attend(query, keys, values, bias, live):
    logits = nt(by_head(query, 0), keys)
    probs = []
    for half in range(2):
        rows = slice(SLOT * half, SLOT * half + SLOT)
        scores = jnp.where(live, logits[rows] + bias[half].astype(F32), MASKED)
        shifted = jnp.exp(scores - jnp.max(scores, -1, keepdims=True))
        probs.append((shifted * (1.0 / jnp.sum(shifted, -1, keepdims=True))).astype(BF16))
    return probs, nn(jnp.concatenate(probs, 1), by_head(values, 0))


def attend_back(query, keys, values, grad, probs):
    probs_grads = nt(by_head(grad, 0), values)
    grad_turned = grad.T
    query_turned = query.T
    keys_parts = []
    values_parts = []
    scores_grads = []
    lows = []
    for half in range(2):
        part = slice(HEAD_DIM * half, HEAD_DIM * half + HEAD_DIM)
        wide = probs[half].astype(F32)
        probs_grad = probs_grads[SLOT * half : SLOT * half + SLOT]
        values_parts.append(nn(grad_turned[part], probs[half]))
        scores_grad = wide * (probs_grad - jnp.sum(wide * probs_grad, -1, keepdims=True))
        scores_grads.append(scores_grad)
        lows.append(scores_grad.astype(BF16))
        keys_parts.append(nn(query_turned[part], lows[half]))
    query_grad = nn(jnp.concatenate(lows, 1), by_head(keys, 0)) * HEAD_DIM ** (-0.5)
    keys_grad = jnp.concatenate(keys_parts, 0).T
    values_grad = jnp.concatenate(values_parts, 0).T
    return query_grad.astype(BF16), keys_grad.astype(BF16), values_grad.astype(BF16), scores_grads


def attention_kernel(
    lengths, buckets, x_ref, vec_ref, weight_ref, qkv_bias_ref, bias_ref,
    normed_ref, qkv_ref, probs_ref, attended_ref,
):
    count = x_ref.shape[0] // SLOT

    def one_block(b, carry):
        rows = pl.ds(pl.multiple_of(b * SLOT, SLOT), SLOT)
        unit, inverse = standardize(x_ref[rows, :].astype(F32))
        normed_ref[rows, :] = (unit * vec_ref[0:1, :] + vec_ref[1:2, :]).astype(BF16)
        return carry

    lax.fori_loop(0, count, one_block, 0)

    def one_panel(n, carry):
        cols = pl.ds(pl.multiple_of(n * 256, 256), 256)
        out = nn(normed_ref[...], weight_ref[:, cols]) + qkv_bias_ref[:, cols]
        out = (out * jnp.where(n < 3, HEAD_DIM ** (-0.5), 1.0)).astype(BF16)
        qkv_ref[2 * n] = out[:, :128]
        qkv_ref[2 * n + 1] = out[:, 128:]
        return carry

    lax.fori_loop(0, 9, one_panel, 0)
    key_slot = lax.broadcasted_iota(jnp.int32, (SLOT, SLOT), 1)

    def one_unit(step, carry):
        pair = step // count
        s = step % count
        rows = pl.ds(pl.multiple_of(s * SLOT, SLOT), SLOT)
        bias = [bias_ref[buckets[s], 2 * pair + half] for half in range(2)]
        probs, out = attend(
            qkv_ref[pair, rows, :], qkv_ref[PAIRS + pair, rows, :], qkv_ref[2 * PAIRS + pair, rows, :],
            bias, key_slot < lengths[s],
        )
        for half in range(2):
            probs_ref[2 * pair + half, s] = probs[half]
        attended_ref[rows, pl.ds(pl.multiple_of(pair * 128, 128), 128)] = out
        return carry

    lax.fori_loop(0, PAIRS * count, one_unit, 0)


def attention(lengths, buckets, tokens, vecs, weight, qkv_bias, bias):
    rows = tokens.shape[0]
    count = rows // SLOT
    smem = pl.BlockSpec(memory_space=pltpu.SMEM)
    vmem = pl.BlockSpec(memory_space=pltpu.VMEM)
    return pl.pallas_call(
        attention_kernel,
        in_specs=[smem, smem] + [vmem] * 5,
        out_shape=[
            jax.ShapeDtypeStruct((rows, D), BF16),
            jax.ShapeDtypeStruct((3 * PAIRS, rows, 128), BF16),
            jax.ShapeDtypeStruct((HEADS, count, SLOT, SLOT), BF16),
            jax.ShapeDtypeStruct((rows, D), F32),
        ],
        compiler_params=params(),
        name="attention_forward",
    )(lengths, buckets, tokens, vecs, weight, qkv_bias, bias)


PANEL = 512


def feed_kernel(*refs):
    @pl.when(pl.program_id(0) == 0)
    def _():
        for ref in refs[17:19]:
            ref[...] = jnp.zeros_like(ref)

    feed_block(*refs, lambda: None)


def feed_block(
    x_ref, attended_ref, cot_ref, out_w, up_w, down_w, vec_ref, wide_ref, scale_ref,
    result_ref, mixed_ref, second_ref, act_ref, low_ref, branch_ref, middle_grad_ref,
    attended_low_ref, sums_ref, wide_sums_ref,
    gelu_ref, slope_ref, grad_ref, before_down,
):
    def add(row, values):
        sums_ref[row : row + 1, :] += column_sum(values)

    rows = x_ref.shape[0]
    attended = attended_ref[...]
    mix_unit, mix_inverse = standardize(attended * scale_ref[...])
    mixed = (mix_unit * vec_ref[2:3, :] + vec_ref[3:4, :]).astype(BF16)
    mixed_ref[...] = mixed
    middle = x_ref[...].astype(F32) + nn(mixed, out_w[...]) + vec_ref[6:7, :]
    second_unit, second_inverse = standardize(middle)
    second = (second_unit * vec_ref[4:5, :] + vec_ref[5:6, :]).astype(BF16)
    second_ref[...] = second
    cot = cot_ref[...]

    panels = [slice(n, n + PANEL) for n in range(0, FF, PANEL)]
    total = jnp.zeros((rows, 1), F32)
    for cols in panels:
        hidden = nn(second, up_w[:, cols]) + wide_ref[0:1, cols]
        cdf = 0.5 + 0.5 * lax.erf(hidden * 0.7071067811865476)
        gelu = hidden * cdf
        gelu_ref[:, cols] = gelu
        slope_ref[:, cols] = cdf + hidden * (jnp.exp(-0.5 * hidden * hidden) * 0.3989422804014327)
        total = total + jnp.sum(gelu, -1, keepdims=True)
    mean = total * (1.0 / FF)
    total = jnp.zeros((rows, 1), F32)
    for cols in panels:
        center = gelu_ref[:, cols] - mean
        total = total + jnp.sum(center * center, -1, keepdims=True)
    inverse = lax.rsqrt(total * (1.0 / FF) + EPS)
    before_down()
    result = middle + vec_ref[7:8, :]
    first = jnp.zeros((rows, 1), F32)
    second_moment = jnp.zeros((rows, 1), F32)
    for cols in panels:
        unit = (gelu_ref[:, cols] - mean) * inverse
        gelu_ref[:, cols] = unit
        act = (unit * wide_ref[1:2, cols] + wide_ref[2:3, cols]).astype(BF16)
        act_ref[:, cols] = act
        result = result + nt(act, down_w[:, cols])
        act_grad = nn(cot, down_w[:, cols])
        wide_sums_ref[1:2, cols] += column_sum(act_grad * unit)
        wide_sums_ref[2:3, cols] += column_sum(act_grad)
        grad = act_grad * wide_ref[1:2, cols]
        grad_ref[:, cols] = grad
        first = first + jnp.sum(grad, -1, keepdims=True)
        second_moment = second_moment + jnp.sum(grad * unit, -1, keepdims=True)
    result_ref[...] = result.astype(BF16)
    first = first * (1.0 / FF)
    second_moment = second_moment * (1.0 / FF)
    second_in = jnp.zeros((rows, D), F32)
    for cols in panels:
        grad = inverse * (grad_ref[:, cols] - first - gelu_ref[:, cols] * second_moment)
        low = (grad * slope_ref[:, cols]).astype(BF16)
        low_ref[:, cols] = low
        wide_sums_ref[0:1, cols] += column_sum(low.astype(F32))
        second_in = second_in + nt(low, up_w[:, cols])
    add(4, second_in * second_unit)
    add(5, second_in)
    cot_wide = cot.astype(F32)
    add(7, cot_wide)
    middle_grad = cot_wide + norm_back(second_in * vec_ref[4:5, :], second_unit, second_inverse)
    middle_grad_ref[...] = middle_grad
    branch = middle_grad.astype(BF16)
    branch_ref[...] = branch
    add(6, branch.astype(F32))
    mixed_in = nt(branch, out_w[...])
    add(2, mixed_in * mix_unit)
    add(3, mixed_in)
    grad = norm_back(mixed_in * vec_ref[2:3, :], mix_unit, mix_inverse)
    add(8, grad * attended)
    attended_low_ref[...] = (grad * scale_ref[...]).astype(BF16)


def feed_forward(tokens, attended, cotangent, out_w, up_w, down_w, vecs, wide, scales):
    rows = tokens.shape[0]
    tile = 256
    block = pl.BlockSpec((tile, D), lambda i: (i, 0))
    wide_block = pl.BlockSpec((tile, FF), lambda i: (i, 0))

    def whole(shape):
        return pl.BlockSpec(shape, lambda i: (0, 0), pipeline_mode=pl.Buffered(1))

    def held(shape):
        return pl.BlockSpec(shape, lambda i: (0, 0))

    return pl.pallas_call(
        feed_kernel,
        grid=(rows // tile,),
        in_specs=[block] * 3
        + [whole((D, D)), whole((D, FF)), whole((D, FF)), whole((8, D)), whole((8, FF)), whole((1, D))],
        out_specs=[block, block, block, wide_block, wide_block, block, block, block]
        + [held((16, D)), held((8, FF))],
        out_shape=[
            jax.ShapeDtypeStruct((rows, D), BF16),
            jax.ShapeDtypeStruct((rows, D), BF16),
            jax.ShapeDtypeStruct((rows, D), BF16),
            jax.ShapeDtypeStruct((rows, FF), BF16),
            jax.ShapeDtypeStruct((rows, FF), BF16),
            jax.ShapeDtypeStruct((rows, D), BF16),
            jax.ShapeDtypeStruct((rows, D), F32),
            jax.ShapeDtypeStruct((rows, D), BF16),
            jax.ShapeDtypeStruct((16, D), F32),
            jax.ShapeDtypeStruct((8, FF), F32),
        ],
        scratch_shapes=[pltpu.VMEM((tile, FF), F32)] * 3,
        compiler_params=params(dimension_semantics=("arbitrary",)),
        name="feed_forward",
    )(tokens, attended, cotangent, out_w, up_w, down_w, vecs, wide, scales)


def outer_kernel(left_ref, right_ref, out_ref, turned):
    @pl.when(pl.program_id(0) == 0)
    def _():
        turned[...] = left_ref[...].T

    out_ref[...] = nn(turned[...], right_ref[...]).astype(BF16)


def outer_product(left, right, panel):
    rows, width = left.shape
    cols = right.shape[1]
    return pl.pallas_call(
        outer_kernel,
        grid=(cols // panel,),
        in_specs=[
            pl.BlockSpec((rows, width), lambda i: (0, 0), pipeline_mode=pl.Buffered(1)),
            pl.BlockSpec((rows, panel), lambda i: (0, i)),
        ],
        out_specs=pl.BlockSpec((width, panel), lambda i: (0, i)),
        out_shape=jax.ShapeDtypeStruct((width, cols), BF16),
        scratch_shapes=[pltpu.VMEM((width, rows), BF16)],
        compiler_params=params(dimension_semantics=("arbitrary",)),
        name="weight_grad",
    )(left, right)


def attention_back_kernel(
    buckets, probs_ref, query_ref, keys_ref, values_ref, low_ref, normed_ref, x_ref, middle_ref,
    weight_q, weight_k, weight_v, vec_ref,
    input_grad_ref, grid_ref, weight_grad_ref, pair_ref, sums_ref,
    turned, first_in, proj_ref,
):
    count = x_ref.shape[0] // SLOT
    step = pl.program_id(0)

    @pl.when(step == 0)
    def _():
        turned[...] = normed_ref[...].T
        first_in[...] = jnp.zeros_like(first_in)

    grid_ref[...] = jnp.zeros_like(grid_ref)

    def one_sequence(s, carry):
        rows = pl.ds(pl.multiple_of(s * SLOT, SLOT), SLOT)
        query_grad, keys_grad, values_grad, scores_grads = attend_back(
            query_ref[0, rows, :], keys_ref[0, rows, :], values_ref[0, rows, :], low_ref[rows, :],
            [probs_ref[half, s] for half in range(2)],
        )
        small = jnp.where(buckets[s] == 0, 1.0, 0.0)
        for half in range(2):
            grid_ref[0, half] += scores_grads[half] * small
            grid_ref[1, half] += scores_grads[half] * (1.0 - small)
        proj_ref[rows, 0:128] = query_grad
        proj_ref[rows, 128:256] = keys_grad
        proj_ref[rows, 256:384] = values_grad
        return carry

    lax.fori_loop(0, count, one_sequence, 0)
    proj = proj_ref[...]
    weight_grad_ref[0] = nn(turned[...], proj).astype(BF16)
    pair_ref[0] = jnp.broadcast_to(column_sum(proj.astype(F32)), (8, 384))
    weights = jnp.concatenate([weight_q[...], weight_k[...], weight_v[...]], 1)
    first_in[...] += nt(proj, weights)

    @pl.when(step == PAIRS - 1)
    def _():
        sums_ref[...] = jnp.zeros_like(sums_ref)

        def one_block(b, carry):
            rows = pl.ds(pl.multiple_of(b * SLOT, SLOT), SLOT)
            unit, inverse = standardize(x_ref[rows, :].astype(F32))
            grad = first_in[rows, :]
            sums_ref[0:1, :] += column_sum(grad * unit)
            sums_ref[1:2, :] += column_sum(grad)
            back = norm_back(grad * vec_ref[0:1, :], unit, inverse)
            input_grad_ref[rows, :] = (middle_ref[rows, :] + back).astype(BF16)
            return carry

        lax.fori_loop(0, count, one_block, 0)


def attention_back(buckets, probs, qkv, attended_low, normed, tokens, middle_grad, weight, vecs):
    rows = tokens.shape[0]
    count = rows // SLOT

    def whole(shape):
        return pl.BlockSpec(shape, lambda i: (0,) * len(shape), pipeline_mode=pl.Buffered(1))

    def held(shape):
        return pl.BlockSpec(shape, lambda i: (0,) * len(shape))

    def panel(base):
        return pl.BlockSpec((1, rows, 128), lambda i: (base + i, 0, 0))

    def weight_panel(base):
        return pl.BlockSpec((D, 128), lambda i: (0, base + i))

    return pl.pallas_call(
        attention_back_kernel,
        grid=(PAIRS,),
        in_specs=[
            pl.BlockSpec(memory_space=pltpu.SMEM),
            pl.BlockSpec((2, count, SLOT, SLOT), lambda i: (i, 0, 0, 0)),
            panel(0), panel(PAIRS), panel(2 * PAIRS),
            pl.BlockSpec((rows, 128), lambda i: (0, i)),
            whole((rows, D)), whole((rows, D)), whole((rows, D)),
            weight_panel(0), weight_panel(PAIRS), weight_panel(2 * PAIRS),
            whole((8, D)),
        ],
        out_specs=[
            held((rows, D)),
            pl.BlockSpec((2, 2, SLOT, SLOT), lambda i: (0, i, 0, 0)),
            pl.BlockSpec((1, D, 384), lambda i: (i, 0, 0)),
            pl.BlockSpec((1, 8, 384), lambda i: (i, 0, 0)),
            held((8, D)),
        ],
        out_shape=[
            jax.ShapeDtypeStruct((rows, D), BF16),
            jax.ShapeDtypeStruct((2, HEADS, SLOT, SLOT), F32),
            jax.ShapeDtypeStruct((PAIRS, D, 384), BF16),
            jax.ShapeDtypeStruct((PAIRS, 8, 384), F32),
            jax.ShapeDtypeStruct((8, D), F32),
        ],
        scratch_shapes=[
            pltpu.VMEM((D, rows), BF16),
            pltpu.VMEM((rows, D), F32),
            pltpu.VMEM((rows, 384), BF16),
        ],
        compiler_params=params(dimension_semantics=("arbitrary",)),
        name="attention_backward",
    )(buckets, probs, qkv, qkv, qkv, attended_low, normed, tokens, middle_grad, weight, weight, weight, vecs)


MESH = pl.DeviceIdType.MESH
ANY = pl.ANY


class Place:
    def __init__(self):
        fsdp = lax.axis_index("fsdp")
        dp = lax.axis_index("dp")
        self.z, self.y, self.x, self.core = fsdp // 2, fsdp % 2, dp // 2, dp % 2

    def at(self, z=None, y=None, x=None, core=None):
        z = self.z if z is None else z
        y = self.y if y is None else y
        x = self.x if x is None else x
        core = self.core if core is None else core
        return (z * 2 + y, x * 2 + core)

    def greet(self):
        barrier = pltpu.get_barrier_semaphore()
        peers = [self.at(z=(self.z + k) % 4, y=self.y) for k in range(1, 4)]
        peers += [self.at(z=(self.z + k) % 4, y=1 - self.y) for k in range(4)]
        peers += [
            self.at(x=1 - self.x),
            self.at(core=1 - self.core),
            self.at(x=1 - self.x, core=1 - self.core),
        ]
        for peer in peers:
            pl.semaphore_signal(barrier, inc=1, device_id=peer, device_id_type=MESH)

    def meet(self):
        pl.semaphore_wait(pltpu.get_barrier_semaphore(), 10)


def remote(src, dst, send, recv, peer):
    return pltpu.make_async_remote_copy(
        src_ref=src, dst_ref=dst, send_sem=send, recv_sem=recv, device_id=peer, device_id_type=MESH
    )


def rows_of(first, size):
    return pl.ds(pl.multiple_of(first * size, size), size)


def chunk(kind, ref, r, d):
    if kind == "panel":
        return ref.at[d, rows_of(r, 96), :]
    if kind == "wide":
        return ref.at[rows_of(r, 96), rows_of(d, 768)]
    return ref.at[rows_of(d, 192), rows_of(r, 384)]


class Gather:
    def __init__(self, place, pieces, fulls, send, recv, local):
        self.place, self.pieces, self.fulls = place, pieces, fulls
        self.send, self.recv, self.local = send, recv, local
        self.made = {}

    def slot(self, w, z, y, x):
        return chunk(GATHER_KINDS[w], self.fulls[w], z * 2 + y, x * 2 + self.place.core)

    def copy(self, w, index, src, dst, peer):
        self.made[w, index] = remote(src, dst, self.send.at[w, index], self.recv.at[w, index], peer)
        return self.made[w, index]

    def sources(self, w, k):
        here = self.place
        over_x = (k + GATHER_TURN[w]) % 2 == 0
        near = (here.y, 1 - here.x) if over_x else (1 - here.y, here.x)
        far = (1 - here.y, here.x) if over_x else (here.y, 1 - here.x)
        upper = here.z // 2
        depth = here.z + upper * (3 - 2 * here.z)
        z = k - depth if k == 1 else k
        z = z + upper * (3 - 2 * z) if k else here.z
        return z, near, far

    def plan(self, w):
        here = self.place
        own = self.slot(w, here.z, here.y, here.x)
        self.made[w, "keep"] = pltpu.make_async_copy(self.pieces[w], own, self.local.at[w])
        sibling = here.at(core=1 - here.core)
        pair = here.at(z=here.z + 1 - 2 * (here.z % 2))
        across = here.at(z=3 - here.z)
        for k in range(4):
            z, near, far = self.sources(w, k)
            mine = self.slot(w, z, here.y, here.x)
            src = mine if k else self.pieces[w]
            if k == 0:
                self.copy(w, 1, src, mine, pair)
                self.copy(w, 2, src, mine, across)
            elif k == 1:
                self.copy(w, 3, src, mine, across)
            else:
                self.made[w, "on", k] = remote(
                    src, mine, self.send.at[w, 30 + k], self.recv.at[w, k], pair
                )
            self.copy(w, 4 + k, src, mine, here.at(y=near[0], x=near[1]))
            passed = self.slot(w, z, *near)
            self.copy(w, 8 + 2 * k, src, mine, here.at(y=far[0], x=far[1]))
            self.copy(w, 9 + 2 * k, passed, passed, here.at(y=far[0], x=far[1]))
            third = self.slot(w, z, *far)
            fourth = self.slot(w, z, 1 - here.y, 1 - here.x)
            for n, part in enumerate((src, passed, third, fourth)):
                dst = mine if n == 0 else part
                self.copy(w, 16 + 4 * k + n, part, dst, sibling)

    def when_middle(self, act):
        pl.when(self.place.z * (3 - self.place.z) > 0)(act)

    def begin(self, w, k=0):
        self.made[w, "keep"].start()
        self.made[w, 1].start()
        self.when_middle(lambda: self.made[w, 2].start())

    def relay(self, w, k):
        def on():
            self.made[w, k].wait_recv()
            (self.made[w, 3] if k == 1 else self.made[w, "on", k]).start()

        self.when_middle(on)

    def first(self, w, k):
        if k:
            pl.when(self.place.z * (3 - self.place.z) == 0)(self.made[w, k].wait_recv)
        self.made[w, 4 + k].start()
        self.made[w, 16 + 4 * k].start()

    def second(self, w, k):
        self.made[w, 4 + k].wait_recv()
        self.made[w, 8 + 2 * k].start()
        self.made[w, 9 + 2 * k].start()
        self.made[w, 17 + 4 * k].start()

    def third(self, w, k):
        for n in range(2):
            self.made[w, 8 + 2 * k + n].wait_recv()
            self.made[w, 18 + 4 * k + n].start()

    def finish(self, w):
        for n in range(16):
            self.made[w, 16 + n].wait_recv()
        for n in [1] + list(range(4, 32)):
            self.made[w, n].wait_send()

        def passed_on():
            for made in (self.made[w, 2], self.made[w, 3], self.made[w, "on", 2], self.made[w, "on", 3]):
                made.wait_send()

        self.when_middle(passed_on)
        self.made[w, "keep"].wait()


MIXED, UP, DOWN = range(3)
GATHER_TURN = (0, 1, 0)
GATHER_KINDS = ("wide", "wide", "turned")


BEGIN, RELAY, FIRST, SECOND, THIRD = "begin", "relay", "first", "second", "third"
GATHER_SCHEDULE = [
    [(BEGIN, MIXED, 0), (FIRST, MIXED, 0), (FIRST, UP, 0)],
    [(FIRST, DOWN, 0)],
    [(BEGIN, DOWN, 0)],
    [],
    [],
    [(SECOND, MIXED, 0), (RELAY, MIXED, 1), (FIRST, MIXED, 1), (RELAY, MIXED, 2), (SECOND, UP, 0)],
    [
        (BEGIN, UP, 0),
        (RELAY, DOWN, 1),
        (FIRST, DOWN, 1),
        (FIRST, MIXED, 2),
        (RELAY, MIXED, 3),
        (RELAY, UP, 1),
        (THIRD, MIXED, 0),
        (FIRST, UP, 1),
        (RELAY, UP, 2),
        (SECOND, MIXED, 1),
        (FIRST, MIXED, 3),
        (SECOND, MIXED, 2),
        (RELAY, DOWN, 3),
        (FIRST, UP, 2),
        (SECOND, UP, 1),
        (RELAY, UP, 3),
        (SECOND, MIXED, 3),
        (FIRST, DOWN, 3),
        (FIRST, UP, 3),
        (THIRD, MIXED, 1),
        (THIRD, MIXED, 2),
        (SECOND, UP, 2),
        (THIRD, MIXED, 3),
    ],
    [],
    [],
    [(THIRD, UP, 1)],
    [(SECOND, UP, 3), (RELAY, DOWN, 2), (SECOND, DOWN, 1)],
    [],
    [(THIRD, UP, 0), (THIRD, UP, 2), (SECOND, DOWN, 0)],
    [],
    [(FIRST, DOWN, 2)],
    [],
    [(THIRD, UP, 3), (SECOND, DOWN, 3)],
    [(THIRD, DOWN, 1)],
    [],
    [(SECOND, DOWN, 2)],
    [(THIRD, DOWN, 0), (THIRD, DOWN, 3), (THIRD, DOWN, 2)],
]


def lined(ref, row, width):
    return jnp.concatenate([ref[f, row : row + 1, :width].astype(F32) for f in range(8)], 1)


def forward_kernel(
    lengths, buckets, x_ref, cot_ref, qkv_p, out_p, up_p, down_t, table_p, head_scale, *refs,
):
    vectors = refs[:12]
    (
    normed_ref, qkv_ref, probs_ref, result_ref, mixed_ref, second_ref, act_ref, low_ref, branch_ref,
    middle_grad_ref, attended_low_ref, sums_ref, wide_sums_ref, vec_ref, qkv_out,
    mixed_p, scale_ref, vec_wide, vec_p, qkv_w, up_w, down_w, vec_f, out_w, bias_ref, wide_ref, qkv_bias_ref, table_ref,
    wall_small, wall_large, visual, attended_ref, gelu_ref, slope_ref, grad_ref,
    send, recv, local, small_send, small_recv, small_local, qkv_sem,
    ) = refs[12:]
    step = pl.program_id(0)
    count = pl.num_programs(0) // 2
    place = Place()
    gather = Gather(place, (mixed_p, up_p, down_t), (qkv_w, up_w, down_w), send, recv, local)
    for w in range(3):
        gather.plan(w)
    f = place.z * 2 + place.y
    small = [pltpu.make_async_copy(vec_p, vec_f.at[f], small_local)]
    for k in range(1, 8):
        peer = (f + k) % 8
        small.append(
            remote(
                vec_p, vec_f.at[f], small_send.at[k], small_recv.at[k],
                place.at(z=peer // 2, y=peer % 2),
            )
        )
    keep_qkv = pltpu.make_async_copy(qkv_w, qkv_out, qkv_sem)

    def follow(point):
        for name, w, k in GATHER_SCHEDULE[point]:
            getattr(gather, name)(w, k)

    @pl.when(step == 0)
    def _():
        place.greet()
        vec_wide[...] = jnp.zeros_like(vec_wide)
        for n, vector in enumerate(vectors):
            size = vector.shape[0]
            vec_wide[n : n + 1, :size] = vector[...].astype(F32).reshape(1, size)
        vec_wide[16 : 16 + HEADS, :192] = table_p[...].astype(F32)
        vec_wide[12:13, :HEADS] = head_scale[...].astype(F32).reshape(1, HEADS)
        vec_p[...] = vec_wide[...].astype(BF16)
        head = lax.broadcasted_iota(jnp.int32, (128, D), 0)
        spread = (head == lax.broadcasted_iota(jnp.int32, (128, D), 1) // HEAD_DIM).astype(F32)
        scale_ref[...] = nn(vec_p[...], jnp.concatenate([spread, jnp.zeros((256, D), F32)], 0).astype(BF16))[8:16]
        mixed_p[:, :576] = qkv_p[...]
        mixed_p[:, 576:] = out_p[...]
        place.meet()
        for made in small:
            made.start()
        follow(0)
        for made in small:
            made.wait()
        for n in range(8):
            vec_ref[n : n + 1, :] = lined(vec_f, n, 96)
        for n in range(3):
            wide_ref[n : n + 1, :] = lined(vec_f, 8 + n, 384)
        pair = lined(vec_f, 11, 192)
        qkv_bias_ref[0:1, :] = jnp.concatenate([pair[:, :D], jnp.zeros((1, D), F32), pair[:, D:]], 1)
        lane = lax.broadcasted_iota(jnp.int32, (1, 3 * D), 1)
        qkv_bias_ref[1:2, :] = jnp.where(lane < D, HEAD_DIM ** (-0.5), 1.0)
        table_ref[...] = jnp.concatenate([vec_f[n, 16:32, :192].astype(F32) for n in range(8)], 1)
        bias_walls(table_ref, wall_small, wall_large, visual)
        heads = functools.partial(bias_head, table_ref, bias_ref, wall_small, wall_large, visual)
        for n, last in enumerate((2, 4, 6, 9, HEADS)):
            follow(1 + n)
            lax.fori_loop((0, 2, 4, 6, 9)[n], last, heads, 0)
        follow(6)
        gather.finish(MIXED)
        keep_qkv.start()
        sums_ref[...] = jnp.zeros_like(sums_ref)
        wide_sums_ref[...] = jnp.zeros_like(wide_sums_ref)

    def progress(spot):
        for s in range(count):
            if GATHER_SCHEDULE[7 + 3 * s + spot]:
                pl.when(step == s)(functools.partial(follow, 7 + 3 * s + spot))

    @pl.when(step < count)
    def _():
        rows = pl.ds(pl.multiple_of(step * SLOT, SLOT), SLOT)
        progress(0)
        unit, inverse = standardize(x_ref[...].astype(F32))
        normed = (unit * vec_ref[0:1, :] + vec_ref[1:2, :]).astype(BF16)
        normed_ref[...] = normed
        for d in range(4):
            cols = slice(576 * d, 576 * d + 576)
            out = (nn(normed, qkv_w[:, 768 * d : 768 * d + 576]) + qkv_bias_ref[0:1, cols]) * qkv_bias_ref[1:2, cols]
            qkv_ref[:, cols] = out.astype(BF16)
        live = lax.broadcasted_iota(jnp.int32, (SLOT, SLOT), 1) < lengths[step]
        bucket = buckets[step]
        for pair in range(PAIRS):
            if pair % 3 == 0:
                progress(1 + pair // 3)
            query = qkv_ref[:, 128 * pair : 128 * pair + 128]
            keys = qkv_ref[:, D + 128 * pair : D + 128 * pair + 128]
            values = qkv_ref[:, 2 * D + 128 * pair : 2 * D + 128 * pair + 128]
            bias = [bias_ref[bucket, 2 * pair + half] for half in range(2)]
            probs, out = attend(query, keys, values, bias, live)
            for half in range(2):
                probs_ref[2 * pair + half, 0] = probs[half]
            attended_ref[rows, 128 * pair : 128 * pair + 128] = out

    @pl.when(step == count)
    def _():
        follow(7 + 3 * count)
        gather.finish(UP)
        for d in range(4):
            out_w[:, 192 * d : 192 * d + 192] = qkv_w[:, 768 * d + 576 : 768 * d + 768]

    @pl.when(step >= count)
    def _():
        rows = pl.ds(pl.multiple_of((step - count) * SLOT, SLOT), SLOT)

        def wait_down():
            @pl.when(step == count)
            def _():
                follow(8 + 3 * count)
                gather.finish(DOWN)

        feed_block(
            x_ref, attended_ref.at[rows, :], cot_ref, out_w, up_w, down_w, vec_ref, wide_ref,
            scale_ref.at[4:5, :],
            result_ref, mixed_ref, second_ref, act_ref, low_ref, branch_ref, middle_grad_ref,
            attended_low_ref, sums_ref, wide_sums_ref, gelu_ref, slope_ref, grad_ref, wait_down,
        )

    @pl.when(step == 2 * count - 1)
    def _():
        keep_qkv.wait()


def forward(lengths, buckets, tokens, cotangent, qkv_p, out_p, up_p, down_p, table_p, head_scale, vectors):
    rows = tokens.shape[0]
    count = rows // SLOT
    smem = pl.BlockSpec(memory_space=pltpu.SMEM)

    def early(shape):
        return pl.BlockSpec(shape, lambda i: (jnp.minimum(i, count - 1),) + (0,) * (len(shape) - 1))

    def late(shape):
        return pl.BlockSpec(shape, lambda i: (jnp.maximum(i - count, 0),) + (0,) * (len(shape) - 1))

    def held(shape):
        return pl.BlockSpec(shape, lambda i: (0,) * len(shape))

    block = (SLOT, D)
    wide = (SLOT, FF)
    return pl.pallas_call(
        forward_kernel,
        grid=(2 * count,),
        in_specs=[
            smem, smem, pl.BlockSpec(block, lambda i: (i % count, 0)), late(block),
            held((96, 576)), held((96, 192)), pl.BlockSpec(memory_space=ANY),
            pl.BlockSpec(memory_space=ANY), held((HEADS, 192)), held((HEADS,)),
        ]
        + [held(vector.shape) for vector in vectors],
        out_specs=[
            early(block), early((SLOT, 3 * D)),
            pl.BlockSpec((HEADS, 1, SLOT, SLOT), lambda i: (0, jnp.minimum(i, count - 1), 0, 0)),
            late(block), late(block), late(block), late(wide), late(wide), late(block), late(block),
            late(block), held((16, D)), held((8, FF)), held((8, D)), pl.BlockSpec(memory_space=ANY),
        ],
        out_shape=[
            jax.ShapeDtypeStruct((rows, D), BF16),
            jax.ShapeDtypeStruct((rows, 3 * D), BF16),
            jax.ShapeDtypeStruct((HEADS, count, SLOT, SLOT), BF16),
            jax.ShapeDtypeStruct((rows, D), BF16),
            jax.ShapeDtypeStruct((rows, D), BF16),
            jax.ShapeDtypeStruct((rows, D), BF16),
            jax.ShapeDtypeStruct((rows, FF), BF16),
            jax.ShapeDtypeStruct((rows, FF), BF16),
            jax.ShapeDtypeStruct((rows, D), BF16),
            jax.ShapeDtypeStruct((rows, D), F32),
            jax.ShapeDtypeStruct((rows, D), BF16),
            jax.ShapeDtypeStruct((16, D), F32),
            jax.ShapeDtypeStruct((8, FF), F32),
            jax.ShapeDtypeStruct((8, D), F32),
            jax.ShapeDtypeStruct((D, FF), BF16),
        ],
        scratch_shapes=[
            pltpu.VMEM((96, D), BF16),
            pltpu.VMEM((8, D), F32),
            pltpu.VMEM((32, 384), F32),
            pltpu.VMEM((32, 384), BF16),
            pltpu.VMEM((D, FF), BF16),
            pltpu.VMEM((D, FF), BF16),
            pltpu.VMEM((D, FF), BF16),
            pltpu.VMEM((8, 32, 384), BF16),
            pltpu.VMEM((D, D), BF16),
            pltpu.VMEM((2, HEADS, SLOT, SLOT), BF16),
            pltpu.VMEM((8, FF), F32),
            pltpu.VMEM((8, 3 * D), F32),
            pltpu.VMEM((16, TABLE), F32),
            pltpu.VMEM((2, 128, 128), F32),
            pltpu.VMEM((4, 256, 128), F32),
            pltpu.VMEM((SLOT, SLOT), F32),
            pltpu.VMEM((rows, D), F32),
            pltpu.VMEM(wide, F32),
            pltpu.VMEM(wide, F32),
            pltpu.VMEM(wide, F32),
            pltpu.SemaphoreType.DMA((3, 34)),
            pltpu.SemaphoreType.DMA((3, 32)),
            pltpu.SemaphoreType.DMA((3,)),
            pltpu.SemaphoreType.DMA((8,)),
            pltpu.SemaphoreType.DMA((8,)),
            pltpu.SemaphoreType.DMA,
            pltpu.SemaphoreType.DMA,
        ],
        compiler_params=params(
            collective_id=1, has_side_effects=True, dimension_semantics=("arbitrary",)
        ),
        name="forward",
    )(lengths, buckets, tokens, cotangent, qkv_p, out_p, up_p, down_p, table_p, head_scale, *vectors)


ORDER = (1, 2, 3, 0)


class Scatter:
    def __init__(self, place, kind, grad, out, buffers, flip=0, offset=0):
        self.place, self.kind, self.grad, self.out = place, kind, grad, out
        self.flip, self.offset = flip, offset
        self.cores, self.over_x, self.over_y, self.far, self.quarter, self.send, self.recv = buffers
        self.made = {}
        here = place
        for k in range(4):
            z = (here.z + k) % 4
            mine = 2 * here.x + here.core
            other = 2 * (1 - here.x) + here.core
            for x in range(2):
                self.copy(
                    k, x, self.block(2 * x + 1 - here.core, z), self.from_core(k, x),
                    here.at(core=1 - here.core),
                )
            if self.x_first(k):
                self.copy(k, 2, self.block(other, z), self.over_x.at[k // 2], here.at(x=1 - here.x))
                self.copy(
                    k, 4, self.part(mine, z, 1 - here.y), self.far.at[k], here.at(y=1 - here.y)
                )
            else:
                for x in range(2):
                    self.copy(
                        k, 2 + x, self.part(2 * x + here.core, z, 1 - here.y),
                        self.over_y.at[k // 2, x], here.at(y=1 - here.y),
                    )
                self.copy(k, 4, self.part(other, z, here.y), self.far.at[k], here.at(x=1 - here.x))
            if k:
                self.copy(k, 5, self.part(mine, z, here.y), self.quarter.at[k - 1], here.at(z=z))

    def x_first(self, k):
        return (k + self.flip) % 2 == 0

    def from_core(self, k, x):
        return self.cores.at[k, x, :, self.offset : self.offset + self.over_x.shape[-1]]

    def block(self, d, z):
        if self.kind == "panel":
            return self.grad.at[d, rows_of(z, 192), :]
        if self.kind == "wide":
            return self.grad.at[rows_of(z, 192), rows_of(d, 768)]
        return self.grad.at[rows_of(d, 192), rows_of(z, 768)]

    def part(self, d, z, y):
        if self.kind == "panel":
            return self.grad.at[d, rows_of(2 * z + y, 96), :]
        if self.kind == "wide":
            return self.grad.at[rows_of(2 * z + y, 96), rows_of(d, 768)]
        return self.grad.at[rows_of(d, 192), rows_of(2 * z + y, 384)]

    def copy(self, k, index, src, dst, peer):
        self.made[k, index] = remote(src, dst, self.send.at[k, index], self.recv.at[k, index], peer)

    def add(self, target, source):
        def some(n, carry):
            at = rows_of(n, 16)
            target[at, :] = target[at, :] + source[at, :]
            return carry

        lax.fori_loop(0, target.shape[0] // 16, some, 0)

    def core(self, k):
        for x in range(2):
            self.made[k, x].start()

    def plane(self, k):
        here = self.place
        z = (here.z + k) % 4
        for x in range(2):
            self.made[k, x].wait_recv()
            self.add(self.block(2 * x + here.core, z), self.from_core(k, x))
        self.made[k, 2].start()
        if not self.x_first(k):
            self.made[k, 3].start()

    def turn(self, k):
        here = self.place
        z = (here.z + k) % 4
        self.made[k, 2].wait_recv()
        if self.x_first(k):
            self.add(self.block(2 * here.x + here.core, z), self.over_x.at[k // 2])
        else:
            self.made[k, 3].wait_recv()
            for x in range(2):
                self.add(self.part(2 * x + here.core, z, here.y), self.over_y.at[k // 2, x])
        self.made[k, 4].start()

    def line(self, k):
        here = self.place
        self.made[k, 4].wait_recv()
        self.add(self.part(2 * here.x + here.core, (here.z + k) % 4, here.y), self.far.at[k])
        if k:
            self.made[k, 5].start()

    def end(self):
        here = self.place
        for k in range(1, 4):
            self.made[k, 5].wait_recv()
        total = self.part(2 * here.x + here.core, here.z, here.y)[...].astype(F32)
        for k in range(3):
            total = total + self.quarter[k].astype(F32)
        self.out[...] = total[:, : self.out.shape[1]]
        for made in self.made.values():
            made.wait_send()


def scatter_scratch(kind, width):
    half = (192, width // 2) if kind == "turned" else (96, width)
    return [
        pltpu.VMEM((4, 2, 192, width), BF16),
        pltpu.VMEM((2, 192, width), BF16),
        pltpu.VMEM((2, 2) + half, BF16),
        pltpu.VMEM((4,) + half, BF16),
        pltpu.VMEM((3,) + half, BF16),
        pltpu.SemaphoreType.DMA((4, 6)),
        pltpu.SemaphoreType.DMA((4, 6)),
    ]


def pack_sums(sums_ref, first_ref, wide_ref, pair, table_ref, packed):
    low = first_ref[0:2, :]
    narrow = sums_ref[...]
    group = lax.broadcasted_iota(jnp.int32, (D, 128), 0) // HEAD_DIM
    pick = (group == lax.broadcasted_iota(jnp.int32, (D, 128), 1)).astype(F32).astype(BF16)
    high, rest = split_low(narrow[8:16])
    heads = (nn(high, pick) + nn(rest, pick))[0:1]
    heads = jnp.concatenate([heads, jnp.zeros((1, 64), F32)], 1)
    for f in range(8):
        at = slice(96 * f, 96 * f + 96)
        packed[f, 0:1, :] = jnp.concatenate(
            [low[0:1, at], low[1:2, at], narrow[2:3, at], narrow[3:4, at]], 1
        )
        packed[f, 1:2, :] = jnp.concatenate([narrow[n : n + 1, at] for n in range(4, 8)], 1)
        packed[f, 2:5, :] = wide_ref[0:3, 384 * f : 384 * f + 384]
        at = slice(192 * f, 192 * f + 192)
        packed[f, 5:6, :] = jnp.concatenate([pair[:, at], heads], 1)
        for n in range(PAIRS):
            packed[f, 6 + n : 7 + n, :] = jnp.concatenate(
                [table_ref[2 * n : 2 * n + 1, at], table_ref[2 * n + 1 : 2 * n + 2, at]], 1
            )
        packed[f, 12:16, :] = jnp.zeros((4, 384), F32)


class SmallSums:
    def __init__(self, place, packed, rows, peers, sems):
        self.place, self.packed, self.rows, self.peers = place, packed, rows, peers
        self.send, self.recv = sems

    def begin(self):
        here = self.place
        f = here.z * 2 + here.y
        self.made = []
        for k in range(1, 8):
            to = (f + k) % 8
            made = remote(
                self.packed.at[to], self.rows.at[k - 1], self.send.at[k], self.recv.at[k],
                here.at(z=to // 2, y=to % 2),
            )
            made.start()
            self.made.append(made)

    def cross(self):
        here = self.place
        f = here.z * 2 + here.y
        for made in self.made:
            made.wait()
        total = self.packed[f]
        for k in range(7):
            total = total + self.rows[k]
        self.peers[0] = total
        d = here.x * 2 + here.core
        self.made = []
        for k in range(1, 4):
            to = (d + k) % 4
            made = remote(
                self.peers.at[0], self.peers.at[k], self.send.at[7 + k], self.recv.at[7 + k],
                here.at(x=to // 2, core=to % 2),
            )
            made.start()
            self.made.append(made)

    def end(self):
        for made in self.made:
            made.wait()
        return (self.peers[0] + self.peers[1]) + (self.peers[2] + self.peers[3])


GRAD_DOWN, GRAD_UP, GRAD_OUT, GRAD_QKV_A, GRAD_QKV_B = range(5)
PLANE, TURN, LINE = "plane", "turn", "line"
BACK_SCHEDULE = {
    3: [(GRAD_DOWN, PLANE, 0)],
    4: [(GRAD_DOWN, PLANE, 1)],
    5: [(GRAD_DOWN, PLANE, 2)],
    6: [(GRAD_DOWN, PLANE, 3), (GRAD_DOWN, TURN, 0)],
    7: [(GRAD_DOWN, TURN, 1)],
    10: [
        (GRAD_UP, PLANE, 0),
        (GRAD_DOWN, TURN, 3),
        (GRAD_DOWN, TURN, 2),
        (GRAD_DOWN, LINE, 1),
        (GRAD_UP, PLANE, 1),
        (GRAD_UP, PLANE, 2),
    ],
    11: [(GRAD_DOWN, LINE, 0)],
    12: [(GRAD_DOWN, LINE, 2)],
    13: [(GRAD_UP, TURN, 0), (GRAD_UP, PLANE, 3)],
    14: [(GRAD_OUT, PLANE, 0), (GRAD_OUT, PLANE, 1)],
    15: [(GRAD_UP, TURN, 1), (GRAD_DOWN, LINE, 3)],
    16: [(GRAD_OUT, PLANE, 3), (GRAD_OUT, PLANE, 2), (GRAD_UP, LINE, 0)],
    17: [(GRAD_UP, TURN, 2)],
    18: [(GRAD_UP, TURN, 3), (GRAD_UP, LINE, 1)],
    19: [(GRAD_OUT, TURN, 3), (GRAD_OUT, TURN, 2), (GRAD_OUT, TURN, 1), (GRAD_OUT, TURN, 0)],
    20: [(GRAD_QKV_A, PLANE, 2), (GRAD_QKV_A, PLANE, 1), (GRAD_UP, LINE, 2), (GRAD_QKV_A, PLANE, 0)],
    21: [(GRAD_QKV_B, PLANE, 0), (GRAD_QKV_B, PLANE, 1)],
}
BACK_DRAIN = [
    (GRAD_QKV_A, TURN, 2),
    (GRAD_QKV_A, TURN, 1),
    (GRAD_OUT, LINE, 2),
    (GRAD_OUT, LINE, 3),
    (GRAD_OUT, LINE, 0),
    (GRAD_QKV_A, PLANE, 3),
    (GRAD_QKV_A, TURN, 0),
    (GRAD_QKV_A, LINE, 2),
    (GRAD_QKV_B, TURN, 0),
    (GRAD_OUT, LINE, 1),
    (GRAD_QKV_B, PLANE, 2),
    (GRAD_QKV_B, TURN, 1),
    (GRAD_QKV_B, PLANE, 3),
    (GRAD_QKV_A, LINE, 1),
    (GRAD_QKV_A, TURN, 3),
    (GRAD_QKV_A, LINE, 0),
    (GRAD_QKV_B, LINE, 0),
    (GRAD_QKV_B, TURN, 2),
    (GRAD_QKV_B, TURN, 3),
    (GRAD_QKV_B, LINE, 1),
    (GRAD_UP, LINE, 3),
    (GRAD_QKV_A, LINE, 3),
    (GRAD_QKV_B, LINE, 2),
    (GRAD_QKV_B, LINE, 3),
]


def backward_kernel(
    buckets, cot_hbm, act_ref, second_hbm, low_ref, mixed_hbm, branch_hbm, normed_hbm,
    probs_ref, query_ref, keys_ref, values_ref, attended_low_ref, vec_ref, sums_ref, wide_ref,
    x_hbm, middle_hbm, weight_hbm,
    input_grad_ref, down_out, up_out, out_out, qkv_out, total_ref,
    left, turned, middle_ref, first_in, proj, grid_ref, down_ref, up_ref, out_ref, qkv_a, qkv_b,
    table_ref, first_ref, wall_small, wall_large, packed, gathered, peers, small_send, small_recv,
    loading, middle_sem, *buffers,
):
    step = pl.program_id(0)
    place = Place()
    parts = [
        Scatter(place, "turned", down_ref, down_out, buffers[0:7]),
        Scatter(place, "wide", up_ref, up_out, buffers[7:14]),
        Scatter(place, "panel", out_ref, out_out, buffers[14:21]),
        Scatter(place, "panel", qkv_a, qkv_out.at[:, 0:256], buffers[0:1] + buffers[21:27]),
        Scatter(
            place, "panel", qkv_b, qkv_out.at[:, 256:576], buffers[0:1] + buffers[27:33], 1, 256
        ),
    ]
    small = SmallSums(place, packed, gathered, peers, (small_send, small_recv))
    count = query_ref.shape[0] // SLOT

    def load(n, src, dst):
        return pltpu.make_async_copy(src, dst, loading.at[n])

    load_cot = load(0, cot_hbm, left.at[0])
    load_second = load(1, second_hbm, left.at[1])
    load_mixed = load(2, mixed_hbm, left.at[0])
    load_branch = load(3, branch_hbm, left.at[1])
    load_normed = load(4, normed_hbm, left.at[0])
    load_x = load(5, x_hbm, left.at[1])

    def load_middle(b):
        n = b % 2
        return pltpu.make_async_copy(middle_hbm.at[rows_of(b, SLOT), :], middle_ref.at[n], middle_sem.at[n])

    load_weight = load(7, weight_hbm, down_ref)

    def progress(at):
        for name, event, n in BACK_SCHEDULE.get(at, []):
            getattr(parts[name], event)(ORDER[n])

    def down_panel():
        z = (place.z + 1 + step) % 4
        down_ref[:, rows_of(z, 768)] = nn(turned[...], act_ref[...]).astype(BF16)

    @pl.when(step == 0)
    def _():
        place.greet()
        load_cot.start()
        load_second.start()
        place.meet()

    for at in BACK_SCHEDULE:
        if at < 19:
            pl.when(step == at)(functools.partial(progress, at))

    @pl.when(step < 4)
    def _():
        @pl.when(step == 0)
        def _():
            load_cot.wait()
            turned[...] = left[0].T
            load_mixed.start()

        down_panel()
        for n in range(4):
            pl.when(step == n)(functools.partial(parts[GRAD_DOWN].core, ORDER[n]))

    @pl.when((step >= 4) & (step < 8))
    def _():
        @pl.when(step == 4)
        def _():
            load_second.wait()
            turned[...] = left[1].T
            load_branch.start()

        up_ref[:, rows_of(step - 4, 768)] = nn(turned[...], low_ref[...]).astype(BF16)

        @pl.when(step == 7)
        def _():
            for k in ORDER:
                parts[GRAD_UP].core(k)

    @pl.when(step == 8)
    def _():
        load_mixed.wait()
        turned[...] = left[0].T
        load_normed.start()
        load_branch.wait()
        for d in range(4):
            out_ref[d] = nn(turned[...], left[1, :, 192 * d : 192 * d + 192]).astype(BF16)
        for k in ORDER:
            parts[GRAD_OUT].core(k)
        load_x.start()
        table_grad_start(table_ref, wall_small, wall_large)

    @pl.when((step >= 9) & (step < 15))
    def _():
        pair = step - 9
        cols = rows_of(pair, 128)
        for s in range(count):
            rows = slice(s * SLOT, s * SLOT + SLOT)
            query_grad, keys_grad, values_grad, scores_grads = attend_back(
                query_ref[rows, :], keys_ref[rows, :], values_ref[rows, :], attended_low_ref[rows, :],
                [probs_ref[half, s] for half in range(2)],
            )
            proj[0, rows, cols] = query_grad
            proj[1, rows, cols] = keys_grad
            proj[2, rows, cols] = values_grad
            chosen = jnp.where(buckets[s] == 0, 1.0, 0.0)
            for half in range(2):
                if s == 0:
                    grid_ref[0, half] = scores_grads[half] * chosen
                    grid_ref[1, half] = scores_grads[half] * (1.0 - chosen)
                else:
                    grid_ref[0, half] += scores_grads[half] * chosen
                    grid_ref[1, half] += scores_grads[half] * (1.0 - chosen)
        for half in range(2):
            table_grad_head(grid_ref, table_ref, wall_small, wall_large, 2 * pair + half, half)

    def lay_panel(d):
        def lay(pieces):
            at = 0
            for n, first, last in pieces:
                left[0, :, at : at + last - first] = proj[n, :, first:last]
                at += last - first

        cuts = (
            [(0, 0, 576)], [(0, 576, 768), (1, 0, 384)], [(1, 384, 768), (2, 0, 192)], [(2, 192, 768)],
        )
        for n, pieces in enumerate(cuts):
            pl.when(d == n)(functools.partial(lay, pieces))

    @pl.when((step >= 15) & (step < 19))
    def _():
        @pl.when(step == 15)
        def _():
            parts[GRAD_DOWN].end()
            load_weight.start()
            load_normed.wait()
            turned[...] = left[0].T
            first_in[...] = jnp.zeros_like(first_in)

        d = step - 15
        lay_panel(d)
        grad = nn(turned[...], left[0, :, :576]).astype(BF16)
        qkv_a[d] = grad[:, :256]
        qkv_b[d] = jnp.concatenate([grad[:, 256:], jnp.zeros((D, 64), BF16)], 1)

        @pl.when(step == 15)
        def _():
            load_weight.wait()

        @pl.when(step == 18)
        def _():
            for k in ORDER:
                parts[GRAD_QKV_A].core(k)
                parts[GRAD_QKV_B].core(k)

        first_in[...] += nt(left[0, :, :576], down_ref[:, pl.ds(pl.multiple_of(768 * d, 768), 576)])

    @pl.when(step == 19)
    def _():
        progress(19)
        load_middle(0).start()
        load_x.wait()
        first_ref[...] = jnp.zeros_like(first_ref)

        def one_block(b, carry):
            rows = pl.ds(pl.multiple_of(b * SLOT, SLOT), SLOT)
            unit, inverse = standardize(left[1, rows, :].astype(F32))
            grad = first_in[rows, :]
            first_ref[0:1, :] += column_sum(grad * unit)
            first_ref[1:2, :] += column_sum(grad)
            back = norm_back(grad * vec_ref[0:1, :], unit, inverse)

            @pl.when(b + 1 < count)
            def _():
                load_middle(b + 1).start()

            load_middle(b).wait()
            input_grad_ref[rows, :] = (middle_ref[b % 2] + back).astype(BF16)
            return carry

        lax.fori_loop(0, count, one_block, 0)
        progress(20)
        table_grad_end(table_ref, wall_small, wall_large)
        pair = jnp.concatenate([tall_sum(proj.at[0]), tall_sum(proj.at[2])], 1)
        progress(21)
        pack_sums(sums_ref, first_ref, wide_ref, pair, table_ref, packed)
        small.begin()
        for n, (name, event, k) in enumerate(BACK_DRAIN):
            if n == len(BACK_DRAIN) // 2:
                small.cross()
            getattr(parts[name], event)(ORDER[k])
        parts[GRAD_UP].end()
        parts[GRAD_OUT].end()
        total_ref[...] = small.end()
        parts[GRAD_QKV_A].end()
        parts[GRAD_QKV_B].end()


def backward(
    buckets, cotangent, act, second, low, mixed, branch, normed, probs, qkv, attended_low, vecs,
    sums, wide, tokens, middle_grad, weight,
):
    rows = cotangent.shape[0]
    count = rows // SLOT
    any_space = pl.BlockSpec(memory_space=ANY)

    def held(shape):
        return pl.BlockSpec(shape, lambda i: (0,) * len(shape))

    def pair(i):
        return jnp.clip(i - 9, 0, PAIRS - 1)

    def panel(base):
        return pl.BlockSpec((rows, 128), lambda i: (0, base + pair(i)))

    def act_panel(i):
        return (0, (lax.axis_index("fsdp") // 2 + 1 + jnp.minimum(i, 3)) % 4)

    outs = [(192, 384), (96, 768), (96, 192), (96, 576), (16, 384)]
    return pl.pallas_call(
        backward_kernel,
        grid=(20,),
        in_specs=[
            pl.BlockSpec(memory_space=pltpu.SMEM),
            any_space,
            pl.BlockSpec((rows, D), act_panel),
            any_space,
            pl.BlockSpec((rows, D), lambda i: (0, jnp.clip(i - 4, 0, 3))),
            any_space, any_space, any_space,
            pl.BlockSpec((2, count, SLOT, SLOT), lambda i: (pair(i), 0, 0, 0)),
            panel(0), panel(PAIRS), panel(2 * PAIRS), panel(0),
            held((8, D)), held((16, D)), held((8, FF)),
            any_space, any_space, any_space,
        ],
        out_specs=[held((rows, D))] + [held(shape) for shape in outs],
        out_shape=[jax.ShapeDtypeStruct((rows, D), BF16)]
        + [jax.ShapeDtypeStruct(shape, F32) for shape in outs],
        scratch_shapes=[
            pltpu.VMEM((2, rows, D), BF16),
            pltpu.VMEM((D, rows), BF16),
            pltpu.VMEM((2, SLOT, D), F32),
            pltpu.VMEM((rows, D), F32),
            pltpu.VMEM((3, rows, D), BF16),
            pltpu.VMEM((2, 2, SLOT, SLOT), F32),
            pltpu.VMEM((D, FF), BF16),
            pltpu.VMEM((D, FF), BF16),
            pltpu.VMEM((4, D, 192), BF16),
            pltpu.VMEM((4, D, 256), BF16),
            pltpu.VMEM((4, D, 384), BF16),
            pltpu.VMEM((16, TABLE), F32),
            pltpu.VMEM((8, D), F32),
            pltpu.VMEM((2, 128, 128), F32),
            pltpu.VMEM((4, 256, 128), F32),
            pltpu.VMEM((8, 16, 384), F32),
            pltpu.VMEM((7, 16, 384), F32),
            pltpu.VMEM((4, 16, 384), F32),
            pltpu.SemaphoreType.DMA((11,)),
            pltpu.SemaphoreType.DMA((11,)),
            pltpu.SemaphoreType.DMA((8,)),
            pltpu.SemaphoreType.DMA((2,)),
        ]
        + scatter_scratch("turned", 768) + scatter_scratch("wide", 768)
        + scatter_scratch("panel", 192) + scatter_scratch("panel", 256)[1:]
        + scatter_scratch("panel", 384)[1:],
        compiler_params=pltpu.CompilerParams(
            collective_id=2, has_side_effects=True, dimension_semantics=("arbitrary",),
            vmem_limit_bytes=BACK_LIMIT,
        ),
        name="backward",
    )(
        buckets, cotangent, act, second, low, mixed, branch, normed, probs, qkv, qkv, qkv,
        attended_low, vecs, sums, wide, tokens, middle_grad, weight,
    )


def emit_kernel(count, total_ref, *refs):
    sources = refs[:count]
    targets = refs[count : 2 * count]
    small = refs[2 * count : 2 * count + 14]
    held = refs[2 * count + 14 : -2]
    into, out = refs[-2:]
    loads = [
        pltpu.make_async_copy(src, dst, into.at[n]) for n, (src, dst) in enumerate(zip(sources, held))
    ]
    made = [
        pltpu.make_async_copy(src, dst, out.at[n]) for n, (src, dst) in enumerate(zip(held, targets))
    ]
    for each in loads:
        each.start()
    for load, each in zip(loads, made):
        load.wait()
        each.start()
    total = total_ref[...]
    for n in range(8):
        at = 96 * (n % 4)
        small[n][...] = total[n // 4 : n // 4 + 1, at : at + 96].reshape(96)
    for n in range(3):
        small[8 + n][...] = total[2 + n : 3 + n, :].reshape(384)
    small[11][...] = total[5:6, 0:192].reshape(192)
    small[12][...] = total[5:6, 192:204].reshape(HEADS)
    for n in range(PAIRS):
        small[13][2 * n : 2 * n + 1, :] = total[6 + n : 7 + n, 0:192]
        small[13][2 * n + 1 : 2 * n + 2, :] = total[6 + n : 7 + n, 192:384]
    for each in made:
        each.wait()


def emit(total, *large):
    vmem = pl.BlockSpec(memory_space=pltpu.VMEM)
    any_space = pl.BlockSpec(memory_space=ANY)
    small = [(96,)] * 8 + [(384,)] * 3 + [(192,), (HEADS,), (HEADS, 192)]
    return pl.pallas_call(
        functools.partial(emit_kernel, len(large)),
        in_specs=[vmem] + [any_space] * len(large),
        out_specs=[any_space] * len(large) + [vmem] * len(small),
        out_shape=[jax.ShapeDtypeStruct(part.shape, part.dtype) for part in large]
        + [jax.ShapeDtypeStruct(shape, F32) for shape in small],
        scratch_shapes=[pltpu.VMEM(part.shape, part.dtype) for part in large]
        + [pltpu.SemaphoreType.DMA((len(large),))] * 2,
        compiler_params=params(),
        name="emit",
    )(total, *large)


def gather_matrix(piece):
    rows = lax.all_gather(piece, "fsdp", axis=0, tiled=True)
    return lax.all_gather(rows, "dp", axis=1, tiled=True)


def scatter_matrix(grad):
    part = lax.psum_scatter(grad, "dp", scatter_dimension=1, tiled=True).astype(F32)
    return lax.psum_scatter(part, "fsdp", scatter_dimension=0, tiled=True)


def body(
    tokens, cotangent, lengths, buckets, qkv_weight, query_value_bias, out_weight, out_bias,
    up_weight, up_bias, down_weight, down_bias, first_gain, first_shift, mix_gain, mix_shift,
    second_gain, second_shift, hidden_gain, hidden_shift, head_scale, position_table,
):
    parts = lax.axis_size("fsdp")
    own_kernels = (parts, lax.axis_size("dp")) == (8, 4)
    narrow = [
        first_gain, first_shift, mix_gain, mix_shift, second_gain, second_shift, out_bias, down_bias,
    ]
    wide = [up_bias, hidden_gain, hidden_shift]
    a = D // parts
    b = FF // parts
    if own_kernels:
        (
            normed, qkv, probs, result, mixed, second, act, low, branch, middle_grad, attended_low,
            sums, wide_sums, vecs, qkv_full,
        ) = forward(
            lengths, buckets, tokens, cotangent, qkv_weight, out_weight, up_weight, down_weight.T,
            position_table.T, head_scale, narrow + wide + [query_value_bias],
        )
        input_grad, down_owned, up_owned, out_owned, qkv_owned, total = backward(
            buckets, cotangent, act, second, low, mixed, branch, normed, probs, qkv, attended_low,
            vecs, sums, wide_sums, tokens, middle_grad, qkv_full,
        )
        result, input_grad, qkv_owned, out_owned, up_owned, down_owned, *small = emit(
            total, result, input_grad, qkv_owned, out_owned, up_owned, down_owned
        )
        down_owned = down_owned.T
        narrow_owned = small[:8]
        wide_owned = small[8:11]
        pair_owned, scale_grad, table_owned = small[11], small[12], small[13].T
    else:
        packed = jnp.concatenate(
            [jnp.pad(jnp.stack(narrow), ((0, 0), (0, b - a))), jnp.stack(wide)]
            + [jnp.pad(query_value_bias, (0, b - 2 * a))[None], jnp.zeros((4, b), BF16)]
            + [jnp.pad(position_table.T, ((0, 4), (0, b - 2 * a)))]
        )
        scales = jnp.repeat(head_scale.astype(F32), HEAD_DIM)[None]
        gathered = lax.all_gather(packed, "fsdp", axis=0)
        qkv_full = gather_matrix(qkv_weight)
        out_full = gather_matrix(out_weight)
        up_full = gather_matrix(up_weight)
        down_full = gather_matrix(down_weight).T
        gathered = gathered.astype(F32)
        vecs = gathered[:, :8, :a].transpose(1, 0, 2).reshape(8, D)
        wides = jnp.pad(gathered[:, 8:11].transpose(1, 0, 2).reshape(3, FF), ((0, 5), (0, 0)))
        pair = gathered[:, 11, : 2 * a].reshape(1, 2 * D)
        table = gathered[:, 16:, : 2 * a].transpose(1, 0, 2).reshape(16, TABLE)
        qkv_bias = jnp.concatenate([pair[:, :D], jnp.zeros((1, D), F32), pair[:, D:]], 1)

        bias = build_bias(table)
        normed, qkv, probs, attended = attention(
            lengths, buckets, tokens, vecs, qkv_full, qkv_bias, bias
        )
        (
            result, mixed, second, act, low, branch, middle_grad, attended_low, sums, wide_sums,
        ) = feed_forward(tokens, attended, cotangent, out_full, up_full, down_full, vecs, wides, scales)
        down_grad = outer_product(cotangent, act, 512)
        up_grad = outer_product(second, low, 512)
        out_grad = outer_product(mixed, branch, 256)
        input_grad, grids, qkv_grad, pair_sums, first_sums = attention_back(
            buckets, probs, qkv, attended_low, normed, tokens, middle_grad, qkv_full, vecs
        )
        table_sums = table_grad(grids)
        qkv_natural = qkv_grad.reshape(PAIRS, D, 3, 128).transpose(1, 2, 0, 3).reshape(D, 3 * D)

        qkv_owned = scatter_matrix(qkv_natural)
        out_owned = scatter_matrix(out_grad)
        up_owned = scatter_matrix(up_grad)
        down_owned = scatter_matrix(down_grad.T)
        pair_grad = pair_sums[:, 0].reshape(PAIRS, 3, 128).transpose(1, 0, 2).reshape(3, D)
        pair_grad = jnp.concatenate([pair_grad[0], pair_grad[2]])
        narrow_sums = jnp.concatenate([first_sums[:2], sums[2:8]], 0)
        packed = jnp.concatenate(
            [
                narrow_sums.reshape(8, parts, a).transpose(1, 0, 2).reshape(parts, -1),
                wide_sums[:3].reshape(3, parts, b).transpose(1, 0, 2).reshape(parts, -1),
                pair_grad.reshape(parts, -1),
                table_sums[:HEADS].T.reshape(parts, -1),
            ],
            1,
        )
        owned = lax.psum(lax.psum_scatter(packed, "fsdp", scatter_dimension=0, tiled=True), "dp")[0]
        scale_grad = lax.psum(sums[8].reshape(HEADS, HEAD_DIM).sum(1), ("fsdp", "dp"))
        narrow_owned = owned[: 8 * a].reshape(8, a)
        edge = 8 * a
        wide_owned = owned[edge : edge + 3 * b].reshape(3, b)
        edge += 3 * b
        pair_owned = owned[edge : edge + 2 * a]
        edge += 2 * a
        table_owned = owned[edge:].reshape(TABLE // parts, HEADS)
    return (
        result, input_grad, qkv_owned, pair_owned, out_owned, narrow_owned[6], up_owned,
        wide_owned[0], down_owned, narrow_owned[7], narrow_owned[0], narrow_owned[1],
        narrow_owned[2], narrow_owned[3], narrow_owned[4], narrow_owned[5], wide_owned[1],
        wide_owned[2], scale_grad, table_owned,
    )


def solution(mesh):
    tokens = P(("fsdp", "dp"), None)
    sequences = P(("fsdp", "dp"))
    matrix = P("fsdp", "dp")
    vector = P("fsdp")
    table = P("fsdp", None)
    in_specs = (
        tokens, tokens, sequences, sequences, matrix, vector, matrix, vector, matrix, vector,
        matrix, vector, vector, vector, vector, vector, vector, vector, vector, vector, P(), table,
    )
    out_specs = (
        tokens, tokens, matrix, vector, matrix, vector, matrix, vector, matrix, vector, vector,
        vector, vector, vector, vector, vector, vector, vector, P(), table,
    )
    return jax.shard_map(body, mesh=mesh, in_specs=in_specs, out_specs=out_specs, check_vma=False)
```

```python
import functools

import jax
import jax.numpy as jnp
from jax import lax
from jax.experimental import pallas as pl
from jax.experimental.pallas import tpu as pltpu
from jax.sharding import PartitionSpec as P

D = 768
HEADS = 12
PAIRS = 6
HEAD_DIM = 64
FF = 3072
SLOT = 256
TABLE = 1536

EPS = 1e-05
MASKED = -1000000000.0
F32 = jnp.float32
BF16 = jnp.bfloat16
VMEM_LIMIT = 60 * 2**20
BACK_LIMIT = 60 * 2**20


def params(**more):
    return pltpu.CompilerParams(vmem_limit_bytes=VMEM_LIMIT, **more)


def nn(left, right):
    return lax.dot_general(left, right, (((1,), (0,)), ((), ())), preferred_element_type=F32)


def nt(left, right):
    return lax.dot_general(left, right, (((1,), (1,)), ((), ())), preferred_element_type=F32)


def standardize(values):
    center = values - jnp.mean(values, -1, keepdims=True)
    inverse = lax.rsqrt(jnp.mean(center * center, -1, keepdims=True) + EPS)
    return center * inverse, inverse


def norm_back(grad, unit, inverse):
    return inverse * (
        grad
        - jnp.mean(grad, -1, keepdims=True)
        - unit * jnp.mean(grad * unit, -1, keepdims=True)
    )


def column_sum(values):
    return jnp.sum(values, 0, keepdims=True)


def tall_sum(ref):
    def some(n, total):
        return total + column_sum(ref[rows_of(n, 64), :].astype(F32))

    return lax.fori_loop(0, ref.shape[0] // 64, some, jnp.zeros((1, ref.shape[1]), F32))


def split_low(values):
    high = values.astype(BF16)
    return high, (values - high.astype(F32)).astype(BF16)


def compaction(side, lanes):
    plane = lax.broadcasted_iota(jnp.int32, (1024, lanes), 0)
    lane = lax.broadcasted_iota(jnp.int32, (1024, lanes), 1)
    across = plane & 31
    return ((lane == side * (plane >> 5) + across) & (across < side)).astype(F32).astype(BF16)


def inside_grid(patches):
    row = lax.broadcasted_iota(jnp.int32, (SLOT, SLOT), 0)
    col = lax.broadcasted_iota(jnp.int32, (SLOT, SLOT), 1)
    return (row < patches) & (col < patches)


def store_tiles(ref, values):
    for k in range(ref.shape[0]):
        ref[k] = values[:, 128 * k : 128 * k + 128]


def load_tiles(ref):
    return jnp.concatenate([ref[k] for k in range(ref.shape[0])], 1)


def load_strided(ref, first, count):
    return jnp.concatenate(
        [ref[k, pl.ds(first, count, 16), :] for k in range(ref.shape[0])], 1
    )


def store_strided(ref, first, values):
    for k in range(ref.shape[0]):
        ref[k, pl.ds(first, values.shape[0], 16), :] = values[:, 128 * k : 128 * k + 128]


def bias_walls(table_ref, wall_small, wall_large, visual):
    plane = table_ref[:, 512:]
    shifted = [pltpu.roll(plane, (ic - 15) % 1024, 1) for ic in range(16)]
    stack = jnp.concatenate(shifted, 0).astype(BF16)
    store_tiles(wall_large, nn(stack, compaction(15, 512)))
    store_tiles(wall_small, nn(stack[:128], compaction(8, 256)))
    visual[...] = jnp.zeros_like(visual)


def bias_head(table_ref, out_ref, wall_small, wall_large, visual, h, carry):
    line = jnp.broadcast_to(table_ref[pl.ds(h, 1), :512], (SLOT, 512))
    textual = pltpu.roll(line, 257, 1, stride=1, stride_axis=0)[:, :SLOT]
    large = load_strided(wall_large, h, 16)
    for ir in range(15):
        visual[pl.ds(ir * 15, 16), :] = pltpu.roll(large, 512 - (15 - ir) * 15, 1)[:, :SLOT]
    out_ref[1, h] = jnp.where(inside_grid(225), visual[...], textual).astype(BF16)
    small = load_strided(wall_small, h, 8)
    rows = [pltpu.roll(small, 256 - (15 - ir) * 8, 1) for ir in range(8)]
    grid = jnp.concatenate(rows + [jnp.zeros((192, SLOT), F32)], 0)
    out_ref[0, h] = jnp.where(inside_grid(64), grid, textual).astype(BF16)
    return carry


def bias_kernel(table_ref, out_ref, wall_small, wall_large, visual):
    bias_walls(table_ref, wall_small, wall_large, visual)
    one_head = functools.partial(bias_head, table_ref, out_ref, wall_small, wall_large, visual)
    lax.fori_loop(0, HEADS, one_head, 0)


def build_bias(table):
    return pl.pallas_call(
        bias_kernel,
        out_shape=jax.ShapeDtypeStruct((2, HEADS, SLOT, SLOT), BF16),
        scratch_shapes=[
            pltpu.VMEM((2, 128, 128), F32),
            pltpu.VMEM((4, 256, 128), F32),
            pltpu.VMEM((SLOT, SLOT), F32),
        ],
        compiler_params=params(),
        name="build_bias",
    )(table)


def table_grad_start(out_ref, wall_small, wall_large):
    wall_small[...] = jnp.zeros_like(wall_small)
    wall_large[...] = jnp.zeros_like(wall_large)
    out_ref[...] = jnp.zeros_like(out_ref)


def table_grad_head(grid_ref, out_ref, wall_small, wall_large, h, slot):
    row = lax.broadcasted_iota(jnp.int32, (SLOT, SLOT), 0)
    col = lax.broadcasted_iota(jnp.int32, (SLOT, SLOT), 1)
    flip = (row + col == SLOT - 1).astype(F32).astype(BF16)
    lane = lax.broadcasted_iota(jnp.int32, (16, SLOT), 1)
    textual = jnp.where(inside_grid(64), 0.0, grid_ref[0, slot]) + jnp.where(
        inside_grid(225), 0.0, grid_ref[1, slot]
    )
    high, low = split_low(textual)
    flipped = nn(flip, high) + nn(flip, low)
    wide = jnp.concatenate([flipped, jnp.zeros((SLOT, SLOT), F32)], 1)
    out_ref[pl.ds(h, 1), :512] = column_sum(pltpu.roll(wide, 0, 1, stride=1, stride_axis=0))
    total = jnp.zeros((16, 512), F32)
    for ir in range(15):
        part = jnp.where(lane < 225, grid_ref[1, slot, pl.ds(ir * 15, 16), :], 0.0)
        part = jnp.concatenate([part, jnp.zeros((16, SLOT), F32)], 1)
        total = total + pltpu.roll(part, (15 - ir) * 15, 1)
    store_strided(wall_large, h, total)
    total = jnp.zeros((8, SLOT), F32)
    for ir in range(8):
        part = jnp.where(lane[:8] < 64, grid_ref[0, slot, pl.ds(ir * 8, 8), :], 0.0)
        total = total + pltpu.roll(part, (15 - ir) * 8, 1)
    store_strided(wall_small, h, total)


def table_grad_end(out_ref, wall_small, wall_large):
    high, low = split_low(load_tiles(wall_large))
    spread = compaction(15, 512)
    large = nt(high, spread) + nt(low, spread)
    high, low = split_low(load_tiles(wall_small))
    spread = compaction(8, 256)
    small = nt(high, spread) + nt(low, spread)
    plane = jnp.zeros((16, 1024), F32)
    for ic in range(15):
        part = large[ic * 16 : ic * 16 + 16]
        if ic < 8:
            part = part + small[ic * 16 : ic * 16 + 16]
        plane = plane + pltpu.roll(part, 15 - ic, 1)
    out_ref[:, 512:] = plane


def table_grad_kernel(grid_ref, out_ref, wall_small, wall_large):
    table_grad_start(out_ref, wall_small, wall_large)

    def one_head(h, carry):
        table_grad_head(grid_ref, out_ref, wall_small, wall_large, h, h)
        return carry

    lax.fori_loop(0, HEADS, one_head, 0)
    table_grad_end(out_ref, wall_small, wall_large)


def table_grad(grids):
    return pl.pallas_call(
        table_grad_kernel,
        out_shape=jax.ShapeDtypeStruct((16, TABLE), F32),
        scratch_shapes=[pltpu.VMEM((2, 128, 128), F32), pltpu.VMEM((4, 256, 128), F32)],
        compiler_params=params(),
        name="table_grad",
    )(grids)


def by_head(pair, axis):
    first = lax.broadcasted_iota(jnp.int32, pair.shape, 1) < HEAD_DIM
    return jnp.concatenate([jnp.where(first, pair, 0), jnp.where(first, 0, pair)], axis)


def attend(query, keys, values, bias, live):
    logits = nt(by_head(query, 0), keys)
    probs = []
    for half in range(2):
        rows = slice(SLOT * half, SLOT * half + SLOT)
        scores = jnp.where(live, logits[rows] + bias[half].astype(F32), MASKED)
        shifted = jnp.exp(scores - jnp.max(scores, -1, keepdims=True))
        probs.append((shifted * (1.0 / jnp.sum(shifted, -1, keepdims=True))).astype(BF16))
    return probs, nn(jnp.concatenate(probs, 1), by_head(values, 0))


def attend_back(query, keys, values, grad, probs):
    probs_grads = nt(by_head(grad, 0), values)
    grad_turned = grad.T
    query_turned = query.T
    keys_parts = []
    values_parts = []
    scores_grads = []
    lows = []
    for half in range(2):
        part = slice(HEAD_DIM * half, HEAD_DIM * half + HEAD_DIM)
        wide = probs[half].astype(F32)
        probs_grad = probs_grads[SLOT * half : SLOT * half + SLOT]
        values_parts.append(nn(grad_turned[part], probs[half]))
        scores_grad = wide * (probs_grad - jnp.sum(wide * probs_grad, -1, keepdims=True))
        scores_grads.append(scores_grad)
        lows.append(scores_grad.astype(BF16))
        keys_parts.append(nn(query_turned[part], lows[half]))
    query_grad = nn(jnp.concatenate(lows, 1), by_head(keys, 0)) * HEAD_DIM ** (-0.5)
    keys_grad = jnp.concatenate(keys_parts, 0).T
    values_grad = jnp.concatenate(values_parts, 0).T
    return query_grad.astype(BF16), keys_grad.astype(BF16), values_grad.astype(BF16), scores_grads


def attention_kernel(
    lengths, buckets, x_ref, vec_ref, weight_ref, qkv_bias_ref, bias_ref,
    normed_ref, qkv_ref, probs_ref, attended_ref,
):
    count = x_ref.shape[0] // SLOT

    def one_block(b, carry):
        rows = pl.ds(pl.multiple_of(b * SLOT, SLOT), SLOT)
        unit, inverse = standardize(x_ref[rows, :].astype(F32))
        normed_ref[rows, :] = (unit * vec_ref[0:1, :] + vec_ref[1:2, :]).astype(BF16)
        return carry

    lax.fori_loop(0, count, one_block, 0)

    def one_panel(n, carry):
        cols = pl.ds(pl.multiple_of(n * 256, 256), 256)
        out = nn(normed_ref[...], weight_ref[:, cols]) + qkv_bias_ref[:, cols]
        out = (out * jnp.where(n < 3, HEAD_DIM ** (-0.5), 1.0)).astype(BF16)
        qkv_ref[2 * n] = out[:, :128]
        qkv_ref[2 * n + 1] = out[:, 128:]
        return carry

    lax.fori_loop(0, 9, one_panel, 0)
    key_slot = lax.broadcasted_iota(jnp.int32, (SLOT, SLOT), 1)

    def one_unit(step, carry):
        pair = step // count
        s = step % count
        rows = pl.ds(pl.multiple_of(s * SLOT, SLOT), SLOT)
        bias = [bias_ref[buckets[s], 2 * pair + half] for half in range(2)]
        probs, out = attend(
            qkv_ref[pair, rows, :], qkv_ref[PAIRS + pair, rows, :], qkv_ref[2 * PAIRS + pair, rows, :],
            bias, key_slot < lengths[s],
        )
        for half in range(2):
            probs_ref[2 * pair + half, s] = probs[half]
        attended_ref[rows, pl.ds(pl.multiple_of(pair * 128, 128), 128)] = out
        return carry

    lax.fori_loop(0, PAIRS * count, one_unit, 0)


def attention(lengths, buckets, tokens, vecs, weight, qkv_bias, bias):
    rows = tokens.shape[0]
    count = rows // SLOT
    smem = pl.BlockSpec(memory_space=pltpu.SMEM)
    vmem = pl.BlockSpec(memory_space=pltpu.VMEM)
    return pl.pallas_call(
        attention_kernel,
        in_specs=[smem, smem] + [vmem] * 5,
        out_shape=[
            jax.ShapeDtypeStruct((rows, D), BF16),
            jax.ShapeDtypeStruct((3 * PAIRS, rows, 128), BF16),
            jax.ShapeDtypeStruct((HEADS, count, SLOT, SLOT), BF16),
            jax.ShapeDtypeStruct((rows, D), F32),
        ],
        compiler_params=params(),
        name="attention_forward",
    )(lengths, buckets, tokens, vecs, weight, qkv_bias, bias)


PANEL = 1024


def feed_kernel(*refs):
    @pl.when(pl.program_id(0) == 0)
    def _():
        for ref in refs[17:19]:
            ref[...] = jnp.zeros_like(ref)

    feed_block(*refs, lambda: None)


def feed_block(
    x_ref, attended_ref, cot_ref, out_w, up_w, down_w, vec_ref, wide_ref, scale_ref,
    result_ref, mixed_ref, second_ref, act_ref, low_ref, branch_ref, middle_grad_ref,
    attended_low_ref, sums_ref, wide_sums_ref,
    gelu_ref, slope_ref, grad_ref, before_down,
):
    def add(row, values):
        sums_ref[row : row + 1, :] += column_sum(values)

    rows = x_ref.shape[0]
    attended = attended_ref[...]
    mix_unit, mix_inverse = standardize(attended * scale_ref[...])
    mixed = (mix_unit * vec_ref[2:3, :] + vec_ref[3:4, :]).astype(BF16)
    mixed_ref[...] = mixed
    middle = x_ref[...].astype(F32) + nn(mixed, out_w[...]) + vec_ref[6:7, :]
    second_unit, second_inverse = standardize(middle)
    second = (second_unit * vec_ref[4:5, :] + vec_ref[5:6, :]).astype(BF16)
    second_ref[...] = second
    cot = cot_ref[...]

    panels = [slice(n, n + PANEL) for n in range(0, FF, PANEL)]
    total = jnp.zeros((rows, 1), F32)
    for cols in panels:
        hidden = nn(second, up_w[:, cols]) + wide_ref[0:1, cols]
        cdf = 0.5 + 0.5 * lax.erf(hidden * 0.7071067811865476)
        gelu = hidden * cdf
        gelu_ref[:, cols] = gelu
        slope_ref[:, cols] = cdf + hidden * (jnp.exp(-0.5 * hidden * hidden) * 0.3989422804014327)
        total = total + jnp.sum(gelu, -1, keepdims=True)
    mean = total * (1.0 / FF)
    total = jnp.zeros((rows, 1), F32)
    for cols in panels:
        center = gelu_ref[:, cols] - mean
        total = total + jnp.sum(center * center, -1, keepdims=True)
    inverse = lax.rsqrt(total * (1.0 / FF) + EPS)
    before_down()
    result = middle + vec_ref[7:8, :]
    first = jnp.zeros((rows, 1), F32)
    second_moment = jnp.zeros((rows, 1), F32)
    for cols in panels:
        unit = (gelu_ref[:, cols] - mean) * inverse
        gelu_ref[:, cols] = unit
        act = (unit * wide_ref[1:2, cols] + wide_ref[2:3, cols]).astype(BF16)
        act_ref[:, cols] = act
        result = result + nt(act, down_w[:, cols])
        act_grad = nn(cot, down_w[:, cols])
        wide_sums_ref[1:2, cols] += column_sum(act_grad * unit)
        wide_sums_ref[2:3, cols] += column_sum(act_grad)
        grad = act_grad * wide_ref[1:2, cols]
        grad_ref[:, cols] = grad
        first = first + jnp.sum(grad, -1, keepdims=True)
        second_moment = second_moment + jnp.sum(grad * unit, -1, keepdims=True)
    result_ref[...] = result.astype(BF16)
    first = first * (1.0 / FF)
    second_moment = second_moment * (1.0 / FF)
    second_in = jnp.zeros((rows, D), F32)
    for cols in panels:
        grad = inverse * (grad_ref[:, cols] - first - gelu_ref[:, cols] * second_moment)
        low = (grad * slope_ref[:, cols]).astype(BF16)
        low_ref[:, cols] = low
        wide_sums_ref[0:1, cols] += column_sum(low.astype(F32))
        second_in = second_in + nt(low, up_w[:, cols])
    add(4, second_in * second_unit)
    add(5, second_in)
    cot_wide = cot.astype(F32)
    add(7, cot_wide)
    middle_grad = cot_wide + norm_back(second_in * vec_ref[4:5, :], second_unit, second_inverse)
    middle_grad_ref[...] = middle_grad
    branch = middle_grad.astype(BF16)
    branch_ref[...] = branch
    add(6, branch.astype(F32))
    mixed_in = nt(branch, out_w[...])
    add(2, mixed_in * mix_unit)
    add(3, mixed_in)
    grad = norm_back(mixed_in * vec_ref[2:3, :], mix_unit, mix_inverse)
    add(8, grad * attended)
    attended_low_ref[...] = (grad * scale_ref[...]).astype(BF16)


def feed_forward(tokens, attended, cotangent, out_w, up_w, down_w, vecs, wide, scales):
    rows = tokens.shape[0]
    tile = 256
    block = pl.BlockSpec((tile, D), lambda i: (i, 0))
    wide_block = pl.BlockSpec((tile, FF), lambda i: (i, 0))

    def whole(shape):
        return pl.BlockSpec(shape, lambda i: (0, 0), pipeline_mode=pl.Buffered(1))

    def held(shape):
        return pl.BlockSpec(shape, lambda i: (0, 0))

    return pl.pallas_call(
        feed_kernel,
        grid=(rows // tile,),
        in_specs=[block] * 3
        + [whole((D, D)), whole((D, FF)), whole((D, FF)), whole((8, D)), whole((8, FF)), whole((1, D))],
        out_specs=[block, block, block, wide_block, wide_block, block, block, block]
        + [held((16, D)), held((8, FF))],
        out_shape=[
            jax.ShapeDtypeStruct((rows, D), BF16),
            jax.ShapeDtypeStruct((rows, D), BF16),
            jax.ShapeDtypeStruct((rows, D), BF16),
            jax.ShapeDtypeStruct((rows, FF), BF16),
            jax.ShapeDtypeStruct((rows, FF), BF16),
            jax.ShapeDtypeStruct((rows, D), BF16),
            jax.ShapeDtypeStruct((rows, D), F32),
            jax.ShapeDtypeStruct((rows, D), BF16),
            jax.ShapeDtypeStruct((16, D), F32),
            jax.ShapeDtypeStruct((8, FF), F32),
        ],
        scratch_shapes=[pltpu.VMEM((tile, FF), F32)] * 3,
        compiler_params=params(dimension_semantics=("arbitrary",)),
        name="feed_forward",
    )(tokens, attended, cotangent, out_w, up_w, down_w, vecs, wide, scales)


def outer_kernel(left_ref, right_ref, out_ref, turned):
    @pl.when(pl.program_id(0) == 0)
    def _():
        turned[...] = left_ref[...].T

    out_ref[...] = nn(turned[...], right_ref[...]).astype(BF16)


def outer_product(left, right, panel):
    rows, width = left.shape
    cols = right.shape[1]
    return pl.pallas_call(
        outer_kernel,
        grid=(cols // panel,),
        in_specs=[
            pl.BlockSpec((rows, width), lambda i: (0, 0), pipeline_mode=pl.Buffered(1)),
            pl.BlockSpec((rows, panel), lambda i: (0, i)),
        ],
        out_specs=pl.BlockSpec((width, panel), lambda i: (0, i)),
        out_shape=jax.ShapeDtypeStruct((width, cols), BF16),
        scratch_shapes=[pltpu.VMEM((width, rows), BF16)],
        compiler_params=params(dimension_semantics=("arbitrary",)),
        name="weight_grad",
    )(left, right)


def attention_back_kernel(
    buckets, probs_ref, query_ref, keys_ref, values_ref, low_ref, normed_ref, x_ref, middle_ref,
    weight_q, weight_k, weight_v, vec_ref,
    input_grad_ref, grid_ref, weight_grad_ref, pair_ref, sums_ref,
    turned, first_in, proj_ref,
):
    count = x_ref.shape[0] // SLOT
    step = pl.program_id(0)

    @pl.when(step == 0)
    def _():
        turned[...] = normed_ref[...].T
        first_in[...] = jnp.zeros_like(first_in)

    grid_ref[...] = jnp.zeros_like(grid_ref)

    def one_sequence(s, carry):
        rows = pl.ds(pl.multiple_of(s * SLOT, SLOT), SLOT)
        query_grad, keys_grad, values_grad, scores_grads = attend_back(
            query_ref[0, rows, :], keys_ref[0, rows, :], values_ref[0, rows, :], low_ref[rows, :],
            [probs_ref[half, s] for half in range(2)],
        )
        small = jnp.where(buckets[s] == 0, 1.0, 0.0)
        for half in range(2):
            grid_ref[0, half] += scores_grads[half] * small
            grid_ref[1, half] += scores_grads[half] * (1.0 - small)
        proj_ref[rows, 0:128] = query_grad
        proj_ref[rows, 128:256] = keys_grad
        proj_ref[rows, 256:384] = values_grad
        return carry

    lax.fori_loop(0, count, one_sequence, 0)
    proj = proj_ref[...]
    weight_grad_ref[0] = nn(turned[...], proj).astype(BF16)
    pair_ref[0] = jnp.broadcast_to(column_sum(proj.astype(F32)), (8, 384))
    weights = jnp.concatenate([weight_q[...], weight_k[...], weight_v[...]], 1)
    first_in[...] += nt(proj, weights)

    @pl.when(step == PAIRS - 1)
    def _():
        sums_ref[...] = jnp.zeros_like(sums_ref)

        def one_block(b, carry):
            rows = pl.ds(pl.multiple_of(b * SLOT, SLOT), SLOT)
            unit, inverse = standardize(x_ref[rows, :].astype(F32))
            grad = first_in[rows, :]
            sums_ref[0:1, :] += column_sum(grad * unit)
            sums_ref[1:2, :] += column_sum(grad)
            back = norm_back(grad * vec_ref[0:1, :], unit, inverse)
            input_grad_ref[rows, :] = (middle_ref[rows, :] + back).astype(BF16)
            return carry

        lax.fori_loop(0, count, one_block, 0)


def attention_back(buckets, probs, qkv, attended_low, normed, tokens, middle_grad, weight, vecs):
    rows = tokens.shape[0]
    count = rows // SLOT

    def whole(shape):
        return pl.BlockSpec(shape, lambda i: (0,) * len(shape), pipeline_mode=pl.Buffered(1))

    def held(shape):
        return pl.BlockSpec(shape, lambda i: (0,) * len(shape))

    def panel(base):
        return pl.BlockSpec((1, rows, 128), lambda i: (base + i, 0, 0))

    def weight_panel(base):
        return pl.BlockSpec((D, 128), lambda i: (0, base + i))

    return pl.pallas_call(
        attention_back_kernel,
        grid=(PAIRS,),
        in_specs=[
            pl.BlockSpec(memory_space=pltpu.SMEM),
            pl.BlockSpec((2, count, SLOT, SLOT), lambda i: (i, 0, 0, 0)),
            panel(0), panel(PAIRS), panel(2 * PAIRS),
            pl.BlockSpec((rows, 128), lambda i: (0, i)),
            whole((rows, D)), whole((rows, D)), whole((rows, D)),
            weight_panel(0), weight_panel(PAIRS), weight_panel(2 * PAIRS),
            whole((8, D)),
        ],
        out_specs=[
            held((rows, D)),
            pl.BlockSpec((2, 2, SLOT, SLOT), lambda i: (0, i, 0, 0)),
            pl.BlockSpec((1, D, 384), lambda i: (i, 0, 0)),
            pl.BlockSpec((1, 8, 384), lambda i: (i, 0, 0)),
            held((8, D)),
        ],
        out_shape=[
            jax.ShapeDtypeStruct((rows, D), BF16),
            jax.ShapeDtypeStruct((2, HEADS, SLOT, SLOT), F32),
            jax.ShapeDtypeStruct((PAIRS, D, 384), BF16),
            jax.ShapeDtypeStruct((PAIRS, 8, 384), F32),
            jax.ShapeDtypeStruct((8, D), F32),
        ],
        scratch_shapes=[
            pltpu.VMEM((D, rows), BF16),
            pltpu.VMEM((rows, D), F32),
            pltpu.VMEM((rows, 384), BF16),
        ],
        compiler_params=params(dimension_semantics=("arbitrary",)),
        name="attention_backward",
    )(buckets, probs, qkv, qkv, qkv, attended_low, normed, tokens, middle_grad, weight, weight, weight, vecs)


MESH = pl.DeviceIdType.MESH
ANY = pl.ANY


class Place:
    def __init__(self):
        fsdp = lax.axis_index("fsdp")
        dp = lax.axis_index("dp")
        self.z, self.y, self.x, self.core = fsdp // 2, fsdp % 2, dp // 2, dp % 2

    def at(self, z=None, y=None, x=None, core=None):
        z = self.z if z is None else z
        y = self.y if y is None else y
        x = self.x if x is None else x
        core = self.core if core is None else core
        return (z * 2 + y, x * 2 + core)

    def greet(self):
        barrier = pltpu.get_barrier_semaphore()
        peers = [self.at(z=(self.z + k) % 4, y=self.y) for k in range(1, 4)]
        peers += [self.at(z=(self.z + k) % 4, y=1 - self.y) for k in range(4)]
        peers += [
            self.at(x=1 - self.x),
            self.at(core=1 - self.core),
            self.at(x=1 - self.x, core=1 - self.core),
        ]
        for peer in peers:
            pl.semaphore_signal(barrier, inc=1, device_id=peer, device_id_type=MESH)

    def meet(self):
        pl.semaphore_wait(pltpu.get_barrier_semaphore(), 10)


def remote(src, dst, send, recv, peer):
    return pltpu.make_async_remote_copy(
        src_ref=src, dst_ref=dst, send_sem=send, recv_sem=recv, device_id=peer, device_id_type=MESH
    )


def rows_of(first, size):
    return pl.ds(pl.multiple_of(first * size, size), size)


def chunk(kind, ref, r, d):
    if kind == "panel":
        return ref.at[d, rows_of(r, 96), :]
    if kind == "wide":
        return ref.at[rows_of(r, 96), rows_of(d, 768)]
    return ref.at[rows_of(d, 192), rows_of(r, 384)]


class Gather:
    def __init__(self, place, pieces, fulls, send, recv, local):
        self.place, self.pieces, self.fulls = place, pieces, fulls
        self.send, self.recv, self.local = send, recv, local
        self.made = {}

    def slot(self, w, z, y, x):
        return chunk(GATHER_KINDS[w], self.fulls[w], z * 2 + y, x * 2 + self.place.core)

    def copy(self, w, index, src, dst, peer):
        self.made[w, index] = remote(src, dst, self.send.at[w, index], self.recv.at[w, index], peer)
        return self.made[w, index]

    def sources(self, w, k):
        here = self.place
        over_x = (k + GATHER_TURN[w]) % 2 == 0
        near = (here.y, 1 - here.x) if over_x else (1 - here.y, here.x)
        far = (1 - here.y, here.x) if over_x else (here.y, 1 - here.x)
        upper = here.z // 2
        depth = here.z + upper * (3 - 2 * here.z)
        z = k - depth if k == 1 else k
        z = z + upper * (3 - 2 * z) if k else here.z
        return z, near, far

    def plan(self, w):
        here = self.place
        own = self.slot(w, here.z, here.y, here.x)
        self.made[w, "keep"] = pltpu.make_async_copy(self.pieces[w], own, self.local.at[w])
        sibling = here.at(core=1 - here.core)
        pair = here.at(z=here.z + 1 - 2 * (here.z % 2))
        across = here.at(z=3 - here.z)
        for k in range(4):
            z, near, far = self.sources(w, k)
            mine = self.slot(w, z, here.y, here.x)
            src = mine if k else self.pieces[w]
            if k == 0:
                self.copy(w, 1, src, mine, pair)
                self.copy(w, 2, src, mine, across)
            elif k == 1:
                self.copy(w, 3, src, mine, across)
            else:
                self.made[w, "on", k] = remote(
                    src, mine, self.send.at[w, 30 + k], self.recv.at[w, k], pair
                )
            self.copy(w, 4 + k, src, mine, here.at(y=near[0], x=near[1]))
            passed = self.slot(w, z, *near)
            self.copy(w, 8 + 2 * k, src, mine, here.at(y=far[0], x=far[1]))
            self.copy(w, 9 + 2 * k, passed, passed, here.at(y=far[0], x=far[1]))
            third = self.slot(w, z, *far)
            fourth = self.slot(w, z, 1 - here.y, 1 - here.x)
            for n, part in enumerate((src, passed, third, fourth)):
                dst = mine if n == 0 else part
                self.copy(w, 16 + 4 * k + n, part, dst, sibling)

    def when_middle(self, act):
        pl.when(self.place.z * (3 - self.place.z) > 0)(act)

    def begin(self, w, k=0):
        self.made[w, "keep"].start()
        self.made[w, 1].start()
        self.when_middle(lambda: self.made[w, 2].start())

    def relay(self, w, k):
        def on():
            self.made[w, k].wait_recv()
            (self.made[w, 3] if k == 1 else self.made[w, "on", k]).start()

        self.when_middle(on)

    def first(self, w, k):
        if k:
            pl.when(self.place.z * (3 - self.place.z) == 0)(self.made[w, k].wait_recv)
        self.made[w, 4 + k].start()
        self.made[w, 16 + 4 * k].start()

    def second(self, w, k):
        self.made[w, 4 + k].wait_recv()
        self.made[w, 8 + 2 * k].start()
        self.made[w, 9 + 2 * k].start()
        self.made[w, 17 + 4 * k].start()

    def third(self, w, k):
        for n in range(2):
            self.made[w, 8 + 2 * k + n].wait_recv()
            self.made[w, 18 + 4 * k + n].start()

    def finish(self, w):
        for n in range(16):
            self.made[w, 16 + n].wait_recv()
        for n in [1] + list(range(4, 32)):
            self.made[w, n].wait_send()

        def passed_on():
            for made in (self.made[w, 2], self.made[w, 3], self.made[w, "on", 2], self.made[w, "on", 3]):
                made.wait_send()

        self.when_middle(passed_on)
        self.made[w, "keep"].wait()


MIXED, UP, DOWN = range(3)
GATHER_TURN = (0, 1, 0)
GATHER_KINDS = ("wide", "wide", "turned")


BEGIN, RELAY, FIRST, SECOND, THIRD = "begin", "relay", "first", "second", "third"
GATHER_SCHEDULE = [
    [(BEGIN, MIXED, 0), (FIRST, MIXED, 0), (FIRST, UP, 0)],
    [(FIRST, DOWN, 0)],
    [(BEGIN, DOWN, 0)],
    [],
    [],
    [(SECOND, MIXED, 0), (RELAY, MIXED, 1), (FIRST, MIXED, 1), (RELAY, MIXED, 2), (SECOND, UP, 0)],
    [
        (BEGIN, UP, 0),
        (RELAY, DOWN, 1),
        (FIRST, DOWN, 1),
        (FIRST, MIXED, 2),
        (RELAY, MIXED, 3),
        (RELAY, UP, 1),
        (THIRD, MIXED, 0),
        (FIRST, UP, 1),
        (RELAY, UP, 2),
        (SECOND, MIXED, 1),
        (FIRST, MIXED, 3),
        (SECOND, MIXED, 2),
        (RELAY, DOWN, 3),
        (FIRST, UP, 2),
        (SECOND, UP, 1),
        (RELAY, UP, 3),
        (SECOND, MIXED, 3),
        (FIRST, DOWN, 3),
        (FIRST, UP, 3),
        (THIRD, MIXED, 1),
        (THIRD, MIXED, 2),
        (SECOND, UP, 2),
        (THIRD, MIXED, 3),
    ],
    [],
    [],
    [(THIRD, UP, 1)],
    [(SECOND, UP, 3), (RELAY, DOWN, 2), (SECOND, DOWN, 1)],
    [],
    [(THIRD, UP, 0), (THIRD, UP, 2), (SECOND, DOWN, 0)],
    [],
    [(FIRST, DOWN, 2)],
    [],
    [(THIRD, UP, 3), (SECOND, DOWN, 3)],
    [(THIRD, DOWN, 1)],
    [],
    [(SECOND, DOWN, 2)],
    [(THIRD, DOWN, 0), (THIRD, DOWN, 3), (THIRD, DOWN, 2)],
]


def lined(ref, row, width):
    return jnp.concatenate([ref[f, row : row + 1, :width].astype(F32) for f in range(8)], 1)


def forward_kernel(
    lengths, buckets, x_ref, cot_ref, qkv_p, out_p, up_p, down_t, table_p, head_scale, *refs,
):
    vectors = refs[:12]
    (
    normed_ref, qkv_ref, probs_ref, result_ref, mixed_ref, second_ref, act_ref, low_ref, branch_ref,
    middle_grad_ref, attended_low_ref, sums_ref, wide_sums_ref, vec_ref, qkv_out,
    mixed_p, scale_ref, vec_wide, vec_p, qkv_w, up_w, down_w, vec_f, out_w, bias_ref, wide_ref, qkv_bias_ref, table_ref,
    wall_small, wall_large, visual, attended_ref, gelu_ref, slope_ref, grad_ref,
    send, recv, local, small_send, small_recv, small_local, qkv_sem,
    ) = refs[12:]
    step = pl.program_id(0)
    count = pl.num_programs(0) // 2
    place = Place()
    gather = Gather(place, (mixed_p, up_p, down_t), (qkv_w, up_w, down_w), send, recv, local)
    for w in range(3):
        gather.plan(w)
    f = place.z * 2 + place.y
    small = [pltpu.make_async_copy(vec_p, vec_f.at[f], small_local)]
    for k in range(1, 8):
        peer = (f + k) % 8
        small.append(
            remote(
                vec_p, vec_f.at[f], small_send.at[k], small_recv.at[k],
                place.at(z=peer // 2, y=peer % 2),
            )
        )
    keep_qkv = pltpu.make_async_copy(qkv_w, qkv_out, qkv_sem)

    def follow(point):
        for name, w, k in GATHER_SCHEDULE[point]:
            getattr(gather, name)(w, k)

    @pl.when(step == 0)
    def _():
        place.greet()
        vec_wide[...] = jnp.zeros_like(vec_wide)
        for n, vector in enumerate(vectors):
            size = vector.shape[0]
            vec_wide[n : n + 1, :size] = vector[...].astype(F32).reshape(1, size)
        vec_wide[16 : 16 + HEADS, :192] = table_p[...].astype(F32)
        vec_wide[12:13, :HEADS] = head_scale[...].astype(F32).reshape(1, HEADS)
        vec_p[...] = vec_wide[...].astype(BF16)
        head = lax.broadcasted_iota(jnp.int32, (128, D), 0)
        spread = (head == lax.broadcasted_iota(jnp.int32, (128, D), 1) // HEAD_DIM).astype(F32)
        scale_ref[...] = nn(vec_p[...], jnp.concatenate([spread, jnp.zeros((256, D), F32)], 0).astype(BF16))[8:16]
        mixed_p[:, :576] = qkv_p[...]
        mixed_p[:, 576:] = out_p[...]
        place.meet()
        for made in small:
            made.start()
        follow(0)
        for made in small:
            made.wait()
        for n in range(8):
            vec_ref[n : n + 1, :] = lined(vec_f, n, 96)
        for n in range(3):
            wide_ref[n : n + 1, :] = lined(vec_f, 8 + n, 384)
        pair = lined(vec_f, 11, 192)
        qkv_bias_ref[0:1, :] = jnp.concatenate([pair[:, :D], jnp.zeros((1, D), F32), pair[:, D:]], 1)
        lane = lax.broadcasted_iota(jnp.int32, (1, 3 * D), 1)
        qkv_bias_ref[1:2, :] = jnp.where(lane < D, HEAD_DIM ** (-0.5), 1.0)
        table_ref[...] = jnp.concatenate([vec_f[n, 16:32, :192].astype(F32) for n in range(8)], 1)
        bias_walls(table_ref, wall_small, wall_large, visual)
        heads = functools.partial(bias_head, table_ref, bias_ref, wall_small, wall_large, visual)
        for n, last in enumerate((2, 4, 6, 9, HEADS)):
            follow(1 + n)
            lax.fori_loop((0, 2, 4, 6, 9)[n], last, heads, 0)
        follow(6)
        gather.finish(MIXED)
        keep_qkv.start()
        sums_ref[...] = jnp.zeros_like(sums_ref)
        wide_sums_ref[...] = jnp.zeros_like(wide_sums_ref)

    def progress(spot):
        for s in range(count):
            if GATHER_SCHEDULE[7 + 3 * s + spot]:
                pl.when(step == s)(functools.partial(follow, 7 + 3 * s + spot))

    @pl.when(step < count)
    def _():
        rows = pl.ds(pl.multiple_of(step * SLOT, SLOT), SLOT)
        progress(0)
        unit, inverse = standardize(x_ref[...].astype(F32))
        normed = (unit * vec_ref[0:1, :] + vec_ref[1:2, :]).astype(BF16)
        normed_ref[...] = normed
        for d in range(4):
            cols = slice(576 * d, 576 * d + 576)
            out = (nn(normed, qkv_w[:, 768 * d : 768 * d + 576]) + qkv_bias_ref[0:1, cols]) * qkv_bias_ref[1:2, cols]
            qkv_ref[:, cols] = out.astype(BF16)
        live = lax.broadcasted_iota(jnp.int32, (SLOT, SLOT), 1) < lengths[step]
        bucket = buckets[step]
        for pair in range(PAIRS):
            if pair % 3 == 0:
                progress(1 + pair // 3)
            query = qkv_ref[:, 128 * pair : 128 * pair + 128]
            keys = qkv_ref[:, D + 128 * pair : D + 128 * pair + 128]
            values = qkv_ref[:, 2 * D + 128 * pair : 2 * D + 128 * pair + 128]
            bias = [bias_ref[bucket, 2 * pair + half] for half in range(2)]
            probs, out = attend(query, keys, values, bias, live)
            for half in range(2):
                probs_ref[2 * pair + half, 0] = probs[half]
            attended_ref[rows, 128 * pair : 128 * pair + 128] = out

    @pl.when(step == count)
    def _():
        follow(7 + 3 * count)
        gather.finish(UP)
        for d in range(4):
            out_w[:, 192 * d : 192 * d + 192] = qkv_w[:, 768 * d + 576 : 768 * d + 768]

    @pl.when(step >= count)
    def _():
        rows = pl.ds(pl.multiple_of((step - count) * SLOT, SLOT), SLOT)

        def wait_down():
            @pl.when(step == count)
            def _():
                follow(8 + 3 * count)
                gather.finish(DOWN)

        feed_block(
            x_ref, attended_ref.at[rows, :], cot_ref, out_w, up_w, down_w, vec_ref, wide_ref,
            scale_ref.at[4:5, :],
            result_ref, mixed_ref, second_ref, act_ref, low_ref, branch_ref, middle_grad_ref,
            attended_low_ref, sums_ref, wide_sums_ref, gelu_ref, slope_ref, grad_ref, wait_down,
        )

    @pl.when(step == 2 * count - 1)
    def _():
        keep_qkv.wait()


def forward(lengths, buckets, tokens, cotangent, qkv_p, out_p, up_p, down_p, table_p, head_scale, vectors):
    rows = tokens.shape[0]
    count = rows // SLOT
    smem = pl.BlockSpec(memory_space=pltpu.SMEM)

    def early(shape):
        return pl.BlockSpec(shape, lambda i: (jnp.minimum(i, count - 1),) + (0,) * (len(shape) - 1))

    def late(shape):
        return pl.BlockSpec(shape, lambda i: (jnp.maximum(i - count, 0),) + (0,) * (len(shape) - 1))

    def held(shape):
        return pl.BlockSpec(shape, lambda i: (0,) * len(shape))

    block = (SLOT, D)
    wide = (SLOT, FF)
    return pl.pallas_call(
        forward_kernel,
        grid=(2 * count,),
        in_specs=[
            smem, smem, pl.BlockSpec(block, lambda i: (i % count, 0)), late(block),
            held((96, 576)), held((96, 192)), pl.BlockSpec(memory_space=ANY),
            pl.BlockSpec(memory_space=ANY), held((HEADS, 192)), held((HEADS,)),
        ]
        + [held(vector.shape) for vector in vectors],
        out_specs=[
            early(block), early((SLOT, 3 * D)),
            pl.BlockSpec((HEADS, 1, SLOT, SLOT), lambda i: (0, jnp.minimum(i, count - 1), 0, 0)),
            late(block), late(block), late(block), late(wide), late(wide), late(block), late(block),
            late(block), held((16, D)), held((8, FF)), held((8, D)), pl.BlockSpec(memory_space=ANY),
        ],
        out_shape=[
            jax.ShapeDtypeStruct((rows, D), BF16),
            jax.ShapeDtypeStruct((rows, 3 * D), BF16),
            jax.ShapeDtypeStruct((HEADS, count, SLOT, SLOT), BF16),
            jax.ShapeDtypeStruct((rows, D), BF16),
            jax.ShapeDtypeStruct((rows, D), BF16),
            jax.ShapeDtypeStruct((rows, D), BF16),
            jax.ShapeDtypeStruct((rows, FF), BF16),
            jax.ShapeDtypeStruct((rows, FF), BF16),
            jax.ShapeDtypeStruct((rows, D), BF16),
            jax.ShapeDtypeStruct((rows, D), F32),
            jax.ShapeDtypeStruct((rows, D), BF16),
            jax.ShapeDtypeStruct((16, D), F32),
            jax.ShapeDtypeStruct((8, FF), F32),
            jax.ShapeDtypeStruct((8, D), F32),
            jax.ShapeDtypeStruct((D, FF), BF16),
        ],
        scratch_shapes=[
            pltpu.VMEM((96, D), BF16),
            pltpu.VMEM((8, D), F32),
            pltpu.VMEM((32, 384), F32),
            pltpu.VMEM((32, 384), BF16),
            pltpu.VMEM((D, FF), BF16),
            pltpu.VMEM((D, FF), BF16),
            pltpu.VMEM((D, FF), BF16),
            pltpu.VMEM((8, 32, 384), BF16),
            pltpu.VMEM((D, D), BF16),
            pltpu.VMEM((2, HEADS, SLOT, SLOT), BF16),
            pltpu.VMEM((8, FF), F32),
            pltpu.VMEM((8, 3 * D), F32),
            pltpu.VMEM((16, TABLE), F32),
            pltpu.VMEM((2, 128, 128), F32),
            pltpu.VMEM((4, 256, 128), F32),
            pltpu.VMEM((SLOT, SLOT), F32),
            pltpu.VMEM((rows, D), F32),
            pltpu.VMEM(wide, F32),
            pltpu.VMEM(wide, F32),
            pltpu.VMEM(wide, F32),
            pltpu.SemaphoreType.DMA((3, 34)),
            pltpu.SemaphoreType.DMA((3, 32)),
            pltpu.SemaphoreType.DMA((3,)),
            pltpu.SemaphoreType.DMA((8,)),
            pltpu.SemaphoreType.DMA((8,)),
            pltpu.SemaphoreType.DMA,
            pltpu.SemaphoreType.DMA,
        ],
        compiler_params=params(
            collective_id=1, has_side_effects=True, dimension_semantics=("arbitrary",)
        ),
        name="forward",
    )(lengths, buckets, tokens, cotangent, qkv_p, out_p, up_p, down_p, table_p, head_scale, *vectors)


ORDER = (1, 2, 3, 0)


class Scatter:
    def __init__(self, place, kind, grad, out, buffers, flip=0, offset=0):
        self.place, self.kind, self.grad, self.out = place, kind, grad, out
        self.flip, self.offset = flip, offset
        self.cores, self.over_x, self.over_y, self.far, self.quarter, self.send, self.recv = buffers
        self.made = {}
        here = place
        for k in range(4):
            z = (here.z + k) % 4
            mine = 2 * here.x + here.core
            other = 2 * (1 - here.x) + here.core
            for x in range(2):
                self.copy(
                    k, x, self.block(2 * x + 1 - here.core, z), self.from_core(k, x),
                    here.at(core=1 - here.core),
                )
            if self.x_first(k):
                self.copy(k, 2, self.block(other, z), self.over_x.at[k // 2], here.at(x=1 - here.x))
                self.copy(
                    k, 4, self.part(mine, z, 1 - here.y), self.far.at[k], here.at(y=1 - here.y)
                )
            else:
                for x in range(2):
                    self.copy(
                        k, 2 + x, self.part(2 * x + here.core, z, 1 - here.y),
                        self.over_y.at[k // 2, x], here.at(y=1 - here.y),
                    )
                self.copy(k, 4, self.part(other, z, here.y), self.far.at[k], here.at(x=1 - here.x))
            if k:
                self.copy(k, 5, self.part(mine, z, here.y), self.quarter.at[k - 1], here.at(z=z))

    def x_first(self, k):
        return (k + self.flip) % 2 == 0

    def from_core(self, k, x):
        return self.cores.at[k, x, :, self.offset : self.offset + self.over_x.shape[-1]]

    def block(self, d, z):
        if self.kind == "panel":
            return self.grad.at[d, rows_of(z, 192), :]
        if self.kind == "wide":
            return self.grad.at[rows_of(z, 192), rows_of(d, 768)]
        return self.grad.at[rows_of(d, 192), rows_of(z, 768)]

    def part(self, d, z, y):
        if self.kind == "panel":
            return self.grad.at[d, rows_of(2 * z + y, 96), :]
        if self.kind == "wide":
            return self.grad.at[rows_of(2 * z + y, 96), rows_of(d, 768)]
        return self.grad.at[rows_of(d, 192), rows_of(2 * z + y, 384)]

    def copy(self, k, index, src, dst, peer):
        self.made[k, index] = remote(src, dst, self.send.at[k, index], self.recv.at[k, index], peer)

    def add(self, target, source):
        def some(n, carry):
            at = rows_of(n, 16)
            target[at, :] = target[at, :] + source[at, :]
            return carry

        lax.fori_loop(0, target.shape[0] // 16, some, 0)

    def core(self, k):
        for x in range(2):
            self.made[k, x].start()

    def plane(self, k):
        here = self.place
        z = (here.z + k) % 4
        for x in range(2):
            self.made[k, x].wait_recv()
            self.add(self.block(2 * x + here.core, z), self.from_core(k, x))
        self.made[k, 2].start()
        if not self.x_first(k):
            self.made[k, 3].start()

    def turn(self, k):
        here = self.place
        z = (here.z + k) % 4
        self.made[k, 2].wait_recv()
        if self.x_first(k):
            self.add(self.block(2 * here.x + here.core, z), self.over_x.at[k // 2])
        else:
            self.made[k, 3].wait_recv()
            for x in range(2):
                self.add(self.part(2 * x + here.core, z, here.y), self.over_y.at[k // 2, x])
        self.made[k, 4].start()

    def line(self, k):
        here = self.place
        self.made[k, 4].wait_recv()
        self.add(self.part(2 * here.x + here.core, (here.z + k) % 4, here.y), self.far.at[k])
        if k:
            self.made[k, 5].start()

    def end(self):
        here = self.place
        for k in range(1, 4):
            self.made[k, 5].wait_recv()
        total = self.part(2 * here.x + here.core, here.z, here.y)[...].astype(F32)
        for k in range(3):
            total = total + self.quarter[k].astype(F32)
        self.out[...] = total[:, : self.out.shape[1]]
        for made in self.made.values():
            made.wait_send()


def scatter_scratch(kind, width):
    half = (192, width // 2) if kind == "turned" else (96, width)
    return [
        pltpu.VMEM((4, 2, 192, width), BF16),
        pltpu.VMEM((2, 192, width), BF16),
        pltpu.VMEM((2, 2) + half, BF16),
        pltpu.VMEM((4,) + half, BF16),
        pltpu.VMEM((3,) + half, BF16),
        pltpu.SemaphoreType.DMA((4, 6)),
        pltpu.SemaphoreType.DMA((4, 6)),
    ]


def pack_sums(sums_ref, first_ref, wide_ref, pair, table_ref, packed):
    low = first_ref[0:2, :]
    narrow = sums_ref[...]
    group = lax.broadcasted_iota(jnp.int32, (D, 128), 0) // HEAD_DIM
    pick = (group == lax.broadcasted_iota(jnp.int32, (D, 128), 1)).astype(F32).astype(BF16)
    high, rest = split_low(narrow[8:16])
    heads = (nn(high, pick) + nn(rest, pick))[0:1]
    heads = jnp.concatenate([heads, jnp.zeros((1, 64), F32)], 1)
    for f in range(8):
        at = slice(96 * f, 96 * f + 96)
        packed[f, 0:1, :] = jnp.concatenate(
            [low[0:1, at], low[1:2, at], narrow[2:3, at], narrow[3:4, at]], 1
        )
        packed[f, 1:2, :] = jnp.concatenate([narrow[n : n + 1, at] for n in range(4, 8)], 1)
        packed[f, 2:5, :] = wide_ref[0:3, 384 * f : 384 * f + 384]
        at = slice(192 * f, 192 * f + 192)
        packed[f, 5:6, :] = jnp.concatenate([pair[:, at], heads], 1)
        for n in range(PAIRS):
            packed[f, 6 + n : 7 + n, :] = jnp.concatenate(
                [table_ref[2 * n : 2 * n + 1, at], table_ref[2 * n + 1 : 2 * n + 2, at]], 1
            )
        packed[f, 12:16, :] = jnp.zeros((4, 384), F32)


class SmallSums:
    def __init__(self, place, packed, rows, peers, sems):
        self.place, self.packed, self.rows, self.peers = place, packed, rows, peers
        self.send, self.recv = sems

    def begin(self):
        here = self.place
        f = here.z * 2 + here.y
        self.made = []
        for k in range(1, 8):
            to = (f + k) % 8
            made = remote(
                self.packed.at[to], self.rows.at[k - 1], self.send.at[k], self.recv.at[k],
                here.at(z=to // 2, y=to % 2),
            )
            made.start()
            self.made.append(made)

    def cross(self):
        here = self.place
        f = here.z * 2 + here.y
        for made in self.made:
            made.wait()
        total = self.packed[f]
        for k in range(7):
            total = total + self.rows[k]
        self.peers[0] = total
        d = here.x * 2 + here.core
        self.made = []
        for k in range(1, 4):
            to = (d + k) % 4
            made = remote(
                self.peers.at[0], self.peers.at[k], self.send.at[7 + k], self.recv.at[7 + k],
                here.at(x=to // 2, core=to % 2),
            )
            made.start()
            self.made.append(made)

    def end(self):
        for made in self.made:
            made.wait()
        return (self.peers[0] + self.peers[1]) + (self.peers[2] + self.peers[3])


GRAD_DOWN, GRAD_UP, GRAD_OUT, GRAD_QKV_A, GRAD_QKV_B = range(5)
PLANE, TURN, LINE = "plane", "turn", "line"
BACK_SCHEDULE = {
    3: [(GRAD_DOWN, PLANE, 0)],
    4: [(GRAD_DOWN, PLANE, 1)],
    5: [(GRAD_DOWN, PLANE, 2)],
    6: [(GRAD_DOWN, PLANE, 3), (GRAD_DOWN, TURN, 0)],
    7: [(GRAD_DOWN, TURN, 1)],
    10: [
        (GRAD_UP, PLANE, 0),
        (GRAD_DOWN, TURN, 3),
        (GRAD_DOWN, TURN, 2),
        (GRAD_DOWN, LINE, 1),
        (GRAD_UP, PLANE, 1),
        (GRAD_UP, PLANE, 2),
    ],
    11: [(GRAD_DOWN, LINE, 0)],
    12: [(GRAD_DOWN, LINE, 2)],
    13: [(GRAD_UP, TURN, 0), (GRAD_UP, PLANE, 3)],
    14: [(GRAD_OUT, PLANE, 0), (GRAD_OUT, PLANE, 1)],
    15: [(GRAD_UP, TURN, 1), (GRAD_DOWN, LINE, 3)],
    16: [(GRAD_OUT, PLANE, 3), (GRAD_OUT, PLANE, 2), (GRAD_UP, LINE, 0)],
    17: [(GRAD_UP, TURN, 2)],
    18: [(GRAD_UP, TURN, 3), (GRAD_UP, LINE, 1)],
    19: [(GRAD_OUT, TURN, 3), (GRAD_OUT, TURN, 2), (GRAD_OUT, TURN, 1), (GRAD_OUT, TURN, 0)],
    20: [(GRAD_QKV_A, PLANE, 2), (GRAD_QKV_A, PLANE, 1), (GRAD_UP, LINE, 2), (GRAD_QKV_A, PLANE, 0)],
    21: [(GRAD_QKV_B, PLANE, 0), (GRAD_QKV_B, PLANE, 1)],
}
BACK_DRAIN = [
    (GRAD_QKV_A, TURN, 2),
    (GRAD_QKV_A, TURN, 1),
    (GRAD_OUT, LINE, 2),
    (GRAD_OUT, LINE, 3),
    (GRAD_OUT, LINE, 0),
    (GRAD_QKV_A, PLANE, 3),
    (GRAD_QKV_A, TURN, 0),
    (GRAD_QKV_A, LINE, 2),
    (GRAD_QKV_B, TURN, 0),
    (GRAD_OUT, LINE, 1),
    (GRAD_QKV_B, PLANE, 2),
    (GRAD_QKV_B, TURN, 1),
    (GRAD_QKV_B, PLANE, 3),
    (GRAD_QKV_A, LINE, 1),
    (GRAD_QKV_A, TURN, 3),
    (GRAD_QKV_A, LINE, 0),
    (GRAD_QKV_B, LINE, 0),
    (GRAD_QKV_B, TURN, 2),
    (GRAD_QKV_B, TURN, 3),
    (GRAD_QKV_B, LINE, 1),
    (GRAD_UP, LINE, 3),
    (GRAD_QKV_A, LINE, 3),
    (GRAD_QKV_B, LINE, 2),
    (GRAD_QKV_B, LINE, 3),
]


def backward_kernel(
    buckets, cot_hbm, act_ref, second_hbm, low_ref, mixed_hbm, branch_hbm, normed_hbm,
    probs_ref, query_ref, keys_ref, values_ref, attended_low_ref, vec_ref, sums_ref, wide_ref,
    x_hbm, middle_hbm, weight_hbm,
    input_grad_ref, down_out, up_out, out_out, qkv_out, total_ref,
    left, turned, middle_ref, first_in, proj, grid_ref, down_ref, up_ref, out_ref, qkv_a, qkv_b,
    table_ref, first_ref, wall_small, wall_large, packed, gathered, peers, small_send, small_recv,
    loading, middle_sem, *buffers,
):
    step = pl.program_id(0)
    place = Place()
    parts = [
        Scatter(place, "turned", down_ref, down_out, buffers[0:7]),
        Scatter(place, "wide", up_ref, up_out, buffers[7:14]),
        Scatter(place, "panel", out_ref, out_out, buffers[14:21]),
        Scatter(place, "panel", qkv_a, qkv_out.at[:, 0:256], buffers[0:1] + buffers[21:27]),
        Scatter(
            place, "panel", qkv_b, qkv_out.at[:, 256:576], buffers[0:1] + buffers[27:33], 1, 256
        ),
    ]
    small = SmallSums(place, packed, gathered, peers, (small_send, small_recv))
    count = query_ref.shape[0] // SLOT

    def load(n, src, dst):
        return pltpu.make_async_copy(src, dst, loading.at[n])

    load_cot = load(0, cot_hbm, left.at[0])
    load_second = load(1, second_hbm, left.at[1])
    load_mixed = load(2, mixed_hbm, left.at[0])
    load_branch = load(3, branch_hbm, left.at[1])
    load_normed = load(4, normed_hbm, left.at[0])
    load_x = load(5, x_hbm, left.at[1])

    def load_middle(b):
        n = b % 2
        return pltpu.make_async_copy(middle_hbm.at[rows_of(b, SLOT), :], middle_ref.at[n], middle_sem.at[n])

    load_weight = load(7, weight_hbm, down_ref)

    def progress(at):
        for name, event, n in BACK_SCHEDULE.get(at, []):
            getattr(parts[name], event)(ORDER[n])

    def down_panel():
        z = (place.z + 1 + step) % 4
        down_ref[:, rows_of(z, 768)] = nn(turned[...], act_ref[...]).astype(BF16)

    @pl.when(step == 0)
    def _():
        place.greet()
        load_cot.start()
        load_second.start()
        place.meet()

    for at in BACK_SCHEDULE:
        if at < 19:
            pl.when(step == at)(functools.partial(progress, at))

    @pl.when(step < 4)
    def _():
        @pl.when(step == 0)
        def _():
            load_cot.wait()
            turned[...] = left[0].T
            load_mixed.start()

        down_panel()
        for n in range(4):
            pl.when(step == n)(functools.partial(parts[GRAD_DOWN].core, ORDER[n]))

    @pl.when((step >= 4) & (step < 8))
    def _():
        @pl.when(step == 4)
        def _():
            load_second.wait()
            turned[...] = left[1].T
            load_branch.start()

        up_ref[:, rows_of(step - 4, 768)] = nn(turned[...], low_ref[...]).astype(BF16)

        @pl.when(step == 7)
        def _():
            for k in ORDER:
                parts[GRAD_UP].core(k)

    @pl.when(step == 8)
    def _():
        load_mixed.wait()
        turned[...] = left[0].T
        load_normed.start()
        load_branch.wait()
        for d in range(4):
            out_ref[d] = nn(turned[...], left[1, :, 192 * d : 192 * d + 192]).astype(BF16)
        for k in ORDER:
            parts[GRAD_OUT].core(k)
        load_x.start()
        table_grad_start(table_ref, wall_small, wall_large)

    @pl.when((step >= 9) & (step < 15))
    def _():
        pair = step - 9
        cols = rows_of(pair, 128)
        for s in range(count):
            rows = slice(s * SLOT, s * SLOT + SLOT)
            query_grad, keys_grad, values_grad, scores_grads = attend_back(
                query_ref[rows, :], keys_ref[rows, :], values_ref[rows, :], attended_low_ref[rows, :],
                [probs_ref[half, s] for half in range(2)],
            )
            proj[0, rows, cols] = query_grad
            proj[1, rows, cols] = keys_grad
            proj[2, rows, cols] = values_grad
            chosen = jnp.where(buckets[s] == 0, 1.0, 0.0)
            for half in range(2):
                if s == 0:
                    grid_ref[0, half] = scores_grads[half] * chosen
                    grid_ref[1, half] = scores_grads[half] * (1.0 - chosen)
                else:
                    grid_ref[0, half] += scores_grads[half] * chosen
                    grid_ref[1, half] += scores_grads[half] * (1.0 - chosen)
        for half in range(2):
            table_grad_head(grid_ref, table_ref, wall_small, wall_large, 2 * pair + half, half)

    def lay_panel(d):
        def lay(pieces):
            at = 0
            for n, first, last in pieces:
                left[0, :, at : at + last - first] = proj[n, :, first:last]
                at += last - first

        cuts = (
            [(0, 0, 576)], [(0, 576, 768), (1, 0, 384)], [(1, 384, 768), (2, 0, 192)], [(2, 192, 768)],
        )
        for n, pieces in enumerate(cuts):
            pl.when(d == n)(functools.partial(lay, pieces))

    @pl.when((step >= 15) & (step < 19))
    def _():
        @pl.when(step == 15)
        def _():
            parts[GRAD_DOWN].end()
            load_weight.start()
            load_normed.wait()
            turned[...] = left[0].T
            first_in[...] = jnp.zeros_like(first_in)

        d = step - 15
        lay_panel(d)
        grad = nn(turned[...], left[0, :, :576]).astype(BF16)
        qkv_a[d] = grad[:, :256]
        qkv_b[d] = jnp.concatenate([grad[:, 256:], jnp.zeros((D, 64), BF16)], 1)

        @pl.when(step == 15)
        def _():
            load_weight.wait()

        @pl.when(step == 18)
        def _():
            for k in ORDER:
                parts[GRAD_QKV_A].core(k)
                parts[GRAD_QKV_B].core(k)

        first_in[...] += nt(left[0, :, :576], down_ref[:, pl.ds(pl.multiple_of(768 * d, 768), 576)])

    @pl.when(step == 19)
    def _():
        progress(19)
        load_middle(0).start()
        load_x.wait()
        first_ref[...] = jnp.zeros_like(first_ref)

        def one_block(b, carry):
            rows = pl.ds(pl.multiple_of(b * SLOT, SLOT), SLOT)
            unit, inverse = standardize(left[1, rows, :].astype(F32))
            grad = first_in[rows, :]
            first_ref[0:1, :] += column_sum(grad * unit)
            first_ref[1:2, :] += column_sum(grad)
            back = norm_back(grad * vec_ref[0:1, :], unit, inverse)

            @pl.when(b + 1 < count)
            def _():
                load_middle(b + 1).start()

            load_middle(b).wait()
            input_grad_ref[rows, :] = (middle_ref[b % 2] + back).astype(BF16)
            return carry

        lax.fori_loop(0, count, one_block, 0)
        progress(20)
        table_grad_end(table_ref, wall_small, wall_large)
        pair = jnp.concatenate([tall_sum(proj.at[0]), tall_sum(proj.at[2])], 1)
        progress(21)
        pack_sums(sums_ref, first_ref, wide_ref, pair, table_ref, packed)
        small.begin()
        for n, (name, event, k) in enumerate(BACK_DRAIN):
            if n == len(BACK_DRAIN) // 2:
                small.cross()
            getattr(parts[name], event)(ORDER[k])
        parts[GRAD_UP].end()
        parts[GRAD_OUT].end()
        total_ref[...] = small.end()
        parts[GRAD_QKV_A].end()
        parts[GRAD_QKV_B].end()


def backward(
    buckets, cotangent, act, second, low, mixed, branch, normed, probs, qkv, attended_low, vecs,
    sums, wide, tokens, middle_grad, weight,
):
    rows = cotangent.shape[0]
    count = rows // SLOT
    any_space = pl.BlockSpec(memory_space=ANY)

    def held(shape):
        return pl.BlockSpec(shape, lambda i: (0,) * len(shape))

    def pair(i):
        return jnp.clip(i - 9, 0, PAIRS - 1)

    def panel(base):
        return pl.BlockSpec((rows, 128), lambda i: (0, base + pair(i)))

    def act_panel(i):
        return (0, (lax.axis_index("fsdp") // 2 + 1 + jnp.minimum(i, 3)) % 4)

    outs = [(192, 384), (96, 768), (96, 192), (96, 576), (16, 384)]
    return pl.pallas_call(
        backward_kernel,
        grid=(20,),
        in_specs=[
            pl.BlockSpec(memory_space=pltpu.SMEM),
            any_space,
            pl.BlockSpec((rows, D), act_panel),
            any_space,
            pl.BlockSpec((rows, D), lambda i: (0, jnp.clip(i - 4, 0, 3))),
            any_space, any_space, any_space,
            pl.BlockSpec((2, count, SLOT, SLOT), lambda i: (pair(i), 0, 0, 0)),
            panel(0), panel(PAIRS), panel(2 * PAIRS), panel(0),
            held((8, D)), held((16, D)), held((8, FF)),
            any_space, any_space, any_space,
        ],
        out_specs=[held((rows, D))] + [held(shape) for shape in outs],
        out_shape=[jax.ShapeDtypeStruct((rows, D), BF16)]
        + [jax.ShapeDtypeStruct(shape, F32) for shape in outs],
        scratch_shapes=[
            pltpu.VMEM((2, rows, D), BF16),
            pltpu.VMEM((D, rows), BF16),
            pltpu.VMEM((2, SLOT, D), F32),
            pltpu.VMEM((rows, D), F32),
            pltpu.VMEM((3, rows, D), BF16),
            pltpu.VMEM((2, 2, SLOT, SLOT), F32),
            pltpu.VMEM((D, FF), BF16),
            pltpu.VMEM((D, FF), BF16),
            pltpu.VMEM((4, D, 192), BF16),
            pltpu.VMEM((4, D, 256), BF16),
            pltpu.VMEM((4, D, 384), BF16),
            pltpu.VMEM((16, TABLE), F32),
            pltpu.VMEM((8, D), F32),
            pltpu.VMEM((2, 128, 128), F32),
            pltpu.VMEM((4, 256, 128), F32),
            pltpu.VMEM((8, 16, 384), F32),
            pltpu.VMEM((7, 16, 384), F32),
            pltpu.VMEM((4, 16, 384), F32),
            pltpu.SemaphoreType.DMA((11,)),
            pltpu.SemaphoreType.DMA((11,)),
            pltpu.SemaphoreType.DMA((8,)),
            pltpu.SemaphoreType.DMA((2,)),
        ]
        + scatter_scratch("turned", 768) + scatter_scratch("wide", 768)
        + scatter_scratch("panel", 192) + scatter_scratch("panel", 256)[1:]
        + scatter_scratch("panel", 384)[1:],
        compiler_params=pltpu.CompilerParams(
            collective_id=2, has_side_effects=True, dimension_semantics=("arbitrary",),
            vmem_limit_bytes=BACK_LIMIT,
        ),
        name="backward",
    )(
        buckets, cotangent, act, second, low, mixed, branch, normed, probs, qkv, qkv, qkv,
        attended_low, vecs, sums, wide, tokens, middle_grad, weight,
    )


def emit_kernel(count, total_ref, *refs):
    sources = refs[:count]
    targets = refs[count : 2 * count]
    small = refs[2 * count : 2 * count + 14]
    held = refs[2 * count + 14 : -2]
    into, out = refs[-2:]
    loads = [
        pltpu.make_async_copy(src, dst, into.at[n]) for n, (src, dst) in enumerate(zip(sources, held))
    ]
    made = [
        pltpu.make_async_copy(src, dst, out.at[n]) for n, (src, dst) in enumerate(zip(held, targets))
    ]
    for each in loads:
        each.start()
    for load, each in zip(loads, made):
        load.wait()
        each.start()
    total = total_ref[...]
    for n in range(8):
        at = 96 * (n % 4)
        small[n][...] = total[n // 4 : n // 4 + 1, at : at + 96].reshape(96)
    for n in range(3):
        small[8 + n][...] = total[2 + n : 3 + n, :].reshape(384)
    small[11][...] = total[5:6, 0:192].reshape(192)
    small[12][...] = total[5:6, 192:204].reshape(HEADS)
    for n in range(PAIRS):
        small[13][2 * n : 2 * n + 1, :] = total[6 + n : 7 + n, 0:192]
        small[13][2 * n + 1 : 2 * n + 2, :] = total[6 + n : 7 + n, 192:384]
    for each in made:
        each.wait()


def emit(total, *large):
    vmem = pl.BlockSpec(memory_space=pltpu.VMEM)
    any_space = pl.BlockSpec(memory_space=ANY)
    small = [(96,)] * 8 + [(384,)] * 3 + [(192,), (HEADS,), (HEADS, 192)]
    return pl.pallas_call(
        functools.partial(emit_kernel, len(large)),
        in_specs=[vmem] + [any_space] * len(large),
        out_specs=[any_space] * len(large) + [vmem] * len(small),
        out_shape=[jax.ShapeDtypeStruct(part.shape, part.dtype) for part in large]
        + [jax.ShapeDtypeStruct(shape, F32) for shape in small],
        scratch_shapes=[pltpu.VMEM(part.shape, part.dtype) for part in large]
        + [pltpu.SemaphoreType.DMA((len(large),))] * 2,
        compiler_params=params(),
        name="emit",
    )(total, *large)


def gather_matrix(piece):
    rows = lax.all_gather(piece, "fsdp", axis=0, tiled=True)
    return lax.all_gather(rows, "dp", axis=1, tiled=True)


def scatter_matrix(grad):
    part = lax.psum_scatter(grad, "dp", scatter_dimension=1, tiled=True).astype(F32)
    return lax.psum_scatter(part, "fsdp", scatter_dimension=0, tiled=True)


def body(
    tokens, cotangent, lengths, buckets, qkv_weight, query_value_bias, out_weight, out_bias,
    up_weight, up_bias, down_weight, down_bias, first_gain, first_shift, mix_gain, mix_shift,
    second_gain, second_shift, hidden_gain, hidden_shift, head_scale, position_table,
):
    parts = lax.axis_size("fsdp")
    own_kernels = (parts, lax.axis_size("dp")) == (8, 4)
    narrow = [
        first_gain, first_shift, mix_gain, mix_shift, second_gain, second_shift, out_bias, down_bias,
    ]
    wide = [up_bias, hidden_gain, hidden_shift]
    a = D // parts
    b = FF // parts
    if own_kernels:
        (
            normed, qkv, probs, result, mixed, second, act, low, branch, middle_grad, attended_low,
            sums, wide_sums, vecs, qkv_full,
        ) = forward(
            lengths, buckets, tokens, cotangent, qkv_weight, out_weight, up_weight, down_weight.T,
            position_table.T, head_scale, narrow + wide + [query_value_bias],
        )
        input_grad, down_owned, up_owned, out_owned, qkv_owned, total = backward(
            buckets, cotangent, act, second, low, mixed, branch, normed, probs, qkv, attended_low,
            vecs, sums, wide_sums, tokens, middle_grad, qkv_full,
        )
        result, input_grad, qkv_owned, out_owned, up_owned, down_owned, *small = emit(
            total, result, input_grad, qkv_owned, out_owned, up_owned, down_owned
        )
        down_owned = down_owned.T
        narrow_owned = small[:8]
        wide_owned = small[8:11]
        pair_owned, scale_grad, table_owned = small[11], small[12], small[13].T
    else:
        packed = jnp.concatenate(
            [jnp.pad(jnp.stack(narrow), ((0, 0), (0, b - a))), jnp.stack(wide)]
            + [jnp.pad(query_value_bias, (0, b - 2 * a))[None], jnp.zeros((4, b), BF16)]
            + [jnp.pad(position_table.T, ((0, 4), (0, b - 2 * a)))]
        )
        scales = jnp.repeat(head_scale.astype(F32), HEAD_DIM)[None]
        gathered = lax.all_gather(packed, "fsdp", axis=0)
        qkv_full = gather_matrix(qkv_weight)
        out_full = gather_matrix(out_weight)
        up_full = gather_matrix(up_weight)
        down_full = gather_matrix(down_weight).T
        gathered = gathered.astype(F32)
        vecs = gathered[:, :8, :a].transpose(1, 0, 2).reshape(8, D)
        wides = jnp.pad(gathered[:, 8:11].transpose(1, 0, 2).reshape(3, FF), ((0, 5), (0, 0)))
        pair = gathered[:, 11, : 2 * a].reshape(1, 2 * D)
        table = gathered[:, 16:, : 2 * a].transpose(1, 0, 2).reshape(16, TABLE)
        qkv_bias = jnp.concatenate([pair[:, :D], jnp.zeros((1, D), F32), pair[:, D:]], 1)

        bias = build_bias(table)
        normed, qkv, probs, attended = attention(
            lengths, buckets, tokens, vecs, qkv_full, qkv_bias, bias
        )
        (
            result, mixed, second, act, low, branch, middle_grad, attended_low, sums, wide_sums,
        ) = feed_forward(tokens, attended, cotangent, out_full, up_full, down_full, vecs, wides, scales)
        down_grad = outer_product(cotangent, act, 512)
        up_grad = outer_product(second, low, 512)
        out_grad = outer_product(mixed, branch, 256)
        input_grad, grids, qkv_grad, pair_sums, first_sums = attention_back(
            buckets, probs, qkv, attended_low, normed, tokens, middle_grad, qkv_full, vecs
        )
        table_sums = table_grad(grids)
        qkv_natural = qkv_grad.reshape(PAIRS, D, 3, 128).transpose(1, 2, 0, 3).reshape(D, 3 * D)

        qkv_owned = scatter_matrix(qkv_natural)
        out_owned = scatter_matrix(out_grad)
        up_owned = scatter_matrix(up_grad)
        down_owned = scatter_matrix(down_grad.T)
        pair_grad = pair_sums[:, 0].reshape(PAIRS, 3, 128).transpose(1, 0, 2).reshape(3, D)
        pair_grad = jnp.concatenate([pair_grad[0], pair_grad[2]])
        narrow_sums = jnp.concatenate([first_sums[:2], sums[2:8]], 0)
        packed = jnp.concatenate(
            [
                narrow_sums.reshape(8, parts, a).transpose(1, 0, 2).reshape(parts, -1),
                wide_sums[:3].reshape(3, parts, b).transpose(1, 0, 2).reshape(parts, -1),
                pair_grad.reshape(parts, -1),
                table_sums[:HEADS].T.reshape(parts, -1),
            ],
            1,
        )
        owned = lax.psum(lax.psum_scatter(packed, "fsdp", scatter_dimension=0, tiled=True), "dp")[0]
        scale_grad = lax.psum(sums[8].reshape(HEADS, HEAD_DIM).sum(1), ("fsdp", "dp"))
        narrow_owned = owned[: 8 * a].reshape(8, a)
        edge = 8 * a
        wide_owned = owned[edge : edge + 3 * b].reshape(3, b)
        edge += 3 * b
        pair_owned = owned[edge : edge + 2 * a]
        edge += 2 * a
        table_owned = owned[edge:].reshape(TABLE // parts, HEADS)
    return (
        result, input_grad, qkv_owned, pair_owned, out_owned, narrow_owned[6], up_owned,
        wide_owned[0], down_owned, narrow_owned[7], narrow_owned[0], narrow_owned[1],
        narrow_owned[2], narrow_owned[3], narrow_owned[4], narrow_owned[5], wide_owned[1],
        wide_owned[2], scale_grad, table_owned,
    )


def solution(mesh):
    tokens = P(("fsdp", "dp"), None)
    sequences = P(("fsdp", "dp"))
    matrix = P("fsdp", "dp")
    vector = P("fsdp")
    table = P("fsdp", None)
    in_specs = (
        tokens, tokens, sequences, sequences, matrix, vector, matrix, vector, matrix, vector,
        matrix, vector, vector, vector, vector, vector, vector, vector, vector, vector, P(), table,
    )
    out_specs = (
        tokens, tokens, matrix, vector, matrix, vector, matrix, vector, matrix, vector, vector,
        vector, vector, vector, vector, vector, vector, vector, P(), table,
    )
    return jax.shard_map(body, mesh=mesh, in_specs=in_specs, out_specs=out_specs, check_vma=False)
```
